32 devices in a mesh: cluster: 4 (over z), sub: 8 (over y, x, core).
Axes of the slice: x: 2, y: 2, z: 4, core: 2. Of those that a mesh axis runs over, the one named last changes fastest.
Arguments:
- features: bfloat16 [12288, 256], P(('cluster', 'sub')), may hold values from -6 to 6
- grad_out: bfloat16 [12288, 256], P(('cluster', 'sub')), may hold values from -6 to 6
- w_self: bfloat16 [256, 256], replicated, may hold values from -0.375 to 0.375
- w_neigh: bfloat16 [256, 256], replicated, may hold values from -0.375 to 0.375
- bias: float32 [256], replicated, may hold values from -3 to 3
- tile_dst: int32 [768], P(('cluster', 'sub')), may hold values from 0 to 2
- tile_src: int32 [768], P(('cluster', 'sub')), may hold values from 0 to 14, as said below
- tile_weight: bfloat16 [768, 128, 128], P(('cluster', 'sub')), may hold values from 0 to 4
- recv_sub: int32 [32, 8], P(('cluster', 'sub')), may hold values from 0 to 1
- recv_cluster: int32 [32, 4], P(('cluster', 'sub')), may hold values from 0 to 1
Outputs:
- grad_features: bfloat16 [12288, 256], P(('cluster', 'sub'))
The draws below stay inside these ranges and needn't reach their ends.
Inputs may be any that keep to these rules, and one draw needn't show every extreme that they name: `tile_src`: within one partition's 24 tiles, each of the source-table entries 3 to 14 is named by exactly one tile; the other tiles name own blocks.
All inputs are finite; a program needn't handle non-finite values.
Results may differ from the reference program's by a relative error of at most 0.005.
Values may be sent and summed in bfloat16 or wider, within the bound.
No kernel may reach another device: no remote copies, remote signals or barrier semaphores. Data moves between devices by JAX's collectives and lax.ppermute only.
A program may use at most 64 MiB of HBM per device.

```python
import jax
import jax.numpy as jnp
from jax import lax

D = 256
BLK = 128
OWN_BLK = 3
LOCAL_TILES = 12
BND = 2
TILES = 24
NODES = 12288
N_CLUSTER = 4
N_SUB = 8
DEVICES = 32


def draw_tile_src(key, part):
    key = jax.random.fold_in(key, 11)
    keys = jax.random.split(key, DEVICES)

    def one_device(device_key):
        first_key, second_key = jax.random.split(device_key)
        local = jax.random.randint(first_key, (LOCAL_TILES,), 0, OWN_BLK, dtype=jnp.int32)
        slots = OWN_BLK + jnp.arange(N_SUB + N_CLUSTER, dtype=jnp.int32)
        return jax.random.permutation(second_key, jnp.concatenate([slots, local])).astype(jnp.int32)
    return jax.vmap(one_device)(keys).reshape(-1)


def draw_tile_weight(key, part):
    key = jax.random.fold_in(key, 23)
    keys = jax.random.split(key, DEVICES * TILES)

    def one_tile(tile_key):
        order_key, heavy_key, extra_key = jax.random.split(tile_key, 3)
        order = jax.random.permutation(order_key, BLK).astype(jnp.int32)
        heavy = jax.random.randint(heavy_key, (BLK,), 2, 4, dtype=jnp.int32)
        extra = (jax.random.randint(extra_key, (BLK, BLK), 0, 64, dtype=jnp.int32) == 0).astype(jnp.int32)
        pattern = (order[:, None] == jnp.arange(BLK, dtype=jnp.int32)[None, :]).astype(jnp.int32)
        return (extra + pattern * heavy[:, None]).astype(jnp.float32)
    return jax.vmap(one_tile)(keys).astype(jnp.bfloat16)


def with_ends(values, stream_key, least, top_value):
    spot = [jax.random.randint(jax.random.fold_in(stream_key, axis), (), 0, length) for axis, length in enumerate(values.shape)]
    longest = values.shape.index(max(values.shape))
    neighbour = spot[:longest] + [(spot[longest] + 1) % values.shape[longest]] + spot[longest + 1:]
    return values.at[tuple(spot)].set(least).at[tuple(neighbour)].set(top_value)


def shard_levels(rng, shape, shards, least, largest):
    gain, own = 1.0, jax.random.fold_in(rng, 6)
    for dim, shards_of in shards:
        steps = jnp.exp(jax.random.uniform(jax.random.fold_in(own, dim), (shards_of,), jnp.float32, least / len(shards), largest / len(shards)))
        gain = gain * jnp.repeat(steps, shape[dim] // shards_of).reshape([-1 if axis == dim else 1 for axis in range(len(shape))])
    return gain


def gaussian(rng, dims, scale, reach, pieces=(), kind=jnp.bfloat16):
    array = scale * jax.random.normal(rng, dims, jnp.float32)
    if pieces:
        array = array * shard_levels(rng, dims, pieces, -0.22, 0.18)
    return jnp.clip(array, -reach, reach).astype(kind)


def setup_inputs(seed: int = 0) -> dict:
    key_list = jax.random.split(jax.random.key(seed), 11)
    features = gaussian(key_list[0], (NODES, D), 1.0, 6.0, ((0, 32),))
    grad_out = gaussian(key_list[1], (NODES, D), 1.0, 6.0, ((0, 32),))
    w_self = gaussian(key_list[2], (D, D), D ** -0.5, 0.375)
    w_neigh = gaussian(key_list[3], (D, D), D ** -0.5, 0.375)
    bias = gaussian(key_list[4], (D,), 0.5, 3.0, (), jnp.float32)
    tile_dst = with_ends(jax.random.randint(key_list[5], (N_CLUSTER * N_SUB * TILES,), 0, OWN_BLK), jax.random.fold_in(key_list[5], 1), 0, OWN_BLK - 1).astype(jnp.int32)
    tile_src = draw_tile_src(jax.random.fold_in(key_list[10], 71), 0)
    tile_weight = draw_tile_weight(jax.random.fold_in(key_list[10], 71), 0)
    recv_sub = with_ends(jax.random.randint(key_list[8], (N_CLUSTER * N_SUB, N_SUB), 0, BND), jax.random.fold_in(key_list[8], 1), 0, BND - 1).astype(jnp.int32)
    recv_cluster = with_ends(jax.random.randint(key_list[9], (N_CLUSTER * N_SUB, N_CLUSTER), 0, BND), jax.random.fold_in(key_list[9], 1), 0, BND - 1).astype(jnp.int32)
    return dict(features=features, grad_out=grad_out, w_self=w_self, w_neigh=w_neigh, bias=bias, tile_dst=tile_dst, tile_src=tile_src, tile_weight=tile_weight, recv_sub=recv_sub, recv_cluster=recv_cluster)


def gelu_tanh(values):
    return 0.5 * values * (1.0 + jnp.tanh(0.7978845608028654 * (values + 0.044715 * values * values * values)))

def reference(features, grad_out, w_self, w_neigh, bias, tile_dst, tile_src, tile_weight, recv_sub, recv_cluster):
    device_count = N_CLUSTER * N_SUB
    source_count = OWN_BLK + N_SUB + N_CLUSTER
    blocks = features.reshape(device_count, OWN_BLK, BLK, D)
    upstream = grad_out.reshape(device_count, OWN_BLK * BLK, D)
    dst_all = tile_dst.reshape(device_count, TILES)
    src_all = tile_src.reshape(device_count, TILES)
    weight_all = tile_weight.reshape(device_count, TILES, BLK, BLK)

    def step(carry, device):
        cluster_id = device // N_SUB
        sub_id = device % N_SUB
        sub_peers = cluster_id * N_SUB + jnp.arange(N_SUB, dtype=jnp.int32)
        cluster_peers = jnp.arange(N_CLUSTER, dtype=jnp.int32) * N_SUB + sub_id
        halo_sub = blocks[sub_peers, recv_sub[device]]
        halo_cluster = blocks[cluster_peers, recv_cluster[device]]
        source = jnp.concatenate([blocks[device], halo_sub, halo_cluster], axis=0)
        counts = weight_all[device].astype(jnp.float32)
        dst_ids = dst_all[device]
        src_ids = src_all[device]
        picked = source[src_ids].astype(jnp.float32)
        products = jnp.einsum('tij,tjd->tid', counts, picked, precision=lax.Precision.HIGHEST)
        aggregate = jnp.zeros((OWN_BLK, BLK, D), jnp.float32).at[dst_ids].add(products)
        degree = jnp.zeros((OWN_BLK, BLK), jnp.float32).at[dst_ids].add(lax.optimization_barrier(jnp.sum(counts, axis=2)))
        inverse = 1.0 / (degree + 1.0)
        neighbour_mean = (aggregate * inverse[:, :, None]).astype(jnp.bfloat16).reshape(OWN_BLK * BLK, D)
        own_rows = blocks[device].reshape(OWN_BLK * BLK, D)
        pre = jnp.dot(own_rows, w_self, preferred_element_type=jnp.float32)
        pre = pre + jnp.dot(neighbour_mean, w_neigh, preferred_element_type=jnp.float32) + bias
        _, pullback = jax.vjp(gelu_tanh, pre)
        grad_pre = pullback(upstream[device].astype(jnp.float32))[0].astype(jnp.bfloat16)
        grad_self = jnp.dot(grad_pre, w_self.T, preferred_element_type=jnp.float32)
        spread = jnp.dot(grad_pre, w_neigh.T, preferred_element_type=jnp.float32).reshape(OWN_BLK, BLK, D)
        spread = (spread * inverse[:, :, None]).astype(jnp.bfloat16)
        returned = jnp.einsum('tij,tid->tjd', counts, spread[dst_ids].astype(jnp.float32), precision=lax.Precision.HIGHEST)
        partial_value = jnp.zeros((source_count, BLK, D), jnp.float32).at[src_ids].add(returned)
        remote = lax.optimization_barrier(partial_value[OWN_BLK:].astype(jnp.bfloat16)).astype(jnp.float32)
        carry = carry.at[device].add(partial_value[:OWN_BLK])
        carry = carry.at[sub_peers, recv_sub[device]].add(remote[:N_SUB])
        carry = carry.at[cluster_peers, recv_cluster[device]].add(remote[N_SUB:])
        return (carry, grad_self)
    start = jnp.zeros((device_count, OWN_BLK, BLK, D), jnp.float32)
    back, grad_self = lax.scan(step, start, jnp.arange(device_count, dtype=jnp.int32))
    total = grad_self.reshape(NODES, D) + back.reshape(NODES, D)
    return total.astype(jnp.bfloat16)
```

```python
import functools

import jax
import jax.numpy as jnp
from jax import lax
from jax.experimental import pallas as pl
from jax.experimental.pallas import tpu as pltpu
from jax.sharding import PartitionSpec as P

BF = jnp.bfloat16
F32 = jnp.float32
BOUNDARY = 2
VMEM = pl.BlockSpec(memory_space=pltpu.VMEM)
SMEM = pl.BlockSpec(memory_space=pltpu.SMEM)
PARAMS = pltpu.CompilerParams(vmem_limit_bytes=24 * 1024 * 1024)


def dot(left, right):
    return jnp.dot(left, right, preferred_element_type=F32)


def dot_right_transposed(left, right):
    return lax.dot_general(left, right, (((1,), (1,)), ((), ())), preferred_element_type=F32)


def gelu_slope(v):
    scale = 0.7978845608028654
    t = jnp.tanh(scale * (v + 0.044715 * v * v * v))
    return 0.5 * (1.0 + t) + (0.5 * scale) * v * (1.0 - t * t) * (1.0 + 3.0 * 0.044715 * v * v)


def prepare_kernel(
    own, sub_count, cluster_count,
    tile_dst, tile_src, features, w_self, bias, tile_weight,
    dense, dense_t, own_sum, own_pre, inverse,
):
    size = tile_weight.shape[1]
    sub_id = lax.axis_index("sub")
    cluster_id = lax.axis_index("cluster")
    dense[...] = jnp.zeros_like(dense)
    dense_t[...] = jnp.zeros_like(dense_t)

    def place(t, carry):
        src = tile_src[t]
        from_sub = own + ((src - own) ^ sub_id)
        from_cluster = own + sub_count + ((src - own - sub_count) ^ cluster_id)
        slot = jnp.where(src < own, src, jnp.where(src < own + sub_count, from_sub, from_cluster))
        dst = pl.ds(pl.multiple_of(tile_dst[t] * size, size), size)
        col = pl.ds(pl.multiple_of(slot * size, size), size)
        tile = tile_weight[t]
        dense[dst, col] = dense[dst, col] + tile
        dense_t[col, dst] = dense_t[col, dst] + tile.T
        return carry

    lax.fori_loop(0, tile_weight.shape[0], place, 0, unroll=4)
    slots = own + sub_count + cluster_count
    total = dense[:, 0:size].astype(F32)
    for slot in range(1, slots):
        total = total + dense[:, slot * size : (slot + 1) * size].astype(F32)
    degree = jnp.sum(total, axis=1, keepdims=True)
    inverse[...] = jnp.broadcast_to(1.0 / (degree + 1.0), inverse.shape)
    own_sum[...] = dot(dense[:, 0 : own * size], features[...])
    own_pre[...] = dot(features[...], w_self[...]) + bias[...]


def middle_kernel(
    own, sub_count, cluster_count,
    recv_sub, recv_cluster, features, grad_out, w_neigh, dense, dense_t, own_sum, own_pre, inverse,
    *rest,
):
    peers = sub_count + cluster_count - 2
    received = rest[:peers]
    sent = rest[peers : 2 * peers]
    kept, spread, grad_pre, halo = rest[2 * peers :]
    size = halo.shape[0] // (sub_count + cluster_count)
    sub_id = lax.axis_index("sub")
    cluster_id = lax.axis_index("cluster")

    def pick(slot, source, index):
        halo[slot * size : (slot + 1) * size, :] = source[
            pl.ds(pl.multiple_of(index * size, size), size), :
        ]

    for d in range(sub_count):
        pick(d, received[d - 1] if d else features, recv_sub[0, sub_id ^ d])
    for d in range(cluster_count):
        source = received[sub_count - 1 + d - 1] if d else features
        pick(sub_count + d, source, recv_cluster[0, cluster_id ^ d])
    inv = jnp.concatenate([inverse[...]] * (features.shape[1] // size), axis=1)
    aggregate = own_sum[...] + dot(dense[:, own * size :], halo[...])
    mean = (aggregate * inv).astype(BF)
    pre = own_pre[...] + dot(mean, w_neigh[...])
    grad = (grad_out[...].astype(F32) * gelu_slope(pre)).astype(BF)
    grad_pre[...] = grad
    spread[...] = (dot_right_transposed(grad, w_neigh[...]) * inv).astype(BF)

    def partial(slot):
        rows = slice((own + slot) * size, (own + slot + 1) * size)
        return dot(dense_t[rows, :], spread[...]).astype(BF)

    for d in range(sub_count):
        if d:
            sent[d - 1][...] = partial(d)
        else:
            kept[0] = partial(0)
    for d in range(cluster_count):
        if d:
            sent[sub_count - 1 + d - 1][...] = partial(sub_count + d)
        else:
            kept[1] = partial(sub_count)


def own_kernel(own, recv_sub, recv_cluster, w_self, dense_t, kept, spread, grad_pre, total):
    size = kept.shape[1]
    total[...] = dot_right_transposed(grad_pre[...], w_self[...]) + dot(
        dense_t[0 : own * size, :], spread[...]
    )
    for i, index in enumerate(
        (recv_sub[0, lax.axis_index("sub")], recv_cluster[0, lax.axis_index("cluster")])
    ):
        rows = pl.ds(pl.multiple_of(index * size, size), size)
        total[rows, :] = total[rows, :] + kept[i].astype(F32)


def final_kernel(sub_count, cluster_count, asked, total, *rest):
    peers = sub_count + cluster_count - 2
    received = rest[:peers]
    out, work = rest[peers:]
    size = received[0].shape[0]
    sub_id = lax.axis_index("sub")
    cluster_id = lax.axis_index("cluster")
    work[...] = total[...]

    def add(part, index):
        rows = pl.ds(pl.multiple_of(index * size, size), size)
        work[rows, :] = work[rows, :] + part[...].astype(F32)

    for d in range(1, sub_count):
        add(received[d - 1], asked[cluster_id * sub_count + (sub_id ^ d), sub_id])
    for d in range(1, cluster_count):
        add(
            received[sub_count - 1 + d - 1],
            asked[(cluster_id ^ d) * sub_count + sub_id, sub_count + cluster_id],
        )
    out[...] = work[...].astype(BF)


def swap(value, axis, count, d):
    return lax.ppermute(value, axis, [(i, i ^ d) for i in range(count)])


def exchange(values, sub_count, cluster_count):
    got = [swap(values[d - 1], "sub", sub_count, d) for d in range(1, sub_count)]
    rest = values[sub_count - 1 :]
    got += [swap(rest[d - 1], "cluster", cluster_count, d) for d in range(1, cluster_count)]
    return got


def cost(flops, moved):
    return pl.CostEstimate(flops=flops, bytes_accessed=moved, transcendentals=0)


def shards(
    features, grad_out, w_self, w_neigh, bias, tile_dst, tile_src, tile_weight, recv_sub, recv_cluster
):
    sub_count = lax.axis_size("sub")
    cluster_count = lax.axis_size("cluster")
    peers = sub_count + cluster_count - 2
    size = tile_weight.shape[1]
    rows, width = features.shape
    own = rows // size
    slots = own + sub_count + cluster_count
    counts = (own, sub_count, cluster_count)

    asked = lax.all_gather(
        jnp.concatenate([recv_sub, recv_cluster], axis=1), ("cluster", "sub"), axis=0, tiled=True
    )
    edge = features[: BOUNDARY * size]
    halos = exchange([edge] * peers, sub_count, cluster_count)

    wide = jax.ShapeDtypeStruct((rows, width), F32)
    narrow = jax.ShapeDtypeStruct((rows, width), BF)
    block = jax.ShapeDtypeStruct((size, width), BF)
    dense, dense_t, own_sum, own_pre, inverse = pl.pallas_call(
        functools.partial(prepare_kernel, *counts),
        out_shape=[
            jax.ShapeDtypeStruct((rows, slots * size), BF),
            jax.ShapeDtypeStruct((slots * size, rows), BF),
            wide,
            wide,
            jax.ShapeDtypeStruct((rows, size), F32),
        ],
        in_specs=[SMEM, SMEM, VMEM, VMEM, VMEM, VMEM],
        out_specs=[VMEM] * 5,
        compiler_params=PARAMS,
        cost_estimate=cost(2 * rows * rows * width * 2, 6 * 1024 * 1024),
        name="prepare",
    )(tile_dst, tile_src, features, w_self, bias.reshape(1, width), tile_weight)

    outs = pl.pallas_call(
        functools.partial(middle_kernel, *counts),
        out_shape=[block] * peers + [jax.ShapeDtypeStruct((2, size, width), BF), narrow, narrow],
        in_specs=[SMEM, SMEM] + [VMEM] * (8 + peers),
        out_specs=[VMEM] * (peers + 3),
        scratch_shapes=[pltpu.VMEM(((sub_count + cluster_count) * size, width), BF)],
        compiler_params=PARAMS,
        cost_estimate=cost(4 * rows * slots * size * width, 6 * 1024 * 1024),
        name="middle",
    )(
        recv_sub, recv_cluster, features, grad_out, w_neigh,
        dense, dense_t, own_sum, own_pre, inverse, *halos,
    )
    sent, (kept, spread, grad_pre) = outs[:peers], outs[peers:]
    returned = exchange(sent, sub_count, cluster_count)

    total = pl.pallas_call(
        functools.partial(own_kernel, own),
        out_shape=wide,
        in_specs=[SMEM, SMEM] + [VMEM] * 5,
        out_specs=VMEM,
        compiler_params=PARAMS,
        cost_estimate=cost(4 * rows * rows * width, 2 * 1024 * 1024),
        name="own",
    )(recv_sub, recv_cluster, w_self, dense_t, kept, spread, grad_pre)

    return pl.pallas_call(
        functools.partial(final_kernel, sub_count, cluster_count),
        out_shape=narrow,
        in_specs=[SMEM, VMEM] + [VMEM] * peers,
        out_specs=VMEM,
        scratch_shapes=[pltpu.VMEM((rows, width), F32)],
        compiler_params=PARAMS,
        cost_estimate=cost(rows * width * 4, 2 * 1024 * 1024),
        name="final",
    )(asked, total, *returned)


def solution(mesh):
    placed = (
        P(("cluster", "sub"), None),
        P(("cluster", "sub"), None),
        P(),
        P(),
        P(),
        P(("cluster", "sub")),
        P(("cluster", "sub")),
        P(("cluster", "sub"), None, None),
        P(("cluster", "sub"), None),
        P(("cluster", "sub"), None),
    )
    return jax.shard_map(
        shards, mesh=mesh, in_specs=placed, out_specs=P(("cluster", "sub"), None), check_vma=False
    )
```

```python
import functools

import jax
import jax.numpy as jnp
from jax import lax
from jax.experimental import pallas as pl
from jax.experimental.pallas import tpu as pltpu
from jax.sharding import PartitionSpec as P

BF = jnp.bfloat16
F32 = jnp.float32
BOUNDARY = 2
EXTRA = 16
VMEM = pl.BlockSpec(memory_space=pltpu.VMEM)
HBM = pl.BlockSpec(memory_space=pltpu.HBM)
PARAMS = pltpu.CompilerParams(vmem_limit_bytes=24 * 1024 * 1024)


def dot(left, right):
    return jnp.dot(left, right, preferred_element_type=F32)


def dot_right_transposed(left, right):
    return lax.dot_general(left, right, (((1,), (1,)), ((), ())), preferred_element_type=F32)


def gelu_slope(v):
    scale = 0.7978845608028654
    t = jnp.tanh(scale * (v + 0.044715 * v * v * v))
    return 0.5 * (1.0 + t) + (0.5 * scale) * v * (1.0 - t * t) * (1.0 + 3.0 * 0.044715 * v * v)


def edge_kernel(recv_sub, recv_cluster, features, edge, rows, sub_row, cluster_row, sems):
    count = rows.shape[0]
    copies = [
        pltpu.make_async_copy(recv_sub, sub_row, sems.at[0]),
        pltpu.make_async_copy(recv_cluster, cluster_row, sems.at[1]),
        pltpu.make_async_copy(features.at[0:count, :], rows, sems.at[2]),
    ]
    for copy in copies:
        copy.start()
    for copy in copies:
        copy.wait()
    edge[0:count, :] = rows[...]
    sub_count, cluster_count = sub_row.shape[1], cluster_row.shape[1]
    pad = jnp.zeros((1, edge.shape[1] - sub_count - cluster_count), F32)
    row = jnp.concatenate([sub_row[...].astype(F32), cluster_row[...].astype(F32), pad], axis=1)
    edge[count:, :] = jnp.broadcast_to(row, (EXTRA, edge.shape[1])).astype(BF)


def prepare_kernel(
    own, sub_count, cluster_count,
    tile_dst_hbm, tile_src_hbm, recv_sub_hbm, recv_cluster_hbm, features_hbm, w_self_hbm, bias,
    tile_weight_hbm, grad_out_hbm, w_neigh_hbm,
    dense, dense_t, own_sum, own_pre, inverse, choice, w_self, w_neigh, grad_out,
    tile_dst, tile_src, recv_sub, recv_cluster, features, tile_weight, sems,
):
    size = tile_weight.shape[1]
    pairs = (
        (tile_dst_hbm, tile_dst), (tile_src_hbm, tile_src), (recv_sub_hbm, recv_sub),
        (recv_cluster_hbm, recv_cluster), (tile_weight_hbm, tile_weight),
        (features_hbm, features), (w_self_hbm, w_self), (w_neigh_hbm, w_neigh),
        (grad_out_hbm, grad_out),
    )
    copies = [pltpu.make_async_copy(a, b, sems.at[i]) for i, (a, b) in enumerate(pairs)]
    for copy in copies:
        copy.start()
    sub_id = lax.axis_index("sub")
    cluster_id = lax.axis_index("cluster")
    dense[...] = jnp.zeros_like(dense)
    dense_t[...] = jnp.zeros_like(dense_t)
    for copy in copies[:5]:
        copy.wait()

    def place(t, carry):
        src = tile_src[t]
        from_sub = own + ((src - own) ^ sub_id)
        from_cluster = own + sub_count + ((src - own - sub_count) ^ cluster_id)
        slot = jnp.where(src < own, src, jnp.where(src < own + sub_count, from_sub, from_cluster))
        dst = pl.ds(pl.multiple_of(tile_dst[t] * size, size), size)
        col = pl.ds(pl.multiple_of(slot * size, size), size)
        tile = tile_weight[t]
        dense[dst, col] = dense[dst, col] + tile
        dense_t[col, dst] = dense_t[col, dst] + tile.T
        return carry

    lax.fori_loop(0, tile_weight.shape[0], place, 0, unroll=4)
    for d in range(sub_count):
        index = recv_sub[0, sub_id ^ d].astype(F32)
        choice[d : d + 1, :] = jnp.full((1, choice.shape[1]), index, F32)
    for d in range(cluster_count):
        index = recv_cluster[0, cluster_id ^ d].astype(F32)
        choice[sub_count + d : sub_count + d + 1, :] = jnp.full((1, choice.shape[1]), index, F32)
    slots = own + sub_count + cluster_count
    total = dense[:, 0:size].astype(F32)
    for slot in range(1, slots):
        total = total + dense[:, slot * size : (slot + 1) * size].astype(F32)
    degree = jnp.sum(total, axis=1, keepdims=True)
    inverse[...] = jnp.broadcast_to(1.0 / (degree + 1.0), inverse.shape)
    for copy in copies[5:]:
        copy.wait()
    own_sum[...] = dot(dense[:, 0 : own * size], features[...])
    own_pre[...] = dot(features[...], w_self[...]) + bias[...]


def middle_kernel(
    own, sub_count, cluster_count,
    choice, edge, grad_out, w_neigh, dense, dense_t, own_sum, own_pre, inverse,
    *rest,
):
    peers = sub_count + cluster_count - 2
    received = rest[:peers]
    sent = rest[peers : 2 * peers]
    kept, spread, grad_pre, halo = rest[2 * peers :]
    size = halo.shape[0] // (sub_count + cluster_count)

    def pick(slot, source):
        second = choice[slot : slot + 1, :] > 0.5
        halo[slot * size : (slot + 1) * size, :] = jnp.where(
            second, source[size : 2 * size, :].astype(F32), source[0:size, :].astype(F32)
        ).astype(BF)

    for d in range(sub_count):
        pick(d, received[d - 1] if d else edge)
    for d in range(cluster_count):
        pick(sub_count + d, received[sub_count - 1 + d - 1] if d else edge)
    inv = jnp.concatenate([inverse[...]] * (edge.shape[1] // size), axis=1)
    aggregate = own_sum[...] + dot(dense[:, own * size :], halo[...])
    mean = (aggregate * inv).astype(BF)
    pre = own_pre[...] + dot(mean, w_neigh[...])
    grad = (grad_out[...].astype(F32) * gelu_slope(pre)).astype(BF)
    grad_pre[...] = grad
    spread[...] = (dot_right_transposed(grad, w_neigh[...]) * inv).astype(BF)

    def partial(slot):
        rows = slice((own + slot) * size, (own + slot + 1) * size)
        return dot(dense_t[rows, :], spread[...]).astype(BF)

    for d in range(sub_count):
        if d:
            sent[d - 1][...] = partial(d)
        else:
            kept[0] = partial(0)
    for d in range(cluster_count):
        if d:
            sent[sub_count - 1 + d - 1][...] = partial(sub_count + d)
        else:
            kept[1] = partial(sub_count)


def split(total, value, second, size):
    zero = jnp.zeros_like(value)
    total[0:size, :] = total[0:size, :] + jnp.where(second, zero, value)
    total[size : 2 * size, :] = total[size : 2 * size, :] + jnp.where(second, value, zero)


def own_kernel(
    own, sub_count, cluster_count, choice, w_self, dense_t, kept, spread, grad_pre, *rest
):
    received, (total, owner) = rest[:-2], rest[-2:]
    size = kept.shape[1]
    width = total.shape[1]
    total[...] = dot_right_transposed(grad_pre[...], w_self[...]) + dot(
        dense_t[0 : own * size, :], spread[...]
    )
    for i, slot in enumerate((0, sub_count)):
        split(total, kept[i].astype(F32), choice[slot : slot + 1, :] > 0.5, size)
    lanes = lax.broadcasted_iota(jnp.int32, (1, width), 1)
    for i, message in enumerate(received):
        row = message[BOUNDARY * size : BOUNDARY * size + EXTRA, :].astype(F32)[0:1, :]
        if i < sub_count - 1:
            lane = lax.axis_index("sub")
        else:
            lane = sub_count + lax.axis_index("cluster")
        index = jnp.sum(jnp.where(lanes == lane, row, 0.0), axis=1, keepdims=True)
        owner[i : i + 1, :] = jnp.broadcast_to(index, (1, width))


def final_kernel(owner, total, *rest):
    received, out = rest[:-1], rest[-1]
    size = received[0].shape[0]
    first = total[0:size, :]
    second = total[size : 2 * size, :]
    for i, message in enumerate(received):
        value = message[...].astype(F32)
        to_second = owner[i : i + 1, :] > 0.5
        first = first + jnp.where(to_second, 0.0, value)
        second = second + jnp.where(to_second, value, 0.0)
    out[0:size, :] = first.astype(BF)
    out[size : 2 * size, :] = second.astype(BF)
    out[2 * size :, :] = total[2 * size :, :].astype(BF)


def swap(value, axis, count, d):
    return lax.ppermute(value, axis, [(i, i ^ d) for i in range(count)])


def gather_edges(edge, sub_count, cluster_count):
    by_cluster = [edge]
    for d in range(1, cluster_count):
        low = d & -d
        by_cluster.append(swap(by_cluster[d - low], "cluster", cluster_count, low))
    by_sub = [edge]
    for d in range(1, sub_count):
        if d % 2:
            by_sub.append(swap(by_sub[d - 1], "sub", sub_count, 1))
        else:
            by_sub.append(swap(edge, "sub", sub_count, d))
    return by_sub[1:] + by_cluster[1:]


def send_back(values, sub_count, cluster_count):
    got = [swap(values[d - 1], "sub", sub_count, d) for d in range(1, sub_count)]
    rest = values[sub_count - 1 :]
    got += [swap(rest[d - 1], "cluster", cluster_count, d) for d in range(1, cluster_count)]
    return got


def cost(flops, moved):
    return pl.CostEstimate(flops=flops, bytes_accessed=moved, transcendentals=0)


def shards(
    features, grad_out, w_self, w_neigh, bias, tile_dst, tile_src, tile_weight, recv_sub, recv_cluster
):
    sub_count = lax.axis_size("sub")
    cluster_count = lax.axis_size("cluster")
    peers = sub_count + cluster_count - 2
    size = tile_weight.shape[1]
    rows, width = features.shape
    own = rows // size
    slots = own + sub_count + cluster_count
    counts = (own, sub_count, cluster_count)

    wide = jax.ShapeDtypeStruct((rows, width), F32)
    narrow = jax.ShapeDtypeStruct((rows, width), BF)
    square = jax.ShapeDtypeStruct((width, width), BF)
    block = jax.ShapeDtypeStruct((size, width), BF)
    marks = jax.ShapeDtypeStruct((sub_count + cluster_count, width), F32)

    edge = pl.pallas_call(
        edge_kernel,
        out_shape=jax.ShapeDtypeStruct((BOUNDARY * size + EXTRA, width), BF),
        in_specs=[HBM] * 3,
        out_specs=VMEM,
        scratch_shapes=[
            pltpu.VMEM((BOUNDARY * size, width), BF),
            pltpu.VMEM(recv_sub.shape, jnp.int32),
            pltpu.VMEM(recv_cluster.shape, jnp.int32),
            pltpu.SemaphoreType.DMA((3,)),
        ],
        compiler_params=PARAMS,
        cost_estimate=cost(1024, 256 * 1024),
        name="edge",
    )(recv_sub, recv_cluster, features)
    halos = gather_edges(edge, sub_count, cluster_count)

    dense, dense_t, own_sum, own_pre, inverse, choice, w_self, w_neigh, grad_out = pl.pallas_call(
        functools.partial(prepare_kernel, *counts),
        out_shape=[
            jax.ShapeDtypeStruct((rows, slots * size), BF),
            jax.ShapeDtypeStruct((slots * size, rows), BF),
            wide,
            wide,
            jax.ShapeDtypeStruct((rows, size), F32),
            marks,
            square,
            square,
            narrow,
        ],
        in_specs=[HBM] * 6 + [VMEM] + [HBM] * 3,
        out_specs=[VMEM] * 9,
        scratch_shapes=[
            pltpu.SMEM(tile_dst.shape, jnp.int32),
            pltpu.SMEM(tile_src.shape, jnp.int32),
            pltpu.SMEM(recv_sub.shape, jnp.int32),
            pltpu.SMEM(recv_cluster.shape, jnp.int32),
            pltpu.VMEM(features.shape, BF),
            pltpu.VMEM(tile_weight.shape, BF),
            pltpu.SemaphoreType.DMA((9,)),
        ],
        compiler_params=PARAMS,
        cost_estimate=cost(2 * rows * rows * width * 2, 6 * 1024 * 1024),
        name="prepare",
    )(
        tile_dst, tile_src, recv_sub, recv_cluster, features, w_self, bias.reshape(1, width),
        tile_weight, grad_out, w_neigh,
    )

    outs = pl.pallas_call(
        functools.partial(middle_kernel, *counts),
        out_shape=[block] * peers + [jax.ShapeDtypeStruct((2, size, width), BF), narrow, narrow],
        in_specs=[VMEM] * (9 + peers),
        out_specs=[VMEM] * (peers + 3),
        scratch_shapes=[pltpu.VMEM(((sub_count + cluster_count) * size, width), BF)],
        compiler_params=PARAMS,
        cost_estimate=cost(4 * rows * slots * size * width, 6 * 1024 * 1024),
        name="middle",
    )(choice, edge, grad_out, w_neigh, dense, dense_t, own_sum, own_pre, inverse, *halos)
    sent, (kept, spread, grad_pre) = outs[:peers], outs[peers:]
    returned = send_back(sent, sub_count, cluster_count)

    total, owner = pl.pallas_call(
        functools.partial(own_kernel, *counts),
        out_shape=[wide, marks],
        in_specs=[VMEM] * (6 + peers),
        out_specs=[VMEM] * 2,
        compiler_params=PARAMS,
        cost_estimate=cost(4 * rows * rows * width, 2 * 1024 * 1024),
        name="own",
    )(choice, w_self, dense_t, kept, spread, grad_pre, *halos)

    return pl.pallas_call(
        final_kernel,
        out_shape=narrow,
        in_specs=[VMEM] * (2 + peers),
        out_specs=VMEM,
        compiler_params=PARAMS,
        cost_estimate=cost(rows * width * 4, 2 * 1024 * 1024),
        name="final",
    )(owner, total, *returned)


def solution(mesh):
    placed = (
        P(("cluster", "sub"), None),
        P(("cluster", "sub"), None),
        P(),
        P(),
        P(),
        P(("cluster", "sub")),
        P(("cluster", "sub")),
        P(("cluster", "sub"), None, None),
        P(("cluster", "sub"), None),
        P(("cluster", "sub"), None),
    )
    return jax.shard_map(
        shards, mesh=mesh, in_specs=placed, out_specs=P(("cluster", "sub"), None), check_vma=False
    )
```

```python
import functools

import jax
import jax.numpy as jnp
from jax import lax
from jax.experimental import pallas as pl
from jax.experimental.pallas import tpu as pltpu
from jax.sharding import PartitionSpec as P

BF = jnp.bfloat16
F32 = jnp.float32
BOUNDARY = 2
EXTRA = 16
VMEM = pl.BlockSpec(memory_space=pltpu.VMEM)
HBM = pl.BlockSpec(memory_space=pltpu.HBM)
PARAMS = pltpu.CompilerParams(vmem_limit_bytes=24 * 1024 * 1024)


def dot(left, right):
    return jnp.dot(left, right, preferred_element_type=F32)


def dot_right_transposed(left, right):
    return lax.dot_general(left, right, (((1,), (1,)), ((), ())), preferred_element_type=F32)


def gelu_slope(v):
    scale = 0.7978845608028654
    t = jnp.tanh(scale * (v + 0.044715 * v * v * v))
    return 0.5 * (1.0 + t) + (0.5 * scale) * v * (1.0 - t * t) * (1.0 + 3.0 * 0.044715 * v * v)


def edge_kernel(recv_sub, recv_cluster, features, edge, sub_row, cluster_row, sems):
    count = edge.shape[0] - EXTRA
    copies = [
        pltpu.make_async_copy(features.at[0:count, :], edge.at[0:count, :], sems.at[0]),
        pltpu.make_async_copy(recv_sub, sub_row, sems.at[1]),
        pltpu.make_async_copy(recv_cluster, cluster_row, sems.at[2]),
    ]
    for copy in copies:
        copy.start()
    for copy in copies:
        copy.wait()
    sub_count, cluster_count = sub_row.shape[1], cluster_row.shape[1]
    pad = jnp.zeros((1, edge.shape[1] - sub_count - cluster_count), F32)
    row = jnp.concatenate([sub_row[...].astype(F32), cluster_row[...].astype(F32), pad], axis=1)
    edge[count:, :] = jnp.broadcast_to(row, (EXTRA, edge.shape[1])).astype(BF)


def prepare_kernel(
    own, sub_count, cluster_count,
    tile_dst_hbm, tile_src_hbm, recv_sub_hbm, recv_cluster_hbm, features_hbm, w_self_hbm, bias_hbm,
    tile_weight_hbm, grad_out_hbm, w_neigh_hbm,
    dense, dense_t, own_sum, own_pre, inverse, choice, w_self, w_neigh, grad_out,
    tile_dst, tile_src, recv_sub, recv_cluster, features, tile_weight, bias, sems,
):
    size = tile_weight.shape[1]
    pairs = (
        (tile_dst_hbm, tile_dst), (tile_src_hbm, tile_src), (recv_sub_hbm, recv_sub),
        (recv_cluster_hbm, recv_cluster), (tile_weight_hbm, tile_weight),
        (features_hbm, features), (w_self_hbm, w_self), (w_neigh_hbm, w_neigh),
        (grad_out_hbm, grad_out), (bias_hbm, bias),
    )
    copies = [pltpu.make_async_copy(a, b, sems.at[i]) for i, (a, b) in enumerate(pairs)]
    for copy in copies:
        copy.start()
    sub_id = lax.axis_index("sub")
    cluster_id = lax.axis_index("cluster")
    dense[...] = jnp.zeros_like(dense)
    dense_t[...] = jnp.zeros_like(dense_t)
    for copy in copies[:5]:
        copy.wait()

    def place(t, carry):
        src = tile_src[t]
        from_sub = own + ((src - own) ^ sub_id)
        from_cluster = own + sub_count + ((src - own - sub_count) ^ cluster_id)
        slot = jnp.where(src < own, src, jnp.where(src < own + sub_count, from_sub, from_cluster))
        dst = pl.ds(pl.multiple_of(tile_dst[t] * size, size), size)
        col = pl.ds(pl.multiple_of(slot * size, size), size)
        tile = tile_weight[t]
        dense[dst, col] = dense[dst, col] + tile
        dense_t[col, dst] = dense_t[col, dst] + tile.T
        return carry

    lax.fori_loop(0, tile_weight.shape[0], place, 0, unroll=4)
    for d in range(sub_count):
        index = recv_sub[0, sub_id ^ d].astype(F32)
        choice[d : d + 1, :] = jnp.full((1, choice.shape[1]), index, F32)
    for d in range(cluster_count):
        index = recv_cluster[0, cluster_id ^ d].astype(F32)
        choice[sub_count + d : sub_count + d + 1, :] = jnp.full((1, choice.shape[1]), index, F32)
    slots = own + sub_count + cluster_count
    total = dense[:, 0:size].astype(F32)
    for slot in range(1, slots):
        total = total + dense[:, slot * size : (slot + 1) * size].astype(F32)
    degree = jnp.sum(total, axis=1, keepdims=True)
    inverse[...] = jnp.broadcast_to(1.0 / (degree + 1.0), inverse.shape)
    for copy in copies[5:]:
        copy.wait()
    own_sum[...] = dot(dense[:, 0 : own * size], features[...])
    own_pre[...] = dot(features[...], w_self[...]) + bias[...].reshape(1, -1)


def middle_kernel(
    own, order, sent_order, sub_count,
    choice, edge, grad_out, w_neigh, dense, dense_t, own_sum, own_pre, inverse,
    *rest,
):
    peers = len(order)
    received = rest[:peers]
    sent = rest[peers : 2 * peers]
    kept, spread, grad_pre, halo = rest[2 * peers :]
    size = halo.shape[0] // (peers + 2)

    def pick(slot, source):
        second = choice[slot : slot + 1, :] > 0.5
        halo[slot * size : (slot + 1) * size, :] = jnp.where(
            second, source[size : 2 * size, :].astype(F32), source[0:size, :].astype(F32)
        ).astype(BF)

    pick(0, edge)
    pick(sub_count, edge)
    for source, slot in zip(received, order):
        pick(slot, source)
    inv = jnp.concatenate([inverse[...]] * (edge.shape[1] // size), axis=1)
    aggregate = own_sum[...] + dot(dense[:, own * size :], halo[...])
    mean = (aggregate * inv).astype(BF)
    pre = own_pre[...] + dot(mean, w_neigh[...])
    grad = (grad_out[...].astype(F32) * gelu_slope(pre)).astype(BF)
    grad_pre[...] = grad
    spread[...] = (dot_right_transposed(grad, w_neigh[...]) * inv).astype(BF)

    def partial(slot):
        rows = slice((own + slot) * size, (own + slot + 1) * size)
        return dot(dense_t[rows, :], spread[...]).astype(BF)

    for target, slot in zip(sent, sent_order):
        target[...] = partial(slot)
    kept[0] = partial(0)
    kept[1] = partial(sub_count)


def split(total, value, second, size):
    zero = jnp.zeros_like(value)
    total[0:size, :] = total[0:size, :] + jnp.where(second, zero, value)
    total[size : 2 * size, :] = total[size : 2 * size, :] + jnp.where(second, value, zero)


def own_kernel(
    own, order, sub_count, choice, w_self, dense_t, kept, spread, grad_pre, *rest
):
    received, (total, owner) = rest[:-2], rest[-2:]
    size = kept.shape[1]
    width = total.shape[1]
    total[...] = dot_right_transposed(grad_pre[...], w_self[...]) + dot(
        dense_t[0 : own * size, :], spread[...]
    )
    for i, slot in enumerate((0, sub_count)):
        split(total, kept[i].astype(F32), choice[slot : slot + 1, :] > 0.5, size)
    lanes = lax.broadcasted_iota(jnp.int32, (1, width), 1)
    for message, slot in zip(received, order):
        row = message[BOUNDARY * size : BOUNDARY * size + EXTRA, :].astype(F32)[0:1, :]
        if slot < sub_count:
            lane = lax.axis_index("sub")
        else:
            lane = sub_count + lax.axis_index("cluster")
        index = jnp.sum(jnp.where(lanes == lane, row, 0.0), axis=1, keepdims=True)
        owner[slot : slot + 1, :] = jnp.broadcast_to(index, (1, width))


def final_kernel(order, owner, total, *rest):
    received, out = rest[:-1], rest[-1]
    size = received[0].shape[0]
    first = total[0:size, :]
    second = total[size : 2 * size, :]
    for message, slot in zip(received, order):
        value = message[...].astype(F32)
        to_second = owner[slot : slot + 1, :] > 0.5
        first = first + jnp.where(to_second, 0.0, value)
        second = second + jnp.where(to_second, value, 0.0)
    out[0:size, :] = first.astype(BF)
    out[size : 2 * size, :] = second.astype(BF)
    out[2 * size :, :] = total[2 * size :, :].astype(BF)


def swap(value, axis, count, d):
    return lax.ppermute(value, axis, [(i, i ^ d) for i in range(count)])


def gather_edges(edge, prepared, sub_count, cluster_count):
    def relay(value):
        return lax.optimization_barrier((value, prepared))[0]

    got = {0: edge, sub_count: edge}
    for d in range(1, cluster_count):
        low = d & -d
        value = edge if d == low else relay(got[sub_count + d - low])
        got[sub_count + d] = swap(value, "cluster", cluster_count, low)
    for d in range(1, sub_count):
        if d % 2:
            got[d] = swap(relay(got[d - 1]), "sub", sub_count, 1)
        else:
            got[d] = swap(edge, "sub", sub_count, d)
    return got


def peer_orders(sub_count, cluster_count):
    along = [sub_count + d for d in range(1, cluster_count)]
    direct = [sub_count + d for d in range(1, cluster_count) if not d & (d - 1)]
    relayed = [sub_count + d for d in range(1, cluster_count) if d & (d - 1)]
    even = list(range(2, sub_count, 2))
    odd = list(range(3, sub_count, 2))
    return [1] + odd + even + relayed + direct, along[::-1] + even[::-1] + odd[::-1] + [1]


def send_back(value, slot, sub_count, cluster_count):
    if slot < sub_count:
        return swap(value, "sub", sub_count, slot)
    return swap(value, "cluster", cluster_count, slot - sub_count)


def in_hbm(value):
    return pltpu.with_memory_space_constraint(value, pltpu.HBM)


def cost(flops, moved):
    return pl.CostEstimate(flops=flops, bytes_accessed=moved, transcendentals=0)


def shards(
    features, grad_out, w_self, w_neigh, bias, tile_dst, tile_src, tile_weight, recv_sub, recv_cluster
):
    sub_count = lax.axis_size("sub")
    cluster_count = lax.axis_size("cluster")
    peers = sub_count + cluster_count - 2
    size = tile_weight.shape[1]
    rows, width = features.shape
    own = rows // size
    slots = own + sub_count + cluster_count
    counts = (own, sub_count, cluster_count)
    order, sent_order = peer_orders(sub_count, cluster_count)

    wide = jax.ShapeDtypeStruct((rows, width), F32)
    narrow = jax.ShapeDtypeStruct((rows, width), BF)
    square = jax.ShapeDtypeStruct((width, width), BF)
    block = jax.ShapeDtypeStruct((size, width), BF)
    marks = jax.ShapeDtypeStruct((sub_count + cluster_count, width), F32)

    edge = pl.pallas_call(
        edge_kernel,
        out_shape=jax.ShapeDtypeStruct((BOUNDARY * size + EXTRA, width), BF),
        in_specs=[HBM] * 3,
        out_specs=VMEM,
        scratch_shapes=[
            pltpu.VMEM(recv_sub.shape, jnp.int32),
            pltpu.VMEM(recv_cluster.shape, jnp.int32),
            pltpu.SemaphoreType.DMA((3,)),
        ],
        compiler_params=PARAMS,
        cost_estimate=cost(1024, 256 * 1024),
        name="edge",
    )(in_hbm(recv_sub), in_hbm(recv_cluster), in_hbm(features))

    dense, dense_t, own_sum, own_pre, inverse, choice, w_self, w_neigh, grad_out = pl.pallas_call(
        functools.partial(prepare_kernel, *counts),
        out_shape=[
            jax.ShapeDtypeStruct((rows, slots * size), BF),
            jax.ShapeDtypeStruct((slots * size, rows), BF),
            wide,
            wide,
            jax.ShapeDtypeStruct((rows, size), F32),
            marks,
            square,
            square,
            narrow,
        ],
        in_specs=[HBM] * 10,
        out_specs=[VMEM] * 9,
        scratch_shapes=[
            pltpu.SMEM(tile_dst.shape, jnp.int32),
            pltpu.SMEM(tile_src.shape, jnp.int32),
            pltpu.SMEM(recv_sub.shape, jnp.int32),
            pltpu.SMEM(recv_cluster.shape, jnp.int32),
            pltpu.VMEM(features.shape, BF),
            pltpu.VMEM(tile_weight.shape, BF),
            pltpu.VMEM(bias.shape, F32),
            pltpu.SemaphoreType.DMA((10,)),
        ],
        compiler_params=PARAMS,
        cost_estimate=cost(2 * rows * rows * width * 2, 6 * 1024 * 1024),
        name="prepare",
    )(
        *map(in_hbm, (tile_dst, tile_src, recv_sub, recv_cluster, features, w_self, bias)),
        *map(in_hbm, (tile_weight, grad_out, w_neigh)),
    )
    got = gather_edges(edge, choice, sub_count, cluster_count)
    halos = [got[slot] for slot in order]

    outs = pl.pallas_call(
        functools.partial(middle_kernel, own, order, sent_order, sub_count),
        out_shape=[block] * peers + [jax.ShapeDtypeStruct((2, size, width), BF), narrow, narrow],
        in_specs=[VMEM] * (9 + peers),
        out_specs=[VMEM] * (peers + 3),
        scratch_shapes=[pltpu.VMEM(((sub_count + cluster_count) * size, width), BF)],
        compiler_params=PARAMS,
        cost_estimate=cost(4 * rows * slots * size * width, 6 * 1024 * 1024),
        name="middle",
    )(choice, edge, grad_out, w_neigh, dense, dense_t, own_sum, own_pre, inverse, *halos)
    sent, (kept, spread, grad_pre) = outs[:peers], outs[peers:]
    returned = [
        send_back(value, slot, sub_count, cluster_count) for value, slot in zip(sent, sent_order)
    ]

    total, owner = pl.pallas_call(
        functools.partial(own_kernel, own, order, sub_count),
        out_shape=[wide, marks],
        in_specs=[VMEM] * (6 + peers),
        out_specs=[VMEM] * 2,
        compiler_params=PARAMS,
        cost_estimate=cost(4 * rows * rows * width, 2 * 1024 * 1024),
        name="own",
    )(choice, w_self, dense_t, kept, spread, grad_pre, *halos)

    return pl.pallas_call(
        functools.partial(final_kernel, sent_order),
        out_shape=narrow,
        in_specs=[VMEM] * (2 + peers),
        out_specs=VMEM,
        compiler_params=PARAMS,
        cost_estimate=cost(rows * width * 4, 2 * 1024 * 1024),
        name="final",
    )(owner, total, *returned)


def solution(mesh):
    placed = (
        P(("cluster", "sub"), None),
        P(("cluster", "sub"), None),
        P(),
        P(),
        P(),
        P(("cluster", "sub")),
        P(("cluster", "sub")),
        P(("cluster", "sub"), None, None),
        P(("cluster", "sub"), None),
        P(("cluster", "sub"), None),
    )
    return jax.shard_map(
        shards, mesh=mesh, in_specs=placed, out_specs=P(("cluster", "sub"), None), check_vma=False
    )
```

```python
import functools

import jax
import jax.numpy as jnp
from jax import lax
from jax.experimental import pallas as pl
from jax.experimental.pallas import tpu as pltpu
from jax.sharding import PartitionSpec as P

BF = jnp.bfloat16
F32 = jnp.float32
BOUNDARY = 2
EXTRA = 16
VMEM = pl.BlockSpec(memory_space=pltpu.VMEM)
HBM = pl.BlockSpec(memory_space=pltpu.HBM)
PARAMS = pltpu.CompilerParams(vmem_limit_bytes=24 * 1024 * 1024)


def dot(left, right):
    return jnp.dot(left, right, preferred_element_type=F32)


def dot_right_transposed(left, right):
    return lax.dot_general(left, right, (((1,), (1,)), ((), ())), preferred_element_type=F32)


def gelu_slope(v):
    scale = 0.7978845608028654
    t = jnp.tanh(scale * (v + 0.044715 * v * v * v))
    return 0.5 * (1.0 + t) + (0.5 * scale) * v * (1.0 - t * t) * (1.0 + 3.0 * 0.044715 * v * v)


def edge_kernel(recv_sub, recv_cluster, features, edge, sub_row, cluster_row, sems):
    count = edge.shape[0] - EXTRA
    copies = [
        pltpu.make_async_copy(features.at[0:count, :], edge.at[0:count, :], sems.at[0]),
        pltpu.make_async_copy(recv_sub, sub_row, sems.at[1]),
        pltpu.make_async_copy(recv_cluster, cluster_row, sems.at[2]),
    ]
    for copy in copies:
        copy.start()
    for copy in copies:
        copy.wait()
    sub_count, cluster_count = sub_row.shape[1], cluster_row.shape[1]
    pad = jnp.zeros((1, edge.shape[1] - sub_count - cluster_count), F32)
    row = jnp.concatenate([sub_row[...].astype(F32), cluster_row[...].astype(F32), pad], axis=1)
    edge[count:, :] = jnp.broadcast_to(row, (EXTRA, edge.shape[1])).astype(BF)


def prepare_kernel(
    own, sub_count, cluster_count,
    tile_dst_hbm, tile_src_hbm, recv_sub_hbm, recv_cluster_hbm, features_hbm, w_self_hbm, bias_hbm,
    tile_weight_hbm, grad_out_hbm, w_neigh_hbm,
    dense, dense_t, own_sum, own_pre, inverse, choice, w_self, w_neigh, grad_out,
    tile_dst, tile_src, recv_sub, recv_cluster, features, tile_weight, bias, sems,
):
    size = tile_weight.shape[1]
    pairs = (
        (tile_dst_hbm, tile_dst), (tile_src_hbm, tile_src), (recv_sub_hbm, recv_sub),
        (recv_cluster_hbm, recv_cluster), (tile_weight_hbm, tile_weight),
        (features_hbm, features), (w_self_hbm, w_self), (w_neigh_hbm, w_neigh),
        (grad_out_hbm, grad_out), (bias_hbm, bias),
    )
    copies = [pltpu.make_async_copy(a, b, sems.at[i]) for i, (a, b) in enumerate(pairs)]
    for copy in copies:
        copy.start()
    sub_id = lax.axis_index("sub")
    cluster_id = lax.axis_index("cluster")
    dense[...] = jnp.zeros_like(dense)
    dense_t[...] = jnp.zeros_like(dense_t)
    for copy in copies[:5]:
        copy.wait()

    def place(t, carry):
        src = tile_src[t]
        from_sub = own + ((src - own) ^ sub_id)
        from_cluster = own + sub_count + ((src - own - sub_count) ^ cluster_id)
        slot = jnp.where(src < own, src, jnp.where(src < own + sub_count, from_sub, from_cluster))
        dst = pl.ds(pl.multiple_of(tile_dst[t] * size, size), size)
        col = pl.ds(pl.multiple_of(slot * size, size), size)
        tile = tile_weight[t]
        dense[dst, col] = dense[dst, col] + tile
        dense_t[col, dst] = dense_t[col, dst] + tile.T
        return carry

    lax.fori_loop(0, tile_weight.shape[0], place, 0, unroll=4)
    for d in range(sub_count):
        index = recv_sub[0, sub_id ^ d].astype(F32)
        choice[d : d + 1, :] = jnp.full((1, choice.shape[1]), index, F32)
    for d in range(cluster_count):
        index = recv_cluster[0, cluster_id ^ d].astype(F32)
        choice[sub_count + d : sub_count + d + 1, :] = jnp.full((1, choice.shape[1]), index, F32)
    slots = own + sub_count + cluster_count
    total = dense[:, 0:size].astype(F32)
    for slot in range(1, slots):
        total = total + dense[:, slot * size : (slot + 1) * size].astype(F32)
    degree = jnp.sum(total, axis=1, keepdims=True)
    inverse[...] = jnp.broadcast_to(1.0 / (degree + 1.0), inverse.shape)
    for copy in copies[5:]:
        copy.wait()
    own_sum[...] = dot(dense[:, 0 : own * size], features[...])
    own_pre[...] = dot(features[...], w_self[...]) + bias[...].reshape(1, -1)


def halo_sum(choice, dense, slots, own, messages, halo):
    size = dense.shape[0] // own
    for i, slot in enumerate(slots):
        message = messages[slot]
        halo[i * size : (i + 1) * size, :] = jnp.where(
            choice[slot : slot + 1, :] > 0.5,
            message[size : 2 * size, :].astype(F32),
            message[0:size, :].astype(F32),
        ).astype(BF)
    columns = slice((own + slots[0]) * size, (own + slots[-1] + 1) * size)
    return dot(dense[:, columns], halo[...])


def near_kernel(own, sub_count, choice, dense, own_sum, edge, *rest):
    received, (out, halo) = rest[:-2], rest[-2:]
    messages = dict(enumerate((edge, *received, edge)))
    out[...] = own_sum[...] + halo_sum(choice, dense, range(sub_count + 1), own, messages, halo)


def middle_kernel(
    own, sent_order, sub_count, cluster_count,
    choice, grad_out, w_neigh, dense, dense_t, near_sum, own_pre, inverse, gathered,
    *rest,
):
    sent, (kept, spread, grad_pre, halo) = rest[: len(sent_order)], rest[len(sent_order) :]
    size = dense.shape[0] // own
    cluster_id = lax.axis_index("cluster")
    messages = {sub_count + d: gathered.at[cluster_id ^ d] for d in range(1, cluster_count)}
    late = range(sub_count + 1, sub_count + cluster_count)
    aggregate = near_sum[...] + halo_sum(choice, dense, late, own, messages, halo)
    inv = jnp.concatenate([inverse[...]] * (grad_out.shape[1] // size), axis=1)
    mean = (aggregate * inv).astype(BF)
    pre = own_pre[...] + dot(mean, w_neigh[...])
    grad = (grad_out[...].astype(F32) * gelu_slope(pre)).astype(BF)
    grad_pre[...] = grad
    spread[...] = (dot_right_transposed(grad, w_neigh[...]) * inv).astype(BF)

    def partial(slot):
        rows = slice((own + slot) * size, (own + slot + 1) * size)
        return dot(dense_t[rows, :], spread[...]).astype(BF)

    for target, slot in zip(sent, sent_order):
        target[...] = partial(slot)
    kept[0] = partial(0)
    kept[1] = partial(sub_count)


def split(total, value, second, size):
    zero = jnp.zeros_like(value)
    total[0:size, :] = total[0:size, :] + jnp.where(second, zero, value)
    total[size : 2 * size, :] = total[size : 2 * size, :] + jnp.where(second, value, zero)


def own_kernel(
    own, order, sub_count, choice, w_self, dense_t, kept, spread, grad_pre, *rest
):
    (gathered, *received), (total, owner) = rest[:-2], rest[-2:]
    size = kept.shape[1]
    width = total.shape[1]
    total[...] = dot_right_transposed(grad_pre[...], w_self[...]) + dot(
        dense_t[0 : own * size, :], spread[...]
    )
    for i, slot in enumerate((0, sub_count)):
        split(total, kept[i].astype(F32), choice[slot : slot + 1, :] > 0.5, size)
    lanes = lax.broadcasted_iota(jnp.int32, (1, width), 1)
    for slot in order:
        if slot < sub_count:
            message, lane = received[slot - 1], lax.axis_index("sub")
        else:
            cluster_id = lax.axis_index("cluster")
            message, lane = gathered.at[cluster_id ^ (slot - sub_count)], sub_count + cluster_id
        last = message.shape[0] - EXTRA
        row = message[last : last + EXTRA, :].astype(F32)[0:1, :]
        index = jnp.sum(jnp.where(lanes == lane, row, 0.0), axis=1, keepdims=True)
        owner[slot : slot + 1, :] = jnp.broadcast_to(index, (1, width))


def final_kernel(order, owner, total, *rest):
    received, out = rest[:-1], rest[-1]
    size = received[0].shape[0]
    first = total[0:size, :]
    second = total[size : 2 * size, :]
    for message, slot in zip(received, order):
        value = message[...].astype(F32)
        to_second = owner[slot : slot + 1, :] > 0.5
        first = first + jnp.where(to_second, 0.0, value)
        second = second + jnp.where(to_second, value, 0.0)
    out[0:size, :] = first.astype(BF)
    out[size : 2 * size, :] = second.astype(BF)
    out[2 * size :, :] = total[2 * size :, :].astype(BF)


def swap(value, axis, count, d):
    return lax.ppermute(value, axis, [(i, i ^ d) for i in range(count)])


def gather_edges(edge, prepared, sub_count):
    got = {}
    for d in range(2, sub_count, 2):
        got[d] = swap(edge, "sub", sub_count, d)
    for d in range(1, sub_count, 2):
        value = edge if d == 1 else lax.optimization_barrier((got[d - 1], prepared))[0]
        got[d] = swap(value, "sub", sub_count, 1)
    return [got[d] for d in range(1, sub_count)]


def sending_order(sub_count, cluster_count):
    along = [sub_count + d for d in range(cluster_count - 1, 0, -1)]
    across = list(range(sub_count - 1, 1, -1))
    across = sorted(across, key=lambda d: (-(d // 2), d % 2))
    return along[:1] + across[:4] + along[1:] + across[4:] + [1]


def send_back(value, slot, sub_count, cluster_count):
    if slot < sub_count:
        return swap(value, "sub", sub_count, slot)
    return swap(value, "cluster", cluster_count, slot - sub_count)


def in_hbm(value):
    return pltpu.with_memory_space_constraint(value, pltpu.HBM)


def cost(flops, moved):
    return pl.CostEstimate(flops=flops, bytes_accessed=moved, transcendentals=0)


def shards(
    features, grad_out, w_self, w_neigh, bias, tile_dst, tile_src, tile_weight, recv_sub, recv_cluster
):
    sub_count = lax.axis_size("sub")
    cluster_count = lax.axis_size("cluster")
    peers = sub_count + cluster_count - 2
    size = tile_weight.shape[1]
    rows, width = features.shape
    own = rows // size
    slots = own + sub_count + cluster_count
    counts = (own, sub_count, cluster_count)
    sent_order = sending_order(sub_count, cluster_count)

    wide = jax.ShapeDtypeStruct((rows, width), F32)
    narrow = jax.ShapeDtypeStruct((rows, width), BF)
    square = jax.ShapeDtypeStruct((width, width), BF)
    block = jax.ShapeDtypeStruct((size, width), BF)
    marks = jax.ShapeDtypeStruct((sub_count + cluster_count, width), F32)

    edge = pl.pallas_call(
        edge_kernel,
        out_shape=jax.ShapeDtypeStruct((BOUNDARY * size + EXTRA, width), BF),
        in_specs=[HBM] * 3,
        out_specs=VMEM,
        scratch_shapes=[
            pltpu.VMEM(recv_sub.shape, jnp.int32),
            pltpu.VMEM(recv_cluster.shape, jnp.int32),
            pltpu.SemaphoreType.DMA((3,)),
        ],
        compiler_params=PARAMS,
        cost_estimate=cost(1024, 256 * 1024),
        name="edge",
    )(in_hbm(recv_sub), in_hbm(recv_cluster), in_hbm(features))
    gathered = lax.all_gather(edge, "cluster", axis=0)

    dense, dense_t, own_sum, own_pre, inverse, choice, w_self, w_neigh, grad_out = pl.pallas_call(
        functools.partial(prepare_kernel, *counts),
        out_shape=[
            jax.ShapeDtypeStruct((rows, slots * size), BF),
            jax.ShapeDtypeStruct((slots * size, rows), BF),
            wide,
            wide,
            jax.ShapeDtypeStruct((rows, size), F32),
            marks,
            square,
            square,
            narrow,
        ],
        in_specs=[HBM] * 10,
        out_specs=[VMEM] * 9,
        scratch_shapes=[
            pltpu.SMEM(tile_dst.shape, jnp.int32),
            pltpu.SMEM(tile_src.shape, jnp.int32),
            pltpu.SMEM(recv_sub.shape, jnp.int32),
            pltpu.SMEM(recv_cluster.shape, jnp.int32),
            pltpu.VMEM(features.shape, BF),
            pltpu.VMEM(tile_weight.shape, BF),
            pltpu.VMEM(bias.shape, F32),
            pltpu.SemaphoreType.DMA((10,)),
        ],
        compiler_params=PARAMS,
        cost_estimate=cost(2 * rows * rows * width * 2, 6 * 1024 * 1024),
        name="prepare",
    )(
        *map(in_hbm, (tile_dst, tile_src, recv_sub, recv_cluster, features, w_self, bias)),
        *map(in_hbm, (tile_weight, grad_out, w_neigh)),
    )
    halos = gather_edges(edge, choice, sub_count)
    near_sum = pl.pallas_call(
        functools.partial(near_kernel, own, sub_count),
        out_shape=wide,
        in_specs=[VMEM] * (3 + sub_count),
        out_specs=VMEM,
        scratch_shapes=[pltpu.VMEM(((sub_count + 1) * size, width), BF)],
        compiler_params=PARAMS,
        cost_estimate=cost(2 * rows * (sub_count + 1) * size * width, 3 * 1024 * 1024),
        name="near",
    )(choice, dense, own_sum, edge, *halos)

    outs = pl.pallas_call(
        functools.partial(middle_kernel, own, sent_order, sub_count, cluster_count),
        out_shape=[block] * peers + [jax.ShapeDtypeStruct((2, size, width), BF), narrow, narrow],
        in_specs=[VMEM] * 9,
        out_specs=[VMEM] * (peers + 3),
        scratch_shapes=[pltpu.VMEM(((cluster_count - 1) * size, width), BF)],
        compiler_params=PARAMS,
        cost_estimate=cost(2 * rows * slots * size * width, 6 * 1024 * 1024),
        name="middle",
    )(choice, grad_out, w_neigh, dense, dense_t, near_sum, own_pre, inverse, gathered)
    sent, (kept, spread, grad_pre) = outs[:peers], outs[peers:]
    returned = [
        send_back(value, slot, sub_count, cluster_count) for value, slot in zip(sent, sent_order)
    ]

    total, owner = pl.pallas_call(
        functools.partial(own_kernel, own, sent_order, sub_count),
        out_shape=[wide, marks],
        in_specs=[VMEM] * (6 + sub_count),
        out_specs=[VMEM] * 2,
        compiler_params=PARAMS,
        cost_estimate=cost(4 * rows * rows * width, 2 * 1024 * 1024),
        name="own",
    )(choice, w_self, dense_t, kept, spread, grad_pre, gathered, *halos)

    return pl.pallas_call(
        functools.partial(final_kernel, sent_order),
        out_shape=narrow,
        in_specs=[VMEM] * (2 + peers),
        out_specs=VMEM,
        compiler_params=PARAMS,
        cost_estimate=cost(rows * width * 4, 2 * 1024 * 1024),
        name="final",
    )(owner, total, *returned)


def solution(mesh):
    placed = (
        P(("cluster", "sub"), None),
        P(("cluster", "sub"), None),
        P(),
        P(),
        P(),
        P(("cluster", "sub")),
        P(("cluster", "sub")),
        P(("cluster", "sub"), None, None),
        P(("cluster", "sub"), None),
        P(("cluster", "sub"), None),
    )
    return jax.shard_map(
        shards, mesh=mesh, in_specs=placed, out_specs=P(("cluster", "sub"), None), check_vma=False
    )
```

```python
import functools

import jax
import jax.numpy as jnp
from jax import lax
from jax.experimental import pallas as pl
from jax.experimental.pallas import tpu as pltpu
from jax.sharding import PartitionSpec as P

BF = jnp.bfloat16
F32 = jnp.float32
BOUNDARY = 2
EXTRA = 16
VMEM = pl.BlockSpec(memory_space=pltpu.VMEM)
HBM = pl.BlockSpec(memory_space=pltpu.HBM)
PARAMS = pltpu.CompilerParams(vmem_limit_bytes=24 * 1024 * 1024)


def dot(left, right):
    return jnp.dot(left, right, preferred_element_type=F32)


def dot_right_transposed(left, right):
    return lax.dot_general(left, right, (((1,), (1,)), ((), ())), preferred_element_type=F32)


def gelu_slope(v):
    scale = 0.7978845608028654
    t = jnp.tanh(scale * (v + 0.044715 * v * v * v))
    return 0.5 * (1.0 + t) + (0.5 * scale) * v * (1.0 - t * t) * (1.0 + 3.0 * 0.044715 * v * v)


def edge_kernel(recv_sub, recv_cluster, features, edge, first, second, sub_row, cluster_row, sems):
    size = first.shape[0]
    copies = [
        pltpu.make_async_copy(features.at[0:size, :], first, sems.at[0]),
        pltpu.make_async_copy(features.at[size : 2 * size, :], second.at[0:size, :], sems.at[1]),
        pltpu.make_async_copy(features.at[0 : 2 * size, :], edge.at[0 : 2 * size, :], sems.at[2]),
        pltpu.make_async_copy(recv_sub, sub_row, sems.at[3]),
        pltpu.make_async_copy(recv_cluster, cluster_row, sems.at[4]),
    ]
    for copy in copies:
        copy.start()
    for copy in copies:
        copy.wait()
    sub_count, cluster_count = sub_row.shape[1], cluster_row.shape[1]
    pad = jnp.zeros((1, edge.shape[1] - sub_count - cluster_count), F32)
    row = jnp.concatenate([sub_row[...].astype(F32), cluster_row[...].astype(F32), pad], axis=1)
    rows = jnp.broadcast_to(row, (EXTRA, edge.shape[1])).astype(BF)
    edge[2 * size :, :] = rows
    second[size:, :] = rows


def prepare_kernel(
    own, sub_count, cluster_count,
    tile_dst_hbm, tile_src_hbm, recv_sub_hbm, recv_cluster_hbm, tile_weight_hbm,
    features_hbm, w_self_hbm, w_neigh_hbm, grad_out_hbm, bias_hbm,
    dense, dense_t, inverse, choice, features, w_self, w_neigh, grad_out, bias,
    tile_dst, tile_src, recv_sub, recv_cluster, tile_weight, sems,
):
    size = tile_weight.shape[1]
    pairs = (
        (tile_dst_hbm, tile_dst), (tile_src_hbm, tile_src), (recv_sub_hbm, recv_sub),
        (recv_cluster_hbm, recv_cluster), (tile_weight_hbm, tile_weight),
        (features_hbm, features), (w_self_hbm, w_self), (w_neigh_hbm, w_neigh),
        (grad_out_hbm, grad_out), (bias_hbm, bias),
    )
    copies = [pltpu.make_async_copy(a, b, sems.at[i]) for i, (a, b) in enumerate(pairs)]
    for copy in copies:
        copy.start()
    sub_id = lax.axis_index("sub")
    cluster_id = lax.axis_index("cluster")
    dense[...] = jnp.zeros_like(dense)
    dense_t[...] = jnp.zeros_like(dense_t)
    for copy in copies[:5]:
        copy.wait()

    def place(t, carry):
        src = tile_src[t]
        from_sub = own + ((src - own) ^ sub_id)
        from_cluster = own + sub_count + ((src - own - sub_count) ^ cluster_id)
        slot = jnp.where(src < own, src, jnp.where(src < own + sub_count, from_sub, from_cluster))
        dst = pl.ds(pl.multiple_of(tile_dst[t] * size, size), size)
        col = pl.ds(pl.multiple_of(slot * size, size), size)
        tile = tile_weight[t]
        dense[dst, col] = dense[dst, col] + tile
        dense_t[col, dst] = dense_t[col, dst] + tile.T
        return carry

    lax.fori_loop(0, tile_weight.shape[0], place, 0, unroll=4)
    for d in range(sub_count):
        index = recv_sub[0, sub_id ^ d].astype(F32)
        choice[d : d + 1, :] = jnp.full((1, choice.shape[1]), index, F32)
    for d in range(cluster_count):
        index = recv_cluster[0, cluster_id ^ d].astype(F32)
        choice[sub_count + d : sub_count + d + 1, :] = jnp.full((1, choice.shape[1]), index, F32)
    slots = own + sub_count + cluster_count
    total = dense[:, 0:size].astype(F32)
    for slot in range(1, slots):
        total = total + dense[:, slot * size : (slot + 1) * size].astype(F32)
    degree = jnp.sum(total, axis=1, keepdims=True)
    inverse[...] = jnp.broadcast_to(1.0 / (degree + 1.0), inverse.shape)
    for copy in copies[5:]:
        copy.wait()


def halo_sum(choice, dense, own, shape, refs, halo):
    size = dense.shape[0] // own
    columns, at = [], 0
    for i, (slot, count) in enumerate(shape.items()):
        if count == 1:
            first, second = refs[at][0:size, :], refs[at][size : 2 * size, :]
        else:
            first, second = refs[at][0:size, :], refs[at + 1][0:size, :]
        at += count
        halo[i * size : (i + 1) * size, :] = jnp.where(
            choice[slot : slot + 1, :] > 0.5, second.astype(F32), first.astype(F32)
        ).astype(BF)
        columns.append(dense[:, (own + slot) * size : (own + slot + 1) * size])
    return dot(jnp.concatenate(columns, axis=1), halo[...])


def first_kernel(own, shape, choice, dense, features, w_self, bias, *rest):
    refs, (total, own_pre, halo) = rest[:-3], rest[-3:]
    size = dense.shape[0] // own
    total[...] = dot(dense[:, 0 : own * size], features[...]) + halo_sum(
        choice, dense, own, shape, refs, halo
    )
    own_pre[...] = dot(features[...], w_self[...]) + bias[...].reshape(1, -1)


def near_kernel(own, shape, choice, dense, before, *rest):
    refs, (total, halo) = rest[:-2], rest[-2:]
    total[...] = before[...] + halo_sum(choice, dense, own, shape, refs, halo)


def middle_kernel(
    own, sub_count, cluster_count, shape,
    choice, grad_out, w_neigh, dense, dense_t, before, own_pre, inverse,
    *rest,
):
    received = sum(shape.values())
    refs, rest = rest[:received], rest[received:]
    pairs, rest = rest[: sub_count // 2 - 1], rest[sub_count // 2 - 1 :]
    along, (sibling, kept, spread, grad_pre, halo) = rest[:-5], rest[-5:]
    size = dense.shape[0] // own
    aggregate = before[...] + halo_sum(choice, dense, own, shape, refs, halo)
    inv = jnp.concatenate([inverse[...]] * (grad_out.shape[1] // size), axis=1)
    mean = (aggregate * inv).astype(BF)
    pre = own_pre[...] + dot(mean, w_neigh[...])
    grad = (grad_out[...].astype(F32) * gelu_slope(pre)).astype(BF)
    grad_pre[...] = grad
    spread[...] = (dot_right_transposed(grad, w_neigh[...]) * inv).astype(BF)

    def partial(slot, count=1):
        rows = slice((own + slot) * size, (own + slot + count) * size)
        return dot(dense_t[rows, :], spread[...]).astype(BF)

    for i, target in enumerate(pairs):
        target[...] = partial(2 * (i + 1), 2)
    for i, target in enumerate(along):
        target[...] = partial(sub_count + 1 + i)
    sibling[...] = partial(1)
    kept[0] = partial(0)
    kept[1] = partial(sub_count)


def split(total, value, second, size):
    zero = jnp.zeros_like(value)
    total[0:size, :] = total[0:size, :] + jnp.where(second, zero, value)
    total[size : 2 * size, :] = total[size : 2 * size, :] + jnp.where(second, value, zero)


def own_kernel(own, sub_count, order, parts, *rest):
    back, rest = rest[: len(parts)], rest[len(parts) :]
    received, rest = rest[: len(order)], rest[len(order) :]
    choice, w_self, dense_t, kept, spread, grad_pre, total, owner = rest
    size = kept.shape[1]
    width = total.shape[1]
    total[...] = dot_right_transposed(grad_pre[...], w_self[...]) + dot(
        dense_t[0 : own * size, :], spread[...]
    )
    for i, slot in enumerate((0, sub_count)):
        split(total, kept[i].astype(F32), choice[slot : slot + 1, :] > 0.5, size)
    lanes = lax.broadcasted_iota(jnp.int32, (1, width), 1)
    for message, slot in zip(received, order):
        lane = lax.axis_index("sub")
        if slot > sub_count:
            lane = sub_count + lax.axis_index("cluster")
        last = message.shape[0] - EXTRA
        row = message[last : last + EXTRA, :].astype(F32)[0:1, :]
        index = jnp.sum(jnp.where(lanes == lane, row, 0.0), axis=1, keepdims=True)
        owner[slot : slot + 1, :] = jnp.broadcast_to(index, (1, width))
    for message, (slot, row) in zip(back, parts):
        value = message[row : row + size, :].astype(F32)
        split(total, value, owner[slot : slot + 1, :] > 0.5, size)


def final_kernel(own, parts, owner, total, *rest):
    received, out = rest[:-1], rest[-1]
    size = total.shape[0] // own
    first = total[0:size, :]
    second = total[size : 2 * size, :]
    for message, (slot, row) in zip(received, parts):
        value = message[row : row + size, :].astype(F32)
        to_second = owner[slot : slot + 1, :] > 0.5
        first = first + jnp.where(to_second, 0.0, value)
        second = second + jnp.where(to_second, value, 0.0)
    out[0:size, :] = first.astype(BF)
    out[size : 2 * size, :] = second.astype(BF)
    out[2 * size :, :] = total[2 * size :, :].astype(BF)


def swap(value, axis, count, d):
    return lax.ppermute(value, axis, [(i, i ^ d) for i in range(count)])


def after(value, other):
    return lax.optimization_barrier((value, other))[0]


def in_hbm(value):
    return pltpu.with_memory_space_constraint(value, pltpu.HBM)


def cost(flops, moved):
    return pl.CostEstimate(flops=flops, bytes_accessed=moved, transcendentals=0)


def shards(
    features, grad_out, w_self, w_neigh, bias, tile_dst, tile_src, tile_weight, recv_sub, recv_cluster
):
    sub_count = lax.axis_size("sub")
    cluster_count = lax.axis_size("cluster")
    peers = sub_count + cluster_count - 2
    size = tile_weight.shape[1]
    rows, width = features.shape
    own = rows // size
    slots = own + sub_count + cluster_count
    counts = (own, sub_count, cluster_count)

    wide = jax.ShapeDtypeStruct((rows, width), F32)
    narrow = jax.ShapeDtypeStruct((rows, width), BF)
    square = jax.ShapeDtypeStruct((width, width), BF)
    block = jax.ShapeDtypeStruct((size, width), BF)
    marks = jax.ShapeDtypeStruct((sub_count + cluster_count, width), F32)

    edge, *halves = pl.pallas_call(
        edge_kernel,
        out_shape=[
            jax.ShapeDtypeStruct((BOUNDARY * size + EXTRA, width), BF),
            block,
            jax.ShapeDtypeStruct((size + EXTRA, width), BF),
        ],
        in_specs=[HBM] * 3,
        out_specs=[VMEM] * 3,
        scratch_shapes=[
            pltpu.VMEM(recv_sub.shape, jnp.int32),
            pltpu.VMEM(recv_cluster.shape, jnp.int32),
            pltpu.SemaphoreType.DMA((5,)),
        ],
        compiler_params=PARAMS,
        cost_estimate=cost(1024, 256 * 1024),
        name="edge",
    )(in_hbm(recv_sub), in_hbm(recv_cluster), in_hbm(features))

    def along(value, d):
        return swap(value, "cluster", cluster_count, d)

    def across(value, d):
        return swap(value, "sub", sub_count, d)

    direct = [d for d in range(2, cluster_count) if not d & (d - 1)]
    relayed = [d for d in range(2, cluster_count) if d & (d - 1)]
    got = {sub_count + d: tuple(along(half, d) for half in halves) for d in direct}
    got[1] = (across(edge, 1),)
    early = (got[1][0], *(got[sub_count + d][0] for d in direct[-1:]))
    start = after(tile_dst, early)

    dense, dense_t, inverse, choice, features, w_self, w_neigh, grad_out, bias = pl.pallas_call(
        functools.partial(prepare_kernel, *counts),
        out_shape=[
            jax.ShapeDtypeStruct((rows, slots * size), BF),
            jax.ShapeDtypeStruct((slots * size, rows), BF),
            jax.ShapeDtypeStruct((rows, size), F32),
            marks,
            narrow,
            square,
            square,
            narrow,
            jax.ShapeDtypeStruct(bias.shape, F32),
        ],
        in_specs=[HBM] * 10,
        out_specs=[VMEM] * 9,
        scratch_shapes=[
            pltpu.SMEM(tile_dst.shape, jnp.int32),
            pltpu.SMEM(tile_src.shape, jnp.int32),
            pltpu.SMEM(recv_sub.shape, jnp.int32),
            pltpu.SMEM(recv_cluster.shape, jnp.int32),
            pltpu.VMEM(tile_weight.shape, BF),
            pltpu.SemaphoreType.DMA((10,)),
        ],
        compiler_params=PARAMS,
        cost_estimate=cost(10**6, 6 * 1024 * 1024),
        name="prepare",
    )(
        *map(in_hbm, (start, tile_src, recv_sub, recv_cluster, tile_weight)),
        *map(in_hbm, (features, w_self, w_neigh, grad_out, bias)),
    )

    def sum_call(kernel, out_shape, name, slots, *operands):
        shape = {slot: len(got[slot]) for slot in slots}
        refs = [part for slot in slots for part in got[slot]]
        return pl.pallas_call(
            functools.partial(kernel, own, shape),
            out_shape=out_shape,
            in_specs=[VMEM] * (len(operands) + len(refs)),
            out_specs=jax.tree.map(lambda _: VMEM, out_shape),
            scratch_shapes=[pltpu.VMEM((len(shape) * size, width), BF)],
            compiler_params=PARAMS,
            cost_estimate=cost(10**10, 3 * 1024 * 1024),
            name=name,
        )(*operands, *refs)

    got[0] = got[sub_count] = (edge,)
    got[sub_count + 1] = (along(edge, 1),)
    first_sum, own_pre = sum_call(
        first_kernel, [wide, wide], "first", [0, sub_count, *(sub_count + d for d in direct), sub_count + 1],
        choice, dense, features, w_self, bias,
    )
    even = list(range(2, sub_count, 2))
    for d in relayed:
        low = d & -d
        one, two = got[sub_count + d - low]
        got[sub_count + d] = (along(one, low), along(two, low))
    for d in even:
        got[d] = (across(edge, d),)
        got[d + 1] = (across(after(got[d][0], own_pre), 1),)
    near_sum = sum_call(near_kernel, wide, "near", [*even, 1], choice, dense, first_sum)

    late = [*(sub_count + d for d in relayed), *(d + 1 for d in even)]
    shape = {slot: len(got[slot]) for slot in late}
    refs = [part for slot in late for part in got[slot]]
    outs = pl.pallas_call(
        functools.partial(middle_kernel, *counts, shape),
        out_shape=[jax.ShapeDtypeStruct((2 * size, width), BF)] * len(even)
        + [block] * cluster_count
        + [jax.ShapeDtypeStruct((2, size, width), BF), narrow, narrow],
        in_specs=[VMEM] * (8 + len(refs)),
        out_specs=[VMEM] * (len(even) + cluster_count + 3),
        scratch_shapes=[pltpu.VMEM((len(shape) * size, width), BF)],
        compiler_params=PARAMS,
        cost_estimate=cost(2 * rows * slots * size * width, 6 * 1024 * 1024),
        name="middle",
    )(choice, grad_out, w_neigh, dense, dense_t, near_sum, own_pre, inverse, *refs)
    *sent, sibling, kept, spread, grad_pre = outs

    back = [(along(sent[len(even) + d - 1], d), sub_count + d, 0) for d in range(1, cluster_count)]
    direct_back, swapped_back = [], []
    for d, value in zip(even, sent):
        value = across(value, d)
        direct_back.append((value, d, 0))
        swapped_back.append((across(value, 1), d + 1, size))
    sibling_back = [(across(sibling, 1), 1, 0)]
    early_back, back = back[::-1], [*direct_back, *swapped_back, *sibling_back]

    order = [*even, *(sub_count + d for d in direct), *(d + 1 for d in even), 1, sub_count + 1, *(sub_count + d for d in relayed)]
    total, owner = pl.pallas_call(
        functools.partial(
            own_kernel, own, sub_count, order, [(slot, row) for _, slot, row in early_back]
        ),
        out_shape=[wide, marks],
        in_specs=[VMEM] * (6 + peers + len(early_back)),
        out_specs=[VMEM] * 2,
        compiler_params=PARAMS,
        cost_estimate=cost(10**10, 2 * 1024 * 1024),
        name="own",
    )(
        *[value for value, _, _ in early_back],
        *[got[slot][-1] for slot in order],
        choice, w_self, dense_t, kept, spread, grad_pre,
    )

    return pl.pallas_call(
        functools.partial(final_kernel, own, [(slot, row) for _, slot, row in back]),
        out_shape=narrow,
        in_specs=[VMEM] * (2 + len(back)),
        out_specs=VMEM,
        compiler_params=PARAMS,
        cost_estimate=cost(rows * width * 4, 2 * 1024 * 1024),
        name="final",
    )(owner, total, *[value for value, _, _ in back])


def solution(mesh):
    placed = (
        P(("cluster", "sub"), None),
        P(("cluster", "sub"), None),
        P(),
        P(),
        P(),
        P(("cluster", "sub")),
        P(("cluster", "sub")),
        P(("cluster", "sub"), None, None),
        P(("cluster", "sub"), None),
        P(("cluster", "sub"), None),
    )
    return jax.shard_map(
        shards, mesh=mesh, in_specs=placed, out_specs=P(("cluster", "sub"), None), check_vma=False
    )
```

```python
import functools

import jax
import jax.numpy as jnp
from jax import lax
from jax.experimental import pallas as pl
from jax.experimental.pallas import tpu as pltpu
from jax.sharding import PartitionSpec as P

BF = jnp.bfloat16
F32 = jnp.float32
BOUNDARY = 2
EXTRA = 16
VMEM = pl.BlockSpec(memory_space=pltpu.VMEM)
HBM = pl.BlockSpec(memory_space=pltpu.HBM)
PARAMS = pltpu.CompilerParams(vmem_limit_bytes=24 * 1024 * 1024)


def dot(left, right):
    return jnp.dot(left, right, preferred_element_type=F32)


def dot_right_transposed(left, right):
    return lax.dot_general(left, right, (((1,), (1,)), ((), ())), preferred_element_type=F32)


def gelu_slope(v):
    scale = 0.7978845608028654
    t = jnp.tanh(scale * (v + 0.044715 * v * v * v))
    return 0.5 * (1.0 + t) + (0.5 * scale) * v * (1.0 - t * t) * (1.0 + 3.0 * 0.044715 * v * v)


def edge_kernel(recv_sub, recv_cluster, features, edge, sub_row, cluster_row, sems):
    count = edge.shape[0] - EXTRA
    copies = [
        pltpu.make_async_copy(features.at[0:count, :], edge.at[0:count, :], sems.at[0]),
        pltpu.make_async_copy(recv_sub, sub_row, sems.at[1]),
        pltpu.make_async_copy(recv_cluster, cluster_row, sems.at[2]),
    ]
    for copy in copies:
        copy.start()
    for copy in copies:
        copy.wait()
    sub_count, cluster_count = sub_row.shape[1], cluster_row.shape[1]
    pad = jnp.zeros((1, edge.shape[1] - sub_count - cluster_count), F32)
    row = jnp.concatenate([sub_row[...].astype(F32), cluster_row[...].astype(F32), pad], axis=1)
    edge[count:, :] = jnp.broadcast_to(row, (EXTRA, edge.shape[1])).astype(BF)


def prepare_kernel(
    own, sub_count, cluster_count,
    tile_dst_hbm, tile_src_hbm, recv_sub_hbm, recv_cluster_hbm, tile_weight_hbm,
    features_hbm, w_self_hbm, w_neigh_hbm, grad_out_hbm, bias_hbm,
    dense, dense_t, inverse, choice, features, w_self, w_neigh, grad_out, bias,
    tile_dst, tile_src, recv_sub, recv_cluster, tile_weight, sems,
):
    size = tile_weight.shape[1]
    pairs = (
        (tile_dst_hbm, tile_dst), (tile_src_hbm, tile_src), (recv_sub_hbm, recv_sub),
        (recv_cluster_hbm, recv_cluster), (tile_weight_hbm, tile_weight),
        (features_hbm, features), (w_self_hbm, w_self), (w_neigh_hbm, w_neigh),
        (grad_out_hbm, grad_out), (bias_hbm, bias),
    )
    copies = [pltpu.make_async_copy(a, b, sems.at[i]) for i, (a, b) in enumerate(pairs)]
    for copy in copies:
        copy.start()
    sub_id = lax.axis_index("sub")
    cluster_id = lax.axis_index("cluster")
    dense[...] = jnp.zeros_like(dense)
    dense_t[...] = jnp.zeros_like(dense_t)
    for copy in copies[:5]:
        copy.wait()

    def place(t, carry):
        src = tile_src[t]
        from_sub = own + ((src - own) ^ sub_id)
        from_cluster = own + sub_count + ((src - own - sub_count) ^ cluster_id)
        slot = jnp.where(src < own, src, jnp.where(src < own + sub_count, from_sub, from_cluster))
        dst = pl.ds(pl.multiple_of(tile_dst[t] * size, size), size)
        col = pl.ds(pl.multiple_of(slot * size, size), size)
        tile = tile_weight[t]
        dense[dst, col] = dense[dst, col] + tile
        dense_t[col, dst] = dense_t[col, dst] + tile.T
        return carry

    lax.fori_loop(0, tile_weight.shape[0], place, 0, unroll=4)
    for d in range(sub_count):
        index = recv_sub[0, sub_id ^ d].astype(F32)
        choice[d : d + 1, :] = jnp.full((1, choice.shape[1]), index, F32)
    for d in range(cluster_count):
        index = recv_cluster[0, cluster_id ^ d].astype(F32)
        choice[sub_count + d : sub_count + d + 1, :] = jnp.full((1, choice.shape[1]), index, F32)
    slots = own + sub_count + cluster_count
    total = dense[:, 0:size].astype(F32)
    for slot in range(1, slots):
        total = total + dense[:, slot * size : (slot + 1) * size].astype(F32)
    degree = jnp.sum(total, axis=1, keepdims=True)
    inverse[...] = jnp.broadcast_to(1.0 / (degree + 1.0), inverse.shape)
    for copy in copies[5:]:
        copy.wait()


def relay_kernel(sub_count, d, near, far, out):
    size = out.shape[0] - EXTRA
    lanes = lax.broadcasted_iota(jnp.int32, (1, out.shape[1]), 1)
    lane = sub_count + (lax.axis_index("cluster") ^ d)
    row = near[2 * size : 2 * size + EXTRA, :].astype(F32)[0:1, :]
    index = jnp.sum(jnp.where(lanes == lane, row, 0.0), axis=1, keepdims=True)
    out[0:size, :] = jnp.where(
        index > 0.5, far[size : 2 * size, :].astype(F32), far[0:size, :].astype(F32)
    ).astype(BF)
    out[size:, :] = far[2 * size :, :]


def halo_sum(choice, dense, own, slots, messages, halo):
    size = dense.shape[0] // own
    columns = []
    for i, (slot, message) in enumerate(zip(slots, messages)):
        block = message[0:size, :]
        if message.shape[0] > 2 * size:
            block = jnp.where(
                choice[slot : slot + 1, :] > 0.5,
                message[size : 2 * size, :].astype(F32),
                block.astype(F32),
            ).astype(BF)
        halo[i * size : (i + 1) * size, :] = block
        columns.append(dense[:, (own + slot) * size : (own + slot + 1) * size])
    return dot(jnp.concatenate(columns, axis=1), halo[...])


def first_kernel(own, slots, choice, dense, features, w_self, bias, *rest):
    refs, (total, own_pre, halo) = rest[:-3], rest[-3:]
    size = dense.shape[0] // own
    total[...] = dot(dense[:, 0 : own * size], features[...]) + halo_sum(
        choice, dense, own, slots, refs, halo
    )
    own_pre[...] = dot(features[...], w_self[...]) + bias[...].reshape(1, -1)


def near_kernel(own, slots, choice, dense, before, *rest):
    refs, (total, halo) = rest[:-2], rest[-2:]
    total[...] = before[...] + halo_sum(choice, dense, own, slots, refs, halo)


def middle_kernel(
    own, sub_count, cluster_count, slots,
    choice, grad_out, w_neigh, dense, dense_t, before, own_pre, inverse,
    *rest,
):
    refs, rest = rest[: len(slots)], rest[len(slots) :]
    pairs, rest = rest[: sub_count // 2 - 1], rest[sub_count // 2 - 1 :]
    along, (sibling, kept, spread, grad_pre, halo) = rest[:-5], rest[-5:]
    size = dense.shape[0] // own
    aggregate = before[...] + halo_sum(choice, dense, own, slots, refs, halo)
    inv = jnp.concatenate([inverse[...]] * (grad_out.shape[1] // size), axis=1)
    mean = (aggregate * inv).astype(BF)
    pre = own_pre[...] + dot(mean, w_neigh[...])
    grad = (grad_out[...].astype(F32) * gelu_slope(pre)).astype(BF)
    grad_pre[...] = grad
    spread[...] = (dot_right_transposed(grad, w_neigh[...]) * inv).astype(BF)

    def partial(slot, count=1):
        rows = slice((own + slot) * size, (own + slot + count) * size)
        return dot(dense_t[rows, :], spread[...]).astype(BF)

    for i, target in enumerate(pairs):
        target[...] = partial(2 * (i + 1), 2)
    for i, target in enumerate(along):
        target[...] = partial(sub_count + 1 + i)
    sibling[...] = partial(1)
    kept[0] = partial(0)
    kept[1] = partial(sub_count)


def split(total, value, second, size):
    zero = jnp.zeros_like(value)
    total[0:size, :] = total[0:size, :] + jnp.where(second, zero, value)
    total[size : 2 * size, :] = total[size : 2 * size, :] + jnp.where(second, value, zero)


def own_kernel(own, sub_count, order, parts, *rest):
    back, rest = rest[: len(parts)], rest[len(parts) :]
    received, rest = rest[: len(order)], rest[len(order) :]
    choice, w_self, dense_t, kept, spread, grad_pre, total, owner = rest
    size = kept.shape[1]
    width = total.shape[1]
    total[...] = dot_right_transposed(grad_pre[...], w_self[...]) + dot(
        dense_t[0 : own * size, :], spread[...]
    )
    for i, slot in enumerate((0, sub_count)):
        split(total, kept[i].astype(F32), choice[slot : slot + 1, :] > 0.5, size)
    lanes = lax.broadcasted_iota(jnp.int32, (1, width), 1)
    for message, slot in zip(received, order):
        lane = lax.axis_index("sub")
        if slot > sub_count:
            lane = sub_count + lax.axis_index("cluster")
        last = message.shape[0] - EXTRA
        row = message[last : last + EXTRA, :].astype(F32)[0:1, :]
        index = jnp.sum(jnp.where(lanes == lane, row, 0.0), axis=1, keepdims=True)
        owner[slot : slot + 1, :] = jnp.broadcast_to(index, (1, width))
    for message, (slot, row) in zip(back, parts):
        value = message[row : row + size, :].astype(F32)
        split(total, value, owner[slot : slot + 1, :] > 0.5, size)


def add_kernel(own, parts, owner, total, *rest):
    received, out = rest[:-1], rest[-1]
    size = total.shape[0] // own
    out[...] = total[...]
    for message, (slot, row) in zip(received, parts):
        value = message[row : row + size, :].astype(F32)
        split(out, value, owner[slot : slot + 1, :] > 0.5, size)


def final_kernel(own, parts, owner, total, *rest):
    received, out = rest[:-1], rest[-1]
    size = total.shape[0] // own
    first = total[0:size, :]
    second = total[size : 2 * size, :]
    for message, (slot, row) in zip(received, parts):
        value = message[row : row + size, :].astype(F32)
        to_second = owner[slot : slot + 1, :] > 0.5
        first = first + jnp.where(to_second, 0.0, value)
        second = second + jnp.where(to_second, value, 0.0)
    out[0:size, :] = first.astype(BF)
    out[size : 2 * size, :] = second.astype(BF)
    out[2 * size :, :] = total[2 * size :, :].astype(BF)


def swap(value, axis, count, d):
    return lax.ppermute(value, axis, [(i, i ^ d) for i in range(count)])


def after(value, other):
    return lax.optimization_barrier((value, other))[0]


def in_hbm(value):
    return pltpu.with_memory_space_constraint(value, pltpu.HBM)


def cost(flops, moved):
    return pl.CostEstimate(flops=flops, bytes_accessed=moved, transcendentals=0)


def shards(
    features, grad_out, w_self, w_neigh, bias, tile_dst, tile_src, tile_weight, recv_sub, recv_cluster
):
    sub_count = lax.axis_size("sub")
    cluster_count = lax.axis_size("cluster")
    peers = sub_count + cluster_count - 2
    size = tile_weight.shape[1]
    rows, width = features.shape
    own = rows // size
    slots = own + sub_count + cluster_count
    counts = (own, sub_count, cluster_count)

    wide = jax.ShapeDtypeStruct((rows, width), F32)
    narrow = jax.ShapeDtypeStruct((rows, width), BF)
    square = jax.ShapeDtypeStruct((width, width), BF)
    block = jax.ShapeDtypeStruct((size, width), BF)
    marks = jax.ShapeDtypeStruct((sub_count + cluster_count, width), F32)

    edge = pl.pallas_call(
        edge_kernel,
        out_shape=jax.ShapeDtypeStruct((BOUNDARY * size + EXTRA, width), BF),
        in_specs=[HBM] * 3,
        out_specs=VMEM,
        scratch_shapes=[
            pltpu.VMEM(recv_sub.shape, jnp.int32),
            pltpu.VMEM(recv_cluster.shape, jnp.int32),
            pltpu.SemaphoreType.DMA((3,)),
        ],
        compiler_params=PARAMS,
        cost_estimate=cost(1024, 256 * 1024),
        name="edge",
    )(in_hbm(recv_sub), in_hbm(recv_cluster), in_hbm(features))

    def along(value, d):
        return swap(value, "cluster", cluster_count, d)

    def across(value, d):
        return swap(value, "sub", sub_count, d)

    even = list(range(2, sub_count, 2))
    direct = list(range(2, cluster_count, 2))
    relayed = list(range(3, cluster_count, 2))
    got = {0: edge, sub_count: edge}
    for d in direct:
        got[sub_count + d] = along(edge, d)
    for d in even:
        got[d] = across(edge, d)
    got[sub_count + 1] = along(edge, 1)
    got[1] = across(edge, 1)
    start = tile_dst

    dense, dense_t, inverse, choice, features, w_self, w_neigh, grad_out, bias = pl.pallas_call(
        functools.partial(prepare_kernel, *counts),
        out_shape=[
            jax.ShapeDtypeStruct((rows, slots * size), BF),
            jax.ShapeDtypeStruct((slots * size, rows), BF),
            jax.ShapeDtypeStruct((rows, size), F32),
            marks,
            narrow,
            square,
            square,
            narrow,
            jax.ShapeDtypeStruct(bias.shape, F32),
        ],
        in_specs=[HBM] * 10,
        out_specs=[VMEM] * 9,
        scratch_shapes=[
            pltpu.SMEM(tile_dst.shape, jnp.int32),
            pltpu.SMEM(tile_src.shape, jnp.int32),
            pltpu.SMEM(recv_sub.shape, jnp.int32),
            pltpu.SMEM(recv_cluster.shape, jnp.int32),
            pltpu.VMEM(tile_weight.shape, BF),
            pltpu.SemaphoreType.DMA((10,)),
        ],
        compiler_params=PARAMS,
        cost_estimate=cost(10**9, 6 * 1024 * 1024),
        name="prepare",
    )(
        *map(in_hbm, (start, tile_src, recv_sub, recv_cluster, tile_weight)),
        *map(in_hbm, (features, w_self, w_neigh, grad_out, bias)),
    )

    def sum_call(kernel, out_shape, name, slots, *operands):
        return pl.pallas_call(
            functools.partial(kernel, own, slots),
            out_shape=out_shape,
            in_specs=[VMEM] * (len(operands) + len(slots)),
            out_specs=jax.tree.map(lambda _: VMEM, out_shape),
            scratch_shapes=[pltpu.VMEM((len(slots) * size, width), BF)],
            compiler_params=PARAMS,
            cost_estimate=cost(dict(first=10**9, near=10**9)[name], 3 * 1024 * 1024),
            name=name,
        )(*operands, *[got[slot] for slot in slots])

    for d in relayed:
        value = pl.pallas_call(
            functools.partial(relay_kernel, sub_count, d - 1),
            out_shape=jax.ShapeDtypeStruct((size + EXTRA, width), BF),
            in_specs=[VMEM] * 2,
            out_specs=VMEM,
            compiler_params=PARAMS,
            cost_estimate=cost(10**6, 256 * 1024),
            name="relay",
        )(got[sub_count + 1], got[sub_count + d - 1])
        got[sub_count + d] = along(value, 1)
    first_sum, own_pre = sum_call(
        first_kernel, [wide, wide], "first", [0, sub_count, *(sub_count + d for d in direct), sub_count + 1],
        choice, dense, features, w_self, bias,
    )
    for d in even:
        got[d + 1] = across(after(got[d], choice), 1)
    near_sum = sum_call(near_kernel, wide, "near", even, choice, dense, first_sum)

    late = [*(sub_count + d for d in relayed), *(d + 1 for d in even), 1]
    outs = pl.pallas_call(
        functools.partial(middle_kernel, *counts, late),
        out_shape=[jax.ShapeDtypeStruct((2 * size, width), BF)] * len(even)
        + [block] * cluster_count
        + [jax.ShapeDtypeStruct((2, size, width), BF), narrow, narrow],
        in_specs=[VMEM] * (8 + len(late)),
        out_specs=[VMEM] * (len(even) + cluster_count + 3),
        scratch_shapes=[pltpu.VMEM((len(late) * size, width), BF)],
        compiler_params=PARAMS,
        cost_estimate=cost(2 * rows * slots * size * width, 6 * 1024 * 1024),
        name="middle",
    )(
        choice, grad_out, w_neigh, dense, dense_t, near_sum, own_pre, inverse,
        *[got[slot] for slot in late],
    )
    *sent, sibling, kept, spread, grad_pre = outs

    back = [(along(sent[len(even) + d - 1], d), sub_count + d, 0) for d in range(1, cluster_count)]
    direct_back = [(across(value, d), d, 0) for d, value in zip(even, sent)]
    sibling_back = [(across(sibling, 1), 1, 0)]
    early_back = back[::-1]

    order = [*even, *(sub_count + d for d in direct), *(d + 1 for d in even), 1, sub_count + 1, *(sub_count + d for d in relayed)]
    total, owner = pl.pallas_call(
        functools.partial(
            own_kernel, own, sub_count, order, [(slot, row) for _, slot, row in early_back]
        ),
        out_shape=[wide, marks],
        in_specs=[VMEM] * (6 + peers + len(early_back)),
        out_specs=[VMEM] * 2,
        compiler_params=PARAMS,
        cost_estimate=cost(10**10, 2 * 1024 * 1024),
        name="own",
    )(
        *[value for value, _, _ in early_back],
        *[got[slot] for slot in order],
        choice, w_self, dense_t, kept, spread, grad_pre,
    )

    swapped_back = [
        (across(after(value, total), 1), d + 1, size) for value, d, _ in direct_back
    ]
    middle_back = []
    if middle_back:
        total = pl.pallas_call(
            functools.partial(add_kernel, own, [(slot, row) for _, slot, row in middle_back]),
            out_shape=wide,
            in_specs=[VMEM] * (2 + len(middle_back)),
            out_specs=VMEM,
            compiler_params=PARAMS,
            cost_estimate=cost(10**9, 2 * 1024 * 1024),
            name="add",
        )(owner, total, *[value for value, _, _ in middle_back])
    back = [*direct_back[::-1], *swapped_back[::-1], *sibling_back]
    return pl.pallas_call(
        functools.partial(final_kernel, own, [(slot, row) for _, slot, row in back]),
        out_shape=narrow,
        in_specs=[VMEM] * (2 + len(back)),
        out_specs=VMEM,
        compiler_params=PARAMS,
        cost_estimate=cost(rows * width * 4, 2 * 1024 * 1024),
        name="final",
    )(owner, total, *[value for value, _, _ in back])


def solution(mesh):
    placed = (
        P(("cluster", "sub"), None),
        P(("cluster", "sub"), None),
        P(),
        P(),
        P(),
        P(("cluster", "sub")),
        P(("cluster", "sub")),
        P(("cluster", "sub"), None, None),
        P(("cluster", "sub"), None),
        P(("cluster", "sub"), None),
    )
    return jax.shard_map(
        shards, mesh=mesh, in_specs=placed, out_specs=P(("cluster", "sub"), None), check_vma=False
    )
```

```python
import functools

import jax
import jax.numpy as jnp
from jax import lax
from jax.experimental import pallas as pl
from jax.experimental.pallas import tpu as pltpu
from jax.sharding import PartitionSpec as P

BF = jnp.bfloat16
F32 = jnp.float32
BOUNDARY = 2
EXTRA = 16
VMEM = pl.BlockSpec(memory_space=pltpu.VMEM)
HBM = pl.BlockSpec(memory_space=pltpu.HBM)
PARAMS = pltpu.CompilerParams(vmem_limit_bytes=24 * 1024 * 1024)


def dot(left, right):
    return jnp.dot(left, right, preferred_element_type=F32)


def dot_right_transposed(left, right):
    return lax.dot_general(left, right, (((1,), (1,)), ((), ())), preferred_element_type=F32)


def gelu_slope(v):
    scale = 0.7978845608028654
    t = jnp.tanh(scale * (v + 0.044715 * v * v * v))
    return 0.5 * (1.0 + t) + (0.5 * scale) * v * (1.0 - t * t) * (1.0 + 3.0 * 0.044715 * v * v)


def edge_kernel(recv_sub, recv_cluster, features, edge, sub_row, cluster_row, sems):
    count = edge.shape[0] - EXTRA
    copies = [
        pltpu.make_async_copy(features.at[0:count, :], edge.at[0:count, :], sems.at[0]),
        pltpu.make_async_copy(recv_sub, sub_row, sems.at[1]),
        pltpu.make_async_copy(recv_cluster, cluster_row, sems.at[2]),
    ]
    for copy in copies:
        copy.start()
    for copy in copies:
        copy.wait()
    sub_count, cluster_count = sub_row.shape[1], cluster_row.shape[1]
    pad = jnp.zeros((1, edge.shape[1] - sub_count - cluster_count), F32)
    row = jnp.concatenate([sub_row[...].astype(F32), cluster_row[...].astype(F32), pad], axis=1)
    edge[count:, :] = jnp.broadcast_to(row, (EXTRA, edge.shape[1])).astype(BF)


def prepare_kernel(
    own, sub_count, cluster_count,
    tile_dst_hbm, tile_src_hbm, recv_sub_hbm, recv_cluster_hbm, tile_weight_hbm,
    features_hbm, w_self_hbm, w_neigh_hbm, grad_out_hbm, bias_hbm,
    dense, dense_t, inverse, choice, features, w_self, w_neigh, grad_out, bias,
    tile_dst, tile_src, recv_sub, recv_cluster, tile_weight, sems,
):
    size = tile_weight.shape[1]
    pairs = (
        (tile_dst_hbm, tile_dst), (tile_src_hbm, tile_src), (recv_sub_hbm, recv_sub),
        (recv_cluster_hbm, recv_cluster), (tile_weight_hbm, tile_weight),
        (features_hbm, features), (w_self_hbm, w_self), (w_neigh_hbm, w_neigh),
        (grad_out_hbm, grad_out), (bias_hbm, bias),
    )
    copies = [pltpu.make_async_copy(a, b, sems.at[i]) for i, (a, b) in enumerate(pairs)]
    for copy in copies:
        copy.start()
    sub_id = lax.axis_index("sub")
    cluster_id = lax.axis_index("cluster")
    dense[...] = jnp.zeros_like(dense)
    dense_t[...] = jnp.zeros_like(dense_t)
    for copy in copies[:5]:
        copy.wait()

    def place(t, carry):
        src = tile_src[t]
        from_sub = own + ((src - own) ^ sub_id)
        from_cluster = own + sub_count + ((src - own - sub_count) ^ cluster_id)
        slot = jnp.where(src < own, src, jnp.where(src < own + sub_count, from_sub, from_cluster))
        dst = pl.ds(pl.multiple_of(tile_dst[t] * size, size), size)
        col = pl.ds(pl.multiple_of(slot * size, size), size)
        tile = tile_weight[t]
        dense[dst, col] = dense[dst, col] + tile
        dense_t[col, dst] = dense_t[col, dst] + tile.T
        return carry

    lax.fori_loop(0, tile_weight.shape[0], place, 0, unroll=4)
    for d in range(sub_count):
        index = recv_sub[0, sub_id ^ d].astype(F32)
        choice[d : d + 1, :] = jnp.full((1, choice.shape[1]), index, F32)
    for d in range(cluster_count):
        index = recv_cluster[0, cluster_id ^ d].astype(F32)
        choice[sub_count + d : sub_count + d + 1, :] = jnp.full((1, choice.shape[1]), index, F32)
    slots = own + sub_count + cluster_count
    total = dense[:, 0:size].astype(F32)
    for slot in range(1, slots):
        total = total + dense[:, slot * size : (slot + 1) * size].astype(F32)
    degree = jnp.sum(total, axis=1, keepdims=True)
    inverse[...] = jnp.broadcast_to(1.0 / (degree + 1.0), inverse.shape)
    for copy in copies[5:]:
        copy.wait()


def index_row(message, size):
    return message[2 * size : 2 * size + EXTRA, :].astype(F32)[0:1, :]


def lane_of(row, lane):
    lanes = lax.broadcasted_iota(jnp.int32, row.shape, 1)
    return jnp.sum(jnp.where(lanes == lane, row, 0.0), axis=1, keepdims=True)


def pick(message, index, size):
    return jnp.where(
        index > 0.5, message[size : 2 * size, :].astype(F32), message[0:size, :].astype(F32)
    ).astype(BF)


def relay_kernel(sub_count, d, far, near, out):
    size = out.shape[0] - EXTRA
    index = lane_of(index_row(near, size), sub_count + (lax.axis_index("cluster") ^ d))
    out[0:size, :] = pick(far, index, size)
    out[size:, :] = far[2 * size :, :]


def trade_kernel(even, sibling, *rest):
    messages, out = rest[:-1], rest[-1]
    size = out.shape[0] // len(even) - EXTRA
    row = index_row(sibling, size)
    for i, (d, message) in enumerate(zip(even, messages)):
        index = lane_of(row, lax.axis_index("sub") ^ d)
        out[i * size : (i + 1) * size, :] = pick(message, index, size)
        at = len(even) * size + i * EXTRA
        out[at : at + EXTRA, :] = message[2 * size :, :]


def turn_kernel(sibling, *rest):
    messages, out = rest[:-1], rest[-1]
    size = sibling.shape[0]
    out[0:size, :] = sibling[...]
    for i, message in enumerate(messages):
        out[(i + 1) * size : (i + 2) * size, :] = message[size : 2 * size, :]


def halo_sum(choice, dense, own, halos, refs, halo):
    size = dense.shape[0] // own
    columns = []
    for i, (slot, at, row, picked) in enumerate(halos):
        if picked:
            block = refs[at][row : row + size, :]
        else:
            block = pick(refs[at], choice[slot : slot + 1, :], size)
        halo[i * size : (i + 1) * size, :] = block
        columns.append(dense[:, (own + slot) * size : (own + slot + 1) * size])
    return dot(jnp.concatenate(columns, axis=1), halo[...])


def first_kernel(own, halos, choice, dense, features, w_self, bias, *rest):
    refs, (total, own_pre, halo) = rest[:-3], rest[-3:]
    size = dense.shape[0] // own
    total[...] = dot(dense[:, 0 : own * size], features[...]) + halo_sum(
        choice, dense, own, halos, refs, halo
    )
    own_pre[...] = dot(features[...], w_self[...]) + bias[...].reshape(1, -1)


def near_kernel(own, halos, choice, dense, before, *rest):
    refs, (total, halo) = rest[:-2], rest[-2:]
    total[...] = before[...] + halo_sum(choice, dense, own, halos, refs, halo)


def middle_kernel(
    own, sub_count, cluster_count, halos, received,
    choice, grad_out, w_neigh, dense, dense_t, before, own_pre, inverse,
    *rest,
):
    refs, rest = rest[:received], rest[received:]
    pairs, rest = rest[: sub_count // 2 - 1], rest[sub_count // 2 - 1 :]
    along, (sibling, kept, spread, grad_pre, halo) = rest[:-5], rest[-5:]
    size = dense.shape[0] // own
    aggregate = before[...] + halo_sum(choice, dense, own, halos, refs, halo)
    inv = jnp.concatenate([inverse[...]] * (grad_out.shape[1] // size), axis=1)
    mean = (aggregate * inv).astype(BF)
    pre = own_pre[...] + dot(mean, w_neigh[...])
    grad = (grad_out[...].astype(F32) * gelu_slope(pre)).astype(BF)
    grad_pre[...] = grad
    spread[...] = (dot_right_transposed(grad, w_neigh[...]) * inv).astype(BF)

    def partial(slot, count=1):
        rows = slice((own + slot) * size, (own + slot + count) * size)
        return dot(dense_t[rows, :], spread[...]).astype(BF)

    for i, target in enumerate(pairs):
        target[...] = partial(2 * (i + 1), 2)
    for i, target in enumerate(along):
        target[...] = partial(sub_count + 1 + i)
    sibling[...] = partial(1)
    kept[0] = partial(0)
    kept[1] = partial(sub_count)


def split(total, value, second, size):
    zero = jnp.zeros_like(value)
    total[0:size, :] = total[0:size, :] + jnp.where(second, zero, value)
    total[size : 2 * size, :] = total[size : 2 * size, :] + jnp.where(second, value, zero)


def own_kernel(own, sub_count, rows, received, parts, *rest):
    back, rest = rest[: len(parts)], rest[len(parts) :]
    messages, rest = rest[:received], rest[received:]
    choice, w_self, dense_t, kept, spread, grad_pre, total, owner = rest
    size = kept.shape[1]
    width = total.shape[1]
    total[...] = dot_right_transposed(grad_pre[...], w_self[...]) + dot(
        dense_t[0 : own * size, :], spread[...]
    )
    for i, slot in enumerate((0, sub_count)):
        split(total, kept[i].astype(F32), choice[slot : slot + 1, :] > 0.5, size)
    for slot, at, row in rows:
        lane = lax.axis_index("sub")
        if slot > sub_count:
            lane = sub_count + lax.axis_index("cluster")
        index = lane_of(messages[at][row : row + EXTRA, :].astype(F32)[0:1, :], lane)
        owner[slot : slot + 1, :] = jnp.broadcast_to(index, (1, width))
    for slot, at, row in parts:
        value = back[at][row : row + size, :].astype(F32)
        split(total, value, owner[slot : slot + 1, :] > 0.5, size)


def add_kernel(own, parts, owner, before, *rest):
    received, total = rest[:-1], rest[-1]
    size = total.shape[0] // own
    total[...] = before[...]
    for slot, at, row in parts:
        value = received[at][row : row + size, :].astype(F32)
        split(total, value, owner[slot : slot + 1, :] > 0.5, size)


def final_kernel(own, parts, owner, total, *rest):
    received, out = rest[:-1], rest[-1]
    size = total.shape[0] // own
    first = total[0:size, :]
    second = total[size : 2 * size, :]
    for slot, at, row in parts:
        value = received[at][row : row + size, :].astype(F32)
        to_second = owner[slot : slot + 1, :] > 0.5
        first = first + jnp.where(to_second, 0.0, value)
        second = second + jnp.where(to_second, value, 0.0)
    out[0:size, :] = first.astype(BF)
    out[size : 2 * size, :] = second.astype(BF)
    out[2 * size :, :] = total[2 * size :, :].astype(BF)


def swap(value, axis, count, d):
    return lax.ppermute(value, axis, [(i, i ^ d) for i in range(count)])


def after(value, other):
    return lax.optimization_barrier((value, other))[0]


def in_hbm(value):
    return pltpu.with_memory_space_constraint(value, pltpu.HBM)


def cost(flops, moved):
    return pl.CostEstimate(flops=flops, bytes_accessed=moved, transcendentals=0)


def shards(
    features, grad_out, w_self, w_neigh, bias, tile_dst, tile_src, tile_weight, recv_sub, recv_cluster
):
    sub_count = lax.axis_size("sub")
    cluster_count = lax.axis_size("cluster")
    peers = sub_count + cluster_count - 2
    size = tile_weight.shape[1]
    rows, width = features.shape
    own = rows // size
    slots = own + sub_count + cluster_count
    counts = (own, sub_count, cluster_count)

    wide = jax.ShapeDtypeStruct((rows, width), F32)
    narrow = jax.ShapeDtypeStruct((rows, width), BF)
    square = jax.ShapeDtypeStruct((width, width), BF)
    block = jax.ShapeDtypeStruct((size, width), BF)
    marks = jax.ShapeDtypeStruct((sub_count + cluster_count, width), F32)

    edge = pl.pallas_call(
        edge_kernel,
        out_shape=jax.ShapeDtypeStruct((BOUNDARY * size + EXTRA, width), BF),
        in_specs=[HBM] * 3,
        out_specs=VMEM,
        scratch_shapes=[
            pltpu.VMEM(recv_sub.shape, jnp.int32),
            pltpu.VMEM(recv_cluster.shape, jnp.int32),
            pltpu.SemaphoreType.DMA((3,)),
        ],
        compiler_params=PARAMS,
        cost_estimate=cost(1024, 256 * 1024),
        name="edge",
    )(in_hbm(recv_sub), in_hbm(recv_cluster), in_hbm(features))

    def along(value, d):
        return swap(value, "cluster", cluster_count, d)

    def across(value, d):
        return swap(value, "sub", sub_count, d)

    even = list(range(2, sub_count, 2))
    direct = list(range(2, cluster_count, 2))
    relayed = list(range(3, cluster_count, 2))
    rows_at = BOUNDARY * size
    got = {0: (edge, 0, False, rows_at), sub_count: (edge, 0, False, rows_at)}
    for d in direct:
        got[sub_count + d] = (along(edge, d), 0, False, rows_at)
    for d in even:
        got[d] = (across(edge, d), 0, False, rows_at)
    got[sub_count + 1] = (along(edge, 1), 0, False, rows_at)
    got[1] = (across(edge, 1), 0, False, rows_at)
    dense, dense_t, inverse, choice, features, w_self, w_neigh, grad_out, bias = pl.pallas_call(
        functools.partial(prepare_kernel, *counts),
        out_shape=[
            jax.ShapeDtypeStruct((rows, slots * size), BF),
            jax.ShapeDtypeStruct((slots * size, rows), BF),
            jax.ShapeDtypeStruct((rows, size), F32),
            marks,
            narrow,
            square,
            square,
            narrow,
            jax.ShapeDtypeStruct(bias.shape, F32),
        ],
        in_specs=[HBM] * 10,
        out_specs=[VMEM] * 9,
        scratch_shapes=[
            pltpu.SMEM(tile_dst.shape, jnp.int32),
            pltpu.SMEM(tile_src.shape, jnp.int32),
            pltpu.SMEM(recv_sub.shape, jnp.int32),
            pltpu.SMEM(recv_cluster.shape, jnp.int32),
            pltpu.VMEM(tile_weight.shape, BF),
            pltpu.SemaphoreType.DMA((10,)),
        ],
        compiler_params=PARAMS,
        cost_estimate=cost(10**8, 6 * 1024 * 1024),
        name="prepare",
    )(
        *map(in_hbm, (tile_dst, tile_src, recv_sub, recv_cluster, tile_weight)),
        *map(in_hbm, (features, w_self, w_neigh, grad_out, bias)),
    )

    def call(kernel, out_shape, name, flops, *operands):
        return pl.pallas_call(
            kernel,
            out_shape=out_shape,
            in_specs=[VMEM] * len(operands),
            out_specs=jax.tree.map(lambda _: VMEM, out_shape),
            compiler_params=PARAMS,
            cost_estimate=cost(flops, 1024 * 1024),
            name=name,
        )(*operands)

    def unique(slots):
        arrays, at = [], {}
        for slot in slots:
            known = [i for i, array in enumerate(arrays) if array is got[slot][0]]
            at[slot] = known[0] if known else len(arrays)
            if not known:
                arrays.append(got[slot][0])
        return arrays, at

    def sum_call(kernel, out_shape, name, slots, *operands):
        arrays, at = unique(slots)
        halos = [(slot, at[slot], got[slot][1], got[slot][2]) for slot in slots]
        return pl.pallas_call(
            functools.partial(kernel, own, halos),
            out_shape=out_shape,
            in_specs=[VMEM] * (len(operands) + len(arrays)),
            out_specs=jax.tree.map(lambda _: VMEM, out_shape),
            scratch_shapes=[pltpu.VMEM((len(slots) * size, width), BF)],
            compiler_params=PARAMS,
            cost_estimate=cost(dict(first=10**9, near=10**10)[name], 3 * 1024 * 1024),
            name=name,
        )(*operands, *arrays)

    for d in relayed:
        value = call(
            functools.partial(relay_kernel, sub_count, d - 1),
            jax.ShapeDtypeStruct((size + EXTRA, width), BF),
            "relay", 10**6, got[sub_count + d - 1][0], got[sub_count + 1][0],
        )
        got[sub_count + d] = (along(value, 1), 0, True, size)
    first_sum, own_pre = sum_call(
        first_kernel, [wide, wide], "first", [0, sub_count, *(sub_count + d for d in direct), sub_count + 1],
        choice, dense, features, w_self, bias,
    )
    value = call(
        functools.partial(trade_kernel, even),
        jax.ShapeDtypeStruct((len(even) * (size + EXTRA), width), BF),
        "trade", 10**6, after(got[1][0], (own_pre, value)), *[got[d][0] for d in even],
    )
    value = across(value, 1)
    for i, d in enumerate(even):
        got[d + 1] = (value, i * size, True, len(even) * size + i * EXTRA)
    near_sum = sum_call(near_kernel, wide, "near", [*even, 1, *(sub_count + d for d in relayed)], choice, dense, first_sum)

    late = [d + 1 for d in even]
    late_arrays, late_at = unique(late)
    late_halos = [(slot, late_at[slot], got[slot][1], got[slot][2]) for slot in late]
    outs = pl.pallas_call(
        functools.partial(middle_kernel, *counts, late_halos, len(late_arrays)),
        out_shape=[jax.ShapeDtypeStruct((2 * size, width), BF)] * len(even)
        + [block] * cluster_count
        + [jax.ShapeDtypeStruct((2, size, width), BF), narrow, narrow],
        in_specs=[VMEM] * (8 + len(late_arrays)),
        out_specs=[VMEM] * (len(even) + cluster_count + 3),
        scratch_shapes=[pltpu.VMEM((len(late) * size, width), BF)],
        compiler_params=PARAMS,
        cost_estimate=cost(2 * rows * slots * size * width, 6 * 1024 * 1024),
        name="middle",
    )(
        choice, grad_out, w_neigh, dense, dense_t, near_sum, own_pre, inverse,
        *late_arrays,
    )
    *sent, sibling, kept, spread, grad_pre = outs

    far = [(sub_count + d, along(sent[len(even) + d - 1], d)) for d in range(1, cluster_count)]
    near = [(d, across(value, d)) for d, value in zip(even, sent)]
    order = [*even, *(sub_count + d for d in direct), *(d + 1 for d in even), 1, sub_count + 1, *(sub_count + d for d in relayed)]
    arrays, at = unique(order)
    early = far[:1:-1]
    total, owner = pl.pallas_call(
        functools.partial(
            own_kernel, own, sub_count, [(slot, at[slot], got[slot][3]) for slot in order],
            len(arrays), [(slot, i, 0) for i, (slot, _) in enumerate(early)],
        ),
        out_shape=[wide, marks],
        in_specs=[VMEM] * (6 + len(arrays) + len(early)),
        out_specs=[VMEM] * 2,
        compiler_params=PARAMS,
        cost_estimate=cost(10**9, 2 * 1024 * 1024),
        name="own",
    )(
        *[value for _, value in early], *arrays,
        choice, w_self, dense_t, kept, spread, grad_pre,
    )

    turned = call(
        turn_kernel,
        jax.ShapeDtypeStruct(((1 + len(even)) * size, width), BF),
        "turn", 10**6, after(sibling, total), *[value for _, value in near],
    )
    turned = across(turned, 1)

    more = [far[1], far[0]]
    if more:
        total = call(
            functools.partial(add_kernel, own, [(slot, i, 0) for i, (slot, _) in enumerate(more)]),
            wide, "add", 10**10, owner, total, *[value for _, value in more],
        )
    last = near[::-1]
    parts = [(slot, i, 0) for i, (slot, _) in enumerate(last)]
    parts += [(d + 1, len(last), (i + 1) * size) for i, d in enumerate(even)]
    parts += [(1, len(last), 0)]
    return call(
        functools.partial(final_kernel, own, parts), narrow, "final", rows * width * 4,
        owner, total, *[value for _, value in last], turned,
    )


def solution(mesh):
    placed = (
        P(("cluster", "sub"), None),
        P(("cluster", "sub"), None),
        P(),
        P(),
        P(),
        P(("cluster", "sub")),
        P(("cluster", "sub")),
        P(("cluster", "sub"), None, None),
        P(("cluster", "sub"), None),
        P(("cluster", "sub"), None),
    )
    return jax.shard_map(
        shards, mesh=mesh, in_specs=placed, out_specs=P(("cluster", "sub"), None), check_vma=False
    )
```

```python
import functools

import jax
import jax.numpy as jnp
from jax import lax
from jax.experimental import pallas as pl
from jax.experimental.pallas import tpu as pltpu
from jax.sharding import PartitionSpec as P

BF = jnp.bfloat16
F32 = jnp.float32
BOUNDARY = 2
EXTRA = 16
VMEM = pl.BlockSpec(memory_space=pltpu.VMEM)
HBM = pl.BlockSpec(memory_space=pltpu.HBM)
PARAMS = pltpu.CompilerParams(vmem_limit_bytes=24 * 1024 * 1024)


def dot(left, right):
    return jnp.dot(left, right, preferred_element_type=F32)


def dot_right_transposed(left, right):
    return lax.dot_general(left, right, (((1,), (1,)), ((), ())), preferred_element_type=F32)


def gelu_slope(v):
    scale = 0.7978845608028654
    t = jnp.tanh(scale * (v + 0.044715 * v * v * v))
    return 0.5 * (1.0 + t) + (0.5 * scale) * v * (1.0 - t * t) * (1.0 + 3.0 * 0.044715 * v * v)


def edge_kernel(recv_sub, recv_cluster, features, edge, rows, sub_row, cluster_row, sems):
    count = edge.shape[0] - EXTRA
    copies = [
        pltpu.make_async_copy(features.at[0:count, :], edge.at[0:count, :], sems.at[0]),
        pltpu.make_async_copy(recv_sub, sub_row, sems.at[1]),
        pltpu.make_async_copy(recv_cluster, cluster_row, sems.at[2]),
    ]
    for copy in copies:
        copy.start()
    copies[1].wait()
    copies[2].wait()
    sub_count, cluster_count = sub_row.shape[1], cluster_row.shape[1]
    pad = jnp.zeros((1, edge.shape[1] - sub_count - cluster_count), F32)
    row = jnp.concatenate([sub_row[...].astype(F32), cluster_row[...].astype(F32), pad], axis=1)
    value = jnp.broadcast_to(row, rows.shape).astype(BF)
    edge[count:, :] = value
    rows[...] = value
    copies[0].wait()


def prepare_kernel(
    own, sub_count, cluster_count,
    tile_dst_hbm, tile_src_hbm, recv_sub_hbm, recv_cluster_hbm, tile_weight_hbm,
    features_hbm, w_self_hbm, w_neigh_hbm, grad_out_hbm, bias_hbm,
    dense, dense_t, inverse, choice, features, w_self, w_neigh, grad_out, bias,
    tile_dst, tile_src, recv_sub, recv_cluster, tile_weight, sems,
):
    size = tile_weight.shape[1]
    pairs = (
        (tile_dst_hbm, tile_dst), (tile_src_hbm, tile_src), (recv_sub_hbm, recv_sub),
        (recv_cluster_hbm, recv_cluster), (tile_weight_hbm, tile_weight),
        (features_hbm, features), (w_self_hbm, w_self), (w_neigh_hbm, w_neigh),
        (grad_out_hbm, grad_out), (bias_hbm, bias),
    )
    copies = [pltpu.make_async_copy(a, b, sems.at[i]) for i, (a, b) in enumerate(pairs)]
    for copy in copies:
        copy.start()
    sub_id = lax.axis_index("sub")
    cluster_id = lax.axis_index("cluster")
    dense[...] = jnp.zeros_like(dense)
    dense_t[...] = jnp.zeros_like(dense_t)
    for copy in copies[:5]:
        copy.wait()

    def place(t, carry):
        src = tile_src[t]
        from_sub = own + ((src - own) ^ sub_id)
        from_cluster = own + sub_count + ((src - own - sub_count) ^ cluster_id)
        slot = jnp.where(src < own, src, jnp.where(src < own + sub_count, from_sub, from_cluster))
        dst = pl.ds(pl.multiple_of(tile_dst[t] * size, size), size)
        col = pl.ds(pl.multiple_of(slot * size, size), size)
        tile = tile_weight[t]
        dense[dst, col] = dense[dst, col] + tile
        dense_t[col, dst] = dense_t[col, dst] + tile.T
        return carry

    lax.fori_loop(0, tile_weight.shape[0], place, 0, unroll=4)
    for d in range(sub_count):
        index = recv_sub[0, sub_id ^ d].astype(F32)
        choice[d : d + 1, :] = jnp.full((1, choice.shape[1]), index, F32)
    for d in range(cluster_count):
        index = recv_cluster[0, cluster_id ^ d].astype(F32)
        choice[sub_count + d : sub_count + d + 1, :] = jnp.full((1, choice.shape[1]), index, F32)
    slots = own + sub_count + cluster_count
    total = dense[:, 0:size].astype(F32)
    for slot in range(1, slots):
        total = total + dense[:, slot * size : (slot + 1) * size].astype(F32)
    degree = jnp.sum(total, axis=1, keepdims=True)
    inverse[...] = jnp.broadcast_to(1.0 / (degree + 1.0), inverse.shape)
    for copy in copies[5:]:
        copy.wait()


def index_row(message, size):
    return message[2 * size : 2 * size + EXTRA, :].astype(F32)[0:1, :]


def lane_of(row, lane):
    lanes = lax.broadcasted_iota(jnp.int32, row.shape, 1)
    return jnp.sum(jnp.where(lanes == lane, row, 0.0), axis=1, keepdims=True)


def pick(message, index, size):
    return jnp.where(
        index > 0.5, message[size : 2 * size, :].astype(F32), message[0:size, :].astype(F32)
    ).astype(BF)


def relay_kernel(sub_count, d, far, near, out):
    size = out.shape[0] - EXTRA
    index = lane_of(index_row(near, size), sub_count + (lax.axis_index("cluster") ^ d))
    out[0:size, :] = pick(far, index, size)
    out[size:, :] = far[2 * size :, :]


def trade_kernel(even, *rest):
    messages, (sibling, out) = rest[:-2], rest[-2:]
    size = out.shape[0] // len(even) - EXTRA
    row = sibling[...].astype(F32)[0:1, :]
    for i, (d, message) in enumerate(zip(even, messages)):
        index = lane_of(row, lax.axis_index("sub") ^ d)
        out[i * size : (i + 1) * size, :] = pick(message, index, size)
        at = len(even) * size + i * EXTRA
        out[at : at + EXTRA, :] = message[2 * size :, :]


def turn_kernel(*rest):
    messages, out = rest[:-1], rest[-1]
    size = out.shape[0] // len(messages)
    for i, message in enumerate(messages):
        out[i * size : (i + 1) * size, :] = message[size : 2 * size, :]


def halo_sum(choice, dense, own, halos, refs, halo):
    size = dense.shape[0] // own
    columns = []
    for i, (slot, at, row, picked) in enumerate(halos):
        if picked:
            block = refs[at][row : row + size, :]
        else:
            block = pick(refs[at], choice[slot : slot + 1, :], size)
        halo[i * size : (i + 1) * size, :] = block
        columns.append(dense[:, (own + slot) * size : (own + slot + 1) * size])
    return dot(jnp.concatenate(columns, axis=1), halo[...])


def first_kernel(own, halos, choice, dense, features, w_self, bias, *rest):
    refs, (total, own_pre, halo) = rest[:-3], rest[-3:]
    size = dense.shape[0] // own
    total[...] = dot(dense[:, 0 : own * size], features[...]) + halo_sum(
        choice, dense, own, halos, refs, halo
    )
    own_pre[...] = dot(features[...], w_self[...]) + bias[...].reshape(1, -1)


def near_kernel(own, halos, choice, dense, before, *rest):
    refs, (total, halo) = rest[:-2], rest[-2:]
    total[...] = before[...] + halo_sum(choice, dense, own, halos, refs, halo)


def middle_kernel(
    own, sub_count, cluster_count, halos, received,
    choice, grad_out, w_neigh, dense, dense_t, before, own_pre, inverse,
    *rest,
):
    refs, rest = rest[:received], rest[received:]
    pairs, rest = rest[: sub_count // 2 - 1], rest[sub_count // 2 - 1 :]
    along, (sibling, kept, spread, grad_pre, halo) = rest[:-5], rest[-5:]
    size = dense.shape[0] // own
    aggregate = before[...] + halo_sum(choice, dense, own, halos, refs, halo)
    inv = jnp.concatenate([inverse[...]] * (grad_out.shape[1] // size), axis=1)
    mean = (aggregate * inv).astype(BF)
    pre = own_pre[...] + dot(mean, w_neigh[...])
    grad = (grad_out[...].astype(F32) * gelu_slope(pre)).astype(BF)
    grad_pre[...] = grad
    spread[...] = (dot_right_transposed(grad, w_neigh[...]) * inv).astype(BF)

    def partial(slot, count=1):
        rows = slice((own + slot) * size, (own + slot + count) * size)
        return dot(dense_t[rows, :], spread[...]).astype(BF)

    for i, target in enumerate(pairs):
        target[...] = partial(2 * (i + 1), 2)
    for i, target in enumerate(along):
        target[...] = partial(sub_count + 1 + i)
    sibling[...] = partial(1)
    kept[0] = partial(0)
    kept[1] = partial(sub_count)


def split(total, value, second, size):
    zero = jnp.zeros_like(value)
    total[0:size, :] = total[0:size, :] + jnp.where(second, zero, value)
    total[size : 2 * size, :] = total[size : 2 * size, :] + jnp.where(second, value, zero)


def own_kernel(own, sub_count, rows, received, parts, *rest):
    back, rest = rest[: len(parts)], rest[len(parts) :]
    messages, rest = rest[:received], rest[received:]
    choice, w_self, dense_t, kept, spread, grad_pre, total, owner = rest
    size = kept.shape[1]
    width = total.shape[1]
    total[...] = dot_right_transposed(grad_pre[...], w_self[...]) + dot(
        dense_t[0 : own * size, :], spread[...]
    )
    for i, slot in enumerate((0, sub_count)):
        split(total, kept[i].astype(F32), choice[slot : slot + 1, :] > 0.5, size)
    for slot, at, row in rows:
        lane = lax.axis_index("sub")
        if slot > sub_count:
            lane = sub_count + lax.axis_index("cluster")
        index = lane_of(messages[at][row : row + EXTRA, :].astype(F32)[0:1, :], lane)
        owner[slot : slot + 1, :] = jnp.broadcast_to(index, (1, width))
    for slot, at, row in parts:
        value = back[at][row : row + size, :].astype(F32)
        split(total, value, owner[slot : slot + 1, :] > 0.5, size)


def add_kernel(own, parts, owner, before, *rest):
    received, total = rest[:-1], rest[-1]
    size = total.shape[0] // own
    total[...] = before[...]
    for slot, at, row in parts:
        value = received[at][row : row + size, :].astype(F32)
        split(total, value, owner[slot : slot + 1, :] > 0.5, size)


def final_kernel(own, parts, owner, total, *rest):
    received, out = rest[:-1], rest[-1]
    size = total.shape[0] // own
    first = total[0:size, :]
    second = total[size : 2 * size, :]
    for slot, at, row in parts:
        value = received[at][row : row + size, :].astype(F32)
        to_second = owner[slot : slot + 1, :] > 0.5
        first = first + jnp.where(to_second, 0.0, value)
        second = second + jnp.where(to_second, value, 0.0)
    out[0:size, :] = first.astype(BF)
    out[size : 2 * size, :] = second.astype(BF)
    out[2 * size :, :] = total[2 * size :, :].astype(BF)


def swap(value, axis, count, d):
    return lax.ppermute(value, axis, [(i, i ^ d) for i in range(count)])


def after(value, other):
    return lax.optimization_barrier((value, other))[0]


def in_hbm(value):
    return pltpu.with_memory_space_constraint(value, pltpu.HBM)


def cost(flops, moved):
    return pl.CostEstimate(flops=flops, bytes_accessed=moved, transcendentals=0)


def shards(
    features, grad_out, w_self, w_neigh, bias, tile_dst, tile_src, tile_weight, recv_sub, recv_cluster
):
    sub_count = lax.axis_size("sub")
    cluster_count = lax.axis_size("cluster")
    peers = sub_count + cluster_count - 2
    size = tile_weight.shape[1]
    rows, width = features.shape
    own = rows // size
    slots = own + sub_count + cluster_count
    counts = (own, sub_count, cluster_count)

    wide = jax.ShapeDtypeStruct((rows, width), F32)
    narrow = jax.ShapeDtypeStruct((rows, width), BF)
    square = jax.ShapeDtypeStruct((width, width), BF)
    block = jax.ShapeDtypeStruct((size, width), BF)
    marks = jax.ShapeDtypeStruct((sub_count + cluster_count, width), F32)

    edge, rows_only = pl.pallas_call(
        edge_kernel,
        out_shape=[
            jax.ShapeDtypeStruct((BOUNDARY * size + EXTRA, width), BF),
            jax.ShapeDtypeStruct((EXTRA, width), BF),
        ],
        in_specs=[HBM] * 3,
        out_specs=[VMEM] * 2,
        scratch_shapes=[
            pltpu.VMEM(recv_sub.shape, jnp.int32),
            pltpu.VMEM(recv_cluster.shape, jnp.int32),
            pltpu.SemaphoreType.DMA((3,)),
        ],
        compiler_params=PARAMS,
        cost_estimate=cost(1024, 256 * 1024),
        name="edge",
    )(in_hbm(recv_sub), in_hbm(recv_cluster), in_hbm(features))

    def along(value, d):
        return swap(value, "cluster", cluster_count, d)

    def across(value, d):
        return swap(value, "sub", sub_count, d)

    even = list(range(2, sub_count, 2))
    direct = list(range(2, cluster_count, 2))
    relayed = list(range(3, cluster_count, 2))
    rows_at = BOUNDARY * size
    got = {0: (edge, 0, False, rows_at), sub_count: (edge, 0, False, rows_at)}
    for d in direct:
        got[sub_count + d] = (along(edge, d), 0, False, rows_at)
    for d in even:
        got[d] = (across(edge, d), 0, False, rows_at)
    got[sub_count + 1] = (along(edge, 1), 0, False, rows_at)
    sibling_rows = across(rows_only, 1)
    dense, dense_t, inverse, choice, features, w_self, w_neigh, grad_out, bias = pl.pallas_call(
        functools.partial(prepare_kernel, *counts),
        out_shape=[
            jax.ShapeDtypeStruct((rows, slots * size), BF),
            jax.ShapeDtypeStruct((slots * size, rows), BF),
            jax.ShapeDtypeStruct((rows, size), F32),
            marks,
            narrow,
            square,
            square,
            narrow,
            jax.ShapeDtypeStruct(bias.shape, F32),
        ],
        in_specs=[HBM] * 10,
        out_specs=[VMEM] * 9,
        scratch_shapes=[
            pltpu.SMEM(tile_dst.shape, jnp.int32),
            pltpu.SMEM(tile_src.shape, jnp.int32),
            pltpu.SMEM(recv_sub.shape, jnp.int32),
            pltpu.SMEM(recv_cluster.shape, jnp.int32),
            pltpu.VMEM(tile_weight.shape, BF),
            pltpu.SemaphoreType.DMA((10,)),
        ],
        compiler_params=PARAMS,
        cost_estimate=cost(10**8, 6 * 1024 * 1024),
        name="prepare",
    )(
        *map(in_hbm, (tile_dst, tile_src, recv_sub, recv_cluster, tile_weight)),
        *map(in_hbm, (features, w_self, w_neigh, grad_out, bias)),
    )

    def call(kernel, out_shape, name, flops, *operands):
        return pl.pallas_call(
            kernel,
            out_shape=out_shape,
            in_specs=[VMEM] * len(operands),
            out_specs=jax.tree.map(lambda _: VMEM, out_shape),
            compiler_params=PARAMS,
            cost_estimate=cost(flops, 1024 * 1024),
            name=name,
        )(*operands)

    def unique(slots):
        arrays, at = [], {}
        for slot in slots:
            known = [i for i, array in enumerate(arrays) if array is got[slot][0]]
            at[slot] = known[0] if known else len(arrays)
            if not known:
                arrays.append(got[slot][0])
        return arrays, at

    def sum_call(kernel, out_shape, name, slots, *operands):
        arrays, at = unique(slots)
        halos = [(slot, at[slot], got[slot][1], got[slot][2]) for slot in slots]
        return pl.pallas_call(
            functools.partial(kernel, own, halos),
            out_shape=out_shape,
            in_specs=[VMEM] * (len(operands) + len(arrays)),
            out_specs=jax.tree.map(lambda _: VMEM, out_shape),
            scratch_shapes=[pltpu.VMEM((len(slots) * size, width), BF)],
            compiler_params=PARAMS,
            cost_estimate=cost(dict(first=10**9, near=10**9, late=10**10)[name], 3 * 1024 * 1024),
            name=name,
        )(*operands, *arrays)

    for d in relayed:
        value = call(
            functools.partial(relay_kernel, sub_count, d - 1),
            jax.ShapeDtypeStruct((size + EXTRA, width), BF),
            "relay", 10**6, got[sub_count + d - 1][0], got[sub_count + 1][0],
        )
        got[sub_count + d] = (along(value, 1), 0, True, size)
    first_sum, own_pre = sum_call(
        first_kernel, [wide, wide], "first", [0, sub_count, *(sub_count + d for d in direct), sub_count + 1],
        choice, dense, features, w_self, bias,
    )
    traded = [0, *even]
    value = call(
        functools.partial(trade_kernel, traded),
        jax.ShapeDtypeStruct((len(traded) * (size + EXTRA), width), BF),
        "trade", 10**6, *[got[d][0] for d in traded], after(sibling_rows, (own_pre, value)),
    )
    value = across(value, 1)
    for i, d in enumerate(traded):
        got[d + 1] = (value, i * size, True, len(traded) * size + i * EXTRA)
    near_sum = sum_call(near_kernel, wide, "near", even, choice, dense, first_sum)
    if relayed:
        slots_late = [sub_count + d for d in relayed]
        near_sum = sum_call(near_kernel, wide, "late", slots_late, choice, dense, near_sum)

    late = [1, *(d + 1 for d in even)]
    late_arrays, late_at = unique(late)
    late_halos = [(slot, late_at[slot], got[slot][1], got[slot][2]) for slot in late]
    outs = pl.pallas_call(
        functools.partial(middle_kernel, *counts, late_halos, len(late_arrays)),
        out_shape=[jax.ShapeDtypeStruct((2 * size, width), BF)] * len(even)
        + [block] * cluster_count
        + [jax.ShapeDtypeStruct((2, size, width), BF), narrow, narrow],
        in_specs=[VMEM] * (8 + len(late_arrays)),
        out_specs=[VMEM] * (len(even) + cluster_count + 3),
        scratch_shapes=[pltpu.VMEM((len(late) * size, width), BF)],
        compiler_params=PARAMS,
        cost_estimate=cost(2 * rows * slots * size * width, 6 * 1024 * 1024),
        name="middle",
    )(
        choice, grad_out, w_neigh, dense, dense_t, near_sum, own_pre, inverse,
        *late_arrays,
    )
    *sent, sibling, kept, spread, grad_pre = outs

    far = [(sub_count + d, along(sent[len(even) + d - 1], d)) for d in range(1, cluster_count)]
    near = [(d, across(value, d)) for d, value in zip(even, sent)]
    beside = (1, across(sibling, 1))
    order = [sub_count + 1, *(sub_count + d for d in direct), *even, *(d + 1 for d in even), 1, *(sub_count + d for d in relayed)]
    arrays, at = unique(order)
    early = far[:1:-1]
    total, owner = pl.pallas_call(
        functools.partial(
            own_kernel, own, sub_count, [(slot, at[slot], got[slot][3]) for slot in order],
            len(arrays), [(slot, i, 0) for i, (slot, _) in enumerate(early)],
        ),
        out_shape=[wide, marks],
        in_specs=[VMEM] * (6 + len(arrays) + len(early)),
        out_specs=[VMEM] * 2,
        compiler_params=PARAMS,
        cost_estimate=cost(10**9, 2 * 1024 * 1024),
        name="own",
    )(
        *[value for _, value in early], *arrays,
        choice, w_self, dense_t, kept, spread, grad_pre,
    )

    turned = call(
        turn_kernel,
        jax.ShapeDtypeStruct((len(even) * size, width), BF),
        "turn", 10**6, *[after(value, total) for _, value in near],
    )
    turned = across(turned, 1)

    more = [far[1], far[0], beside, *near[::-1]]
    if more:
        total = call(
            functools.partial(add_kernel, own, [(slot, i, 0) for i, (slot, _) in enumerate(more)]),
            wide, "add", 10**10, owner, total, *[value for _, value in more],
        )
    last = []
    parts = [(slot, i, 0) for i, (slot, _) in enumerate(last)]
    parts += [(d + 1, len(last), i * size) for i, d in enumerate(even)]
    return call(
        functools.partial(final_kernel, own, parts), narrow, "final", rows * width * 4,
        owner, total, *[value for _, value in last], turned,
    )


def solution(mesh):
    placed = (
        P(("cluster", "sub"), None),
        P(("cluster", "sub"), None),
        P(),
        P(),
        P(),
        P(("cluster", "sub")),
        P(("cluster", "sub")),
        P(("cluster", "sub"), None, None),
        P(("cluster", "sub"), None),
        P(("cluster", "sub"), None),
    )
    return jax.shard_map(
        shards, mesh=mesh, in_specs=placed, out_specs=P(("cluster", "sub"), None), check_vma=False
    )
```

```python
import functools

import jax
import jax.numpy as jnp
from jax import lax
from jax.experimental import pallas as pl
from jax.experimental.pallas import tpu as pltpu
from jax.sharding import PartitionSpec as P

BF = jnp.bfloat16
F32 = jnp.float32
BOUNDARY = 2
EXTRA = 16
VMEM = pl.BlockSpec(memory_space=pltpu.VMEM)
HBM = pl.BlockSpec(memory_space=pltpu.HBM)
PARAMS = pltpu.CompilerParams(vmem_limit_bytes=24 * 1024 * 1024)


def dot(left, right):
    return jnp.dot(left, right, preferred_element_type=F32)


def dot_right_transposed(left, right):
    return lax.dot_general(left, right, (((1,), (1,)), ((), ())), preferred_element_type=F32)


def gelu_slope(v):
    scale = 0.7978845608028654
    t = jnp.tanh(scale * (v + 0.044715 * v * v * v))
    return 0.5 * (1.0 + t) + (0.5 * scale) * v * (1.0 - t * t) * (1.0 + 3.0 * 0.044715 * v * v)


def edge_kernel(recv_sub, recv_cluster, features, edge, rows, sub_row, cluster_row, sems):
    count = edge.shape[0] - EXTRA
    copies = [
        pltpu.make_async_copy(features.at[0:count, :], edge.at[0:count, :], sems.at[0]),
        pltpu.make_async_copy(recv_sub, sub_row, sems.at[1]),
        pltpu.make_async_copy(recv_cluster, cluster_row, sems.at[2]),
    ]
    for copy in copies:
        copy.start()
    copies[1].wait()
    copies[2].wait()
    sub_count, cluster_count = sub_row.shape[1], cluster_row.shape[1]
    pad = jnp.zeros((1, edge.shape[1] - sub_count - cluster_count), F32)
    row = jnp.concatenate([sub_row[...].astype(F32), cluster_row[...].astype(F32), pad], axis=1)
    value = jnp.broadcast_to(row, rows.shape).astype(BF)
    edge[count:, :] = value
    rows[...] = value
    copies[0].wait()


def prepare_kernel(
    own, sub_count, cluster_count,
    tile_dst_hbm, tile_src_hbm, recv_sub_hbm, recv_cluster_hbm, tile_weight_hbm,
    features_hbm, w_self_hbm, w_neigh_hbm, grad_out_hbm, bias_hbm,
    dense, dense_t, inverse, choice, features, w_self, w_neigh, grad_out, bias,
    tile_dst, tile_src, recv_sub, recv_cluster, tile_weight, sems,
):
    size = tile_weight.shape[1]
    pairs = (
        (tile_dst_hbm, tile_dst), (tile_src_hbm, tile_src), (recv_sub_hbm, recv_sub),
        (recv_cluster_hbm, recv_cluster), (tile_weight_hbm, tile_weight),
        (features_hbm, features), (w_self_hbm, w_self), (w_neigh_hbm, w_neigh),
        (grad_out_hbm, grad_out), (bias_hbm, bias),
    )
    copies = [pltpu.make_async_copy(a, b, sems.at[i]) for i, (a, b) in enumerate(pairs)]
    for copy in copies:
        copy.start()
    sub_id = lax.axis_index("sub")
    cluster_id = lax.axis_index("cluster")
    dense[...] = jnp.zeros_like(dense)
    dense_t[...] = jnp.zeros_like(dense_t)
    for copy in copies[:5]:
        copy.wait()

    def place(t, carry):
        src = tile_src[t]
        from_sub = own + ((src - own) ^ sub_id)
        from_cluster = own + sub_count + ((src - own - sub_count) ^ cluster_id)
        slot = jnp.where(src < own, src, jnp.where(src < own + sub_count, from_sub, from_cluster))
        dst = pl.ds(pl.multiple_of(tile_dst[t] * size, size), size)
        col = pl.ds(pl.multiple_of(slot * size, size), size)
        tile = tile_weight[t]
        dense[dst, col] = dense[dst, col] + tile
        dense_t[col, dst] = dense_t[col, dst] + tile.T
        return carry

    lax.fori_loop(0, tile_weight.shape[0], place, 0, unroll=4)
    for d in range(sub_count):
        index = recv_sub[0, sub_id ^ d].astype(F32)
        choice[d : d + 1, :] = jnp.full((1, choice.shape[1]), index, F32)
    for d in range(cluster_count):
        index = recv_cluster[0, cluster_id ^ d].astype(F32)
        choice[sub_count + d : sub_count + d + 1, :] = jnp.full((1, choice.shape[1]), index, F32)
    slots = own + sub_count + cluster_count
    total = dense[:, 0:size].astype(F32)
    for slot in range(1, slots):
        total = total + dense[:, slot * size : (slot + 1) * size].astype(F32)
    degree = jnp.sum(total, axis=1, keepdims=True)
    inverse[...] = jnp.broadcast_to(1.0 / (degree + 1.0), inverse.shape)
    for copy in copies[5:]:
        copy.wait()


def index_row(message, size):
    return message[2 * size : 2 * size + EXTRA, :].astype(F32)[0:1, :]


def lane_of(row, lane):
    lanes = lax.broadcasted_iota(jnp.int32, row.shape, 1)
    return jnp.sum(jnp.where(lanes == lane, row, 0.0), axis=1, keepdims=True)


def pick(message, index, size):
    return jnp.where(
        index > 0.5, message[size : 2 * size, :].astype(F32), message[0:size, :].astype(F32)
    ).astype(BF)


def rows_kernel(message, out):
    out[...] = message[message.shape[0] - EXTRA :, :]


def relay_kernel(sub_count, d, far, rows, near, out):
    size = out.shape[0] - EXTRA
    index = lane_of(index_row(near, size), sub_count + (lax.axis_index("cluster") ^ d))
    out[0:size, :] = pick(far, index, size)
    out[size:, :] = rows[...]


def trade_kernel(even, *rest):
    messages, (sibling, out) = rest[:-2], rest[-2:]
    size = out.shape[0] // len(even) - EXTRA
    row = sibling[...].astype(F32)[0:1, :]
    for i, (d, message) in enumerate(zip(even, messages)):
        index = lane_of(row, lax.axis_index("sub") ^ d)
        out[i * size : (i + 1) * size, :] = pick(message, index, size)
        at = len(even) * size + i * EXTRA
        out[at : at + EXTRA, :] = message[2 * size :, :]


def turn_kernel(*rest):
    messages, out = rest[:-1], rest[-1]
    size = out.shape[0] // len(messages)
    for i, message in enumerate(messages):
        out[i * size : (i + 1) * size, :] = message[size : 2 * size, :]


def halo_sum(choice, dense, own, halos, refs, halo):
    size = dense.shape[0] // own
    columns = []
    for i, (slot, at, row, picked) in enumerate(halos):
        if picked:
            block = refs[at][row : row + size, :]
        else:
            block = pick(refs[at], choice[slot : slot + 1, :], size)
        halo[i * size : (i + 1) * size, :] = block
        columns.append(dense[:, (own + slot) * size : (own + slot + 1) * size])
    return dot(jnp.concatenate(columns, axis=1), halo[...])


def first_kernel(own, halos, choice, dense, features, w_self, bias, *rest):
    refs, (total, own_pre, halo) = rest[:-3], rest[-3:]
    size = dense.shape[0] // own
    total[...] = dot(dense[:, 0 : own * size], features[...]) + halo_sum(
        choice, dense, own, halos, refs, halo
    )
    own_pre[...] = dot(features[...], w_self[...]) + bias[...].reshape(1, -1)


def near_kernel(own, halos, choice, dense, before, *rest):
    refs, (total, halo) = rest[:-2], rest[-2:]
    total[...] = before[...] + halo_sum(choice, dense, own, halos, refs, halo)


def middle_kernel(
    own, sub_count, cluster_count, halos, received,
    choice, grad_out, w_neigh, dense, dense_t, before, own_pre, inverse,
    *rest,
):
    refs, rest = rest[:received], rest[received:]
    pairs, rest = rest[: sub_count // 2 - 1], rest[sub_count // 2 - 1 :]
    along, (sibling, kept, spread, grad_pre, halo) = rest[:-5], rest[-5:]
    size = dense.shape[0] // own
    aggregate = before[...] + halo_sum(choice, dense, own, halos, refs, halo)
    inv = jnp.concatenate([inverse[...]] * (grad_out.shape[1] // size), axis=1)
    mean = (aggregate * inv).astype(BF)
    pre = own_pre[...] + dot(mean, w_neigh[...])
    grad = (grad_out[...].astype(F32) * gelu_slope(pre)).astype(BF)
    grad_pre[...] = grad
    spread[...] = (dot_right_transposed(grad, w_neigh[...]) * inv).astype(BF)

    def partial(slot, count=1):
        rows = slice((own + slot) * size, (own + slot + count) * size)
        return dot(dense_t[rows, :], spread[...]).astype(BF)

    for i, target in enumerate(pairs):
        target[...] = partial(2 * (i + 1), 2)
    for i, target in enumerate(along):
        target[...] = partial(sub_count + 1 + i)
    sibling[...] = partial(1)
    kept[0] = partial(0)
    kept[1] = partial(sub_count)


def split(total, value, second, size):
    zero = jnp.zeros_like(value)
    total[0:size, :] = total[0:size, :] + jnp.where(second, zero, value)
    total[size : 2 * size, :] = total[size : 2 * size, :] + jnp.where(second, value, zero)


def own_kernel(own, sub_count, rows, received, parts, *rest):
    back, rest = rest[: len(parts)], rest[len(parts) :]
    messages, rest = rest[:received], rest[received:]
    choice, w_self, dense_t, kept, spread, grad_pre, total, owner = rest
    size = kept.shape[1]
    width = total.shape[1]
    total[...] = dot_right_transposed(grad_pre[...], w_self[...]) + dot(
        dense_t[0 : own * size, :], spread[...]
    )
    for i, slot in enumerate((0, sub_count)):
        split(total, kept[i].astype(F32), choice[slot : slot + 1, :] > 0.5, size)
    for slot, at, row in rows:
        lane = lax.axis_index("sub")
        if slot > sub_count:
            lane = sub_count + lax.axis_index("cluster")
        index = lane_of(messages[at][row : row + EXTRA, :].astype(F32)[0:1, :], lane)
        owner[slot : slot + 1, :] = jnp.broadcast_to(index, (1, width))
    for slot, at, row in parts:
        value = back[at][row : row + size, :].astype(F32)
        split(total, value, owner[slot : slot + 1, :] > 0.5, size)


def add_kernel(own, parts, owner, before, *rest):
    received, total = rest[:-1], rest[-1]
    size = total.shape[0] // own
    total[...] = before[...]
    for slot, at, row in parts:
        value = received[at][row : row + size, :].astype(F32)
        split(total, value, owner[slot : slot + 1, :] > 0.5, size)


def final_kernel(own, parts, owner, total, *rest):
    received, out = rest[:-1], rest[-1]
    size = total.shape[0] // own
    first = total[0:size, :]
    second = total[size : 2 * size, :]
    for slot, at, row in parts:
        value = received[at][row : row + size, :].astype(F32)
        to_second = owner[slot : slot + 1, :] > 0.5
        first = first + jnp.where(to_second, 0.0, value)
        second = second + jnp.where(to_second, value, 0.0)
    out[0:size, :] = first.astype(BF)
    out[size : 2 * size, :] = second.astype(BF)
    out[2 * size :, :] = total[2 * size :, :].astype(BF)


def swap(value, axis, count, d):
    return lax.ppermute(value, axis, [(i, i ^ d) for i in range(count)])


def after(value, other):
    return lax.optimization_barrier((value, other))[0]


def in_hbm(value):
    return pltpu.with_memory_space_constraint(value, pltpu.HBM)


def cost(flops, moved):
    return pl.CostEstimate(flops=flops, bytes_accessed=moved, transcendentals=0)


def shards(
    features, grad_out, w_self, w_neigh, bias, tile_dst, tile_src, tile_weight, recv_sub, recv_cluster
):
    sub_count = lax.axis_size("sub")
    cluster_count = lax.axis_size("cluster")
    peers = sub_count + cluster_count - 2
    size = tile_weight.shape[1]
    rows, width = features.shape
    own = rows // size
    slots = own + sub_count + cluster_count
    counts = (own, sub_count, cluster_count)

    wide = jax.ShapeDtypeStruct((rows, width), F32)
    narrow = jax.ShapeDtypeStruct((rows, width), BF)
    square = jax.ShapeDtypeStruct((width, width), BF)
    block = jax.ShapeDtypeStruct((size, width), BF)
    marks = jax.ShapeDtypeStruct((sub_count + cluster_count, width), F32)

    edge, rows_only = pl.pallas_call(
        edge_kernel,
        out_shape=[
            jax.ShapeDtypeStruct((BOUNDARY * size + EXTRA, width), BF),
            jax.ShapeDtypeStruct((EXTRA, width), BF),
        ],
        in_specs=[HBM] * 3,
        out_specs=[VMEM] * 2,
        scratch_shapes=[
            pltpu.VMEM(recv_sub.shape, jnp.int32),
            pltpu.VMEM(recv_cluster.shape, jnp.int32),
            pltpu.SemaphoreType.DMA((3,)),
        ],
        compiler_params=PARAMS,
        cost_estimate=cost(1024, 256 * 1024),
        name="edge",
    )(in_hbm(recv_sub), in_hbm(recv_cluster), in_hbm(features))

    def along(value, d):
        return swap(value, "cluster", cluster_count, d)

    def across(value, d):
        return swap(value, "sub", sub_count, d)

    even = list(range(2, sub_count, 2))
    direct = list(range(2, cluster_count, 2))
    relayed = list(range(3, cluster_count, 2))
    rows_at = BOUNDARY * size
    got = {0: (edge, 0, False, rows_at), sub_count: (edge, 0, False, rows_at)}
    for d in direct:
        got[sub_count + d] = (along(edge, d), 0, False, rows_at)
    for d in even:
        got[d] = (across(edge, d), 0, False, rows_at)
    got[sub_count + 1] = (along(edge, 1), 0, False, rows_at)
    sibling_rows = across(rows_only, 1)
    dense, dense_t, inverse, choice, features, w_self, w_neigh, grad_out, bias = pl.pallas_call(
        functools.partial(prepare_kernel, *counts),
        out_shape=[
            jax.ShapeDtypeStruct((rows, slots * size), BF),
            jax.ShapeDtypeStruct((slots * size, rows), BF),
            jax.ShapeDtypeStruct((rows, size), F32),
            marks,
            narrow,
            square,
            square,
            narrow,
            jax.ShapeDtypeStruct(bias.shape, F32),
        ],
        in_specs=[HBM] * 10,
        out_specs=[VMEM] * 9,
        scratch_shapes=[
            pltpu.SMEM(tile_dst.shape, jnp.int32),
            pltpu.SMEM(tile_src.shape, jnp.int32),
            pltpu.SMEM(recv_sub.shape, jnp.int32),
            pltpu.SMEM(recv_cluster.shape, jnp.int32),
            pltpu.VMEM(tile_weight.shape, BF),
            pltpu.SemaphoreType.DMA((10,)),
        ],
        compiler_params=PARAMS,
        cost_estimate=cost(10**8, 6 * 1024 * 1024),
        name="prepare",
    )(
        *map(in_hbm, (tile_dst, tile_src, recv_sub, recv_cluster, tile_weight)),
        *map(in_hbm, (features, w_self, w_neigh, grad_out, bias)),
    )

    def call(kernel, out_shape, name, flops, *operands):
        return pl.pallas_call(
            kernel,
            out_shape=out_shape,
            in_specs=[VMEM] * len(operands),
            out_specs=jax.tree.map(lambda _: VMEM, out_shape),
            compiler_params=PARAMS,
            cost_estimate=cost(flops, 1024 * 1024),
            name=name,
        )(*operands)

    def unique(slots):
        arrays, at = [], {}
        for slot in slots:
            known = [i for i, array in enumerate(arrays) if array is got[slot][0]]
            at[slot] = known[0] if known else len(arrays)
            if not known:
                arrays.append(got[slot][0])
        return arrays, at

    def sum_call(kernel, out_shape, name, slots, *operands):
        arrays, at = unique(slots)
        halos = [(slot, at[slot], got[slot][1], got[slot][2]) for slot in slots]
        return pl.pallas_call(
            functools.partial(kernel, own, halos),
            out_shape=out_shape,
            in_specs=[VMEM] * (len(operands) + len(arrays)),
            out_specs=jax.tree.map(lambda _: VMEM, out_shape),
            scratch_shapes=[pltpu.VMEM((len(slots) * size, width), BF)],
            compiler_params=PARAMS,
            cost_estimate=cost(dict(first=10**9, near=10**9, late=10**10)[name], 3 * 1024 * 1024),
            name=name,
        )(*operands, *arrays)

    for d in relayed:
        far = got[sub_count + d - 1][0]
        far_rows = call(
            rows_kernel, jax.ShapeDtypeStruct((EXTRA, width), BF), "rows", 10**9, far
        )
        value = call(
            functools.partial(relay_kernel, sub_count, d - 1),
            jax.ShapeDtypeStruct((size + EXTRA, width), BF),
            "relay", 10**6, far, far_rows, got[sub_count + 1][0],
        )
        got[sub_count + d] = (along(value, 1), 0, True, size)
    first_sum, own_pre = sum_call(
        first_kernel, [wide, wide], "first", [0, sub_count, *(sub_count + d for d in direct)],
        choice, dense, features, w_self, bias,
    )
    traded = [0, *even]
    value = call(
        functools.partial(trade_kernel, traded),
        jax.ShapeDtypeStruct((len(traded) * (size + EXTRA), width), BF),
        "trade", 10**6, *[got[d][0] for d in traded], after(sibling_rows, (choice, value)),
    )
    value = across(value, 1)
    for i, d in enumerate(traded):
        got[d + 1] = (value, i * size, True, len(traded) * size + i * EXTRA)
    near_sum = sum_call(near_kernel, wide, "near", [sub_count + 1, *even], choice, dense, first_sum)
    if relayed:
        slots_late = [sub_count + d for d in relayed]
        near_sum = sum_call(near_kernel, wide, "late", slots_late, choice, dense, near_sum)

    late = [1, *(d + 1 for d in even)]
    late_arrays, late_at = unique(late)
    late_halos = [(slot, late_at[slot], got[slot][1], got[slot][2]) for slot in late]
    outs = pl.pallas_call(
        functools.partial(middle_kernel, *counts, late_halos, len(late_arrays)),
        out_shape=[jax.ShapeDtypeStruct((2 * size, width), BF)] * len(even)
        + [block] * cluster_count
        + [jax.ShapeDtypeStruct((2, size, width), BF), narrow, narrow],
        in_specs=[VMEM] * (8 + len(late_arrays)),
        out_specs=[VMEM] * (len(even) + cluster_count + 3),
        scratch_shapes=[pltpu.VMEM((len(late) * size, width), BF)],
        compiler_params=PARAMS,
        cost_estimate=cost(2 * rows * slots * size * width, 6 * 1024 * 1024),
        name="middle",
    )(
        choice, grad_out, w_neigh, dense, dense_t, near_sum, own_pre, inverse,
        *late_arrays,
    )
    *sent, sibling, kept, spread, grad_pre = outs

    far = [(sub_count + d, along(sent[len(even) + d - 1], d)) for d in range(1, cluster_count)]
    near = [(d, across(value, d)) for d, value in zip(even, sent)]
    beside = (1, across(sibling, 1))
    order = [sub_count + 1, *(sub_count + d for d in direct), *even, *(d + 1 for d in even), 1, *(sub_count + d for d in relayed)]
    arrays, at = unique(order)
    early = far[:1:-1]
    total, owner = pl.pallas_call(
        functools.partial(
            own_kernel, own, sub_count, [(slot, at[slot], got[slot][3]) for slot in order],
            len(arrays), [(slot, i, 0) for i, (slot, _) in enumerate(early)],
        ),
        out_shape=[wide, marks],
        in_specs=[VMEM] * (6 + len(arrays) + len(early)),
        out_specs=[VMEM] * 2,
        compiler_params=PARAMS,
        cost_estimate=cost(10**9, 2 * 1024 * 1024),
        name="own",
    )(
        *[value for _, value in early], *arrays,
        choice, w_self, dense_t, kept, spread, grad_pre,
    )

    turned = call(
        turn_kernel,
        jax.ShapeDtypeStruct((len(even) * size, width), BF),
        "turn", 10**6, *[after(value, total) for _, value in near],
    )
    turned = across(turned, 1)

    more = [far[1], far[0], *near[::-1]]
    if more:
        total = call(
            functools.partial(add_kernel, own, [(slot, i, 0) for i, (slot, _) in enumerate(more)]),
            wide, "add", 10**10, owner, total, *[value for _, value in more],
        )
    last = [beside]
    parts = [(slot, i, 0) for i, (slot, _) in enumerate(last)]
    parts += [(d + 1, len(last), i * size) for i, d in enumerate(even)]
    return call(
        functools.partial(final_kernel, own, parts), narrow, "final", rows * width * 4,
        owner, total, *[value for _, value in last], turned,
    )


def solution(mesh):
    placed = (
        P(("cluster", "sub"), None),
        P(("cluster", "sub"), None),
        P(),
        P(),
        P(),
        P(("cluster", "sub")),
        P(("cluster", "sub")),
        P(("cluster", "sub"), None, None),
        P(("cluster", "sub"), None),
        P(("cluster", "sub"), None),
    )
    return jax.shard_map(
        shards, mesh=mesh, in_specs=placed, out_specs=P(("cluster", "sub"), None), check_vma=False
    )
```

```python
import functools

import jax
import jax.numpy as jnp
from jax import lax
from jax.experimental import pallas as pl
from jax.experimental.pallas import tpu as pltpu
from jax.sharding import PartitionSpec as P

BF = jnp.bfloat16
F32 = jnp.float32
BOUNDARY = 2
EXTRA = 16
VMEM = pl.BlockSpec(memory_space=pltpu.VMEM)
HBM = pl.BlockSpec(memory_space=pltpu.HBM)
PARAMS = pltpu.CompilerParams(vmem_limit_bytes=24 * 1024 * 1024)


def dot(left, right):
    return jnp.dot(left, right, preferred_element_type=F32)


def dot_right_transposed(left, right):
    return lax.dot_general(left, right, (((1,), (1,)), ((), ())), preferred_element_type=F32)


def gelu_slope(v):
    scale = 0.7978845608028654
    t = jnp.tanh(scale * (v + 0.044715 * v * v * v))
    return 0.5 * (1.0 + t) + (0.5 * scale) * v * (1.0 - t * t) * (1.0 + 3.0 * 0.044715 * v * v)


def edge_kernel(recv_sub, recv_cluster, features, edge, rows, sub_row, cluster_row, sems):
    count = edge.shape[0] - EXTRA
    copies = [
        pltpu.make_async_copy(features.at[0:count, :], edge.at[0:count, :], sems.at[0]),
        pltpu.make_async_copy(recv_sub, sub_row, sems.at[1]),
        pltpu.make_async_copy(recv_cluster, cluster_row, sems.at[2]),
    ]
    for copy in copies:
        copy.start()
    copies[1].wait()
    copies[2].wait()
    sub_count, cluster_count = sub_row.shape[1], cluster_row.shape[1]
    pad = jnp.zeros((1, edge.shape[1] - sub_count - cluster_count), F32)
    row = jnp.concatenate([sub_row[...].astype(F32), cluster_row[...].astype(F32), pad], axis=1)
    value = jnp.broadcast_to(row, rows.shape).astype(BF)
    edge[count:, :] = value
    rows[...] = value
    copies[0].wait()


def prepare_kernel(
    own, sub_count, cluster_count,
    tile_dst_hbm, tile_src_hbm, recv_sub_hbm, recv_cluster_hbm, tile_weight_hbm,
    features_hbm, w_self_hbm, w_neigh_hbm, grad_out_hbm, bias_hbm,
    dense, dense_t, inverse, choice, features, w_self, w_neigh, grad_out, bias,
    tile_dst, tile_src, recv_sub, recv_cluster, tile_weight, sems,
):
    size = tile_weight.shape[1]
    pairs = (
        (tile_dst_hbm, tile_dst), (tile_src_hbm, tile_src), (recv_sub_hbm, recv_sub),
        (recv_cluster_hbm, recv_cluster), (tile_weight_hbm, tile_weight),
        (features_hbm, features), (w_self_hbm, w_self), (w_neigh_hbm, w_neigh),
        (grad_out_hbm, grad_out), (bias_hbm, bias),
    )
    copies = [pltpu.make_async_copy(a, b, sems.at[i]) for i, (a, b) in enumerate(pairs)]
    for copy in copies:
        copy.start()
    sub_id = lax.axis_index("sub")
    cluster_id = lax.axis_index("cluster")
    dense[...] = jnp.zeros_like(dense)
    dense_t[...] = jnp.zeros_like(dense_t)
    for copy in copies[:5]:
        copy.wait()

    def place(t, carry):
        src = tile_src[t]
        from_sub = own + ((src - own) ^ sub_id)
        from_cluster = own + sub_count + ((src - own - sub_count) ^ cluster_id)
        slot = jnp.where(src < own, src, jnp.where(src < own + sub_count, from_sub, from_cluster))
        dst = pl.ds(pl.multiple_of(tile_dst[t] * size, size), size)
        col = pl.ds(pl.multiple_of(slot * size, size), size)
        tile = tile_weight[t]
        dense[dst, col] = dense[dst, col] + tile
        dense_t[col, dst] = dense_t[col, dst] + tile.T
        return carry

    lax.fori_loop(0, tile_weight.shape[0], place, 0, unroll=4)
    for d in range(sub_count):
        index = recv_sub[0, sub_id ^ d].astype(F32)
        choice[d : d + 1, :] = jnp.full((1, choice.shape[1]), index, F32)
    for d in range(cluster_count):
        index = recv_cluster[0, cluster_id ^ d].astype(F32)
        choice[sub_count + d : sub_count + d + 1, :] = jnp.full((1, choice.shape[1]), index, F32)
    slots = own + sub_count + cluster_count
    total = dense[:, 0:size].astype(F32)
    for slot in range(1, slots):
        total = total + dense[:, slot * size : (slot + 1) * size].astype(F32)
    degree = jnp.sum(total, axis=1, keepdims=True)
    inverse[...] = jnp.broadcast_to(1.0 / (degree + 1.0), inverse.shape)
    for copy in copies[5:]:
        copy.wait()


def index_row(message, size):
    return message[2 * size : 2 * size + EXTRA, :].astype(F32)[0:1, :]


def lane_of(row, lane):
    lanes = lax.broadcasted_iota(jnp.int32, row.shape, 1)
    return jnp.sum(jnp.where(lanes == lane, row, 0.0), axis=1, keepdims=True)


def pick(message, index, size):
    return jnp.where(
        index > 0.5, message[size : 2 * size, :].astype(F32), message[0:size, :].astype(F32)
    ).astype(BF)


def rows_kernel(message, out):
    out[...] = message[message.shape[0] - EXTRA :, :]


def relay_kernel(sub_count, d, far, rows, near, out):
    size = out.shape[0] - EXTRA
    index = lane_of(index_row(near, size), sub_count + (lax.axis_index("cluster") ^ d))
    out[0:size, :] = pick(far, index, size)
    out[size:, :] = rows[...]


def trade_kernel(even, *rest):
    messages, (sibling, out) = rest[:-2], rest[-2:]
    size = out.shape[0] // len(even) - EXTRA
    row = sibling[...].astype(F32)[0:1, :]
    for i, (d, message) in enumerate(zip(even, messages)):
        index = lane_of(row, lax.axis_index("sub") ^ d)
        out[i * size : (i + 1) * size, :] = pick(message, index, size)
        at = len(even) * size + i * EXTRA
        out[at : at + EXTRA, :] = message[2 * size :, :]


def turn_kernel(*rest):
    messages, out = rest[:-1], rest[-1]
    size = out.shape[0] // len(messages)
    for i, message in enumerate(messages):
        out[i * size : (i + 1) * size, :] = message[size : 2 * size, :]


def halo_sum(choice, dense, own, halos, refs, halo):
    size = dense.shape[0] // own
    columns = []
    for i, (slot, at, row, picked) in enumerate(halos):
        if picked:
            block = refs[at][row : row + size, :]
        else:
            block = pick(refs[at], choice[slot : slot + 1, :], size)
        halo[i * size : (i + 1) * size, :] = block
        columns.append(dense[:, (own + slot) * size : (own + slot + 1) * size])
    return dot(jnp.concatenate(columns, axis=1), halo[...])


def first_kernel(own, halos, choice, dense, features, w_self, bias, *rest):
    refs, (total, own_pre, halo) = rest[:-3], rest[-3:]
    size = dense.shape[0] // own
    total[...] = dot(dense[:, 0 : own * size], features[...]) + halo_sum(
        choice, dense, own, halos, refs, halo
    )
    own_pre[...] = dot(features[...], w_self[...]) + bias[...].reshape(1, -1)


def near_kernel(own, halos, choice, dense, before, *rest):
    refs, (total, halo) = rest[:-2], rest[-2:]
    total[...] = before[...] + halo_sum(choice, dense, own, halos, refs, halo)


def middle_kernel(
    own, sub_count, cluster_count, halos, received,
    choice, grad_out, w_neigh, dense, dense_t, before, own_pre, inverse,
    *rest,
):
    refs, rest = rest[:received], rest[received:]
    pairs, rest = rest[: sub_count // 2 - 1], rest[sub_count // 2 - 1 :]
    along, (sibling, kept, spread, grad_pre, halo) = rest[:-5], rest[-5:]
    size = dense.shape[0] // own
    aggregate = before[...] + halo_sum(choice, dense, own, halos, refs, halo)
    inv = jnp.concatenate([inverse[...]] * (grad_out.shape[1] // size), axis=1)
    mean = (aggregate * inv).astype(BF)
    pre = own_pre[...] + dot(mean, w_neigh[...])
    grad = (grad_out[...].astype(F32) * gelu_slope(pre)).astype(BF)
    grad_pre[...] = grad
    spread[...] = (dot_right_transposed(grad, w_neigh[...]) * inv).astype(BF)

    def partial(slot, count=1):
        rows = slice((own + slot) * size, (own + slot + count) * size)
        return dot(dense_t[rows, :], spread[...]).astype(BF)

    for i, target in enumerate(pairs):
        target[...] = partial(2 * (i + 1), 2)
    for i, target in enumerate(along):
        target[...] = partial(sub_count + 1 + i)
    sibling[...] = partial(1)
    kept[0] = partial(0)
    kept[1] = partial(sub_count)


def split(total, value, second, size):
    zero = jnp.zeros_like(value)
    total[0:size, :] = total[0:size, :] + jnp.where(second, zero, value)
    total[size : 2 * size, :] = total[size : 2 * size, :] + jnp.where(second, value, zero)


def own_kernel(own, sub_count, rows, received, parts, *rest):
    back, rest = rest[: len(parts)], rest[len(parts) :]
    messages, rest = rest[:received], rest[received:]
    choice, w_self, dense_t, kept, spread, grad_pre, total, owner = rest
    size = kept.shape[1]
    width = total.shape[1]
    total[...] = dot_right_transposed(grad_pre[...], w_self[...]) + dot(
        dense_t[0 : own * size, :], spread[...]
    )
    for i, slot in enumerate((0, sub_count)):
        split(total, kept[i].astype(F32), choice[slot : slot + 1, :] > 0.5, size)
    for slot, at, row in rows:
        lane = lax.axis_index("sub")
        if slot > sub_count:
            lane = sub_count + lax.axis_index("cluster")
        index = lane_of(messages[at][row : row + EXTRA, :].astype(F32)[0:1, :], lane)
        owner[slot : slot + 1, :] = jnp.broadcast_to(index, (1, width))
    for slot, at, row in parts:
        value = back[at][row : row + size, :].astype(F32)
        split(total, value, owner[slot : slot + 1, :] > 0.5, size)


def add_kernel(own, parts, owner, before, *rest):
    received, total = rest[:-1], rest[-1]
    size = total.shape[0] // own
    total[...] = before[...]
    for slot, at, row in parts:
        value = received[at][row : row + size, :].astype(F32)
        split(total, value, owner[slot : slot + 1, :] > 0.5, size)


def final_kernel(own, parts, owner, total, *rest):
    received, (out, done, sems) = rest[:-3], rest[-3:]
    size = total.shape[0] // own
    copies = []

    def leave(first, last, value):
        done[first:last, :] = value.astype(BF)
        copies.append(
            pltpu.make_async_copy(
                done.at[first:last, :], out.at[first:last, :], sems.at[len(copies)]
            )
        )
        copies[-1].start()

    leave(2 * size, own * size, total[2 * size :, :])
    for block in range(2):
        value = total[block * size : (block + 1) * size, :]
        for slot, at, row in parts:
            index = owner[slot : slot + 1, :]
            mine = index > 0.5 if block else index <= 0.5
            value = value + jnp.where(mine, received[at][row : row + size, :].astype(F32), 0.0)
        leave(block * size, (block + 1) * size, value)
    for copy in copies:
        copy.wait()


def swap(value, axis, count, d):
    return lax.ppermute(value, axis, [(i, i ^ d) for i in range(count)])


def after(value, other):
    return lax.optimization_barrier((value, other))[0]


def in_hbm(value):
    return pltpu.with_memory_space_constraint(value, pltpu.HBM)


def cost(flops, moved):
    return pl.CostEstimate(flops=flops, bytes_accessed=moved, transcendentals=0)


def shards(
    features, grad_out, w_self, w_neigh, bias, tile_dst, tile_src, tile_weight, recv_sub, recv_cluster
):
    sub_count = lax.axis_size("sub")
    cluster_count = lax.axis_size("cluster")
    peers = sub_count + cluster_count - 2
    size = tile_weight.shape[1]
    rows, width = features.shape
    own = rows // size
    slots = own + sub_count + cluster_count
    counts = (own, sub_count, cluster_count)

    wide = jax.ShapeDtypeStruct((rows, width), F32)
    narrow = jax.ShapeDtypeStruct((rows, width), BF)
    square = jax.ShapeDtypeStruct((width, width), BF)
    block = jax.ShapeDtypeStruct((size, width), BF)
    marks = jax.ShapeDtypeStruct((sub_count + cluster_count, width), F32)

    edge, rows_only = pl.pallas_call(
        edge_kernel,
        out_shape=[
            jax.ShapeDtypeStruct((BOUNDARY * size + EXTRA, width), BF),
            jax.ShapeDtypeStruct((EXTRA, width), BF),
        ],
        in_specs=[HBM] * 3,
        out_specs=[VMEM] * 2,
        scratch_shapes=[
            pltpu.VMEM(recv_sub.shape, jnp.int32),
            pltpu.VMEM(recv_cluster.shape, jnp.int32),
            pltpu.SemaphoreType.DMA((3,)),
        ],
        compiler_params=PARAMS,
        cost_estimate=cost(1024, 256 * 1024),
        name="edge",
    )(in_hbm(recv_sub), in_hbm(recv_cluster), in_hbm(features))

    def along(value, d):
        return swap(value, "cluster", cluster_count, d)

    def across(value, d):
        return swap(value, "sub", sub_count, d)

    even = list(range(2, sub_count, 2))
    direct = list(range(2, cluster_count, 2))
    relayed = list(range(3, cluster_count, 2))
    rows_at = BOUNDARY * size
    got = {0: (edge, 0, False, rows_at), sub_count: (edge, 0, False, rows_at)}
    for d in direct:
        got[sub_count + d] = (along(edge, d), 0, False, rows_at)
    for d in even:
        got[d] = (across(edge, d), 0, False, rows_at)
    got[sub_count + 1] = (along(edge, 1), 0, False, rows_at)
    dense, dense_t, inverse, choice, features, w_self, w_neigh, grad_out, bias = pl.pallas_call(
        functools.partial(prepare_kernel, *counts),
        out_shape=[
            jax.ShapeDtypeStruct((rows, slots * size), BF),
            jax.ShapeDtypeStruct((slots * size, rows), BF),
            jax.ShapeDtypeStruct((rows, size), F32),
            marks,
            narrow,
            square,
            square,
            narrow,
            jax.ShapeDtypeStruct(bias.shape, F32),
        ],
        in_specs=[HBM] * 10,
        out_specs=[VMEM] * 9,
        scratch_shapes=[
            pltpu.SMEM(tile_dst.shape, jnp.int32),
            pltpu.SMEM(tile_src.shape, jnp.int32),
            pltpu.SMEM(recv_sub.shape, jnp.int32),
            pltpu.SMEM(recv_cluster.shape, jnp.int32),
            pltpu.VMEM(tile_weight.shape, BF),
            pltpu.SemaphoreType.DMA((10,)),
        ],
        compiler_params=PARAMS,
        cost_estimate=cost(10**8, 6 * 1024 * 1024),
        name="prepare",
    )(
        *map(in_hbm, (tile_dst, tile_src, recv_sub, recv_cluster, tile_weight)),
        *map(in_hbm, (features, w_self, w_neigh, grad_out, bias)),
    )

    def call(kernel, out_shape, name, flops, *operands):
        return pl.pallas_call(
            kernel,
            out_shape=out_shape,
            in_specs=[VMEM] * len(operands),
            out_specs=jax.tree.map(lambda _: VMEM, out_shape),
            compiler_params=PARAMS,
            cost_estimate=cost(flops, 1024 * 1024),
            name=name,
        )(*operands)

    def unique(slots):
        arrays, at = [], {}
        for slot in slots:
            known = [i for i, array in enumerate(arrays) if array is got[slot][0]]
            at[slot] = known[0] if known else len(arrays)
            if not known:
                arrays.append(got[slot][0])
        return arrays, at

    def sum_call(kernel, out_shape, name, slots, *operands):
        arrays, at = unique(slots)
        halos = [(slot, at[slot], got[slot][1], got[slot][2]) for slot in slots]
        return pl.pallas_call(
            functools.partial(kernel, own, halos),
            out_shape=out_shape,
            in_specs=[VMEM] * (len(operands) + len(arrays)),
            out_specs=jax.tree.map(lambda _: VMEM, out_shape),
            scratch_shapes=[pltpu.VMEM((len(slots) * size, width), BF)],
            compiler_params=PARAMS,
            cost_estimate=cost(dict(first=10**9, near=10**9, late=10**10)[name], 3 * 1024 * 1024),
            name=name,
        )(*operands, *arrays)

    for d in relayed:
        far = got[sub_count + d - 1][0]
        far_rows = call(
            rows_kernel, jax.ShapeDtypeStruct((EXTRA, width), BF), "rows", 10**9, far
        )
        value = call(
            functools.partial(relay_kernel, sub_count, d - 1),
            jax.ShapeDtypeStruct((size + EXTRA, width), BF),
            "relay", 10**6, far, far_rows, got[sub_count + 1][0],
        )
        got[sub_count + d] = (along(value, 1), 0, True, size)
    first_sum, own_pre = sum_call(
        first_kernel, [wide, wide], "first", [0, sub_count, *(sub_count + d for d in direct)],
        choice, dense, features, w_self, bias,
    )
    traded = [0, *even]
    sibling_rows = across(after(rows_only, value), 1)
    value = call(
        functools.partial(trade_kernel, traded),
        jax.ShapeDtypeStruct((len(traded) * (size + EXTRA), width), BF),
        "trade", 10**6, *[got[d][0] for d in traded], after(sibling_rows, (choice, value)),
    )
    trade_value = value
    value = across(value, 1)
    for i, d in enumerate(traded):
        got[d + 1] = (value, i * size, True, len(traded) * size + i * EXTRA)
    near_sum = sum_call(
        near_kernel, wide, "near", [sub_count + 1, *even], after(choice, trade_value), dense, first_sum
    )
    if relayed:
        slots_late = [sub_count + d for d in relayed]
        near_sum = sum_call(near_kernel, wide, "late", slots_late, choice, dense, near_sum)

    late = [1, *(d + 1 for d in even)]
    late_arrays, late_at = unique(late)
    late_halos = [(slot, late_at[slot], got[slot][1], got[slot][2]) for slot in late]
    outs = pl.pallas_call(
        functools.partial(middle_kernel, *counts, late_halos, len(late_arrays)),
        out_shape=[jax.ShapeDtypeStruct((2 * size, width), BF)] * len(even)
        + [block] * cluster_count
        + [jax.ShapeDtypeStruct((2, size, width), BF), narrow, narrow],
        in_specs=[VMEM] * (8 + len(late_arrays)),
        out_specs=[VMEM] * (len(even) + cluster_count + 3),
        scratch_shapes=[pltpu.VMEM((len(late) * size, width), BF)],
        compiler_params=PARAMS,
        cost_estimate=cost(2 * rows * slots * size * width, 6 * 1024 * 1024),
        name="middle",
    )(
        choice, grad_out, w_neigh, dense, dense_t, near_sum, own_pre, inverse,
        *late_arrays,
    )
    *sent, sibling, kept, spread, grad_pre = outs

    far = [(sub_count + d, along(sent[len(even) + d - 1], d)) for d in range(1, cluster_count)]
    near = [(d, across(value, d)) for d, value in zip(even, sent)]
    beside = (1, across(sibling, 1))
    order = [sub_count + 1, *(sub_count + d for d in direct), *even, *(d + 1 for d in even), 1, *(sub_count + d for d in relayed)]
    arrays, at = unique(order)
    early = []
    total, owner = pl.pallas_call(
        functools.partial(
            own_kernel, own, sub_count, [(slot, at[slot], got[slot][3]) for slot in order],
            len(arrays), [(slot, i, 0) for i, (slot, _) in enumerate(early)],
        ),
        out_shape=[wide, marks],
        in_specs=[VMEM] * (6 + len(arrays) + len(early)),
        out_specs=[VMEM] * 2,
        compiler_params=PARAMS,
        cost_estimate=cost(2*10**9, 2 * 1024 * 1024),
        name="own",
    )(
        *[value for _, value in early], *arrays,
        choice, w_self, dense_t, kept, spread, grad_pre,
    )

    turned = call(
        turn_kernel,
        jax.ShapeDtypeStruct((len(even) * size, width), BF),
        "turn", 10**6, *[after(value, total) for _, value in near],
    )
    turned = across(turned, 1)

    more = [far[2], far[1], far[0], *near[::-1]]
    if more:
        total = call(
            functools.partial(add_kernel, own, [(slot, i, 0) for i, (slot, _) in enumerate(more)]),
            wide, "add", 10**10, owner, total, *[value for _, value in more],
        )
    last = [beside]
    parts = [(slot, i, 0) for i, (slot, _) in enumerate(last)]
    parts += [(d + 1, len(last), i * size) for i, d in enumerate(even)]
    values = [value for _, value in last]
    return pl.pallas_call(
        functools.partial(final_kernel, own, parts),
        out_shape=narrow,
        in_specs=[VMEM] * (3 + len(values)),
        out_specs=HBM,
        scratch_shapes=[pltpu.VMEM((rows, width), BF), pltpu.SemaphoreType.DMA((3,))],
        compiler_params=PARAMS,
        cost_estimate=cost(rows * width * 4, 1024 * 1024),
        name="final",
    )(owner, total, *values, turned)


def solution(mesh):
    placed = (
        P(("cluster", "sub"), None),
        P(("cluster", "sub"), None),
        P(),
        P(),
        P(),
        P(("cluster", "sub")),
        P(("cluster", "sub")),
        P(("cluster", "sub"), None, None),
        P(("cluster", "sub"), None),
        P(("cluster", "sub"), None),
    )
    return jax.shard_map(
        shards, mesh=mesh, in_specs=placed, out_specs=P(("cluster", "sub"), None), check_vma=False
    )
```

```python
import functools

import jax
import jax.numpy as jnp
from jax import lax
from jax.experimental import pallas as pl
from jax.experimental.pallas import tpu as pltpu
from jax.sharding import PartitionSpec as P

BF = jnp.bfloat16
F32 = jnp.float32
BOUNDARY = 2
EXTRA = 16
CHUNKS = 4
VMEM = pl.BlockSpec(memory_space=pltpu.VMEM)
HBM = pl.BlockSpec(memory_space=pltpu.HBM)
PARAMS = pltpu.CompilerParams(vmem_limit_bytes=24 * 1024 * 1024)


def dot(left, right):
    return jnp.dot(left, right, preferred_element_type=F32)


def dot_right_transposed(left, right):
    return lax.dot_general(left, right, (((1,), (1,)), ((), ())), preferred_element_type=F32)


def gelu_slope(v):
    scale = 0.7978845608028654
    t = jnp.tanh(scale * (v + 0.044715 * v * v * v))
    return 0.5 * (1.0 + t) + (0.5 * scale) * v * (1.0 - t * t) * (1.0 + 3.0 * 0.044715 * v * v)


def edge_kernel(recv_sub, recv_cluster, features, edge, rows, sub_row, cluster_row, sems):
    count = edge.shape[0] - EXTRA
    step = count // CHUNKS
    small = [
        pltpu.make_async_copy(recv_sub, sub_row, sems.at[0]),
        pltpu.make_async_copy(recv_cluster, cluster_row, sems.at[1]),
    ]
    large = []
    for i in range(CHUNKS):
        part = slice(i * step, (i + 1) * step)
        large.append(
            pltpu.make_async_copy(features.at[part, :], edge.at[part, :], sems.at[2 + i])
        )
    for copy in small + large:
        copy.start()
    for copy in small:
        copy.wait()
    sub_count, cluster_count = sub_row.shape[1], cluster_row.shape[1]
    pad = jnp.zeros((1, edge.shape[1] - sub_count - cluster_count), F32)
    row = jnp.concatenate([sub_row[...].astype(F32), cluster_row[...].astype(F32), pad], axis=1)
    value = jnp.broadcast_to(row, rows.shape).astype(BF)
    edge[count:, :] = value
    rows[...] = value
    for copy in large:
        copy.wait()


def prepare_kernel(
    own, sub_count, cluster_count,
    tile_dst_hbm, tile_src_hbm, recv_sub_hbm, recv_cluster_hbm, tile_weight_hbm,
    features_hbm, w_self_hbm, w_neigh_hbm, grad_out_hbm, bias_hbm,
    dense, dense_t, inverse, choice, features, w_self, w_neigh, grad_out, bias,
    tile_dst, tile_src, recv_sub, recv_cluster, tile_weight, sems,
):
    size = tile_weight.shape[1]
    step = tile_weight.shape[0] // CHUNKS
    pairs = (
        (tile_dst_hbm, tile_dst), (tile_src_hbm, tile_src), (recv_sub_hbm, recv_sub),
        (recv_cluster_hbm, recv_cluster),
        *(
            (tile_weight_hbm.at[i * step : (i + 1) * step], tile_weight.at[i * step : (i + 1) * step])
            for i in range(CHUNKS)
        ),
        (features_hbm, features), (w_self_hbm, w_self), (w_neigh_hbm, w_neigh),
        (grad_out_hbm, grad_out), (bias_hbm, bias),
    )
    copies = [pltpu.make_async_copy(a, b, sems.at[i]) for i, (a, b) in enumerate(pairs)]
    for copy in copies:
        copy.start()
    sub_id = lax.axis_index("sub")
    cluster_id = lax.axis_index("cluster")
    dense[...] = jnp.zeros_like(dense)
    dense_t[...] = jnp.zeros_like(dense_t)
    for copy in copies[: 4 + CHUNKS]:
        copy.wait()

    def place(t, carry):
        src = tile_src[t]
        from_sub = own + ((src - own) ^ sub_id)
        from_cluster = own + sub_count + ((src - own - sub_count) ^ cluster_id)
        slot = jnp.where(src < own, src, jnp.where(src < own + sub_count, from_sub, from_cluster))
        dst = pl.ds(pl.multiple_of(tile_dst[t] * size, size), size)
        col = pl.ds(pl.multiple_of(slot * size, size), size)
        tile = tile_weight[t]
        dense[dst, col] = dense[dst, col] + tile
        dense_t[col, dst] = dense_t[col, dst] + tile.T
        return carry

    lax.fori_loop(0, tile_weight.shape[0], place, 0, unroll=4)
    for d in range(sub_count):
        index = recv_sub[0, sub_id ^ d].astype(F32)
        choice[d : d + 1, :] = jnp.full((1, choice.shape[1]), index, F32)
    for d in range(cluster_count):
        index = recv_cluster[0, cluster_id ^ d].astype(F32)
        choice[sub_count + d : sub_count + d + 1, :] = jnp.full((1, choice.shape[1]), index, F32)
    slots = own + sub_count + cluster_count
    total = dense[:, 0:size].astype(F32)
    for slot in range(1, slots):
        total = total + dense[:, slot * size : (slot + 1) * size].astype(F32)
    degree = jnp.sum(total, axis=1, keepdims=True)
    inverse[...] = jnp.broadcast_to(1.0 / (degree + 1.0), inverse.shape)
    for copy in copies[4 + CHUNKS :]:
        copy.wait()


def index_row(message, size):
    return message[2 * size : 2 * size + EXTRA, :].astype(F32)[0:1, :]


def lane_of(row, lane):
    lanes = lax.broadcasted_iota(jnp.int32, row.shape, 1)
    return jnp.sum(jnp.where(lanes == lane, row, 0.0), axis=1, keepdims=True)


def pick(message, index, size):
    return jnp.where(
        index > 0.5, message[size : 2 * size, :].astype(F32), message[0:size, :].astype(F32)
    ).astype(BF)


def rows_kernel(message, out):
    out[...] = message[message.shape[0] - EXTRA :, :]


def relay_kernel(sub_count, d, far, rows, near, out):
    size = out.shape[0]
    index = lane_of(index_row(near, size), sub_count + (lax.axis_index("cluster") ^ d))
    out[...] = pick(far, index, size)


def trade_kernel(even, *rest):
    messages, (sibling, out) = rest[:-2], rest[-2:]
    size = out.shape[0] // len(even) - EXTRA
    row = sibling[...].astype(F32)[0:1, :]
    for i, (d, message) in enumerate(zip(even, messages)):
        index = lane_of(row, lax.axis_index("sub") ^ d)
        out[i * size : (i + 1) * size, :] = pick(message, index, size)
        at = len(even) * size + i * EXTRA
        out[at : at + EXTRA, :] = message[2 * size :, :]


def turn_kernel(*rest):
    messages, out = rest[:-1], rest[-1]
    size = out.shape[0] // len(messages)
    for i, message in enumerate(messages):
        last = message.shape[0]
        out[i * size : (i + 1) * size, :] = message[last - size : last, :]


def halo_sum(choice, dense, own, halos, refs, halo):
    size = dense.shape[0] // own
    columns = []
    for i, (slot, at, row, picked) in enumerate(halos):
        if picked:
            block = refs[at][row : row + size, :]
        else:
            block = pick(refs[at], choice[slot : slot + 1, :], size)
        halo[i * size : (i + 1) * size, :] = block
        columns.append(dense[:, (own + slot) * size : (own + slot + 1) * size])
    return dot(jnp.concatenate(columns, axis=1), halo[...])


def first_kernel(own, halos, choice, dense, features, w_self, bias, *rest):
    refs, (total, own_pre, halo) = rest[:-3], rest[-3:]
    size = dense.shape[0] // own
    total[...] = dot(dense[:, 0 : own * size], features[...]) + halo_sum(
        choice, dense, own, halos, refs, halo
    )
    own_pre[...] = dot(features[...], w_self[...]) + bias[...].reshape(1, -1)


def near_kernel(own, halos, choice, dense, before, *rest):
    refs, (total, halo) = rest[:-2], rest[-2:]
    total[...] = before[...] + halo_sum(choice, dense, own, halos, refs, halo)


def middle_kernel(
    own, sub_count, cluster_count, halos, received, carried,
    choice, grad_out, w_neigh, dense, dense_t, before, own_pre, inverse,
    *rest,
):
    refs, rest = rest[:received], rest[received:]
    rows, rest = rest[:carried], rest[carried:]
    pairs, rest = rest[: sub_count // 2 - 1], rest[sub_count // 2 - 1 :]
    along, (sibling, kept, spread, grad_pre, halo) = rest[:-5], rest[-5:]
    size = dense.shape[0] // own
    aggregate = before[...] + halo_sum(choice, dense, own, halos, refs, halo)
    inv = jnp.concatenate([inverse[...]] * (grad_out.shape[1] // size), axis=1)
    mean = (aggregate * inv).astype(BF)
    pre = own_pre[...] + dot(mean, w_neigh[...])
    grad = (grad_out[...].astype(F32) * gelu_slope(pre)).astype(BF)
    grad_pre[...] = grad
    spread[...] = (dot_right_transposed(grad, w_neigh[...]) * inv).astype(BF)

    def partial(slot, count=1):
        rows = slice((own + slot) * size, (own + slot + count) * size)
        return dot(dense_t[rows, :], spread[...]).astype(BF)

    for i, target in enumerate(pairs):
        target[...] = partial(2 * (i + 1), 2)
    for i, target in enumerate(along):
        target[0:size, :] = partial(sub_count + 1 + i)
    for i, value in enumerate(rows):
        along[0][size + i * EXTRA : size + (i + 1) * EXTRA, :] = value[...]
    sibling[...] = partial(1)
    kept[0] = partial(0)
    kept[1] = partial(sub_count)


def split(total, value, second, size):
    zero = jnp.zeros_like(value)
    total[0:size, :] = total[0:size, :] + jnp.where(second, zero, value)
    total[size : 2 * size, :] = total[size : 2 * size, :] + jnp.where(second, value, zero)


def own_kernel(own, sub_count, rows, received, *rest):
    messages, rest = rest[:received], rest[received:]
    choice, w_self, dense_t, kept, spread, grad_pre, total, owner = rest
    size = kept.shape[1]
    width = total.shape[1]
    total[...] = dot_right_transposed(grad_pre[...], w_self[...]) + dot(
        dense_t[0 : own * size, :], spread[...]
    )
    for i, slot in enumerate((0, sub_count)):
        split(total, kept[i].astype(F32), choice[slot : slot + 1, :] > 0.5, size)
    for slot, at, row in rows:
        lane = lax.axis_index("sub")
        if slot > sub_count:
            lane = sub_count + lax.axis_index("cluster")
        index = lane_of(messages[at][row : row + EXTRA, :].astype(F32)[0:1, :], lane)
        owner[slot : slot + 1, :] = jnp.broadcast_to(index, (1, width))


def add_kernel(own, sub_count, parts, rows, owner, before, *rest):
    received, total = rest[:-1], rest[-1]
    size = total.shape[0] // own
    total[...] = before[...]
    for slot, at, row in parts:
        value = received[at][row : row + size, :].astype(F32)
        index = owner[slot : slot + 1, :]
        if slot in rows:
            where, first = rows[slot]
            indices = received[where][first : first + EXTRA, :].astype(F32)[0:1, :]
            index = lane_of(indices, sub_count + lax.axis_index("cluster"))
        split(total, value, index > 0.5, size)


def final_kernel(own, parts, owner, total, *rest):
    received, (out, done, sems) = rest[:-3], rest[-3:]
    size = total.shape[0] // own
    copies = []

    def leave(first, last, value):
        done[first:last, :] = value.astype(BF)
        copies.append(
            pltpu.make_async_copy(
                done.at[first:last, :], out.at[first:last, :], sems.at[len(copies)]
            )
        )
        copies[-1].start()

    leave(2 * size, own * size, total[2 * size :, :])
    for block in range(2):
        value = total[block * size : (block + 1) * size, :]
        for slot, at, row in parts:
            index = owner[slot : slot + 1, :]
            mine = index > 0.5 if block else index <= 0.5
            value = value + jnp.where(mine, received[at][row : row + size, :].astype(F32), 0.0)
        leave(block * size, (block + 1) * size, value)
    for copy in copies:
        copy.wait()


def swap(value, axis, count, d):
    return lax.ppermute(value, axis, [(i, i ^ d) for i in range(count)])


def after(value, other):
    return lax.optimization_barrier((value, other))[0]


def in_hbm(value):
    return pltpu.with_memory_space_constraint(value, pltpu.HBM)


def cost(flops, moved):
    return pl.CostEstimate(flops=flops, bytes_accessed=moved, transcendentals=0)


def shards(
    features, grad_out, w_self, w_neigh, bias, tile_dst, tile_src, tile_weight, recv_sub, recv_cluster
):
    sub_count = lax.axis_size("sub")
    cluster_count = lax.axis_size("cluster")
    peers = sub_count + cluster_count - 2
    size = tile_weight.shape[1]
    rows, width = features.shape
    own = rows // size
    slots = own + sub_count + cluster_count
    counts = (own, sub_count, cluster_count)

    wide = jax.ShapeDtypeStruct((rows, width), F32)
    narrow = jax.ShapeDtypeStruct((rows, width), BF)
    square = jax.ShapeDtypeStruct((width, width), BF)
    block = jax.ShapeDtypeStruct((size, width), BF)
    marks = jax.ShapeDtypeStruct((sub_count + cluster_count, width), F32)

    edge, rows_only = pl.pallas_call(
        edge_kernel,
        out_shape=[
            jax.ShapeDtypeStruct((BOUNDARY * size + EXTRA, width), BF),
            jax.ShapeDtypeStruct((EXTRA, width), BF),
        ],
        in_specs=[HBM] * 3,
        out_specs=[VMEM] * 2,
        scratch_shapes=[
            pltpu.VMEM(recv_sub.shape, jnp.int32),
            pltpu.VMEM(recv_cluster.shape, jnp.int32),
            pltpu.SemaphoreType.DMA((2 + CHUNKS,)),
        ],
        compiler_params=PARAMS,
        cost_estimate=cost(1024, 256 * 1024),
        name="edge",
    )(in_hbm(recv_sub), in_hbm(recv_cluster), in_hbm(features))

    def along(value, d):
        return swap(value, "cluster", cluster_count, d)

    def across(value, d):
        return swap(value, "sub", sub_count, d)

    even = list(range(2, sub_count, 2))
    direct = list(range(2, cluster_count, 2))
    relayed = list(range(3, cluster_count, 2))
    rows_at = BOUNDARY * size
    got = {0: (edge, 0, False, rows_at), sub_count: (edge, 0, False, rows_at)}
    for d in direct:
        got[sub_count + d] = (along(edge, d), 0, False, rows_at)
    for d in even:
        got[d] = (across(edge, d), 0, False, rows_at)
    got[sub_count + 1] = (along(edge, 1), 0, False, rows_at)
    dense, dense_t, inverse, choice, features, w_self, w_neigh, grad_out, bias = pl.pallas_call(
        functools.partial(prepare_kernel, *counts),
        out_shape=[
            jax.ShapeDtypeStruct((rows, slots * size), BF),
            jax.ShapeDtypeStruct((slots * size, rows), BF),
            jax.ShapeDtypeStruct((rows, size), F32),
            marks,
            narrow,
            square,
            square,
            narrow,
            jax.ShapeDtypeStruct(bias.shape, F32),
        ],
        in_specs=[HBM] * 10,
        out_specs=[VMEM] * 9,
        scratch_shapes=[
            pltpu.SMEM(tile_dst.shape, jnp.int32),
            pltpu.SMEM(tile_src.shape, jnp.int32),
            pltpu.SMEM(recv_sub.shape, jnp.int32),
            pltpu.SMEM(recv_cluster.shape, jnp.int32),
            pltpu.VMEM(tile_weight.shape, BF),
            pltpu.SemaphoreType.DMA((9 + CHUNKS,)),
        ],
        compiler_params=PARAMS,
        cost_estimate=cost(10**8, 6 * 1024 * 1024),
        name="prepare",
    )(
        *map(in_hbm, (tile_dst, tile_src, recv_sub, recv_cluster, tile_weight)),
        *map(in_hbm, (features, w_self, w_neigh, grad_out, bias)),
    )

    def call(kernel, out_shape, name, flops, *operands):
        return pl.pallas_call(
            kernel,
            out_shape=out_shape,
            in_specs=[VMEM] * len(operands),
            out_specs=jax.tree.map(lambda _: VMEM, out_shape),
            compiler_params=PARAMS,
            cost_estimate=cost(flops, 1024 * 1024),
            name=name,
        )(*operands)

    def unique(slots):
        arrays, at = [], {}
        for slot in slots:
            known = [i for i, array in enumerate(arrays) if array is got[slot][0]]
            at[slot] = known[0] if known else len(arrays)
            if not known:
                arrays.append(got[slot][0])
        return arrays, at

    def sum_call(kernel, out_shape, name, slots, *operands):
        arrays, at = unique(slots)
        halos = [(slot, at[slot], got[slot][1], got[slot][2]) for slot in slots]
        return pl.pallas_call(
            functools.partial(kernel, own, halos),
            out_shape=out_shape,
            in_specs=[VMEM] * (len(operands) + len(arrays)),
            out_specs=jax.tree.map(lambda _: VMEM, out_shape),
            scratch_shapes=[pltpu.VMEM((len(slots) * size, width), BF)],
            compiler_params=PARAMS,
            cost_estimate=cost(dict(first=10**9, near=10**9, late=10**10)[name], 3 * 1024 * 1024),
            name=name,
        )(*operands, *arrays)

    carried = []
    for d in relayed:
        far = got[sub_count + d - 1][0]
        far_rows = call(
            rows_kernel, jax.ShapeDtypeStruct((EXTRA, width), BF), "rows", 10**9, far
        )
        value = call(
            functools.partial(relay_kernel, sub_count, d - 1),
            block,
            "relay", 10**6, far, far_rows, got[sub_count + 1][0],
        )
        carried.append(far_rows)
        got[sub_count + d] = (along(value, 1), 0, True, None)
    first_sum, own_pre = sum_call(
        first_kernel, [wide, wide], "first", [0, sub_count, *(sub_count + d for d in direct)],
        choice, dense, features, w_self, bias,
    )
    traded = [0, *even]
    sibling_rows = across(after(rows_only, value), 1)
    value = call(
        functools.partial(trade_kernel, traded),
        jax.ShapeDtypeStruct((len(traded) * (size + EXTRA), width), BF),
        "trade", 10**6, *[got[d][0] for d in traded], after(sibling_rows, (choice, value)),
    )
    trade_value = value
    value = across(value, 1)
    for i, d in enumerate(traded):
        got[d + 1] = (value, i * size, True, len(traded) * size + i * EXTRA)
    near_sum = sum_call(
        near_kernel, wide, "near", [sub_count + 1, *even], after(choice, trade_value), dense, first_sum
    )
    if relayed:
        slots_late = [sub_count + d for d in relayed]
        near_sum = sum_call(near_kernel, wide, "late", slots_late, choice, dense, near_sum)

    late = [1, *(d + 1 for d in even)]
    late_arrays, late_at = unique(late)
    late_halos = [(slot, late_at[slot], got[slot][1], got[slot][2]) for slot in late]
    outs = pl.pallas_call(
        functools.partial(middle_kernel, *counts, late_halos, len(late_arrays), len(carried)),
        out_shape=[jax.ShapeDtypeStruct((2 * size, width), BF)] * len(even)
        + [jax.ShapeDtypeStruct((size + len(carried) * EXTRA, width), BF)]
        + [block] * (cluster_count - 1)
        + [jax.ShapeDtypeStruct((2, size, width), BF), narrow, narrow],
        in_specs=[VMEM] * (8 + len(late_arrays) + len(carried)),
        out_specs=[VMEM] * (len(even) + cluster_count + 3),
        scratch_shapes=[pltpu.VMEM((len(late) * size, width), BF)],
        compiler_params=PARAMS,
        cost_estimate=cost(2 * rows * slots * size * width, 6 * 1024 * 1024),
        name="middle",
    )(
        choice, grad_out, w_neigh, dense, dense_t, near_sum, own_pre, inverse,
        *late_arrays, *carried,
    )
    *sent, sibling, kept, spread, grad_pre = outs

    far = [(sub_count + d, along(sent[len(even) + d - 1], d)) for d in range(1, cluster_count)]
    near = [(d, across(value, d)) for d, value in zip(even, sent)]
    order = [sub_count + 1, *(sub_count + d for d in direct), *even, *(d + 1 for d in even), 1]
    arrays, at = unique(order)
    total, owner = pl.pallas_call(
        functools.partial(
            own_kernel, own, sub_count, [(slot, at[slot], got[slot][3]) for slot in order],
            len(arrays),
        ),
        out_shape=[wide, marks],
        in_specs=[VMEM] * (6 + len(arrays)),
        out_specs=[VMEM] * 2,
        compiler_params=PARAMS,
        cost_estimate=cost(10**9, 2 * 1024 * 1024),
        name="own",
    )(*arrays, after(choice, far[-1][1]), w_self, dense_t, kept, spread, grad_pre)

    soon, rest = near[-1:], near[:-1]
    early = call(
        turn_kernel, jax.ShapeDtypeStruct((2 * size, width), BF), "early", 10**6,
        sibling, *[value for _, value in soon],
    )
    early = across(early, 1)
    turned = call(
        turn_kernel, jax.ShapeDtypeStruct((len(rest) * size, width), BF), "turn", 10**6,
        *[after(value, total) for _, value in rest],
    )
    turned = across(turned, 1)
    more = [*far, *near[::-1]]
    places = {slot: (0, size + i * EXTRA) for i, slot in enumerate(sub_count + d for d in relayed)}
    total = call(
        functools.partial(
            add_kernel, own, sub_count, [(slot, i, 0) for i, (slot, _) in enumerate(more)], places
        ),
        wide, "add", 10**10, owner, total, *[value for _, value in more],
    )
    parts = [(1, 0, 0), *[(d + 1, 0, size) for d, _ in soon]]
    parts += [(d + 1, 1, i * size) for i, (d, _) in enumerate(rest)]
    values = [early]
    return pl.pallas_call(
        functools.partial(final_kernel, own, parts),
        out_shape=narrow,
        in_specs=[VMEM] * (3 + len(values)),
        out_specs=HBM,
        scratch_shapes=[pltpu.VMEM((rows, width), BF), pltpu.SemaphoreType.DMA((3,))],
        compiler_params=PARAMS,
        cost_estimate=cost(rows * width * 4, 1024 * 1024),
        name="final",
    )(owner, total, *values, turned)


def solution(mesh):
    placed = (
        P(("cluster", "sub"), None),
        P(("cluster", "sub"), None),
        P(),
        P(),
        P(),
        P(("cluster", "sub")),
        P(("cluster", "sub")),
        P(("cluster", "sub"), None, None),
        P(("cluster", "sub"), None),
        P(("cluster", "sub"), None),
    )
    return jax.shard_map(
        shards, mesh=mesh, in_specs=placed, out_specs=P(("cluster", "sub"), None), check_vma=False
    )
```

```python
import functools

import jax
import jax.numpy as jnp
from jax import lax
from jax.experimental import pallas as pl
from jax.experimental.pallas import tpu as pltpu
from jax.sharding import PartitionSpec as P

BF = jnp.bfloat16
F32 = jnp.float32
BOUNDARY = 2
EXTRA = 16
CHUNKS = 4
VMEM = pl.BlockSpec(memory_space=pltpu.VMEM)
HBM = pl.BlockSpec(memory_space=pltpu.HBM)
PARAMS = pltpu.CompilerParams(vmem_limit_bytes=24 * 1024 * 1024)


def dot(left, right):
    return jnp.dot(left, right, preferred_element_type=F32)


def dot_right_transposed(left, right):
    return lax.dot_general(left, right, (((1,), (1,)), ((), ())), preferred_element_type=F32)


def gelu_slope(v):
    scale = 0.7978845608028654
    t = jnp.tanh(scale * (v + 0.044715 * v * v * v))
    return 0.5 * (1.0 + t) + (0.5 * scale) * v * (1.0 - t * t) * (1.0 + 3.0 * 0.044715 * v * v)


def edge_kernel(recv_sub, recv_cluster, features, edge, rows, sub_row, cluster_row, sems):
    count = edge.shape[0] - EXTRA
    step = count // CHUNKS
    small = [
        pltpu.make_async_copy(recv_sub, sub_row, sems.at[0]),
        pltpu.make_async_copy(recv_cluster, cluster_row, sems.at[1]),
    ]
    large = []
    for i in range(CHUNKS):
        part = slice(i * step, (i + 1) * step)
        large.append(
            pltpu.make_async_copy(features.at[part, :], edge.at[part, :], sems.at[2 + i])
        )
    for copy in small + large:
        copy.start()
    for copy in small:
        copy.wait()
    sub_count, cluster_count = sub_row.shape[1], cluster_row.shape[1]
    pad = jnp.zeros((1, edge.shape[1] - sub_count - cluster_count), F32)
    row = jnp.concatenate([sub_row[...].astype(F32), cluster_row[...].astype(F32), pad], axis=1)
    value = jnp.broadcast_to(row, rows.shape).astype(BF)
    edge[count:, :] = value
    rows[...] = value
    for copy in large:
        copy.wait()


def prepare_kernel(
    own, sub_count, cluster_count,
    tile_dst_hbm, tile_src_hbm, recv_sub_hbm, recv_cluster_hbm, tile_weight_hbm,
    features_hbm, w_self_hbm, w_neigh_hbm, grad_out_hbm, bias_hbm,
    dense, choice, features, w_self, w_neigh, grad_out, bias,
    tile_dst, tile_src, recv_sub, recv_cluster, tile_weight, sems,
):
    size = tile_weight.shape[1]
    step = tile_weight.shape[0] // CHUNKS
    pairs = (
        (tile_dst_hbm, tile_dst), (tile_src_hbm, tile_src), (recv_sub_hbm, recv_sub),
        (recv_cluster_hbm, recv_cluster),
        *(
            (tile_weight_hbm.at[i * step : (i + 1) * step], tile_weight.at[i * step : (i + 1) * step])
            for i in range(CHUNKS)
        ),
        (features_hbm, features), (w_self_hbm, w_self), (w_neigh_hbm, w_neigh),
        (grad_out_hbm, grad_out), (bias_hbm, bias),
    )
    copies = [pltpu.make_async_copy(a, b, sems.at[i]) for i, (a, b) in enumerate(pairs)]
    for copy in copies:
        copy.start()
    sub_id = lax.axis_index("sub")
    cluster_id = lax.axis_index("cluster")
    dense[...] = jnp.zeros_like(dense)
    for copy in copies[: 4 + CHUNKS]:
        copy.wait()

    def place(t, carry):
        src = tile_src[t]
        from_sub = own + ((src - own) ^ sub_id)
        from_cluster = own + sub_count + ((src - own - sub_count) ^ cluster_id)
        slot = jnp.where(src < own, src, jnp.where(src < own + sub_count, from_sub, from_cluster))
        dst = pl.ds(pl.multiple_of(tile_dst[t] * size, size), size)
        col = pl.ds(pl.multiple_of(slot * size, size), size)
        dense[dst, col] = dense[dst, col] + tile_weight[t]
        return carry

    lax.fori_loop(0, tile_weight.shape[0], place, 0, unroll=4)
    for d in range(sub_count):
        index = recv_sub[0, sub_id ^ d].astype(F32)
        choice[d : d + 1, :] = jnp.full((1, choice.shape[1]), index, F32)
    for d in range(cluster_count):
        index = recv_cluster[0, cluster_id ^ d].astype(F32)
        choice[sub_count + d : sub_count + d + 1, :] = jnp.full((1, choice.shape[1]), index, F32)
    for copy in copies[4 + CHUNKS :]:
        copy.wait()


def index_row(message, size):
    return message[2 * size : 2 * size + EXTRA, :].astype(F32)[0:1, :]


def lane_of(row, lane):
    lanes = lax.broadcasted_iota(jnp.int32, row.shape, 1)
    return jnp.sum(jnp.where(lanes == lane, row, 0.0), axis=1, keepdims=True)


def pick(message, index, size):
    return jnp.where(
        index > 0.5, message[size : 2 * size, :].astype(F32), message[0:size, :].astype(F32)
    ).astype(BF)


def rows_kernel(message, out):
    out[...] = message[message.shape[0] - EXTRA :, :]


def relay_kernel(sub_count, d, far, rows, near, out):
    size = out.shape[0]
    index = lane_of(index_row(near, size), sub_count + (lax.axis_index("cluster") ^ d))
    out[...] = pick(far, index, size)


def trade_kernel(even, *rest):
    messages, (sibling, out) = rest[:-2], rest[-2:]
    size = out.shape[0] // len(even) - EXTRA
    row = sibling[...].astype(F32)[0:1, :]
    for i, (d, message) in enumerate(zip(even, messages)):
        index = lane_of(row, lax.axis_index("sub") ^ d)
        out[i * size : (i + 1) * size, :] = pick(message, index, size)
        at = len(even) * size + i * EXTRA
        out[at : at + EXTRA, :] = message[2 * size :, :]


def turn_kernel(*rest):
    messages, out = rest[:-1], rest[-1]
    size = out.shape[0] // len(messages)
    for i, message in enumerate(messages):
        last = message.shape[0]
        out[i * size : (i + 1) * size, :] = message[last - size : last, :]


def halo_sum(choice, dense, own, halos, refs, halo):
    size = dense.shape[0] // own
    columns = []
    for i, (slot, at, row, picked) in enumerate(halos):
        if picked:
            block = refs[at][row : row + size, :]
        else:
            block = pick(refs[at], choice[slot : slot + 1, :], size)
        halo[i * size : (i + 1) * size, :] = block
        columns.append(dense[:, (own + slot) * size : (own + slot + 1) * size])
    return dot(jnp.concatenate(columns, axis=1), halo[...])


def flip_kernel(size, dense, dense_t):
    for at in range(0, dense.shape[1], size):
        dense_t[at : at + size, :] = dense[:, at : at + size].T


def first_kernel(own, halos, choice, dense, features, w_self, bias, *rest):
    refs, (total, own_pre, inverse, halo) = rest[:-4], rest[-4:]
    size = dense.shape[0] // own
    count = dense[:, 0:size].astype(F32)
    for at in range(size, dense.shape[1], size):
        count = count + dense[:, at : at + size].astype(F32)
    degree = jnp.sum(count, axis=1, keepdims=True)
    inverse[...] = jnp.broadcast_to(1.0 / (degree + 1.0), inverse.shape)
    total[...] = dot(dense[:, 0 : own * size], features[...]) + halo_sum(
        choice, dense, own, halos, refs, halo
    )
    own_pre[...] = dot(features[...], w_self[...]) + bias[...].reshape(1, -1)


def near_kernel(own, halos, choice, dense, before, *rest):
    refs, (total, halo) = rest[:-2], rest[-2:]
    total[...] = before[...] + halo_sum(choice, dense, own, halos, refs, halo)


def middle_kernel(
    own, sub_count, cluster_count, halos, received, carried,
    choice, grad_out, w_neigh, dense, dense_t, before, own_pre, inverse,
    *rest,
):
    refs, rest = rest[:received], rest[received:]
    rows, rest = rest[:carried], rest[carried:]
    pairs, rest = rest[: sub_count // 2 - 1], rest[sub_count // 2 - 1 :]
    along, (sibling, kept, spread, grad_pre, halo) = rest[:-5], rest[-5:]
    size = dense.shape[0] // own
    aggregate = before[...] + halo_sum(choice, dense, own, halos, refs, halo)
    inv = jnp.concatenate([inverse[...]] * (grad_out.shape[1] // size), axis=1)
    mean = (aggregate * inv).astype(BF)
    pre = own_pre[...] + dot(mean, w_neigh[...])
    grad = (grad_out[...].astype(F32) * gelu_slope(pre)).astype(BF)
    grad_pre[...] = grad
    spread[...] = (dot_right_transposed(grad, w_neigh[...]) * inv).astype(BF)

    def partial(slot, count=1):
        rows = slice((own + slot) * size, (own + slot + count) * size)
        return dot(dense_t[rows, :], spread[...]).astype(BF)

    for i, target in enumerate(pairs):
        target[...] = partial(2 * (i + 1), 2)
    for i, target in enumerate(along):
        target[0:size, :] = partial(sub_count + 1 + i)
    for i, value in enumerate(rows):
        along[0][size + i * EXTRA : size + (i + 1) * EXTRA, :] = value[...]
    sibling[...] = partial(1)
    kept[0] = partial(0)
    kept[1] = partial(sub_count)


def split(total, value, second, size):
    zero = jnp.zeros_like(value)
    total[0:size, :] = total[0:size, :] + jnp.where(second, zero, value)
    total[size : 2 * size, :] = total[size : 2 * size, :] + jnp.where(second, value, zero)


def own_kernel(own, sub_count, rows, received, *rest):
    messages, rest = rest[:received], rest[received:]
    choice, w_self, dense_t, kept, spread, grad_pre, total, owner = rest
    size = kept.shape[1]
    width = total.shape[1]
    total[...] = dot_right_transposed(grad_pre[...], w_self[...]) + dot(
        dense_t[0 : own * size, :], spread[...]
    )
    for i, slot in enumerate((0, sub_count)):
        split(total, kept[i].astype(F32), choice[slot : slot + 1, :] > 0.5, size)
    for slot, at, row in rows:
        lane = lax.axis_index("sub")
        if slot > sub_count:
            lane = sub_count + lax.axis_index("cluster")
        index = lane_of(messages[at][row : row + EXTRA, :].astype(F32)[0:1, :], lane)
        owner[slot : slot + 1, :] = jnp.broadcast_to(index, (1, width))


def add_kernel(own, sub_count, parts, rows, owner, before, *rest):
    received, total = rest[:-1], rest[-1]
    size = total.shape[0] // own
    total[...] = before[...]
    for slot, at, row in parts:
        value = received[at][row : row + size, :].astype(F32)
        index = owner[slot : slot + 1, :]
        if slot in rows:
            where, first = rows[slot]
            indices = received[where][first : first + EXTRA, :].astype(F32)[0:1, :]
            index = lane_of(indices, sub_count + lax.axis_index("cluster"))
        split(total, value, index > 0.5, size)


def final_kernel(own, parts, owner, total, *rest):
    received, (out, done, sems) = rest[:-3], rest[-3:]
    size = total.shape[0] // own
    copies = []

    def leave(first, last, value):
        done[first:last, :] = value.astype(BF)
        copies.append(
            pltpu.make_async_copy(
                done.at[first:last, :], out.at[first:last, :], sems.at[len(copies)]
            )
        )
        copies[-1].start()

    leave(2 * size, own * size, total[2 * size :, :])
    for block in range(2):
        value = total[block * size : (block + 1) * size, :]
        for slot, at, row in parts:
            index = owner[slot : slot + 1, :]
            mine = index > 0.5 if block else index <= 0.5
            value = value + jnp.where(mine, received[at][row : row + size, :].astype(F32), 0.0)
        leave(block * size, (block + 1) * size, value)
    for copy in copies:
        copy.wait()


def swap(value, axis, count, d):
    return lax.ppermute(value, axis, [(i, i ^ d) for i in range(count)])


def after(value, other):
    return lax.optimization_barrier((value, other))[0]


def in_hbm(value):
    return pltpu.with_memory_space_constraint(value, pltpu.HBM)


def cost(flops, moved):
    return pl.CostEstimate(flops=flops, bytes_accessed=moved, transcendentals=0)


def shards(
    features, grad_out, w_self, w_neigh, bias, tile_dst, tile_src, tile_weight, recv_sub, recv_cluster
):
    sub_count = lax.axis_size("sub")
    cluster_count = lax.axis_size("cluster")
    peers = sub_count + cluster_count - 2
    size = tile_weight.shape[1]
    rows, width = features.shape
    own = rows // size
    slots = own + sub_count + cluster_count
    counts = (own, sub_count, cluster_count)

    wide = jax.ShapeDtypeStruct((rows, width), F32)
    narrow = jax.ShapeDtypeStruct((rows, width), BF)
    square = jax.ShapeDtypeStruct((width, width), BF)
    block = jax.ShapeDtypeStruct((size, width), BF)
    marks = jax.ShapeDtypeStruct((sub_count + cluster_count, width), F32)

    edge, rows_only = pl.pallas_call(
        edge_kernel,
        out_shape=[
            jax.ShapeDtypeStruct((BOUNDARY * size + EXTRA, width), BF),
            jax.ShapeDtypeStruct((EXTRA, width), BF),
        ],
        in_specs=[HBM] * 3,
        out_specs=[VMEM] * 2,
        scratch_shapes=[
            pltpu.VMEM(recv_sub.shape, jnp.int32),
            pltpu.VMEM(recv_cluster.shape, jnp.int32),
            pltpu.SemaphoreType.DMA((2 + CHUNKS,)),
        ],
        compiler_params=PARAMS,
        cost_estimate=cost(1024, 256 * 1024),
        name="edge",
    )(in_hbm(recv_sub), in_hbm(recv_cluster), in_hbm(features))

    def along(value, d):
        return swap(value, "cluster", cluster_count, d)

    def across(value, d):
        return swap(value, "sub", sub_count, d)

    even = list(range(2, sub_count, 2))
    direct = list(range(2, cluster_count, 2))
    relayed = list(range(3, cluster_count, 2))
    rows_at = BOUNDARY * size
    got = {0: (edge, 0, False, rows_at), sub_count: (edge, 0, False, rows_at)}
    for d in direct:
        got[sub_count + d] = (along(edge, d), 0, False, rows_at)
    for d in even:
        got[d] = (across(edge, d), 0, False, rows_at)
    got[sub_count + 1] = (along(edge, 1), 0, False, rows_at)
    dense, choice, features, w_self, w_neigh, grad_out, bias = pl.pallas_call(
        functools.partial(prepare_kernel, *counts),
        out_shape=[
            jax.ShapeDtypeStruct((rows, slots * size), BF),
            marks,
            narrow,
            square,
            square,
            narrow,
            jax.ShapeDtypeStruct(bias.shape, F32),
        ],
        in_specs=[HBM] * 10,
        out_specs=[VMEM] * 7,
        scratch_shapes=[
            pltpu.SMEM(tile_dst.shape, jnp.int32),
            pltpu.SMEM(tile_src.shape, jnp.int32),
            pltpu.SMEM(recv_sub.shape, jnp.int32),
            pltpu.SMEM(recv_cluster.shape, jnp.int32),
            pltpu.VMEM(tile_weight.shape, BF),
            pltpu.SemaphoreType.DMA((9 + CHUNKS,)),
        ],
        compiler_params=PARAMS,
        cost_estimate=cost(10**8, 6 * 1024 * 1024),
        name="prepare",
    )(
        *map(in_hbm, (tile_dst, tile_src, recv_sub, recv_cluster, tile_weight)),
        *map(in_hbm, (features, w_self, w_neigh, grad_out, bias)),
    )

    def call(kernel, out_shape, name, flops, *operands):
        return pl.pallas_call(
            kernel,
            out_shape=out_shape,
            in_specs=[VMEM] * len(operands),
            out_specs=jax.tree.map(lambda _: VMEM, out_shape),
            compiler_params=PARAMS,
            cost_estimate=cost(flops, 1024 * 1024),
            name=name,
        )(*operands)

    def unique(slots):
        arrays, at = [], {}
        for slot in slots:
            known = [i for i, array in enumerate(arrays) if array is got[slot][0]]
            at[slot] = known[0] if known else len(arrays)
            if not known:
                arrays.append(got[slot][0])
        return arrays, at

    def sum_call(kernel, out_shape, name, slots, *operands):
        arrays, at = unique(slots)
        halos = [(slot, at[slot], got[slot][1], got[slot][2]) for slot in slots]
        return pl.pallas_call(
            functools.partial(kernel, own, halos),
            out_shape=out_shape,
            in_specs=[VMEM] * (len(operands) + len(arrays)),
            out_specs=jax.tree.map(lambda _: VMEM, out_shape),
            scratch_shapes=[pltpu.VMEM((len(slots) * size, width), BF)],
            compiler_params=PARAMS,
            cost_estimate=cost(dict(first=10**9, near=10**9, late=10**10)[name], 3 * 1024 * 1024),
            name=name,
        )(*operands, *arrays)

    carried = []
    for d in relayed:
        far = got[sub_count + d - 1][0]
        far_rows = call(
            rows_kernel, jax.ShapeDtypeStruct((EXTRA, width), BF), "rows", 10**9, far
        )
        value = call(
            functools.partial(relay_kernel, sub_count, d - 1),
            block,
            "relay", 10**6, far, far_rows, got[sub_count + 1][0],
        )
        carried.append(far_rows)
        got[sub_count + d] = (along(value, 1), 0, True, None)
    first_sum, own_pre, inverse = sum_call(
        first_kernel, [wide, wide, jax.ShapeDtypeStruct((rows, size), F32)], "first", [0, sub_count, *(sub_count + d for d in direct)],
        choice, dense, features, w_self, bias,
    )
    traded = [0, *even]
    sibling_rows = across(after(rows_only, value), 1)
    value = call(
        functools.partial(trade_kernel, traded),
        jax.ShapeDtypeStruct((len(traded) * (size + EXTRA), width), BF),
        "trade", 10**6, *[got[d][0] for d in traded], after(sibling_rows, (choice, value)),
    )
    trade_value = value
    value = across(value, 1)
    for i, d in enumerate(traded):
        got[d + 1] = (value, i * size, True, len(traded) * size + i * EXTRA)
    near_sum = sum_call(
        near_kernel, wide, "near", [sub_count + 1, *even], after(choice, trade_value), dense, first_sum
    )
    dense_t = call(
        functools.partial(flip_kernel, size), jax.ShapeDtypeStruct((slots * size, rows), BF), "flip", 10**7,
        after(dense, near_sum),
    )
    if relayed:
        slots_late = [sub_count + d for d in relayed]
        near_sum = sum_call(
            near_kernel, wide, "late", slots_late, after(choice, dense_t), dense, near_sum
        )

    late = [1, *(d + 1 for d in even)]
    late_arrays, late_at = unique(late)
    late_halos = [(slot, late_at[slot], got[slot][1], got[slot][2]) for slot in late]
    outs = pl.pallas_call(
        functools.partial(middle_kernel, *counts, late_halos, len(late_arrays), len(carried)),
        out_shape=[jax.ShapeDtypeStruct((2 * size, width), BF)] * len(even)
        + [jax.ShapeDtypeStruct((size + len(carried) * EXTRA, width), BF)]
        + [block] * (cluster_count - 1)
        + [jax.ShapeDtypeStruct((2, size, width), BF), narrow, narrow],
        in_specs=[VMEM] * (8 + len(late_arrays) + len(carried)),
        out_specs=[VMEM] * (len(even) + cluster_count + 3),
        scratch_shapes=[pltpu.VMEM((len(late) * size, width), BF)],
        compiler_params=PARAMS,
        cost_estimate=cost(2 * rows * slots * size * width, 6 * 1024 * 1024),
        name="middle",
    )(
        choice, grad_out, w_neigh, dense, dense_t, near_sum, own_pre, inverse,
        *late_arrays, *carried,
    )
    *sent, sibling, kept, spread, grad_pre = outs

    far = [(sub_count + d, along(sent[len(even) + d - 1], d)) for d in range(1, cluster_count)]
    near = [(d, across(value, d)) for d, value in zip(even, sent)]
    soon, rest = near[-1:], near[:-1]
    early = call(
        turn_kernel, jax.ShapeDtypeStruct((2 * size, width), BF), "early", 10**8,
        sibling, *[value for _, value in soon],
    )
    order = [sub_count + 1, *(sub_count + d for d in direct), *even, *(d + 1 for d in even), 1]
    arrays, at = unique(order)
    total, owner = pl.pallas_call(
        functools.partial(
            own_kernel, own, sub_count, [(slot, at[slot], got[slot][3]) for slot in order],
            len(arrays),
        ),
        out_shape=[wide, marks],
        in_specs=[VMEM] * (6 + len(arrays)),
        out_specs=[VMEM] * 2,
        compiler_params=PARAMS,
        cost_estimate=cost(10**9, 2 * 1024 * 1024),
        name="own",
    )(*arrays, after(choice, (far[-1][1], early)), w_self, dense_t, kept, spread, grad_pre)

    early = across(early, 1)
    turned = call(
        turn_kernel, jax.ShapeDtypeStruct((len(rest) * size, width), BF), "turn", 10**6,
        *[after(value, total) for _, value in rest],
    )
    turned = across(turned, 1)
    more = [*far, *near[::-1]]
    places = {slot: (0, size + i * EXTRA) for i, slot in enumerate(sub_count + d for d in relayed)}
    total = call(
        functools.partial(
            add_kernel, own, sub_count, [(slot, i, 0) for i, (slot, _) in enumerate(more)], places
        ),
        wide, "add", 10**10, owner, total, *[value for _, value in more],
    )
    parts = [(1, 0, 0), *[(d + 1, 0, size) for d, _ in soon]]
    parts += [(d + 1, 1, i * size) for i, (d, _) in enumerate(rest)]
    values = [early]
    return pl.pallas_call(
        functools.partial(final_kernel, own, parts),
        out_shape=narrow,
        in_specs=[VMEM] * (3 + len(values)),
        out_specs=HBM,
        scratch_shapes=[pltpu.VMEM((rows, width), BF), pltpu.SemaphoreType.DMA((3,))],
        compiler_params=PARAMS,
        cost_estimate=cost(rows * width * 4, 1024 * 1024),
        name="final",
    )(owner, total, *values, turned)


def solution(mesh):
    placed = (
        P(("cluster", "sub"), None),
        P(("cluster", "sub"), None),
        P(),
        P(),
        P(),
        P(("cluster", "sub")),
        P(("cluster", "sub")),
        P(("cluster", "sub"), None, None),
        P(("cluster", "sub"), None),
        P(("cluster", "sub"), None),
    )
    return jax.shard_map(
        shards, mesh=mesh, in_specs=placed, out_specs=P(("cluster", "sub"), None), check_vma=False
    )
```

```python
import functools

import jax
import jax.numpy as jnp
from jax import lax
from jax.experimental import pallas as pl
from jax.experimental.pallas import tpu as pltpu
from jax.sharding import PartitionSpec as P

BF = jnp.bfloat16
F32 = jnp.float32
BOUNDARY = 2
EXTRA = 16
CHUNKS = 4
VMEM = pl.BlockSpec(memory_space=pltpu.VMEM)
HBM = pl.BlockSpec(memory_space=pltpu.HBM)
PARAMS = pltpu.CompilerParams(vmem_limit_bytes=24 * 1024 * 1024)


def dot(left, right):
    return jnp.dot(left, right, preferred_element_type=F32)


def dot_right_transposed(left, right):
    return lax.dot_general(left, right, (((1,), (1,)), ((), ())), preferred_element_type=F32)


def gelu_slope(v):
    scale = 0.7978845608028654
    t = jnp.tanh(scale * (v + 0.044715 * v * v * v))
    return 0.5 * (1.0 + t) + (0.5 * scale) * v * (1.0 - t * t) * (1.0 + 3.0 * 0.044715 * v * v)


def edge_kernel(recv_sub, recv_cluster, features, edge, rows, sub_row, cluster_row, sems):
    count = edge.shape[0] - EXTRA
    step = count // CHUNKS
    small = [
        pltpu.make_async_copy(recv_sub, sub_row, sems.at[0]),
        pltpu.make_async_copy(recv_cluster, cluster_row, sems.at[1]),
    ]
    large = []
    for i in range(CHUNKS):
        part = slice(i * step, (i + 1) * step)
        large.append(
            pltpu.make_async_copy(features.at[part, :], edge.at[part, :], sems.at[2 + i])
        )
    for copy in small + large:
        copy.start()
    for copy in small:
        copy.wait()
    sub_count, cluster_count = sub_row.shape[1], cluster_row.shape[1]
    pad = jnp.zeros((1, edge.shape[1] - sub_count - cluster_count), F32)
    row = jnp.concatenate([sub_row[...].astype(F32), cluster_row[...].astype(F32), pad], axis=1)
    value = jnp.broadcast_to(row, rows.shape).astype(BF)
    edge[count:, :] = value
    rows[...] = value
    for copy in large:
        copy.wait()


def prepare_kernel(
    own, sub_count, cluster_count,
    tile_dst_hbm, tile_src_hbm, recv_sub_hbm, recv_cluster_hbm, tile_weight_hbm,
    features_hbm, w_self_hbm, w_neigh_hbm, grad_out_hbm, bias_hbm,
    dense, choice, features, w_self, w_neigh, grad_out, bias,
    tile_dst, tile_src, recv_sub, recv_cluster, tile_weight, sems,
):
    size = tile_weight.shape[1]
    step = tile_weight.shape[0] // CHUNKS
    pairs = (
        (tile_dst_hbm, tile_dst), (tile_src_hbm, tile_src), (recv_sub_hbm, recv_sub),
        (recv_cluster_hbm, recv_cluster),
        *(
            (tile_weight_hbm.at[i * step : (i + 1) * step], tile_weight.at[i * step : (i + 1) * step])
            for i in range(CHUNKS)
        ),
        (features_hbm, features), (w_self_hbm, w_self), (w_neigh_hbm, w_neigh),
        (grad_out_hbm, grad_out), (bias_hbm, bias),
    )
    copies = [pltpu.make_async_copy(a, b, sems.at[i]) for i, (a, b) in enumerate(pairs)]
    for copy in copies:
        copy.start()
    sub_id = lax.axis_index("sub")
    cluster_id = lax.axis_index("cluster")
    dense[...] = jnp.zeros_like(dense)
    for copy in copies[: 4 + CHUNKS]:
        copy.wait()

    def place(t, carry):
        src = tile_src[t]
        from_sub = own + ((src - own) ^ sub_id)
        from_cluster = own + sub_count + ((src - own - sub_count) ^ cluster_id)
        slot = jnp.where(src < own, src, jnp.where(src < own + sub_count, from_sub, from_cluster))
        dst = pl.ds(pl.multiple_of(tile_dst[t] * size, size), size)
        col = pl.ds(pl.multiple_of(slot * size, size), size)
        dense[dst, col] = dense[dst, col] + tile_weight[t]
        return carry

    lax.fori_loop(0, tile_weight.shape[0], place, 0, unroll=4)
    for d in range(sub_count):
        index = recv_sub[0, sub_id ^ d].astype(F32)
        choice[d : d + 1, :] = jnp.full((1, choice.shape[1]), index, F32)
    for d in range(cluster_count):
        index = recv_cluster[0, cluster_id ^ d].astype(F32)
        choice[sub_count + d : sub_count + d + 1, :] = jnp.full((1, choice.shape[1]), index, F32)
    for copy in copies[4 + CHUNKS :]:
        copy.wait()


def index_row(message, size):
    return message[2 * size : 2 * size + EXTRA, :].astype(F32)[0:1, :]


def lane_of(row, lane):
    lanes = lax.broadcasted_iota(jnp.int32, row.shape, 1)
    return jnp.sum(jnp.where(lanes == lane, row, 0.0), axis=1, keepdims=True)


def pick(message, index, size):
    return jnp.where(
        index > 0.5, message[size : 2 * size, :].astype(F32), message[0:size, :].astype(F32)
    ).astype(BF)


def rows_kernel(message, out):
    out[...] = message[message.shape[0] - EXTRA :, :]


def relay_kernel(sub_count, d, far, rows, near, out):
    size = out.shape[0]
    index = lane_of(index_row(near, size), sub_count + (lax.axis_index("cluster") ^ d))
    out[...] = pick(far, index, size)


def trade_kernel(even, *rest):
    messages, (sibling, out) = rest[:-2], rest[-2:]
    size = out.shape[0] // len(even) - EXTRA
    row = sibling[...].astype(F32)[0:1, :]
    for i, (d, message) in enumerate(zip(even, messages)):
        index = lane_of(row, lax.axis_index("sub") ^ d)
        out[i * size : (i + 1) * size, :] = pick(message, index, size)
        at = len(even) * size + i * EXTRA
        out[at : at + EXTRA, :] = message[2 * size :, :]


def turn_kernel(*rest):
    messages, out = rest[:-1], rest[-1]
    size = out.shape[0] // len(messages)
    for i, message in enumerate(messages):
        last = message.shape[0]
        out[i * size : (i + 1) * size, :] = message[last - size : last, :]


def halo_blocks(choice, size, halos, refs, halo):
    first = halos[0]
    if all(
        (at, row, picked) == (first[1], first[2] + i * size, True)
        for i, (_, at, row, picked) in enumerate(halos)
    ):
        return refs[first[1]][first[2] : first[2] + len(halos) * size, :]
    for i, (slot, at, row, picked) in enumerate(halos):
        if picked:
            block = refs[at][row : row + size, :]
        else:
            block = pick(refs[at], choice[slot : slot + 1, :], size)
        halo[i * size : (i + 1) * size, :] = block
    return halo[...]


def halo_sum(choice, dense, own, halos, refs, halo):
    size = dense.shape[0] // own
    blocks = halo_blocks(choice, size, halos, refs, halo)
    columns = [dense[:, (own + slot) * size : (own + slot + 1) * size] for slot, *_ in halos]
    return dot(jnp.concatenate(columns, axis=1), blocks)


def flip_kernel(size, dense, dense_t):
    for at in range(0, dense.shape[1], size):
        dense_t[at : at + size, :] = dense[:, at : at + size].T


def first_kernel(own, halos, choice, dense, features, w_self, bias, *rest):
    refs, (total, own_pre, inverse, halo) = rest[:-4], rest[-4:]
    size = dense.shape[0] // own
    count = dense[:, 0:size].astype(F32)
    for at in range(size, dense.shape[1], size):
        count = count + dense[:, at : at + size].astype(F32)
    degree = jnp.sum(count, axis=1, keepdims=True)
    inverse[...] = jnp.broadcast_to(1.0 / (degree + 1.0), inverse.shape)
    total[...] = dot(dense[:, 0 : own * size], features[...]) + halo_sum(
        choice, dense, own, halos, refs, halo
    )
    own_pre[...] = dot(features[...], w_self[...]) + bias[...].reshape(1, -1)


def near_kernel(own, halos, choice, dense, before, *rest):
    refs, (total, halo) = rest[:-2], rest[-2:]
    total[...] = before[...] + halo_sum(choice, dense, own, halos, refs, halo)


def middle_kernel(
    own, sub_count, cluster_count, halos, received, carried,
    choice, grad_out, w_neigh, dense, dense_t, before, own_pre, inverse,
    *rest,
):
    refs, rest = rest[:received], rest[received:]
    rows, rest = rest[:carried], rest[carried:]
    pairs, rest = rest[: sub_count // 2 - 1], rest[sub_count // 2 - 1 :]
    along, (sibling, kept, spread, grad_pre, halo) = rest[:-5], rest[-5:]
    size = dense.shape[0] // own
    blocks = halo_blocks(choice, size, halos, refs, halo)
    for at in range(0, own * size, size):
        part = slice(at, at + size)
        columns = [dense[part, (own + slot) * size : (own + slot + 1) * size] for slot, *_ in halos]
        inv = jnp.concatenate([inverse[part, :]] * (grad_out.shape[1] // size), axis=1)
        aggregate = before[part, :] + dot(jnp.concatenate(columns, axis=1), blocks)
        mean = (aggregate * inv).astype(BF)
        pre = own_pre[part, :] + dot(mean, w_neigh[...])
        grad = (grad_out[part, :].astype(F32) * gelu_slope(pre)).astype(BF)
        grad_pre[part, :] = grad
        spread[part, :] = (dot_right_transposed(grad, w_neigh[...]) * inv).astype(BF)

    def partial(slot, count=1):
        rows = slice((own + slot) * size, (own + slot + count) * size)
        return dot(dense_t[rows, :], spread[...]).astype(BF)

    for i, target in enumerate(pairs):
        target[...] = partial(2 * (i + 1), 2)
    for i, target in enumerate(along):
        target[0:size, :] = partial(sub_count + 1 + i)
    for i, value in enumerate(rows):
        along[0][size + i * EXTRA : size + (i + 1) * EXTRA, :] = value[...]
    sibling[...] = partial(1)
    kept[0] = partial(0)
    kept[1] = partial(sub_count)


def split(total, value, second, size):
    zero = jnp.zeros_like(value)
    total[0:size, :] = total[0:size, :] + jnp.where(second, zero, value)
    total[size : 2 * size, :] = total[size : 2 * size, :] + jnp.where(second, value, zero)


def own_kernel(own, sub_count, rows, received, *rest):
    messages, rest = rest[:received], rest[received:]
    choice, w_self, dense_t, kept, spread, grad_pre, total, owner = rest
    size = kept.shape[1]
    width = total.shape[1]
    total[...] = dot_right_transposed(grad_pre[...], w_self[...]) + dot(
        dense_t[0 : own * size, :], spread[...]
    )
    for i, slot in enumerate((0, sub_count)):
        split(total, kept[i].astype(F32), choice[slot : slot + 1, :] > 0.5, size)
    for slot, at, row in rows:
        lane = lax.axis_index("sub")
        if slot > sub_count:
            lane = sub_count + lax.axis_index("cluster")
        index = lane_of(messages[at][row : row + EXTRA, :].astype(F32)[0:1, :], lane)
        owner[slot : slot + 1, :] = jnp.broadcast_to(index, (1, width))


def add_kernel(own, sub_count, parts, rows, owner, before, *rest):
    received, total = rest[:-1], rest[-1]
    size = total.shape[0] // own
    total[...] = before[...]
    for slot, at, row in parts:
        value = received[at][row : row + size, :].astype(F32)
        index = owner[slot : slot + 1, :]
        if slot in rows:
            where, first = rows[slot]
            indices = received[where][first : first + EXTRA, :].astype(F32)[0:1, :]
            index = lane_of(indices, sub_count + lax.axis_index("cluster"))
        split(total, value, index > 0.5, size)


def final_kernel(own, parts, owner, total, *rest):
    received, (out, done, sems) = rest[:-3], rest[-3:]
    size = total.shape[0] // own
    copies = []

    def leave(first, last, value):
        done[first:last, :] = value.astype(BF)
        copies.append(
            pltpu.make_async_copy(
                done.at[first:last, :], out.at[first:last, :], sems.at[len(copies)]
            )
        )
        copies[-1].start()

    leave(2 * size, own * size, total[2 * size :, :])
    for block in range(2):
        value = total[block * size : (block + 1) * size, :]
        for slot, at, row in parts:
            index = owner[slot : slot + 1, :]
            mine = index > 0.5 if block else index <= 0.5
            value = value + jnp.where(mine, received[at][row : row + size, :].astype(F32), 0.0)
        leave(block * size, (block + 1) * size, value)
    for copy in copies:
        copy.wait()


def swap(value, axis, count, d):
    return lax.ppermute(value, axis, [(i, i ^ d) for i in range(count)])


def after(value, other):
    return lax.optimization_barrier((value, other))[0]


def in_hbm(value):
    return pltpu.with_memory_space_constraint(value, pltpu.HBM)


def cost(flops, moved):
    return pl.CostEstimate(flops=flops, bytes_accessed=moved, transcendentals=0)


def shards(
    features, grad_out, w_self, w_neigh, bias, tile_dst, tile_src, tile_weight, recv_sub, recv_cluster
):
    sub_count = lax.axis_size("sub")
    cluster_count = lax.axis_size("cluster")
    peers = sub_count + cluster_count - 2
    size = tile_weight.shape[1]
    rows, width = features.shape
    own = rows // size
    slots = own + sub_count + cluster_count
    counts = (own, sub_count, cluster_count)

    wide = jax.ShapeDtypeStruct((rows, width), F32)
    narrow = jax.ShapeDtypeStruct((rows, width), BF)
    square = jax.ShapeDtypeStruct((width, width), BF)
    block = jax.ShapeDtypeStruct((size, width), BF)
    marks = jax.ShapeDtypeStruct((sub_count + cluster_count, width), F32)

    edge, rows_only = pl.pallas_call(
        edge_kernel,
        out_shape=[
            jax.ShapeDtypeStruct((BOUNDARY * size + EXTRA, width), BF),
            jax.ShapeDtypeStruct((EXTRA, width), BF),
        ],
        in_specs=[HBM] * 3,
        out_specs=[VMEM] * 2,
        scratch_shapes=[
            pltpu.VMEM(recv_sub.shape, jnp.int32),
            pltpu.VMEM(recv_cluster.shape, jnp.int32),
            pltpu.SemaphoreType.DMA((2 + CHUNKS,)),
        ],
        compiler_params=PARAMS,
        cost_estimate=cost(1024, 256 * 1024),
        name="edge",
    )(in_hbm(recv_sub), in_hbm(recv_cluster), in_hbm(features))

    def along(value, d):
        return swap(value, "cluster", cluster_count, d)

    def across(value, d):
        return swap(value, "sub", sub_count, d)

    even = list(range(2, sub_count, 2))
    direct = list(range(2, cluster_count, 2))
    relayed = list(range(3, cluster_count, 2))
    rows_at = BOUNDARY * size
    got = {0: (edge, 0, False, rows_at), sub_count: (edge, 0, False, rows_at)}
    for d in direct:
        got[sub_count + d] = (along(edge, d), 0, False, rows_at)
    for d in even:
        got[d] = (across(edge, d), 0, False, rows_at)
    got[sub_count + 1] = (along(edge, 1), 0, False, rows_at)
    dense, choice, features, w_self, w_neigh, grad_out, bias = pl.pallas_call(
        functools.partial(prepare_kernel, *counts),
        out_shape=[
            jax.ShapeDtypeStruct((rows, slots * size), BF),
            marks,
            narrow,
            square,
            square,
            narrow,
            jax.ShapeDtypeStruct(bias.shape, F32),
        ],
        in_specs=[HBM] * 10,
        out_specs=[VMEM] * 7,
        scratch_shapes=[
            pltpu.SMEM(tile_dst.shape, jnp.int32),
            pltpu.SMEM(tile_src.shape, jnp.int32),
            pltpu.SMEM(recv_sub.shape, jnp.int32),
            pltpu.SMEM(recv_cluster.shape, jnp.int32),
            pltpu.VMEM(tile_weight.shape, BF),
            pltpu.SemaphoreType.DMA((9 + CHUNKS,)),
        ],
        compiler_params=PARAMS,
        cost_estimate=cost(10**8, 6 * 1024 * 1024),
        name="prepare",
    )(
        *map(in_hbm, (tile_dst, tile_src, recv_sub, recv_cluster, tile_weight)),
        *map(in_hbm, (features, w_self, w_neigh, grad_out, bias)),
    )

    def call(kernel, out_shape, name, flops, *operands):
        return pl.pallas_call(
            kernel,
            out_shape=out_shape,
            in_specs=[VMEM] * len(operands),
            out_specs=jax.tree.map(lambda _: VMEM, out_shape),
            compiler_params=PARAMS,
            cost_estimate=cost(flops, 1024 * 1024),
            name=name,
        )(*operands)

    def unique(slots):
        arrays, at = [], {}
        for slot in slots:
            known = [i for i, array in enumerate(arrays) if array is got[slot][0]]
            at[slot] = known[0] if known else len(arrays)
            if not known:
                arrays.append(got[slot][0])
        return arrays, at

    def sum_call(kernel, out_shape, name, slots, *operands):
        arrays, at = unique(slots)
        halos = [(slot, at[slot], got[slot][1], got[slot][2]) for slot in slots]
        return pl.pallas_call(
            functools.partial(kernel, own, halos),
            out_shape=out_shape,
            in_specs=[VMEM] * (len(operands) + len(arrays)),
            out_specs=jax.tree.map(lambda _: VMEM, out_shape),
            scratch_shapes=[pltpu.VMEM((len(slots) * size, width), BF)],
            compiler_params=PARAMS,
            cost_estimate=cost(dict(first=10**9, near=10**9, late=10**10)[name], 3 * 1024 * 1024),
            name=name,
        )(*operands, *arrays)

    carried = []
    for d in relayed:
        far = got[sub_count + d - 1][0]
        far_rows = call(
            rows_kernel, jax.ShapeDtypeStruct((EXTRA, width), BF), "rows", 10**9, far
        )
        value = call(
            functools.partial(relay_kernel, sub_count, d - 1),
            block,
            "relay", 10**6, far, far_rows, got[sub_count + 1][0],
        )
        carried.append(far_rows)
        got[sub_count + d] = (along(value, 1), 0, True, None)
    first_sum, own_pre, inverse = sum_call(
        first_kernel, [wide, wide, jax.ShapeDtypeStruct((rows, size), F32)], "first", [0, sub_count, *(sub_count + d for d in direct)],
        choice, dense, features, w_self, bias,
    )
    traded = [0, *even]
    sibling_rows = across(after(rows_only, value), 1)
    value = call(
        functools.partial(trade_kernel, traded),
        jax.ShapeDtypeStruct((len(traded) * (size + EXTRA), width), BF),
        "trade", 10**6, *[got[d][0] for d in traded], after(sibling_rows, (choice, value)),
    )
    trade_value = value
    value = across(value, 1)
    for i, d in enumerate(traded):
        got[d + 1] = (value, i * size, True, len(traded) * size + i * EXTRA)
    near_sum = sum_call(
        near_kernel, wide, "near", [sub_count + 1, *even], after(choice, trade_value), dense, first_sum
    )
    dense_t = call(
        functools.partial(flip_kernel, size), jax.ShapeDtypeStruct((slots * size, rows), BF), "flip", 10**7,
        after(dense, near_sum),
    )
    if relayed:
        slots_late = [sub_count + d for d in relayed]
        near_sum = sum_call(
            near_kernel, wide, "late", slots_late, after(choice, dense_t), dense, near_sum
        )

    late = [1, *(d + 1 for d in even)]
    late_arrays, late_at = unique(late)
    late_halos = [(slot, late_at[slot], got[slot][1], got[slot][2]) for slot in late]
    outs = pl.pallas_call(
        functools.partial(middle_kernel, *counts, late_halos, len(late_arrays), len(carried)),
        out_shape=[jax.ShapeDtypeStruct((2 * size, width), BF)] * len(even)
        + [jax.ShapeDtypeStruct((size + len(carried) * EXTRA, width), BF)]
        + [block] * (cluster_count - 1)
        + [jax.ShapeDtypeStruct((2, size, width), BF), narrow, narrow],
        in_specs=[VMEM] * (8 + len(late_arrays) + len(carried)),
        out_specs=[VMEM] * (len(even) + cluster_count + 3),
        scratch_shapes=[pltpu.VMEM((len(late) * size, width), BF)],
        compiler_params=PARAMS,
        cost_estimate=cost(2 * rows * slots * size * width, 6 * 1024 * 1024),
        name="middle",
    )(
        choice, grad_out, w_neigh, dense, dense_t, near_sum, own_pre, inverse,
        *late_arrays, *carried,
    )
    *sent, sibling, kept, spread, grad_pre = outs

    far = [(sub_count + d, along(sent[len(even) + d - 1], d)) for d in range(1, cluster_count)]
    near = [(d, across(value, d)) for d, value in zip(even, sent)]
    soon, rest = near[-1:], near[:-1]
    early = call(
        turn_kernel, jax.ShapeDtypeStruct((2 * size, width), BF), "early", 10**8,
        sibling, *[value for _, value in soon],
    )
    order = [sub_count + 1, *(sub_count + d for d in direct), *even, *(d + 1 for d in even), 1]
    arrays, at = unique(order)
    total, owner = pl.pallas_call(
        functools.partial(
            own_kernel, own, sub_count, [(slot, at[slot], got[slot][3]) for slot in order],
            len(arrays),
        ),
        out_shape=[wide, marks],
        in_specs=[VMEM] * (6 + len(arrays)),
        out_specs=[VMEM] * 2,
        compiler_params=PARAMS,
        cost_estimate=cost(10**9, 2 * 1024 * 1024),
        name="own",
    )(*arrays, after(choice, (far[-1][1], early)), w_self, dense_t, kept, spread, grad_pre)

    early = across(early, 1)
    turned = call(
        turn_kernel, jax.ShapeDtypeStruct((len(rest) * size, width), BF), "turn", 10**6,
        *[after(value, total) for _, value in rest],
    )
    turned = across(turned, 1)
    more = [*far, *near[::-1]]
    parts = [(slot, i, 0) for i, (slot, _) in enumerate(more)]
    places = {slot: (0, size + i * EXTRA) for i, slot in enumerate(sub_count + d for d in relayed)}
    total = call(
        functools.partial(
            add_kernel, own, sub_count, parts, places
        ),
        wide, "add", 10**10, owner, total, *[value for _, value in more],
    )
    parts = [(1, 0, 0), *[(d + 1, 0, size) for d, _ in soon]]
    parts += [(d + 1, 1, i * size) for i, (d, _) in enumerate(rest)]
    return pl.pallas_call(
        functools.partial(final_kernel, own, parts),
        out_shape=narrow,
        in_specs=[VMEM] * 4,
        out_specs=HBM,
        scratch_shapes=[pltpu.VMEM((rows, width), BF), pltpu.SemaphoreType.DMA((3,))],
        compiler_params=PARAMS,
        cost_estimate=cost(rows * width * 4, 1024 * 1024),
        name="final",
    )(owner, total, early, turned)


def solution(mesh):
    placed = (
        P(("cluster", "sub"), None),
        P(("cluster", "sub"), None),
        P(),
        P(),
        P(),
        P(("cluster", "sub")),
        P(("cluster", "sub")),
        P(("cluster", "sub"), None, None),
        P(("cluster", "sub"), None),
        P(("cluster", "sub"), None),
    )
    return jax.shard_map(
        shards, mesh=mesh, in_specs=placed, out_specs=P(("cluster", "sub"), None), check_vma=False
    )
```

```python
import functools

import jax
import jax.numpy as jnp
from jax import lax
from jax.experimental import pallas as pl
from jax.experimental.pallas import tpu as pltpu
from jax.sharding import PartitionSpec as P

BF = jnp.bfloat16
F32 = jnp.float32
BOUNDARY = 2
EXTRA = 16
CHUNKS = 4
VMEM = pl.BlockSpec(memory_space=pltpu.VMEM)
HBM = pl.BlockSpec(memory_space=pltpu.HBM)
PARAMS = pltpu.CompilerParams(vmem_limit_bytes=24 * 1024 * 1024)


def dot(left, right):
    return jnp.dot(left, right, preferred_element_type=F32)


def dot_right_transposed(left, right):
    return lax.dot_general(left, right, (((1,), (1,)), ((), ())), preferred_element_type=F32)


def gelu_slope(v):
    scale = 0.7978845608028654
    t = jnp.tanh(scale * (v + 0.044715 * v * v * v))
    return 0.5 * (1.0 + t) + (0.5 * scale) * v * (1.0 - t * t) * (1.0 + 3.0 * 0.044715 * v * v)


def edge_kernel(recv_sub, recv_cluster, features, edge, rows, sub_row, cluster_row, sems):
    count = edge.shape[0] - EXTRA
    step = count // CHUNKS
    small = [
        pltpu.make_async_copy(recv_sub, sub_row, sems.at[0]),
        pltpu.make_async_copy(recv_cluster, cluster_row, sems.at[1]),
    ]
    large = []
    for i in range(CHUNKS):
        part = slice(i * step, (i + 1) * step)
        large.append(
            pltpu.make_async_copy(features.at[part, :], edge.at[part, :], sems.at[2 + i])
        )
    for copy in small + large:
        copy.start()
    for copy in small:
        copy.wait()
    sub_count, cluster_count = sub_row.shape[1], cluster_row.shape[1]
    pad = jnp.zeros((1, edge.shape[1] - sub_count - cluster_count), F32)
    row = jnp.concatenate([sub_row[...].astype(F32), cluster_row[...].astype(F32), pad], axis=1)
    value = jnp.broadcast_to(row, rows.shape).astype(BF)
    edge[count:, :] = value
    rows[...] = value
    for copy in large:
        copy.wait()


def prepare_kernel(
    own, sub_count, cluster_count,
    tile_dst_hbm, tile_src_hbm, recv_sub_hbm, recv_cluster_hbm, tile_weight_hbm,
    features_hbm, w_self_hbm, w_neigh_hbm, grad_out_hbm, bias_hbm,
    dense, choice, features, w_self, w_neigh, grad_out, bias,
    tile_dst, tile_src, recv_sub, recv_cluster, tile_weight, sems,
):
    size = tile_weight.shape[1]
    step = tile_weight.shape[0] // CHUNKS
    pairs = (
        (tile_dst_hbm, tile_dst), (tile_src_hbm, tile_src), (recv_sub_hbm, recv_sub),
        (recv_cluster_hbm, recv_cluster),
        *(
            (tile_weight_hbm.at[i * step : (i + 1) * step], tile_weight.at[i * step : (i + 1) * step])
            for i in range(CHUNKS)
        ),
        (features_hbm, features), (w_self_hbm, w_self), (w_neigh_hbm, w_neigh),
        (grad_out_hbm, grad_out), (bias_hbm, bias),
    )
    copies = [pltpu.make_async_copy(a, b, sems.at[i]) for i, (a, b) in enumerate(pairs)]
    for copy in copies:
        copy.start()
    sub_id = lax.axis_index("sub")
    cluster_id = lax.axis_index("cluster")
    dense[...] = jnp.zeros_like(dense)
    for copy in copies[: 4 + CHUNKS]:
        copy.wait()

    def place(t, carry):
        src = tile_src[t]
        from_sub = own + ((src - own) ^ sub_id)
        from_cluster = own + sub_count + ((src - own - sub_count) ^ cluster_id)
        slot = jnp.where(src < own, src, jnp.where(src < own + sub_count, from_sub, from_cluster))
        dst = pl.ds(pl.multiple_of(tile_dst[t] * size, size), size)
        col = pl.ds(pl.multiple_of(slot * size, size), size)
        dense[dst, col] = dense[dst, col] + tile_weight[t]
        return carry

    lax.fori_loop(0, tile_weight.shape[0], place, 0, unroll=4)
    for d in range(sub_count):
        index = recv_sub[0, sub_id ^ d].astype(F32)
        choice[d : d + 1, :] = jnp.full((1, choice.shape[1]), index, F32)
    for d in range(cluster_count):
        index = recv_cluster[0, cluster_id ^ d].astype(F32)
        choice[sub_count + d : sub_count + d + 1, :] = jnp.full((1, choice.shape[1]), index, F32)
    for copy in copies[4 + CHUNKS :]:
        copy.wait()


def index_row(message, size):
    return message[2 * size : 2 * size + EXTRA, :].astype(F32)[0:1, :]


def lane_of(row, lane):
    lanes = lax.broadcasted_iota(jnp.int32, row.shape, 1)
    return jnp.sum(jnp.where(lanes == lane, row, 0.0), axis=1, keepdims=True)


def pick(message, index, size):
    return jnp.where(
        index > 0.5, message[size : 2 * size, :].astype(F32), message[0:size, :].astype(F32)
    ).astype(BF)


def rows_kernel(message, out):
    out[...] = message[message.shape[0] - EXTRA :, :]


def relay_kernel(sub_count, d, far, rows, near, out):
    size = out.shape[0]
    index = lane_of(index_row(near, size), sub_count + (lax.axis_index("cluster") ^ d))
    out[...] = pick(far, index, size)


def trade_kernel(even, *rest):
    messages, (sibling, out) = rest[:-2], rest[-2:]
    size = out.shape[0] // len(even) - EXTRA
    row = sibling[...].astype(F32)[0:1, :]
    for i, (d, message) in enumerate(zip(even, messages)):
        index = lane_of(row, lax.axis_index("sub") ^ d)
        out[i * size : (i + 1) * size, :] = pick(message, index, size)
        at = len(even) * size + i * EXTRA
        out[at : at + EXTRA, :] = message[2 * size :, :]


def turn_kernel(*rest):
    messages, out = rest[:-1], rest[-1]
    size = out.shape[0] // len(messages)
    for i, message in enumerate(messages):
        last = message.shape[0]
        out[i * size : (i + 1) * size, :] = message[last - size : last, :]


def halo_blocks(choice, size, halos, refs, halo):
    first = halos[0]
    if all(
        (at, row, picked) == (first[1], first[2] + i * size, True)
        for i, (_, at, row, picked) in enumerate(halos)
    ):
        return refs[first[1]][first[2] : first[2] + len(halos) * size, :]
    for i, (slot, at, row, picked) in enumerate(halos):
        if picked:
            block = refs[at][row : row + size, :]
        else:
            block = pick(refs[at], choice[slot : slot + 1, :], size)
        halo[i * size : (i + 1) * size, :] = block
    return halo[...]


def halo_sum(choice, dense, own, halos, refs, halo):
    size = dense.shape[0] // own
    blocks = halo_blocks(choice, size, halos, refs, halo)
    columns = [dense[:, (own + slot) * size : (own + slot + 1) * size] for slot, *_ in halos]
    return dot(jnp.concatenate(columns, axis=1), blocks)


def flip_kernel(size, dense, dense_t):
    for at in range(0, dense.shape[1], size):
        dense_t[at : at + size, :] = dense[:, at : at + size].T


def first_kernel(own, halos, choice, dense, features, w_self, bias, *rest):
    refs, (total, own_pre, inverse, halo) = rest[:-4], rest[-4:]
    size = dense.shape[0] // own
    count = dense[:, 0:size].astype(F32)
    for at in range(size, dense.shape[1], size):
        count = count + dense[:, at : at + size].astype(F32)
    degree = jnp.sum(count, axis=1, keepdims=True)
    inverse[...] = jnp.broadcast_to(1.0 / (degree + 1.0), inverse.shape)
    total[...] = dot(dense[:, 0 : own * size], features[...]) + halo_sum(
        choice, dense, own, halos, refs, halo
    )
    own_pre[...] = dot(features[...], w_self[...]) + bias[...].reshape(1, -1)


def near_kernel(own, halos, choice, dense, before, *rest):
    refs, (total, halo) = rest[:-2], rest[-2:]
    total[...] = before[...] + halo_sum(choice, dense, own, halos, refs, halo)


def middle_kernel(
    own, sub_count, cluster_count, halos, received, carried,
    choice, grad_out, w_neigh, dense, dense_t, before, own_pre, inverse,
    *rest,
):
    refs, rest = rest[:received], rest[received:]
    rows, rest = rest[:carried], rest[carried:]
    pairs, rest = rest[: sub_count // 2 - 1], rest[sub_count // 2 - 1 :]
    along, (sibling, kept, spread, grad_pre, halo) = rest[:-5], rest[-5:]
    size = dense.shape[0] // own
    aggregate = before[...] + halo_sum(choice, dense, own, halos, refs, halo)
    inv = jnp.concatenate([inverse[...]] * (grad_out.shape[1] // size), axis=1)
    mean = (aggregate * inv).astype(BF)
    pre = own_pre[...] + dot(mean, w_neigh[...])
    grad = (grad_out[...].astype(F32) * gelu_slope(pre)).astype(BF)
    grad_pre[...] = grad
    spread[...] = (dot_right_transposed(grad, w_neigh[...]) * inv).astype(BF)
    partial = dot(dense_t[own * size :, :], spread[...]).astype(BF)

    def of(slot, count=1):
        return partial[slot * size : (slot + count) * size, :]

    for i, target in enumerate(pairs):
        target[...] = of(2 * (i + 1), 2)
    for i, target in enumerate(along):
        target[0:size, :] = of(sub_count + 1 + i)
    for i, value in enumerate(rows):
        along[0][size + i * EXTRA : size + (i + 1) * EXTRA, :] = value[...]
    sibling[...] = of(1)
    kept[0] = of(0)
    kept[1] = of(sub_count)


def split(total, value, second, size):
    zero = jnp.zeros_like(value)
    total[0:size, :] = total[0:size, :] + jnp.where(second, zero, value)
    total[size : 2 * size, :] = total[size : 2 * size, :] + jnp.where(second, value, zero)


def own_kernel(own, sub_count, rows, received, *rest):
    messages, rest = rest[:received], rest[received:]
    choice, w_self, dense_t, kept, spread, grad_pre, total, owner = rest
    size = kept.shape[1]
    width = total.shape[1]
    total[...] = dot_right_transposed(grad_pre[...], w_self[...]) + dot(
        dense_t[0 : own * size, :], spread[...]
    )
    for i, slot in enumerate((0, sub_count)):
        split(total, kept[i].astype(F32), choice[slot : slot + 1, :] > 0.5, size)
    for slot, at, row in rows:
        lane = lax.axis_index("sub")
        if slot > sub_count:
            lane = sub_count + lax.axis_index("cluster")
        index = lane_of(messages[at][row : row + EXTRA, :].astype(F32)[0:1, :], lane)
        owner[slot : slot + 1, :] = jnp.broadcast_to(index, (1, width))


def add_kernel(own, sub_count, parts, rows, owner, before, *rest):
    received, total = rest[:-1], rest[-1]
    size = total.shape[0] // own
    total[...] = before[...]
    for slot, at, row in parts:
        value = received[at][row : row + size, :].astype(F32)
        index = owner[slot : slot + 1, :]
        if slot in rows:
            where, first = rows[slot]
            indices = received[where][first : first + EXTRA, :].astype(F32)[0:1, :]
            index = lane_of(indices, sub_count + lax.axis_index("cluster"))
        split(total, value, index > 0.5, size)


def final_kernel(own, parts, owner, total, *rest):
    received, (out, done, sems) = rest[:-3], rest[-3:]
    size = total.shape[0] // own
    copies = []

    def leave(first, last, value):
        done[first:last, :] = value.astype(BF)
        copies.append(
            pltpu.make_async_copy(
                done.at[first:last, :], out.at[first:last, :], sems.at[len(copies)]
            )
        )
        copies[-1].start()

    leave(2 * size, own * size, total[2 * size :, :])
    for block in range(2):
        value = total[block * size : (block + 1) * size, :]
        for slot, at, row in parts:
            index = owner[slot : slot + 1, :]
            mine = index > 0.5 if block else index <= 0.5
            value = value + jnp.where(mine, received[at][row : row + size, :].astype(F32), 0.0)
        leave(block * size, (block + 1) * size, value)
    for copy in copies:
        copy.wait()


def swap(value, axis, count, d):
    return lax.ppermute(value, axis, [(i, i ^ d) for i in range(count)])


def after(value, other):
    return lax.optimization_barrier((value, other))[0]


def in_hbm(value):
    return pltpu.with_memory_space_constraint(value, pltpu.HBM)


def cost(flops, moved):
    return pl.CostEstimate(flops=flops, bytes_accessed=moved, transcendentals=0)


def shards(
    features, grad_out, w_self, w_neigh, bias, tile_dst, tile_src, tile_weight, recv_sub, recv_cluster
):
    sub_count = lax.axis_size("sub")
    cluster_count = lax.axis_size("cluster")
    peers = sub_count + cluster_count - 2
    size = tile_weight.shape[1]
    rows, width = features.shape
    own = rows // size
    slots = own + sub_count + cluster_count
    counts = (own, sub_count, cluster_count)

    wide = jax.ShapeDtypeStruct((rows, width), F32)
    narrow = jax.ShapeDtypeStruct((rows, width), BF)
    square = jax.ShapeDtypeStruct((width, width), BF)
    block = jax.ShapeDtypeStruct((size, width), BF)
    marks = jax.ShapeDtypeStruct((sub_count + cluster_count, width), F32)

    edge, rows_only = pl.pallas_call(
        edge_kernel,
        out_shape=[
            jax.ShapeDtypeStruct((BOUNDARY * size + EXTRA, width), BF),
            jax.ShapeDtypeStruct((EXTRA, width), BF),
        ],
        in_specs=[HBM] * 3,
        out_specs=[VMEM] * 2,
        scratch_shapes=[
            pltpu.VMEM(recv_sub.shape, jnp.int32),
            pltpu.VMEM(recv_cluster.shape, jnp.int32),
            pltpu.SemaphoreType.DMA((2 + CHUNKS,)),
        ],
        compiler_params=PARAMS,
        cost_estimate=cost(1024, 256 * 1024),
        name="edge",
    )(in_hbm(recv_sub), in_hbm(recv_cluster), in_hbm(features))

    def along(value, d):
        return swap(value, "cluster", cluster_count, d)

    def across(value, d):
        return swap(value, "sub", sub_count, d)

    even = list(range(2, sub_count, 2))
    direct = list(range(2, cluster_count, 2))
    relayed = list(range(3, cluster_count, 2))
    rows_at = BOUNDARY * size
    got = {0: (edge, 0, False, rows_at), sub_count: (edge, 0, False, rows_at)}
    for d in direct:
        got[sub_count + d] = (along(edge, d), 0, False, rows_at)
    for d in even:
        got[d] = (across(edge, d), 0, False, rows_at)
    got[sub_count + 1] = (along(edge, 1), 0, False, rows_at)
    dense, choice, features, w_self, w_neigh, grad_out, bias = pl.pallas_call(
        functools.partial(prepare_kernel, *counts),
        out_shape=[
            jax.ShapeDtypeStruct((rows, slots * size), BF),
            marks,
            narrow,
            square,
            square,
            narrow,
            jax.ShapeDtypeStruct(bias.shape, F32),
        ],
        in_specs=[HBM] * 10,
        out_specs=[VMEM] * 7,
        scratch_shapes=[
            pltpu.SMEM(tile_dst.shape, jnp.int32),
            pltpu.SMEM(tile_src.shape, jnp.int32),
            pltpu.SMEM(recv_sub.shape, jnp.int32),
            pltpu.SMEM(recv_cluster.shape, jnp.int32),
            pltpu.VMEM(tile_weight.shape, BF),
            pltpu.SemaphoreType.DMA((9 + CHUNKS,)),
        ],
        compiler_params=PARAMS,
        cost_estimate=cost(10**8, 6 * 1024 * 1024),
        name="prepare",
    )(
        *map(in_hbm, (tile_dst, tile_src, recv_sub, recv_cluster, tile_weight)),
        *map(in_hbm, (features, w_self, w_neigh, grad_out, bias)),
    )

    def call(kernel, out_shape, name, flops, *operands):
        return pl.pallas_call(
            kernel,
            out_shape=out_shape,
            in_specs=[VMEM] * len(operands),
            out_specs=jax.tree.map(lambda _: VMEM, out_shape),
            compiler_params=PARAMS,
            cost_estimate=cost(flops, 1024 * 1024),
            name=name,
        )(*operands)

    def unique(slots):
        arrays, at = [], {}
        for slot in slots:
            known = [i for i, array in enumerate(arrays) if array is got[slot][0]]
            at[slot] = known[0] if known else len(arrays)
            if not known:
                arrays.append(got[slot][0])
        return arrays, at

    def sum_call(kernel, out_shape, name, slots, *operands):
        arrays, at = unique(slots)
        halos = [(slot, at[slot], got[slot][1], got[slot][2]) for slot in slots]
        return pl.pallas_call(
            functools.partial(kernel, own, halos),
            out_shape=out_shape,
            in_specs=[VMEM] * (len(operands) + len(arrays)),
            out_specs=jax.tree.map(lambda _: VMEM, out_shape),
            scratch_shapes=[pltpu.VMEM((len(slots) * size, width), BF)],
            compiler_params=PARAMS,
            cost_estimate=cost(dict(first=10**9, near=10**9, late=10**10)[name], 3 * 1024 * 1024),
            name=name,
        )(*operands, *arrays)

    carried = []
    for d in relayed:
        far = got[sub_count + d - 1][0]
        far_rows = call(
            rows_kernel, jax.ShapeDtypeStruct((EXTRA, width), BF), "rows", 10**9, far
        )
        value = call(
            functools.partial(relay_kernel, sub_count, d - 1),
            block,
            "relay", 10**6, far, far_rows, got[sub_count + 1][0],
        )
        carried.append(far_rows)
        got[sub_count + d] = (along(value, 1), 0, True, None)
    first_sum, own_pre, inverse = sum_call(
        first_kernel, [wide, wide, jax.ShapeDtypeStruct((rows, size), F32)], "first", [0, sub_count, *(sub_count + d for d in direct)],
        choice, dense, features, w_self, bias,
    )
    traded = [0, *even]
    sibling_rows = across(after(rows_only, value), 1)
    value = call(
        functools.partial(trade_kernel, traded),
        jax.ShapeDtypeStruct((len(traded) * (size + EXTRA), width), BF),
        "trade", 10**6, *[got[d][0] for d in traded], after(sibling_rows, (choice, value)),
    )
    trade_value = value
    value = across(value, 1)
    for i, d in enumerate(traded):
        got[d + 1] = (value, i * size, True, len(traded) * size + i * EXTRA)
    near_sum = sum_call(
        near_kernel, wide, "near", [sub_count + 1, *even], after(choice, trade_value), dense, first_sum
    )
    dense_t = call(
        functools.partial(flip_kernel, size), jax.ShapeDtypeStruct((slots * size, rows), BF), "flip", 10**7,
        after(dense, near_sum),
    )
    if relayed:
        slots_late = [sub_count + d for d in relayed]
        near_sum = sum_call(
            near_kernel, wide, "late", slots_late, after(choice, dense_t), dense, near_sum
        )

    late = [1, *(d + 1 for d in even)]
    late_arrays, late_at = unique(late)
    late_halos = [(slot, late_at[slot], got[slot][1], got[slot][2]) for slot in late]
    outs = pl.pallas_call(
        functools.partial(middle_kernel, *counts, late_halos, len(late_arrays), len(carried)),
        out_shape=[jax.ShapeDtypeStruct((2 * size, width), BF)] * len(even)
        + [jax.ShapeDtypeStruct((size + len(carried) * EXTRA, width), BF)]
        + [block] * (cluster_count - 1)
        + [jax.ShapeDtypeStruct((2, size, width), BF), narrow, narrow],
        in_specs=[VMEM] * (8 + len(late_arrays) + len(carried)),
        out_specs=[VMEM] * (len(even) + cluster_count + 3),
        scratch_shapes=[pltpu.VMEM((len(late) * size, width), BF)],
        compiler_params=PARAMS,
        cost_estimate=cost(2 * rows * slots * size * width, 6 * 1024 * 1024),
        name="middle",
    )(
        choice, grad_out, w_neigh, dense, dense_t, near_sum, own_pre, inverse,
        *late_arrays, *carried,
    )
    *sent, sibling, kept, spread, grad_pre = outs

    far = [(sub_count + d, along(sent[len(even) + d - 1], d)) for d in range(1, cluster_count)]
    near = [(d, across(value, d)) for d, value in zip(even, sent)]
    soon, rest = near[-1:], near[:-1]
    early = call(
        turn_kernel, jax.ShapeDtypeStruct((2 * size, width), BF), "early", 10**8,
        sibling, *[value for _, value in soon],
    )
    order = [sub_count + 1, *(sub_count + d for d in direct), *even, *(d + 1 for d in even), 1]
    arrays, at = unique(order)
    total, owner = pl.pallas_call(
        functools.partial(
            own_kernel, own, sub_count, [(slot, at[slot], got[slot][3]) for slot in order],
            len(arrays),
        ),
        out_shape=[wide, marks],
        in_specs=[VMEM] * (6 + len(arrays)),
        out_specs=[VMEM] * 2,
        compiler_params=PARAMS,
        cost_estimate=cost(10**9, 2 * 1024 * 1024),
        name="own",
    )(*arrays, after(choice, (far[-1][1], early)), w_self, dense_t, kept, spread, grad_pre)

    early = across(early, 1)
    turned = call(
        turn_kernel, jax.ShapeDtypeStruct((len(rest) * size, width), BF), "turn", 10**6,
        *[after(value, total) for _, value in rest],
    )
    turned = across(turned, 1)
    more = [*far, *near[::-1]]
    parts = [(slot, i, 0) for i, (slot, _) in enumerate(more)]
    places = {slot: (0, size + i * EXTRA) for i, slot in enumerate(sub_count + d for d in relayed)}
    total = call(
        functools.partial(
            add_kernel, own, sub_count, parts, places
        ),
        wide, "add", 10**10, owner, total, *[value for _, value in more],
    )
    parts = [(1, 0, 0), *[(d + 1, 0, size) for d, _ in soon]]
    parts += [(d + 1, 1, i * size) for i, (d, _) in enumerate(rest)]
    return pl.pallas_call(
        functools.partial(final_kernel, own, parts),
        out_shape=narrow,
        in_specs=[VMEM] * 4,
        out_specs=HBM,
        scratch_shapes=[pltpu.VMEM((rows, width), BF), pltpu.SemaphoreType.DMA((3,))],
        compiler_params=PARAMS,
        cost_estimate=cost(rows * width * 4, 1024 * 1024),
        name="final",
    )(owner, total, early, turned)


def solution(mesh):
    placed = (
        P(("cluster", "sub"), None),
        P(("cluster", "sub"), None),
        P(),
        P(),
        P(),
        P(("cluster", "sub")),
        P(("cluster", "sub")),
        P(("cluster", "sub"), None, None),
        P(("cluster", "sub"), None),
        P(("cluster", "sub"), None),
    )
    return jax.shard_map(
        shards, mesh=mesh, in_specs=placed, out_specs=P(("cluster", "sub"), None), check_vma=False
    )
```

```python
import functools

import jax
import jax.numpy as jnp
from jax import lax
from jax.experimental import pallas as pl
from jax.experimental.pallas import tpu as pltpu
from jax.sharding import PartitionSpec as P

BF = jnp.bfloat16
F32 = jnp.float32
BOUNDARY = 2
EXTRA = 16
CHUNKS = 4
VMEM = pl.BlockSpec(memory_space=pltpu.VMEM)
HBM = pl.BlockSpec(memory_space=pltpu.HBM)
PARAMS = pltpu.CompilerParams(vmem_limit_bytes=24 * 1024 * 1024)


def dot(left, right):
    return jnp.dot(left, right, preferred_element_type=F32)


def dot_right_transposed(left, right):
    return lax.dot_general(left, right, (((1,), (1,)), ((), ())), preferred_element_type=F32)


def gelu_slope(v):
    scale = 0.7978845608028654
    t = jnp.tanh(scale * (v + 0.044715 * v * v * v))
    return 0.5 * (1.0 + t) + (0.5 * scale) * v * (1.0 - t * t) * (1.0 + 3.0 * 0.044715 * v * v)


def edge_kernel(recv_sub, recv_cluster, features, edge, rows, sub_row, cluster_row, sems):
    count = edge.shape[0] - EXTRA
    step = count // CHUNKS
    small = [
        pltpu.make_async_copy(recv_sub, sub_row, sems.at[0]),
        pltpu.make_async_copy(recv_cluster, cluster_row, sems.at[1]),
    ]
    large = []
    for i in range(CHUNKS):
        part = slice(i * step, (i + 1) * step)
        large.append(
            pltpu.make_async_copy(features.at[part, :], edge.at[part, :], sems.at[2 + i])
        )
    for copy in small + large:
        copy.start()
    for copy in small:
        copy.wait()
    sub_count, cluster_count = sub_row.shape[1], cluster_row.shape[1]
    pad = jnp.zeros((1, edge.shape[1] - sub_count - cluster_count), F32)
    row = jnp.concatenate([sub_row[...].astype(F32), cluster_row[...].astype(F32), pad], axis=1)
    value = jnp.broadcast_to(row, rows.shape).astype(BF)
    edge[count:, :] = value
    rows[...] = value
    for copy in large:
        copy.wait()


def prepare_kernel(
    own, sub_count, cluster_count,
    tile_dst_hbm, tile_src_hbm, recv_sub_hbm, recv_cluster_hbm, tile_weight_hbm,
    features_hbm, w_self_hbm, w_neigh_hbm, grad_out_hbm, bias_hbm,
    dense, choice, features, w_self, w_neigh, grad_out, bias,
    tile_dst, tile_src, recv_sub, recv_cluster, tile_weight, sems,
):
    size = tile_weight.shape[1]
    step = tile_weight.shape[0] // CHUNKS
    pairs = (
        (tile_dst_hbm, tile_dst), (tile_src_hbm, tile_src), (recv_sub_hbm, recv_sub),
        (recv_cluster_hbm, recv_cluster),
        *(
            (tile_weight_hbm.at[i * step : (i + 1) * step], tile_weight.at[i * step : (i + 1) * step])
            for i in range(CHUNKS)
        ),
        (features_hbm, features), (w_self_hbm, w_self), (w_neigh_hbm, w_neigh),
        (grad_out_hbm, grad_out), (bias_hbm, bias),
    )
    copies = [pltpu.make_async_copy(a, b, sems.at[i]) for i, (a, b) in enumerate(pairs)]
    for copy in copies:
        copy.start()
    sub_id = lax.axis_index("sub")
    cluster_id = lax.axis_index("cluster")
    dense[...] = jnp.zeros_like(dense)
    for copy in copies[: 4 + CHUNKS]:
        copy.wait()

    def place(t, carry):
        src = tile_src[t]
        from_sub = own + ((src - own) ^ sub_id)
        from_cluster = own + sub_count + ((src - own - sub_count) ^ cluster_id)
        slot = jnp.where(src < own, src, jnp.where(src < own + sub_count, from_sub, from_cluster))
        dst = pl.ds(pl.multiple_of(tile_dst[t] * size, size), size)
        col = pl.ds(pl.multiple_of(slot * size, size), size)
        dense[dst, col] = dense[dst, col] + tile_weight[t]
        return carry

    lax.fori_loop(0, tile_weight.shape[0], place, 0, unroll=4)
    for d in range(sub_count):
        index = recv_sub[0, sub_id ^ d].astype(F32)
        choice[d : d + 1, :] = jnp.full((1, choice.shape[1]), index, F32)
    for d in range(cluster_count):
        index = recv_cluster[0, cluster_id ^ d].astype(F32)
        choice[sub_count + d : sub_count + d + 1, :] = jnp.full((1, choice.shape[1]), index, F32)
    for copy in copies[4 + CHUNKS :]:
        copy.wait()


def index_row(message, size):
    return message[2 * size : 2 * size + EXTRA, :].astype(F32)[0:1, :]


def lane_of(row, lane):
    lanes = lax.broadcasted_iota(jnp.int32, row.shape, 1)
    return jnp.sum(jnp.where(lanes == lane, row, 0.0), axis=1, keepdims=True)


def pick(message, index, size):
    return jnp.where(
        index > 0.5, message[size : 2 * size, :].astype(F32), message[0:size, :].astype(F32)
    ).astype(BF)


def rows_kernel(message, out):
    out[...] = message[message.shape[0] - EXTRA :, :]


def relay_kernel(sub_count, d, far, rows, near, out):
    size = out.shape[0]
    index = lane_of(index_row(near, size), sub_count + (lax.axis_index("cluster") ^ d))
    out[...] = pick(far, index, size)


def trade_kernel(even, *rest):
    messages, (sibling, out) = rest[:-2], rest[-2:]
    size = out.shape[0] // len(even) - EXTRA
    row = sibling[...].astype(F32)[0:1, :]
    for i, (d, message) in enumerate(zip(even, messages)):
        index = lane_of(row, lax.axis_index("sub") ^ d)
        out[i * size : (i + 1) * size, :] = pick(message, index, size)
        at = len(even) * size + i * EXTRA
        out[at : at + EXTRA, :] = message[2 * size :, :]


def turn_kernel(*rest):
    messages, out = rest[:-1], rest[-1]
    size = out.shape[0] // len(messages)
    for i, message in enumerate(messages):
        last = message.shape[0]
        out[i * size : (i + 1) * size, :] = message[last - size : last, :]


def halo_blocks(choice, size, halos, refs, halo):
    first = halos[0]
    if all(
        (at, row, picked) == (first[1], first[2] + i * size, True)
        for i, (_, at, row, picked) in enumerate(halos)
    ):
        return refs[first[1]][first[2] : first[2] + len(halos) * size, :]
    for i, (slot, at, row, picked) in enumerate(halos):
        if picked:
            block = refs[at][row : row + size, :]
        else:
            block = pick(refs[at], choice[slot : slot + 1, :], size)
        halo[i * size : (i + 1) * size, :] = block
    return halo[...]


def halo_sum(choice, dense, own, halos, refs, halo):
    size = dense.shape[0] // own
    blocks = halo_blocks(choice, size, halos, refs, halo)
    columns = [dense[:, (own + slot) * size : (own + slot + 1) * size] for slot, *_ in halos]
    return dot(jnp.concatenate(columns, axis=1), blocks)


def flip_kernel(size, dense, dense_t):
    for at in range(0, dense.shape[1], size):
        dense_t[at : at + size, :] = dense[:, at : at + size].T


def first_kernel(own, halos, choice, dense, features, w_self, bias, *rest):
    refs, (total, own_pre, inverse, halo) = rest[:-4], rest[-4:]
    size = dense.shape[0] // own
    count = dense[:, 0:size].astype(F32)
    for at in range(size, dense.shape[1], size):
        count = count + dense[:, at : at + size].astype(F32)
    degree = jnp.sum(count, axis=1, keepdims=True)
    inverse[...] = jnp.broadcast_to(1.0 / (degree + 1.0), inverse.shape)
    total[...] = dot(dense[:, 0 : own * size], features[...]) + halo_sum(
        choice, dense, own, halos, refs, halo
    )
    own_pre[...] = dot(features[...], w_self[...]) + bias[...].reshape(1, -1)


def near_kernel(own, halos, choice, dense, before, *rest):
    refs, (total, halo) = rest[:-2], rest[-2:]
    total[...] = before[...] + halo_sum(choice, dense, own, halos, refs, halo)


def middle_kernel(
    own, sub_count, cluster_count, halos, received, carried,
    choice, grad_out, w_neigh, dense, dense_t, before, own_pre, inverse,
    *rest,
):
    refs, rest = rest[:received], rest[received:]
    rows, rest = rest[:carried], rest[carried:]
    pairs, rest = rest[: sub_count // 2 - 1], rest[sub_count // 2 - 1 :]
    along, (sibling, kept, spread, grad_pre, halo) = rest[:-5], rest[-5:]
    size = dense.shape[0] // own
    aggregate = before[...] + halo_sum(choice, dense, own, halos, refs, halo)
    inv = jnp.concatenate([inverse[...]] * (grad_out.shape[1] // size), axis=1)
    mean = (aggregate * inv).astype(BF)
    pre = own_pre[...] + dot(mean, w_neigh[...])
    grad = (grad_out[...].astype(F32) * gelu_slope(pre)).astype(BF)
    grad_pre[...] = grad
    spread[...] = (dot_right_transposed(grad, w_neigh[...]) * inv).astype(BF)

    def partial(slot, count=1):
        rows = slice((own + slot) * size, (own + slot + count) * size)
        return dot(dense_t[rows, :], spread[...]).astype(BF)

    for i, target in enumerate(pairs):
        target[...] = partial(2 * (i + 1), 2)
    for i, target in enumerate(along):
        target[0:size, :] = partial(sub_count + 1 + i)
    for i, value in enumerate(rows):
        along[0][size + i * EXTRA : size + (i + 1) * EXTRA, :] = value[...]
    sibling[...] = partial(1)
    kept[0] = partial(0)
    kept[1] = partial(sub_count)


def split(total, value, second, size):
    zero = jnp.zeros_like(value)
    total[0:size, :] = total[0:size, :] + jnp.where(second, zero, value)
    total[size : 2 * size, :] = total[size : 2 * size, :] + jnp.where(second, value, zero)


def own_kernel(own, sub_count, rows, received, *rest):
    messages, rest = rest[:received], rest[received:]
    choice, w_self, dense_t, kept, spread, grad_pre, total, owner = rest
    size = kept.shape[1]
    width = total.shape[1]
    total[...] = dot_right_transposed(grad_pre[...], w_self[...]) + dot(
        dense_t[0 : own * size, :], spread[...]
    )
    for i, slot in enumerate((0, sub_count)):
        split(total, kept[i].astype(F32), choice[slot : slot + 1, :] > 0.5, size)
    for slot, at, row in rows:
        lane = lax.axis_index("sub")
        if slot > sub_count:
            lane = sub_count + lax.axis_index("cluster")
        index = lane_of(messages[at][row : row + EXTRA, :].astype(F32)[0:1, :], lane)
        owner[slot : slot + 1, :] = jnp.broadcast_to(index, (1, width))


def add_kernel(own, parts, owner, before, *rest):
    received, total = rest[:-1], rest[-1]
    size = total.shape[0] // own
    total[...] = before[...]
    for slot, at, row in parts:
        value = received[at][row : row + size, :].astype(F32)
        split(total, value, owner[slot : slot + 1, :] > 0.5, size)


def final_kernel(own, sub_count, parts, rows, owner, total, *rest):
    received, (out, done, sems) = rest[:-3], rest[-3:]
    size = total.shape[0] // own
    copies = []

    def leave(first, last, value):
        done[first:last, :] = value.astype(BF)
        copies.append(
            pltpu.make_async_copy(
                done.at[first:last, :], out.at[first:last, :], sems.at[len(copies)]
            )
        )
        copies[-1].start()

    leave(2 * size, own * size, total[2 * size :, :])
    indices = []
    for slot, at, row in parts:
        index = owner[slot : slot + 1, :]
        if slot in rows:
            where, first = rows[slot]
            row_of = received[where][first : first + EXTRA, :].astype(F32)[0:1, :]
            index = lane_of(row_of, sub_count + lax.axis_index("cluster"))
        indices.append(index)
    for block in range(2):
        value = total[block * size : (block + 1) * size, :]
        for index, (slot, at, row) in zip(indices, parts):
            mine = index > 0.5 if block else index <= 0.5
            value = value + jnp.where(mine, received[at][row : row + size, :].astype(F32), 0.0)
        leave(block * size, (block + 1) * size, value)
    for copy in copies:
        copy.wait()


def swap(value, axis, count, d):
    return lax.ppermute(value, axis, [(i, i ^ d) for i in range(count)])


def after(value, other):
    return lax.optimization_barrier((value, other))[0]


def in_hbm(value):
    return pltpu.with_memory_space_constraint(value, pltpu.HBM)


def cost(flops, moved):
    return pl.CostEstimate(flops=flops, bytes_accessed=moved, transcendentals=0)


def shards(
    features, grad_out, w_self, w_neigh, bias, tile_dst, tile_src, tile_weight, recv_sub, recv_cluster
):
    sub_count = lax.axis_size("sub")
    cluster_count = lax.axis_size("cluster")
    peers = sub_count + cluster_count - 2
    size = tile_weight.shape[1]
    rows, width = features.shape
    own = rows // size
    slots = own + sub_count + cluster_count
    counts = (own, sub_count, cluster_count)

    wide = jax.ShapeDtypeStruct((rows, width), F32)
    narrow = jax.ShapeDtypeStruct((rows, width), BF)
    square = jax.ShapeDtypeStruct((width, width), BF)
    block = jax.ShapeDtypeStruct((size, width), BF)
    marks = jax.ShapeDtypeStruct((sub_count + cluster_count, width), F32)

    edge, rows_only = pl.pallas_call(
        edge_kernel,
        out_shape=[
            jax.ShapeDtypeStruct((BOUNDARY * size + EXTRA, width), BF),
            jax.ShapeDtypeStruct((EXTRA, width), BF),
        ],
        in_specs=[HBM] * 3,
        out_specs=[VMEM] * 2,
        scratch_shapes=[
            pltpu.VMEM(recv_sub.shape, jnp.int32),
            pltpu.VMEM(recv_cluster.shape, jnp.int32),
            pltpu.SemaphoreType.DMA((2 + CHUNKS,)),
        ],
        compiler_params=PARAMS,
        cost_estimate=cost(1024, 256 * 1024),
        name="edge",
    )(in_hbm(recv_sub), in_hbm(recv_cluster), in_hbm(features))

    def along(value, d):
        return swap(value, "cluster", cluster_count, d)

    def across(value, d):
        return swap(value, "sub", sub_count, d)

    even = list(range(2, sub_count, 2))
    direct = list(range(2, cluster_count, 2))
    relayed = list(range(3, cluster_count, 2))
    rows_at = BOUNDARY * size
    got = {0: (edge, 0, False, rows_at), sub_count: (edge, 0, False, rows_at)}
    for d in direct:
        got[sub_count + d] = (along(edge, d), 0, False, rows_at)
    for d in even:
        got[d] = (across(edge, d), 0, False, rows_at)
    got[sub_count + 1] = (along(edge, 1), 0, False, rows_at)
    dense, choice, features, w_self, w_neigh, grad_out, bias = pl.pallas_call(
        functools.partial(prepare_kernel, *counts),
        out_shape=[
            jax.ShapeDtypeStruct((rows, slots * size), BF),
            marks,
            narrow,
            square,
            square,
            narrow,
            jax.ShapeDtypeStruct(bias.shape, F32),
        ],
        in_specs=[HBM] * 10,
        out_specs=[VMEM] * 7,
        scratch_shapes=[
            pltpu.SMEM(tile_dst.shape, jnp.int32),
            pltpu.SMEM(tile_src.shape, jnp.int32),
            pltpu.SMEM(recv_sub.shape, jnp.int32),
            pltpu.SMEM(recv_cluster.shape, jnp.int32),
            pltpu.VMEM(tile_weight.shape, BF),
            pltpu.SemaphoreType.DMA((9 + CHUNKS,)),
        ],
        compiler_params=PARAMS,
        cost_estimate=cost(10**8, 6 * 1024 * 1024),
        name="prepare",
    )(
        *map(in_hbm, (tile_dst, tile_src, recv_sub, recv_cluster, tile_weight)),
        *map(in_hbm, (features, w_self, w_neigh, grad_out, bias)),
    )

    def call(kernel, out_shape, name, flops, *operands):
        return pl.pallas_call(
            kernel,
            out_shape=out_shape,
            in_specs=[VMEM] * len(operands),
            out_specs=jax.tree.map(lambda _: VMEM, out_shape),
            compiler_params=PARAMS,
            cost_estimate=cost(flops, 1024 * 1024),
            name=name,
        )(*operands)

    def unique(slots):
        arrays, at = [], {}
        for slot in slots:
            known = [i for i, array in enumerate(arrays) if array is got[slot][0]]
            at[slot] = known[0] if known else len(arrays)
            if not known:
                arrays.append(got[slot][0])
        return arrays, at

    def sum_call(kernel, out_shape, name, slots, *operands):
        arrays, at = unique(slots)
        halos = [(slot, at[slot], got[slot][1], got[slot][2]) for slot in slots]
        return pl.pallas_call(
            functools.partial(kernel, own, halos),
            out_shape=out_shape,
            in_specs=[VMEM] * (len(operands) + len(arrays)),
            out_specs=jax.tree.map(lambda _: VMEM, out_shape),
            scratch_shapes=[pltpu.VMEM((len(slots) * size, width), BF)],
            compiler_params=PARAMS,
            cost_estimate=cost(dict(first=10**9, near=10**9, late=10**10)[name], 3 * 1024 * 1024),
            name=name,
        )(*operands, *arrays)

    carried = []
    for d in relayed:
        far = got[sub_count + d - 1][0]
        far_rows = call(
            rows_kernel, jax.ShapeDtypeStruct((EXTRA, width), BF), "rows", 10**9, far
        )
        value = call(
            functools.partial(relay_kernel, sub_count, d - 1),
            block,
            "relay", 10**6, far, far_rows, got[sub_count + 1][0],
        )
        carried.append(far_rows)
        got[sub_count + d] = (along(value, 1), 0, True, None)
    first_sum, own_pre, inverse = sum_call(
        first_kernel, [wide, wide, jax.ShapeDtypeStruct((rows, size), F32)], "first", [0, sub_count, *(sub_count + d for d in direct)],
        choice, dense, features, w_self, bias,
    )
    traded = [0, *even]
    sibling_rows = across(after(rows_only, value), 1)
    value = call(
        functools.partial(trade_kernel, traded),
        jax.ShapeDtypeStruct((len(traded) * (size + EXTRA), width), BF),
        "trade", 10**6, *[got[d][0] for d in traded], after(sibling_rows, (choice, value)),
    )
    trade_value = value
    value = across(value, 1)
    for i, d in enumerate(traded):
        got[d + 1] = (value, i * size, True, len(traded) * size + i * EXTRA)
    near_sum = sum_call(
        near_kernel, wide, "near", [sub_count + 1, *even], after(choice, trade_value), dense, first_sum
    )
    dense_t = call(
        functools.partial(flip_kernel, size), jax.ShapeDtypeStruct((slots * size, rows), BF), "flip", 10**7,
        after(dense, near_sum),
    )
    if relayed:
        slots_late = [sub_count + d for d in relayed]
        near_sum = sum_call(
            near_kernel, wide, "late", slots_late, after(choice, dense_t), dense, near_sum
        )

    late = [1, *(d + 1 for d in even)]
    late_arrays, late_at = unique(late)
    late_halos = [(slot, late_at[slot], got[slot][1], got[slot][2]) for slot in late]
    outs = pl.pallas_call(
        functools.partial(middle_kernel, *counts, late_halos, len(late_arrays), len(carried)),
        out_shape=[jax.ShapeDtypeStruct((2 * size, width), BF)] * len(even)
        + [jax.ShapeDtypeStruct((size + len(carried) * EXTRA, width), BF)]
        + [block] * (cluster_count - 1)
        + [jax.ShapeDtypeStruct((2, size, width), BF), narrow, narrow],
        in_specs=[VMEM] * (8 + len(late_arrays) + len(carried)),
        out_specs=[VMEM] * (len(even) + cluster_count + 3),
        scratch_shapes=[pltpu.VMEM((len(late) * size, width), BF)],
        compiler_params=PARAMS,
        cost_estimate=cost(2 * rows * slots * size * width, 6 * 1024 * 1024),
        name="middle",
    )(
        choice, grad_out, w_neigh, dense, dense_t, near_sum, own_pre, inverse,
        *late_arrays, *carried,
    )
    *sent, sibling, kept, spread, grad_pre = outs

    far = [(sub_count + d, along(sent[len(even) + d - 1], d)) for d in range(1, cluster_count)]
    near = [(d, across(value, d)) for d, value in zip(even, sent)]
    soon, rest = near[-1:], near[:-1]
    early = call(
        turn_kernel, jax.ShapeDtypeStruct((2 * size, width), BF), "early", 10**8,
        sibling, *[value for _, value in soon],
    )
    order = [sub_count + 1, *(sub_count + d for d in direct), *even, *(d + 1 for d in even), 1]
    arrays, at = unique(order)
    total, owner = pl.pallas_call(
        functools.partial(
            own_kernel, own, sub_count, [(slot, at[slot], got[slot][3]) for slot in order],
            len(arrays),
        ),
        out_shape=[wide, marks],
        in_specs=[VMEM] * (6 + len(arrays)),
        out_specs=[VMEM] * 2,
        compiler_params=PARAMS,
        cost_estimate=cost(10**9, 2 * 1024 * 1024),
        name="own",
    )(*arrays, after(choice, (far[-1][1], early)), w_self, dense_t, kept, spread, grad_pre)

    early = across(early, 1)
    turned = call(
        turn_kernel, jax.ShapeDtypeStruct((len(rest) * size, width), BF), "turn", 10**6,
        *[after(value, total) for _, value in rest],
    )
    turned = across(turned, 1)
    more = [*[pair for pair in far if pair[0] - sub_count in direct], *near[::-1]]
    parts = [(slot, i, 0) for i, (slot, _) in enumerate(more)]
    total = call(
        functools.partial(add_kernel, own, parts), wide, "add", 10**10,
        owner, total, *[value for _, value in more],
    )
    last = [pair for pair in far if pair[0] - sub_count not in direct]
    parts = [(slot, i, 0) for i, (slot, _) in enumerate(last)]
    parts += [(1, len(last), 0), *[(d + 1, len(last), size) for d, _ in soon]]
    parts += [(d + 1, len(last) + 1, i * size) for i, (d, _) in enumerate(rest)]
    beside = [i for i, (slot, _) in enumerate(last) if slot == sub_count + 1]
    places = {
        sub_count + d: (beside[0], size + i * EXTRA) for i, d in enumerate(relayed)
    }
    return pl.pallas_call(
        functools.partial(final_kernel, own, sub_count, parts, places),
        out_shape=narrow,
        in_specs=[VMEM] * (4 + len(last)),
        out_specs=HBM,
        scratch_shapes=[pltpu.VMEM((rows, width), BF), pltpu.SemaphoreType.DMA((3,))],
        compiler_params=PARAMS,
        cost_estimate=cost(rows * width * 4, 1024 * 1024),
        name="final",
    )(owner, total, *[value for _, value in last], early, turned)


def solution(mesh):
    placed = (
        P(("cluster", "sub"), None),
        P(("cluster", "sub"), None),
        P(),
        P(),
        P(),
        P(("cluster", "sub")),
        P(("cluster", "sub")),
        P(("cluster", "sub"), None, None),
        P(("cluster", "sub"), None),
        P(("cluster", "sub"), None),
    )
    return jax.shard_map(
        shards, mesh=mesh, in_specs=placed, out_specs=P(("cluster", "sub"), None), check_vma=False
    )
```

```python
import functools

import jax
import jax.numpy as jnp
from jax import lax
from jax.experimental import pallas as pl
from jax.experimental.pallas import tpu as pltpu
from jax.sharding import PartitionSpec as P

BF = jnp.bfloat16
F32 = jnp.float32
BOUNDARY = 2
EXTRA = 16
CHUNKS = 4
VMEM = pl.BlockSpec(memory_space=pltpu.VMEM)
HBM = pl.BlockSpec(memory_space=pltpu.HBM)
PARAMS = pltpu.CompilerParams(vmem_limit_bytes=24 * 1024 * 1024)


def dot(left, right):
    return jnp.dot(left, right, preferred_element_type=F32)


def dot_right_transposed(left, right):
    return lax.dot_general(left, right, (((1,), (1,)), ((), ())), preferred_element_type=F32)


def gelu_slope(v):
    scale = 0.7978845608028654
    t = jnp.tanh(scale * (v + 0.044715 * v * v * v))
    return 0.5 * (1.0 + t) + (0.5 * scale) * v * (1.0 - t * t) * (1.0 + 3.0 * 0.044715 * v * v)


def edge_kernel(recv_sub, recv_cluster, features, edge, rows, sub_row, cluster_row, sems):
    count = edge.shape[0] - EXTRA
    step = count // CHUNKS
    small = [
        pltpu.make_async_copy(recv_sub, sub_row, sems.at[0]),
        pltpu.make_async_copy(recv_cluster, cluster_row, sems.at[1]),
    ]
    large = []
    for i in range(CHUNKS):
        part = slice(i * step, (i + 1) * step)
        large.append(
            pltpu.make_async_copy(features.at[part, :], edge.at[part, :], sems.at[2 + i])
        )
    for copy in small + large:
        copy.start()
    for copy in small:
        copy.wait()
    sub_count, cluster_count = sub_row.shape[1], cluster_row.shape[1]
    pad = jnp.zeros((1, edge.shape[1] - sub_count - cluster_count), F32)
    row = jnp.concatenate([sub_row[...].astype(F32), cluster_row[...].astype(F32), pad], axis=1)
    value = jnp.broadcast_to(row, rows.shape).astype(BF)
    edge[count:, :] = value
    rows[...] = value
    for copy in large:
        copy.wait()


def prepare_kernel(
    own, sub_count, cluster_count,
    tile_dst_hbm, tile_src_hbm, recv_sub_hbm, recv_cluster_hbm, tile_weight_hbm,
    features_hbm, w_self_hbm, w_neigh_hbm, grad_out_hbm, bias_hbm,
    dense, choice, features, w_self, w_neigh, grad_out, bias,
    tile_dst, tile_src, recv_sub, recv_cluster, tile_weight, sems,
):
    size = tile_weight.shape[1]
    step = tile_weight.shape[0] // CHUNKS
    pairs = (
        (tile_dst_hbm, tile_dst), (tile_src_hbm, tile_src), (recv_sub_hbm, recv_sub),
        (recv_cluster_hbm, recv_cluster),
        *(
            (tile_weight_hbm.at[i * step : (i + 1) * step], tile_weight.at[i * step : (i + 1) * step])
            for i in range(CHUNKS)
        ),
        (features_hbm, features), (w_self_hbm, w_self), (w_neigh_hbm, w_neigh),
        (grad_out_hbm, grad_out), (bias_hbm, bias),
    )
    copies = [pltpu.make_async_copy(a, b, sems.at[i]) for i, (a, b) in enumerate(pairs)]
    for copy in copies:
        copy.start()
    sub_id = lax.axis_index("sub")
    cluster_id = lax.axis_index("cluster")
    dense[...] = jnp.zeros_like(dense)
    for copy in copies[: 4 + CHUNKS]:
        copy.wait()

    def place(t, carry):
        src = tile_src[t]
        from_sub = own + ((src - own) ^ sub_id)
        from_cluster = own + sub_count + ((src - own - sub_count) ^ cluster_id)
        slot = jnp.where(src < own, src, jnp.where(src < own + sub_count, from_sub, from_cluster))
        dst = pl.ds(pl.multiple_of(tile_dst[t] * size, size), size)
        col = pl.ds(pl.multiple_of(slot * size, size), size)
        dense[dst, col] = dense[dst, col] + tile_weight[t]
        return carry

    lax.fori_loop(0, tile_weight.shape[0], place, 0, unroll=4)
    for d in range(sub_count):
        index = recv_sub[0, sub_id ^ d].astype(F32)
        choice[d : d + 1, :] = jnp.full((1, choice.shape[1]), index, F32)
    for d in range(cluster_count):
        index = recv_cluster[0, cluster_id ^ d].astype(F32)
        choice[sub_count + d : sub_count + d + 1, :] = jnp.full((1, choice.shape[1]), index, F32)
    for copy in copies[4 + CHUNKS :]:
        copy.wait()


def index_row(message, size):
    return message[2 * size : 2 * size + EXTRA, :].astype(F32)[0:1, :]


def lane_of(row, lane):
    lanes = lax.broadcasted_iota(jnp.int32, row.shape, 1)
    return jnp.sum(jnp.where(lanes == lane, row, 0.0), axis=1, keepdims=True)


def pick(message, index, size):
    return jnp.where(
        index > 0.5, message[size : 2 * size, :].astype(F32), message[0:size, :].astype(F32)
    ).astype(BF)


def rows_kernel(message, out):
    out[...] = message[message.shape[0] - EXTRA :, :]


def relay_kernel(sub_count, d, far, rows, near, out):
    size = out.shape[0]
    index = lane_of(index_row(near, size), sub_count + (lax.axis_index("cluster") ^ d))
    out[...] = pick(far, index, size)


def trade_kernel(even, *rest):
    messages, (sibling, out) = rest[:-2], rest[-2:]
    size = out.shape[0] // len(even) - EXTRA
    row = sibling[...].astype(F32)[0:1, :]
    for i, (d, message) in enumerate(zip(even, messages)):
        index = lane_of(row, lax.axis_index("sub") ^ d)
        out[i * size : (i + 1) * size, :] = pick(message, index, size)
        at = len(even) * size + i * EXTRA
        out[at : at + EXTRA, :] = message[2 * size :, :]


def turn_kernel(*rest):
    messages, out = rest[:-1], rest[-1]
    size = out.shape[0] // len(messages)
    for i, message in enumerate(messages):
        last = message.shape[0]
        out[i * size : (i + 1) * size, :] = message[last - size : last, :]


def halo_blocks(choice, size, halos, refs, halo):
    first = halos[0]
    if all(
        (at, row, picked) == (first[1], first[2] + i * size, True)
        for i, (_, at, row, picked) in enumerate(halos)
    ):
        return refs[first[1]][first[2] : first[2] + len(halos) * size, :]
    for i, (slot, at, row, picked) in enumerate(halos):
        if picked:
            block = refs[at][row : row + size, :]
        else:
            block = pick(refs[at], choice[slot : slot + 1, :], size)
        halo[i * size : (i + 1) * size, :] = block
    return halo[...]


def halo_sum(choice, dense, own, halos, refs, halo):
    size = dense.shape[0] // own
    blocks = halo_blocks(choice, size, halos, refs, halo)
    columns = [dense[:, (own + slot) * size : (own + slot + 1) * size] for slot, *_ in halos]
    return dot(jnp.concatenate(columns, axis=1), blocks)


def flip_kernel(size, dense, dense_t):
    for at in range(0, dense.shape[1], size):
        dense_t[at : at + size, :] = dense[:, at : at + size].T


def first_kernel(own, halos, choice, dense, features, w_self, bias, *rest):
    refs, (total, own_pre, inverse, halo) = rest[:-4], rest[-4:]
    size = dense.shape[0] // own
    count = dense[:, 0:size].astype(F32)
    for at in range(size, dense.shape[1], size):
        count = count + dense[:, at : at + size].astype(F32)
    degree = jnp.sum(count, axis=1, keepdims=True)
    inverse[...] = jnp.broadcast_to(1.0 / (degree + 1.0), inverse.shape)
    total[...] = dot(dense[:, 0 : own * size], features[...]) + halo_sum(
        choice, dense, own, halos, refs, halo
    )
    own_pre[...] = dot(features[...], w_self[...]) + bias[...].reshape(1, -1)


def near_kernel(own, halos, choice, dense, before, *rest):
    refs, (total, halo) = rest[:-2], rest[-2:]
    total[...] = before[...] + halo_sum(choice, dense, own, halos, refs, halo)


def middle_kernel(
    own, sub_count, cluster_count, halos, received, carried,
    choice, grad_out, w_neigh, dense, dense_t, before, own_pre, inverse,
    *rest,
):
    refs, rest = rest[:received], rest[received:]
    rows, rest = rest[:carried], rest[carried:]
    pairs, rest = rest[: sub_count // 2 - 1], rest[sub_count // 2 - 1 :]
    along, (sibling, kept, spread, grad_pre, halo) = rest[:-5], rest[-5:]
    size = dense.shape[0] // own
    aggregate = before[...] + halo_sum(choice, dense, own, halos, refs, halo)
    inv = jnp.concatenate([inverse[...]] * (grad_out.shape[1] // size), axis=1)
    mean = (aggregate * inv).astype(BF)
    pre = own_pre[...] + dot(mean, w_neigh[...])
    grad = (grad_out[...].astype(F32) * gelu_slope(pre)).astype(BF)
    grad_pre[...] = grad
    spread[...] = (dot_right_transposed(grad, w_neigh[...]) * inv).astype(BF)

    def partial(slot, count=1):
        rows = slice((own + slot) * size, (own + slot + count) * size)
        return dot(dense_t[rows, :], spread[...]).astype(BF)

    for i, target in enumerate(pairs):
        target[...] = partial(2 * (i + 1), 2)
    for i, target in enumerate(along):
        target[0:size, :] = partial(sub_count + 1 + i)
    for i, value in enumerate(rows):
        along[0][size + i * EXTRA : size + (i + 1) * EXTRA, :] = value[...]
    sibling[...] = partial(1)
    kept[0] = partial(0)
    kept[1] = partial(sub_count)


def split(total, value, second, size):
    zero = jnp.zeros_like(value)
    total[0:size, :] = total[0:size, :] + jnp.where(second, zero, value)
    total[size : 2 * size, :] = total[size : 2 * size, :] + jnp.where(second, value, zero)


def own_kernel(own, sub_count, rows, received, *rest):
    messages, rest = rest[:received], rest[received:]
    choice, w_self, dense_t, kept, spread, grad_pre, total, owner = rest
    size = kept.shape[1]
    width = total.shape[1]
    total[...] = dot_right_transposed(grad_pre[...], w_self[...]) + dot(
        dense_t[0 : own * size, :], spread[...]
    )
    for i, slot in enumerate((0, sub_count)):
        split(total, kept[i].astype(F32), choice[slot : slot + 1, :] > 0.5, size)
    for slot, at, row in rows:
        lane = lax.axis_index("sub")
        if slot > sub_count:
            lane = sub_count + lax.axis_index("cluster")
        index = lane_of(messages[at][row : row + EXTRA, :].astype(F32)[0:1, :], lane)
        owner[slot : slot + 1, :] = jnp.broadcast_to(index, (1, width))


def add_kernel(own, sub_count, parts, rows, owner, before, *rest):
    received, total = rest[:-1], rest[-1]
    size = total.shape[0] // own
    total[...] = before[...]
    for slot, at, row in parts:
        value = received[at][row : row + size, :].astype(F32)
        index = owner[slot : slot + 1, :]
        if slot in rows:
            where, first = rows[slot]
            indices = received[where][first : first + EXTRA, :].astype(F32)[0:1, :]
            index = lane_of(indices, sub_count + lax.axis_index("cluster"))
        split(total, value, index > 0.5, size)


def final_kernel(own, parts, owner, total, *rest):
    received, (out, done, sems) = rest[:-3], rest[-3:]
    size = total.shape[0] // own
    copies = []

    def leave(first, last, value):
        done[first:last, :] = value.astype(BF)
        copies.append(
            pltpu.make_async_copy(
                done.at[first:last, :], out.at[first:last, :], sems.at[len(copies)]
            )
        )
        copies[-1].start()

    leave(2 * size, own * size, total[2 * size :, :])
    for block in range(2):
        value = total[block * size : (block + 1) * size, :]
        for slot, at, row in parts:
            index = owner[slot : slot + 1, :]
            mine = index > 0.5 if block else index <= 0.5
            value = value + jnp.where(mine, received[at][row : row + size, :].astype(F32), 0.0)
        leave(block * size, (block + 1) * size, value)
    for copy in copies:
        copy.wait()


def swap(value, axis, count, d):
    return lax.ppermute(value, axis, [(i, i ^ d) for i in range(count)])


def after(value, other):
    return lax.optimization_barrier((value, other))[0]


def in_hbm(value):
    return pltpu.with_memory_space_constraint(value, pltpu.HBM)


def cost(flops, moved):
    return pl.CostEstimate(flops=flops, bytes_accessed=moved, transcendentals=0)


def shards(
    features, grad_out, w_self, w_neigh, bias, tile_dst, tile_src, tile_weight, recv_sub, recv_cluster
):
    sub_count = lax.axis_size("sub")
    cluster_count = lax.axis_size("cluster")
    peers = sub_count + cluster_count - 2
    size = tile_weight.shape[1]
    rows, width = features.shape
    own = rows // size
    slots = own + sub_count + cluster_count
    counts = (own, sub_count, cluster_count)

    wide = jax.ShapeDtypeStruct((rows, width), F32)
    narrow = jax.ShapeDtypeStruct((rows, width), BF)
    square = jax.ShapeDtypeStruct((width, width), BF)
    block = jax.ShapeDtypeStruct((size, width), BF)
    marks = jax.ShapeDtypeStruct((sub_count + cluster_count, width), F32)

    edge, rows_only = pl.pallas_call(
        edge_kernel,
        out_shape=[
            jax.ShapeDtypeStruct((BOUNDARY * size + EXTRA, width), BF),
            jax.ShapeDtypeStruct((EXTRA, width), BF),
        ],
        in_specs=[HBM] * 3,
        out_specs=[VMEM] * 2,
        scratch_shapes=[
            pltpu.VMEM(recv_sub.shape, jnp.int32),
            pltpu.VMEM(recv_cluster.shape, jnp.int32),
            pltpu.SemaphoreType.DMA((2 + CHUNKS,)),
        ],
        compiler_params=PARAMS,
        cost_estimate=cost(1024, 256 * 1024),
        name="edge",
    )(in_hbm(recv_sub), in_hbm(recv_cluster), in_hbm(features))

    def along(value, d):
        return swap(value, "cluster", cluster_count, d)

    def across(value, d):
        return swap(value, "sub", sub_count, d)

    even = list(range(2, sub_count, 2))
    direct = list(range(2, cluster_count, 2))
    relayed = list(range(3, cluster_count, 2))
    rows_at = BOUNDARY * size
    got = {0: (edge, 0, False, rows_at), sub_count: (edge, 0, False, rows_at)}
    for d in direct:
        got[sub_count + d] = (along(edge, d), 0, False, rows_at)
    for d in even:
        got[d] = (across(edge, d), 0, False, rows_at)
    got[sub_count + 1] = (along(edge, 1), 0, False, rows_at)
    dense, choice, features, w_self, w_neigh, grad_out, bias = pl.pallas_call(
        functools.partial(prepare_kernel, *counts),
        out_shape=[
            jax.ShapeDtypeStruct((rows, slots * size), BF),
            marks,
            narrow,
            square,
            square,
            narrow,
            jax.ShapeDtypeStruct(bias.shape, F32),
        ],
        in_specs=[HBM] * 10,
        out_specs=[VMEM] * 7,
        scratch_shapes=[
            pltpu.SMEM(tile_dst.shape, jnp.int32),
            pltpu.SMEM(tile_src.shape, jnp.int32),
            pltpu.SMEM(recv_sub.shape, jnp.int32),
            pltpu.SMEM(recv_cluster.shape, jnp.int32),
            pltpu.VMEM(tile_weight.shape, BF),
            pltpu.SemaphoreType.DMA((9 + CHUNKS,)),
        ],
        compiler_params=PARAMS,
        cost_estimate=cost(10**8, 6 * 1024 * 1024),
        name="prepare",
    )(
        *map(in_hbm, (tile_dst, tile_src, recv_sub, recv_cluster, tile_weight)),
        *map(in_hbm, (features, w_self, w_neigh, grad_out, bias)),
    )

    def call(kernel, out_shape, name, flops, *operands):
        return pl.pallas_call(
            kernel,
            out_shape=out_shape,
            in_specs=[VMEM] * len(operands),
            out_specs=jax.tree.map(lambda _: VMEM, out_shape),
            compiler_params=PARAMS,
            cost_estimate=cost(flops, 1024 * 1024),
            name=name,
        )(*operands)

    def unique(slots):
        arrays, at = [], {}
        for slot in slots:
            known = [i for i, array in enumerate(arrays) if array is got[slot][0]]
            at[slot] = known[0] if known else len(arrays)
            if not known:
                arrays.append(got[slot][0])
        return arrays, at

    def sum_call(kernel, out_shape, name, slots, *operands):
        arrays, at = unique(slots)
        halos = [(slot, at[slot], got[slot][1], got[slot][2]) for slot in slots]
        return pl.pallas_call(
            functools.partial(kernel, own, halos),
            out_shape=out_shape,
            in_specs=[VMEM] * (len(operands) + len(arrays)),
            out_specs=jax.tree.map(lambda _: VMEM, out_shape),
            scratch_shapes=[pltpu.VMEM((len(slots) * size, width), BF)],
            compiler_params=PARAMS,
            cost_estimate=cost(dict(first=10**9, near=10**10)[name], 3 * 1024 * 1024),
            name=name,
        )(*operands, *arrays)

    carried = []
    for d in relayed:
        far = got[sub_count + d - 1][0]
        far_rows = call(
            rows_kernel, jax.ShapeDtypeStruct((EXTRA, width), BF), "rows", 10**9, far
        )
        value = call(
            functools.partial(relay_kernel, sub_count, d - 1),
            block,
            "relay", 10**6, far, far_rows, got[sub_count + 1][0],
        )
        carried.append(far_rows)
        got[sub_count + d] = (along(value, 1), 0, True, None)
    first_sum, own_pre, inverse = sum_call(
        first_kernel, [wide, wide, jax.ShapeDtypeStruct((rows, size), F32)], "first", [0, sub_count, *(sub_count + d for d in direct)],
        choice, dense, features, w_self, bias,
    )
    traded = [0, *even]
    sibling_rows = across(after(rows_only, value), 1)
    value = call(
        functools.partial(trade_kernel, traded),
        jax.ShapeDtypeStruct((len(traded) * (size + EXTRA), width), BF),
        "trade", 10**6, *[got[d][0] for d in traded], after(sibling_rows, (choice, value)),
    )
    trade_value = value
    value = across(value, 1)
    for i, d in enumerate(traded):
        got[d + 1] = (value, i * size, True, len(traded) * size + i * EXTRA)
    near_sum = sum_call(
        near_kernel, wide, "near", [sub_count + 1, *even], after(choice, trade_value), dense, first_sum
    )
    dense_t = call(
        functools.partial(flip_kernel, size), jax.ShapeDtypeStruct((slots * size, rows), BF), "flip", 10**7,
        after(dense, near_sum),
    )

    late = [*(sub_count + d for d in relayed), 1, *(d + 1 for d in even)]
    late_arrays, late_at = unique(late)
    late_halos = [(slot, late_at[slot], got[slot][1], got[slot][2]) for slot in late]
    outs = pl.pallas_call(
        functools.partial(middle_kernel, *counts, late_halos, len(late_arrays), len(carried)),
        out_shape=[jax.ShapeDtypeStruct((2 * size, width), BF)] * len(even)
        + [jax.ShapeDtypeStruct((size + len(carried) * EXTRA, width), BF)]
        + [block] * (cluster_count - 1)
        + [jax.ShapeDtypeStruct((2, size, width), BF), narrow, narrow],
        in_specs=[VMEM] * (8 + len(late_arrays) + len(carried)),
        out_specs=[VMEM] * (len(even) + cluster_count + 3),
        scratch_shapes=[pltpu.VMEM((len(late) * size, width), BF)],
        compiler_params=PARAMS,
        cost_estimate=cost(2 * rows * slots * size * width, 6 * 1024 * 1024),
        name="middle",
    )(
        choice, grad_out, w_neigh, dense, dense_t, near_sum, own_pre, inverse,
        *late_arrays, *carried,
    )
    *sent, sibling, kept, spread, grad_pre = outs

    far = [(sub_count + d, along(sent[len(even) + d - 1], d)) for d in range(1, cluster_count)]
    near = [(d, across(value, d)) for d, value in zip(even, sent)]
    soon, rest = near[-1:], near[:-1]
    early = call(
        turn_kernel, jax.ShapeDtypeStruct((2 * size, width), BF), "early", 10**8,
        sibling, *[value for _, value in soon],
    )
    order = [sub_count + 1, *(sub_count + d for d in direct), *even, *(d + 1 for d in even), 1]
    arrays, at = unique(order)
    total, owner = pl.pallas_call(
        functools.partial(
            own_kernel, own, sub_count, [(slot, at[slot], got[slot][3]) for slot in order],
            len(arrays),
        ),
        out_shape=[wide, marks],
        in_specs=[VMEM] * (6 + len(arrays)),
        out_specs=[VMEM] * 2,
        compiler_params=PARAMS,
        cost_estimate=cost(10**9, 2 * 1024 * 1024),
        name="own",
    )(*arrays, after(choice, (far[-1][1], early)), w_self, dense_t, kept, spread, grad_pre)

    early = across(early, 1)
    turned = call(
        turn_kernel, jax.ShapeDtypeStruct((len(rest) * size, width), BF), "turn", 10**6,
        *[after(value, total) for _, value in rest],
    )
    turned = across(turned, 1)
    more = [*far, *near[::-1]]
    places = {slot: (0, size + i * EXTRA) for i, slot in enumerate(sub_count + d for d in relayed)}
    total = call(
        functools.partial(
            add_kernel, own, sub_count, [(slot, i, 0) for i, (slot, _) in enumerate(more)], places
        ),
        wide, "add", 10**10, owner, total, *[value for _, value in more],
    )
    parts = [(1, 0, 0), *[(d + 1, 0, size) for d, _ in soon]]
    parts += [(d + 1, 1, i * size) for i, (d, _) in enumerate(rest)]
    values = [early]
    return pl.pallas_call(
        functools.partial(final_kernel, own, parts),
        out_shape=narrow,
        in_specs=[VMEM] * (3 + len(values)),
        out_specs=HBM,
        scratch_shapes=[pltpu.VMEM((rows, width), BF), pltpu.SemaphoreType.DMA((3,))],
        compiler_params=PARAMS,
        cost_estimate=cost(rows * width * 4, 1024 * 1024),
        name="final",
    )(owner, total, *values, turned)


def solution(mesh):
    placed = (
        P(("cluster", "sub"), None),
        P(("cluster", "sub"), None),
        P(),
        P(),
        P(),
        P(("cluster", "sub")),
        P(("cluster", "sub")),
        P(("cluster", "sub"), None, None),
        P(("cluster", "sub"), None),
        P(("cluster", "sub"), None),
    )
    return jax.shard_map(
        shards, mesh=mesh, in_specs=placed, out_specs=P(("cluster", "sub"), None), check_vma=False
    )
```

```python
import functools

import jax
import jax.numpy as jnp
from jax import lax
from jax.experimental import pallas as pl
from jax.experimental.pallas import tpu as pltpu
from jax.sharding import PartitionSpec as P

BF = jnp.bfloat16
F32 = jnp.float32
BOUNDARY = 2
EXTRA = 16
CHUNKS = 4
VMEM = pl.BlockSpec(memory_space=pltpu.VMEM)
HBM = pl.BlockSpec(memory_space=pltpu.HBM)
PARAMS = pltpu.CompilerParams(vmem_limit_bytes=24 * 1024 * 1024)


def dot(left, right):
    return jnp.dot(left, right, preferred_element_type=F32)


def dot_right_transposed(left, right):
    return lax.dot_general(left, right, (((1,), (1,)), ((), ())), preferred_element_type=F32)


def gelu_slope(v):
    scale = 0.7978845608028654
    t = jnp.tanh(scale * (v + 0.044715 * v * v * v))
    return 0.5 * (1.0 + t) + (0.5 * scale) * v * (1.0 - t * t) * (1.0 + 3.0 * 0.044715 * v * v)


def edge_kernel(recv_sub, recv_cluster, features, edge, rows, sub_row, cluster_row, sems):
    count = edge.shape[0] - EXTRA
    step = count // CHUNKS
    small = [
        pltpu.make_async_copy(recv_sub, sub_row, sems.at[0]),
        pltpu.make_async_copy(recv_cluster, cluster_row, sems.at[1]),
    ]
    large = []
    for i in range(CHUNKS):
        part = slice(i * step, (i + 1) * step)
        large.append(
            pltpu.make_async_copy(features.at[part, :], edge.at[part, :], sems.at[2 + i])
        )
    for copy in small + large:
        copy.start()
    for copy in small:
        copy.wait()
    sub_count, cluster_count = sub_row.shape[1], cluster_row.shape[1]
    pad = jnp.zeros((1, edge.shape[1] - sub_count - cluster_count), F32)
    row = jnp.concatenate([sub_row[...].astype(F32), cluster_row[...].astype(F32), pad], axis=1)
    value = jnp.broadcast_to(row, rows.shape).astype(BF)
    edge[count:, :] = value
    rows[...] = value
    for copy in large:
        copy.wait()


def prepare_kernel(
    own, sub_count, cluster_count,
    tile_dst_hbm, tile_src_hbm, recv_sub_hbm, recv_cluster_hbm, tile_weight_hbm,
    features_hbm, w_self_hbm, w_neigh_hbm, grad_out_hbm, bias_hbm,
    dense, choice, features, w_self, w_neigh, grad_out, bias,
    tile_dst, tile_src, recv_sub, recv_cluster, tile_weight, sems,
):
    size = tile_weight.shape[1]
    step = tile_weight.shape[0] // CHUNKS
    pairs = (
        (tile_dst_hbm, tile_dst), (tile_src_hbm, tile_src), (recv_sub_hbm, recv_sub),
        (recv_cluster_hbm, recv_cluster),
        *(
            (tile_weight_hbm.at[i * step : (i + 1) * step], tile_weight.at[i * step : (i + 1) * step])
            for i in range(CHUNKS)
        ),
        (features_hbm, features), (w_self_hbm, w_self), (w_neigh_hbm, w_neigh),
        (grad_out_hbm, grad_out), (bias_hbm, bias),
    )
    copies = [pltpu.make_async_copy(a, b, sems.at[i]) for i, (a, b) in enumerate(pairs)]
    for copy in copies:
        copy.start()
    sub_id = lax.axis_index("sub")
    cluster_id = lax.axis_index("cluster")
    dense[...] = jnp.zeros_like(dense)
    for copy in copies[: 4 + CHUNKS]:
        copy.wait()

    def place(t, carry):
        src = tile_src[t]
        from_sub = own + ((src - own) ^ sub_id)
        from_cluster = own + sub_count + ((src - own - sub_count) ^ cluster_id)
        slot = jnp.where(src < own, src, jnp.where(src < own + sub_count, from_sub, from_cluster))
        dst = pl.ds(pl.multiple_of(tile_dst[t] * size, size), size)
        col = pl.ds(pl.multiple_of(slot * size, size), size)
        dense[dst, col] = dense[dst, col] + tile_weight[t]
        return carry

    lax.fori_loop(0, tile_weight.shape[0], place, 0, unroll=4)
    for d in range(sub_count):
        index = recv_sub[0, sub_id ^ d].astype(F32)
        choice[d : d + 1, :] = jnp.full((1, choice.shape[1]), index, F32)
    for d in range(cluster_count):
        index = recv_cluster[0, cluster_id ^ d].astype(F32)
        choice[sub_count + d : sub_count + d + 1, :] = jnp.full((1, choice.shape[1]), index, F32)
    for copy in copies[4 + CHUNKS :]:
        copy.wait()


def index_row(message, size):
    return message[2 * size : 2 * size + EXTRA, :].astype(F32)[0:1, :]


def lane_of(row, lane):
    lanes = lax.broadcasted_iota(jnp.int32, row.shape, 1)
    return jnp.sum(jnp.where(lanes == lane, row, 0.0), axis=1, keepdims=True)


def pick(message, index, size):
    return jnp.where(
        index > 0.5, message[size : 2 * size, :].astype(F32), message[0:size, :].astype(F32)
    ).astype(BF)


def rows_kernel(message, out):
    out[...] = message[message.shape[0] - EXTRA :, :]


def relay_kernel(sub_count, d, far, rows, near, out):
    size = out.shape[0]
    index = lane_of(index_row(near, size), sub_count + (lax.axis_index("cluster") ^ d))
    out[...] = pick(far, index, size)


def trade_kernel(even, *rest):
    messages, (sibling, out) = rest[:-2], rest[-2:]
    size = out.shape[0] // len(even) - EXTRA
    row = sibling[...].astype(F32)[0:1, :]
    for i, (d, message) in enumerate(zip(even, messages)):
        index = lane_of(row, lax.axis_index("sub") ^ d)
        out[i * size : (i + 1) * size, :] = pick(message, index, size)
        at = len(even) * size + i * EXTRA
        out[at : at + EXTRA, :] = message[2 * size :, :]


def turn_kernel(*rest):
    messages, out = rest[:-1], rest[-1]
    size = out.shape[0] // len(messages)
    for i, message in enumerate(messages):
        last = message.shape[0]
        out[i * size : (i + 1) * size, :] = message[last - size : last, :]


def halo_sum(choice, dense, own, halos, refs, halo):
    size = dense.shape[0] // own
    columns = []
    for i, (slot, at, row, picked) in enumerate(halos):
        if picked:
            block = refs[at][row : row + size, :]
        else:
            block = pick(refs[at], choice[slot : slot + 1, :], size)
        halo[i * size : (i + 1) * size, :] = block
        columns.append(dense[:, (own + slot) * size : (own + slot + 1) * size])
    return dot(jnp.concatenate(columns, axis=1), halo[...])


def flip_kernel(size, dense, dense_t):
    for at in range(0, dense.shape[1], size):
        dense_t[at : at + size, :] = dense[:, at : at + size].T


def first_kernel(own, halos, choice, dense, features, w_self, bias, *rest):
    refs, (total, own_pre, inverse, halo) = rest[:-4], rest[-4:]
    size = dense.shape[0] // own
    count = dense[:, 0:size].astype(F32)
    for at in range(size, dense.shape[1], size):
        count = count + dense[:, at : at + size].astype(F32)
    degree = jnp.sum(count, axis=1, keepdims=True)
    inverse[...] = jnp.broadcast_to(1.0 / (degree + 1.0), inverse.shape)
    total[...] = dot(dense[:, 0 : own * size], features[...]) + halo_sum(
        choice, dense, own, halos, refs, halo
    )
    own_pre[...] = dot(features[...], w_self[...]) + bias[...].reshape(1, -1)


def near_kernel(own, halos, choice, dense, before, *rest):
    refs, (total, halo) = rest[:-2], rest[-2:]
    total[...] = before[...] + halo_sum(choice, dense, own, halos, refs, halo)


def middle_kernel(
    own, sub_count, cluster_count, halos, received, carried,
    choice, grad_out, w_neigh, dense, dense_t, before, own_pre, inverse,
    *rest,
):
    refs, rest = rest[:received], rest[received:]
    rows, rest = rest[:carried], rest[carried:]
    pairs, rest = rest[: sub_count // 2 - 1], rest[sub_count // 2 - 1 :]
    along, (sibling, kept, spread, grad_pre, halo) = rest[:-5], rest[-5:]
    size = dense.shape[0] // own
    aggregate = before[...] + halo_sum(choice, dense, own, halos, refs, halo)
    inv = jnp.concatenate([inverse[...]] * (grad_out.shape[1] // size), axis=1)
    mean = (aggregate * inv).astype(BF)
    pre = own_pre[...] + dot(mean, w_neigh[...])
    grad = (grad_out[...].astype(F32) * gelu_slope(pre)).astype(BF)
    grad_pre[...] = grad
    spread[...] = (dot_right_transposed(grad, w_neigh[...]) * inv).astype(BF)

    def partial(slot, count=1):
        rows = slice((own + slot) * size, (own + slot + count) * size)
        return dot(dense_t[rows, :], spread[...]).astype(BF)

    for i, target in enumerate(pairs):
        target[...] = partial(2 * (i + 1), 2)
    for i, target in enumerate(along):
        target[0:size, :] = partial(sub_count + 1 + i)
    for i, value in enumerate(rows):
        along[0][size + i * EXTRA : size + (i + 1) * EXTRA, :] = value[...]
    sibling[...] = partial(1)
    kept[0] = partial(0)
    kept[1] = partial(sub_count)


def split(total, value, second, size):
    zero = jnp.zeros_like(value)
    total[0:size, :] = total[0:size, :] + jnp.where(second, zero, value)
    total[size : 2 * size, :] = total[size : 2 * size, :] + jnp.where(second, value, zero)


def own_kernel(own, sub_count, rows, received, *rest):
    messages, rest = rest[:received], rest[received:]
    choice, w_self, dense_t, kept, spread, grad_pre, total, owner = rest
    size = kept.shape[1]
    width = total.shape[1]
    total[...] = dot_right_transposed(grad_pre[...], w_self[...]) + dot(
        dense_t[0 : own * size, :], spread[...]
    )
    for i, slot in enumerate((0, sub_count)):
        split(total, kept[i].astype(F32), choice[slot : slot + 1, :] > 0.5, size)
    for slot, at, row in rows:
        lane = lax.axis_index("sub")
        if slot > sub_count:
            lane = sub_count + lax.axis_index("cluster")
        index = lane_of(messages[at][row : row + EXTRA, :].astype(F32)[0:1, :], lane)
        owner[slot : slot + 1, :] = jnp.broadcast_to(index, (1, width))


def add_kernel(own, sub_count, parts, rows, owner, before, *rest):
    received, total = rest[:-1], rest[-1]
    size = total.shape[0] // own
    total[...] = before[...]
    for slot, at, row in parts:
        value = received[at][row : row + size, :].astype(F32)
        index = owner[slot : slot + 1, :]
        if slot in rows:
            where, first = rows[slot]
            indices = received[where][first : first + EXTRA, :].astype(F32)[0:1, :]
            index = lane_of(indices, sub_count + lax.axis_index("cluster"))
        split(total, value, index > 0.5, size)


def final_kernel(own, parts, owner, total, *rest):
    received, (out, done, sems) = rest[:-3], rest[-3:]
    size = total.shape[0] // own
    copies = []

    def leave(first, last, value):
        done[first:last, :] = value.astype(BF)
        copies.append(
            pltpu.make_async_copy(
                done.at[first:last, :], out.at[first:last, :], sems.at[len(copies)]
            )
        )
        copies[-1].start()

    leave(2 * size, own * size, total[2 * size :, :])
    for block in range(2):
        value = total[block * size : (block + 1) * size, :]
        for slot, at, row in parts:
            index = owner[slot : slot + 1, :]
            mine = index > 0.5 if block else index <= 0.5
            value = value + jnp.where(mine, received[at][row : row + size, :].astype(F32), 0.0)
        leave(block * size, (block + 1) * size, value)
    for copy in copies:
        copy.wait()


def swap(value, axis, count, d):
    return lax.ppermute(value, axis, [(i, i ^ d) for i in range(count)])


def after(value, other):
    return lax.optimization_barrier((value, other))[0]


def in_hbm(value):
    return pltpu.with_memory_space_constraint(value, pltpu.HBM)


def cost(flops, moved):
    return pl.CostEstimate(flops=flops, bytes_accessed=moved, transcendentals=0)


def shards(
    features, grad_out, w_self, w_neigh, bias, tile_dst, tile_src, tile_weight, recv_sub, recv_cluster
):
    sub_count = lax.axis_size("sub")
    cluster_count = lax.axis_size("cluster")
    peers = sub_count + cluster_count - 2
    size = tile_weight.shape[1]
    rows, width = features.shape
    own = rows // size
    slots = own + sub_count + cluster_count
    counts = (own, sub_count, cluster_count)

    wide = jax.ShapeDtypeStruct((rows, width), F32)
    narrow = jax.ShapeDtypeStruct((rows, width), BF)
    square = jax.ShapeDtypeStruct((width, width), BF)
    block = jax.ShapeDtypeStruct((size, width), BF)
    marks = jax.ShapeDtypeStruct((sub_count + cluster_count, width), F32)

    edge, rows_only = pl.pallas_call(
        edge_kernel,
        out_shape=[
            jax.ShapeDtypeStruct((BOUNDARY * size + EXTRA, width), BF),
            jax.ShapeDtypeStruct((EXTRA, width), BF),
        ],
        in_specs=[HBM] * 3,
        out_specs=[VMEM] * 2,
        scratch_shapes=[
            pltpu.VMEM(recv_sub.shape, jnp.int32),
            pltpu.VMEM(recv_cluster.shape, jnp.int32),
            pltpu.SemaphoreType.DMA((2 + CHUNKS,)),
        ],
        compiler_params=PARAMS,
        cost_estimate=cost(1024, 256 * 1024),
        name="edge",
    )(in_hbm(recv_sub), in_hbm(recv_cluster), in_hbm(features))

    def along(value, d):
        return swap(value, "cluster", cluster_count, d)

    def across(value, d):
        return swap(value, "sub", sub_count, d)

    even = list(range(2, sub_count, 2))
    direct = list(range(2, cluster_count, 2))
    relayed = list(range(3, cluster_count, 2))
    rows_at = BOUNDARY * size
    got = {0: (edge, 0, False, rows_at), sub_count: (edge, 0, False, rows_at)}
    for d in direct:
        got[sub_count + d] = (along(edge, d), 0, False, rows_at)
    for d in even:
        got[d] = (across(edge, d), 0, False, rows_at)
    got[sub_count + 1] = (along(edge, 1), 0, False, rows_at)
    dense, choice, features, w_self, w_neigh, grad_out, bias = pl.pallas_call(
        functools.partial(prepare_kernel, *counts),
        out_shape=[
            jax.ShapeDtypeStruct((rows, slots * size), BF),
            marks,
            narrow,
            square,
            square,
            narrow,
            jax.ShapeDtypeStruct(bias.shape, F32),
        ],
        in_specs=[HBM] * 10,
        out_specs=[VMEM] * 7,
        scratch_shapes=[
            pltpu.SMEM(tile_dst.shape, jnp.int32),
            pltpu.SMEM(tile_src.shape, jnp.int32),
            pltpu.SMEM(recv_sub.shape, jnp.int32),
            pltpu.SMEM(recv_cluster.shape, jnp.int32),
            pltpu.VMEM(tile_weight.shape, BF),
            pltpu.SemaphoreType.DMA((9 + CHUNKS,)),
        ],
        compiler_params=PARAMS,
        cost_estimate=cost(10**8, 6 * 1024 * 1024),
        name="prepare",
    )(
        *map(in_hbm, (tile_dst, tile_src, recv_sub, recv_cluster, tile_weight)),
        *map(in_hbm, (features, w_self, w_neigh, grad_out, bias)),
    )

    def call(kernel, out_shape, name, flops, *operands):
        return pl.pallas_call(
            kernel,
            out_shape=out_shape,
            in_specs=[VMEM] * len(operands),
            out_specs=jax.tree.map(lambda _: VMEM, out_shape),
            compiler_params=PARAMS,
            cost_estimate=cost(flops, 1024 * 1024),
            name=name,
        )(*operands)

    def unique(slots):
        arrays, at = [], {}
        for slot in slots:
            known = [i for i, array in enumerate(arrays) if array is got[slot][0]]
            at[slot] = known[0] if known else len(arrays)
            if not known:
                arrays.append(got[slot][0])
        return arrays, at

    def sum_call(kernel, out_shape, name, slots, *operands):
        arrays, at = unique(slots)
        halos = [(slot, at[slot], got[slot][1], got[slot][2]) for slot in slots]
        return pl.pallas_call(
            functools.partial(kernel, own, halos),
            out_shape=out_shape,
            in_specs=[VMEM] * (len(operands) + len(arrays)),
            out_specs=jax.tree.map(lambda _: VMEM, out_shape),
            scratch_shapes=[pltpu.VMEM((len(slots) * size, width), BF)],
            compiler_params=PARAMS,
            cost_estimate=cost(dict(first=10**9, near=10**9, late=10**10)[name], 3 * 1024 * 1024),
            name=name,
        )(*operands, *arrays)

    carried = []
    for d in relayed:
        far = got[sub_count + d - 1][0]
        far_rows = call(
            rows_kernel, jax.ShapeDtypeStruct((EXTRA, width), BF), "rows", 10**9, far
        )
        value = call(
            functools.partial(relay_kernel, sub_count, d - 1),
            block,
            "relay", 10**6, far, far_rows, got[sub_count + 1][0],
        )
        carried.append(far_rows)
        relay_value = value
        got[sub_count + d] = (along(value, 1), 0, True, None)
    first_sum, own_pre, inverse = sum_call(
        first_kernel, [wide, wide, jax.ShapeDtypeStruct((rows, size), F32)], "first", [0, sub_count, *(sub_count + d for d in direct)],
        choice, dense, features, w_self, bias,
    )
    sibling_rows = across(after(rows_only, relay_value), 1)
    trade_value = relay_value
    for name, traded in (("trade", [0, *even[-1:]]), ("trade2", even[:-1])):
        trade_value = call(
            functools.partial(trade_kernel, traded),
            jax.ShapeDtypeStruct((len(traded) * (size + EXTRA), width), BF),
            name, 10**6, *[got[d][0] for d in traded], after(sibling_rows, (choice, trade_value)),
        )
        value = across(trade_value, 1)
        for i, d in enumerate(traded):
            got[d + 1] = (value, i * size, True, len(traded) * size + i * EXTRA)
    near_sum = sum_call(
        near_kernel, wide, "near", [sub_count + 1, *even], after(choice, trade_value), dense, first_sum
    )
    dense_t = call(
        functools.partial(flip_kernel, size), jax.ShapeDtypeStruct((slots * size, rows), BF), "flip", 10**7,
        after(dense, near_sum),
    )
    if relayed:
        slots_late = [sub_count + d for d in relayed]
        near_sum = sum_call(
            near_kernel, wide, "late", slots_late, after(choice, dense_t), dense, near_sum
        )

    late = [1, even[-1] + 1, *(d + 1 for d in even[:-1])]
    late_arrays, late_at = unique(late)
    late_halos = [(slot, late_at[slot], got[slot][1], got[slot][2]) for slot in late]
    outs = pl.pallas_call(
        functools.partial(middle_kernel, *counts, late_halos, len(late_arrays), len(carried)),
        out_shape=[jax.ShapeDtypeStruct((2 * size, width), BF)] * len(even)
        + [jax.ShapeDtypeStruct((size + len(carried) * EXTRA, width), BF)]
        + [block] * (cluster_count - 1)
        + [jax.ShapeDtypeStruct((2, size, width), BF), narrow, narrow],
        in_specs=[VMEM] * (8 + len(late_arrays) + len(carried)),
        out_specs=[VMEM] * (len(even) + cluster_count + 3),
        scratch_shapes=[pltpu.VMEM((len(late) * size, width), BF)],
        compiler_params=PARAMS,
        cost_estimate=cost(2 * rows * slots * size * width, 6 * 1024 * 1024),
        name="middle",
    )(
        choice, grad_out, w_neigh, dense, dense_t, near_sum, own_pre, inverse,
        *late_arrays, *carried,
    )
    *sent, sibling, kept, spread, grad_pre = outs

    far = [(sub_count + d, along(sent[len(even) + d - 1], d)) for d in range(1, cluster_count)]
    near = [(d, across(value, d)) for d, value in zip(even, sent)]
    soon, rest = near[-1:], near[:-1]
    early = call(
        turn_kernel, jax.ShapeDtypeStruct((2 * size, width), BF), "early", 10**8,
        sibling, *[value for _, value in soon],
    )
    order = [sub_count + 1, *(sub_count + d for d in direct), *even, *(d + 1 for d in even), 1]
    arrays, at = unique(order)
    total, owner = pl.pallas_call(
        functools.partial(
            own_kernel, own, sub_count, [(slot, at[slot], got[slot][3]) for slot in order],
            len(arrays),
        ),
        out_shape=[wide, marks],
        in_specs=[VMEM] * (6 + len(arrays)),
        out_specs=[VMEM] * 2,
        compiler_params=PARAMS,
        cost_estimate=cost(10**9, 2 * 1024 * 1024),
        name="own",
    )(*arrays, after(choice, (far[-1][1], early)), w_self, dense_t, kept, spread, grad_pre)

    early = across(early, 1)
    turned = call(
        turn_kernel, jax.ShapeDtypeStruct((len(rest) * size, width), BF), "turn", 10**6,
        *[after(value, total) for _, value in rest],
    )
    turned = across(turned, 1)
    more = [*far, *near[::-1]]
    places = {slot: (0, size + i * EXTRA) for i, slot in enumerate(sub_count + d for d in relayed)}
    total = call(
        functools.partial(
            add_kernel, own, sub_count, [(slot, i, 0) for i, (slot, _) in enumerate(more)], places
        ),
        wide, "add", 10**10, owner, total, *[value for _, value in more],
    )
    parts = [(1, 0, 0), *[(d + 1, 0, size) for d, _ in soon]]
    parts += [(d + 1, 1, i * size) for i, (d, _) in enumerate(rest)]
    values = [early]
    return pl.pallas_call(
        functools.partial(final_kernel, own, parts),
        out_shape=narrow,
        in_specs=[VMEM] * (3 + len(values)),
        out_specs=HBM,
        scratch_shapes=[pltpu.VMEM((rows, width), BF), pltpu.SemaphoreType.DMA((3,))],
        compiler_params=PARAMS,
        cost_estimate=cost(rows * width * 4, 1024 * 1024),
        name="final",
    )(owner, total, *values, turned)


def solution(mesh):
    placed = (
        P(("cluster", "sub"), None),
        P(("cluster", "sub"), None),
        P(),
        P(),
        P(),
        P(("cluster", "sub")),
        P(("cluster", "sub")),
        P(("cluster", "sub"), None, None),
        P(("cluster", "sub"), None),
        P(("cluster", "sub"), None),
    )
    return jax.shard_map(
        shards, mesh=mesh, in_specs=placed, out_specs=P(("cluster", "sub"), None), check_vma=False
    )
```

```python
import functools

import jax
import jax.numpy as jnp
from jax import lax
from jax.experimental import pallas as pl
from jax.experimental.pallas import tpu as pltpu
from jax.sharding import PartitionSpec as P

BF = jnp.bfloat16
F32 = jnp.float32
BOUNDARY = 2
EXTRA = 16
CHUNKS = 4
VMEM = pl.BlockSpec(memory_space=pltpu.VMEM)
HBM = pl.BlockSpec(memory_space=pltpu.HBM)
PARAMS = pltpu.CompilerParams(vmem_limit_bytes=24 * 1024 * 1024)


def dot(left, right):
    return jnp.dot(left, right, preferred_element_type=F32)


def dot_right_transposed(left, right):
    return lax.dot_general(left, right, (((1,), (1,)), ((), ())), preferred_element_type=F32)


def gelu_slope(v):
    scale = 0.7978845608028654
    t = jnp.tanh(scale * (v + 0.044715 * v * v * v))
    return 0.5 * (1.0 + t) + (0.5 * scale) * v * (1.0 - t * t) * (1.0 + 3.0 * 0.044715 * v * v)


def edge_kernel(recv_sub, recv_cluster, features, edge, rows, sub_row, cluster_row, sems):
    count = edge.shape[0] - EXTRA
    step = count // CHUNKS
    small = [
        pltpu.make_async_copy(recv_sub, sub_row, sems.at[0]),
        pltpu.make_async_copy(recv_cluster, cluster_row, sems.at[1]),
    ]
    large = []
    for i in range(CHUNKS):
        part = slice(i * step, (i + 1) * step)
        large.append(
            pltpu.make_async_copy(features.at[part, :], edge.at[part, :], sems.at[2 + i])
        )
    for copy in small + large:
        copy.start()
    for copy in small:
        copy.wait()
    sub_count, cluster_count = sub_row.shape[1], cluster_row.shape[1]
    pad = jnp.zeros((1, edge.shape[1] - sub_count - cluster_count), F32)
    row = jnp.concatenate([sub_row[...].astype(F32), cluster_row[...].astype(F32), pad], axis=1)
    value = jnp.broadcast_to(row, rows.shape).astype(BF)
    edge[count:, :] = value
    rows[...] = value
    for copy in large:
        copy.wait()


def prepare_kernel(
    own, sub_count, cluster_count,
    tile_dst_hbm, tile_src_hbm, recv_sub_hbm, recv_cluster_hbm, tile_weight_hbm,
    features_hbm, w_self_hbm, w_neigh_hbm, grad_out_hbm, bias_hbm,
    dense, choice, features, w_self, w_neigh, grad_out, bias,
    tile_dst, tile_src, recv_sub, recv_cluster, tile_weight, sems,
):
    size = tile_weight.shape[1]
    step = tile_weight.shape[0] // CHUNKS
    pairs = (
        (tile_dst_hbm, tile_dst), (tile_src_hbm, tile_src), (recv_sub_hbm, recv_sub),
        (recv_cluster_hbm, recv_cluster),
        *(
            (tile_weight_hbm.at[i * step : (i + 1) * step], tile_weight.at[i * step : (i + 1) * step])
            for i in range(CHUNKS)
        ),
        (features_hbm, features), (w_self_hbm, w_self), (w_neigh_hbm, w_neigh),
        (grad_out_hbm, grad_out), (bias_hbm, bias),
    )
    copies = [pltpu.make_async_copy(a, b, sems.at[i]) for i, (a, b) in enumerate(pairs)]
    for copy in copies:
        copy.start()
    sub_id = lax.axis_index("sub")
    cluster_id = lax.axis_index("cluster")
    dense[...] = jnp.zeros_like(dense)
    for copy in copies[: 4 + CHUNKS]:
        copy.wait()

    def place(t, carry):
        src = tile_src[t]
        from_sub = own + ((src - own) ^ sub_id)
        from_cluster = own + sub_count + ((src - own - sub_count) ^ cluster_id)
        slot = jnp.where(src < own, src, jnp.where(src < own + sub_count, from_sub, from_cluster))
        dst = pl.ds(pl.multiple_of(tile_dst[t] * size, size), size)
        col = pl.ds(pl.multiple_of(slot * size, size), size)
        dense[dst, col] = dense[dst, col] + tile_weight[t]
        return carry

    lax.fori_loop(0, tile_weight.shape[0], place, 0, unroll=4)
    for d in range(sub_count):
        index = recv_sub[0, sub_id ^ d].astype(F32)
        choice[d : d + 1, :] = jnp.full((1, choice.shape[1]), index, F32)
    for d in range(cluster_count):
        index = recv_cluster[0, cluster_id ^ d].astype(F32)
        choice[sub_count + d : sub_count + d + 1, :] = jnp.full((1, choice.shape[1]), index, F32)
    for copy in copies[4 + CHUNKS :]:
        copy.wait()


def index_row(message, size):
    return message[2 * size : 2 * size + EXTRA, :].astype(F32)[0:1, :]


def lane_of(row, lane):
    lanes = lax.broadcasted_iota(jnp.int32, row.shape, 1)
    return jnp.sum(jnp.where(lanes == lane, row, 0.0), axis=1, keepdims=True)


def pick(message, index, size):
    return jnp.where(
        index > 0.5, message[size : 2 * size, :].astype(F32), message[0:size, :].astype(F32)
    ).astype(BF)


def rows_kernel(message, out):
    out[...] = message[message.shape[0] - EXTRA :, :]


def relay_kernel(sub_count, d, far, rows, near, out):
    size = out.shape[0]
    index = lane_of(index_row(near, size), sub_count + (lax.axis_index("cluster") ^ d))
    out[...] = pick(far, index, size)


def trade_kernel(even, *rest):
    messages, (sibling, out) = rest[:-2], rest[-2:]
    size = out.shape[0] // len(even) - EXTRA
    row = sibling[...].astype(F32)[0:1, :]
    for i, (d, message) in enumerate(zip(even, messages)):
        index = lane_of(row, lax.axis_index("sub") ^ d)
        out[i * size : (i + 1) * size, :] = pick(message, index, size)
        at = len(even) * size + i * EXTRA
        out[at : at + EXTRA, :] = message[2 * size :, :]


def turn_kernel(*rest):
    messages, out = rest[:-1], rest[-1]
    size = out.shape[0] // len(messages)
    for i, message in enumerate(messages):
        last = message.shape[0]
        out[i * size : (i + 1) * size, :] = message[last - size : last, :]


def halo_sum(choice, dense, own, halos, refs, halo):
    size = dense.shape[0] // own
    columns = []
    for i, (slot, at, row, picked) in enumerate(halos):
        if picked:
            block = refs[at][row : row + size, :]
        else:
            block = pick(refs[at], choice[slot : slot + 1, :], size)
        halo[i * size : (i + 1) * size, :] = block
        columns.append(dense[:, (own + slot) * size : (own + slot + 1) * size])
    return dot(jnp.concatenate(columns, axis=1), halo[...])


def flip_kernel(size, dense, dense_t):
    for at in range(0, dense.shape[1], size):
        dense_t[at : at + size, :] = dense[:, at : at + size].T


def first_kernel(own, halos, choice, dense, features, w_self, bias, *rest):
    refs, (total, own_pre, inverse, halo) = rest[:-4], rest[-4:]
    size = dense.shape[0] // own
    count = dense[:, 0:size].astype(F32)
    for at in range(size, dense.shape[1], size):
        count = count + dense[:, at : at + size].astype(F32)
    degree = jnp.sum(count, axis=1, keepdims=True)
    inverse[...] = jnp.broadcast_to(1.0 / (degree + 1.0), inverse.shape)
    total[...] = dot(dense[:, 0 : own * size], features[...]) + halo_sum(
        choice, dense, own, halos, refs, halo
    )
    own_pre[...] = dot(features[...], w_self[...]) + bias[...].reshape(1, -1)


def near_kernel(own, halos, choice, dense, before, *rest):
    refs, (total, halo) = rest[:-2], rest[-2:]
    total[...] = before[...] + halo_sum(choice, dense, own, halos, refs, halo)


def middle_kernel(
    own, sub_count, cluster_count, halos, received, carried,
    choice, grad_out, w_neigh, dense, dense_t, before, own_pre, inverse,
    *rest,
):
    refs, rest = rest[:received], rest[received:]
    rows, rest = rest[:carried], rest[carried:]
    pairs, rest = rest[: sub_count // 2 - 1], rest[sub_count // 2 - 1 :]
    along, (sibling, kept, spread, grad_pre, halo) = rest[:-5], rest[-5:]
    size = dense.shape[0] // own
    aggregate = before[...] + halo_sum(choice, dense, own, halos, refs, halo)
    inv = jnp.concatenate([inverse[...]] * (grad_out.shape[1] // size), axis=1)
    mean = (aggregate * inv).astype(BF)
    pre = own_pre[...] + dot(mean, w_neigh[...])
    grad = (grad_out[...].astype(F32) * gelu_slope(pre)).astype(BF)
    grad_pre[...] = grad
    spread[...] = (dot_right_transposed(grad, w_neigh[...]) * inv).astype(BF)

    def partial(slot, count=1):
        rows = slice((own + slot) * size, (own + slot + count) * size)
        return dot(dense_t[rows, :], spread[...]).astype(BF)

    for i, target in enumerate(pairs):
        target[...] = partial(2 * (i + 1), 2)
    for i, target in enumerate(along):
        target[0:size, :] = partial(sub_count + 1 + i)
    for i, value in enumerate(rows):
        along[0][size + i * EXTRA : size + (i + 1) * EXTRA, :] = value[...]
    sibling[...] = partial(1)
    kept[0] = partial(0)
    kept[1] = partial(sub_count)


def split(total, value, second, size):
    zero = jnp.zeros_like(value)
    total[0:size, :] = total[0:size, :] + jnp.where(second, zero, value)
    total[size : 2 * size, :] = total[size : 2 * size, :] + jnp.where(second, value, zero)


def own_kernel(own, sub_count, rows, received, *rest):
    messages, rest = rest[:received], rest[received:]
    choice, w_self, dense_t, kept, spread, grad_pre, total, owner = rest
    size = kept.shape[1]
    width = total.shape[1]
    total[...] = dot_right_transposed(grad_pre[...], w_self[...]) + dot(
        dense_t[0 : own * size, :], spread[...]
    )
    for i, slot in enumerate((0, sub_count)):
        split(total, kept[i].astype(F32), choice[slot : slot + 1, :] > 0.5, size)
    for slot, at, row in rows:
        lane = lax.axis_index("sub")
        if slot > sub_count:
            lane = sub_count + lax.axis_index("cluster")
        index = lane_of(messages[at][row : row + EXTRA, :].astype(F32)[0:1, :], lane)
        owner[slot : slot + 1, :] = jnp.broadcast_to(index, (1, width))


def add_kernel(own, sub_count, parts, rows, owner, before, *rest):
    received, total = rest[:-1], rest[-1]
    size = total.shape[0] // own
    total[...] = before[...]
    for slot, at, row in parts:
        value = received[at][row : row + size, :].astype(F32)
        index = owner[slot : slot + 1, :]
        if slot in rows:
            where, first = rows[slot]
            indices = received[where][first : first + EXTRA, :].astype(F32)[0:1, :]
            index = lane_of(indices, sub_count + lax.axis_index("cluster"))
        split(total, value, index > 0.5, size)


def final_kernel(own, parts, owner, total, *rest):
    received, (out, done, sems) = rest[:-3], rest[-3:]
    size = total.shape[0] // own
    copies = []

    def leave(first, last, value):
        done[first:last, :] = value.astype(BF)
        copies.append(
            pltpu.make_async_copy(
                done.at[first:last, :], out.at[first:last, :], sems.at[len(copies)]
            )
        )
        copies[-1].start()

    leave(2 * size, own * size, total[2 * size :, :])
    for block in range(2):
        value = total[block * size : (block + 1) * size, :]
        for slot, at, row in parts:
            index = owner[slot : slot + 1, :]
            mine = index > 0.5 if block else index <= 0.5
            value = value + jnp.where(mine, received[at][row : row + size, :].astype(F32), 0.0)
        leave(block * size, (block + 1) * size, value)
    for copy in copies:
        copy.wait()


def swap(value, axis, count, d):
    return lax.ppermute(value, axis, [(i, i ^ d) for i in range(count)])


def after(value, other):
    return lax.optimization_barrier((value, other))[0]


def in_hbm(value):
    return pltpu.with_memory_space_constraint(value, pltpu.HBM)


def cost(flops, moved):
    return pl.CostEstimate(flops=flops, bytes_accessed=moved, transcendentals=0)


def shards(
    features, grad_out, w_self, w_neigh, bias, tile_dst, tile_src, tile_weight, recv_sub, recv_cluster
):
    sub_count = lax.axis_size("sub")
    cluster_count = lax.axis_size("cluster")
    peers = sub_count + cluster_count - 2
    size = tile_weight.shape[1]
    rows, width = features.shape
    own = rows // size
    slots = own + sub_count + cluster_count
    counts = (own, sub_count, cluster_count)

    wide = jax.ShapeDtypeStruct((rows, width), F32)
    narrow = jax.ShapeDtypeStruct((rows, width), BF)
    square = jax.ShapeDtypeStruct((width, width), BF)
    block = jax.ShapeDtypeStruct((size, width), BF)
    marks = jax.ShapeDtypeStruct((sub_count + cluster_count, width), F32)

    edge, rows_only = pl.pallas_call(
        edge_kernel,
        out_shape=[
            jax.ShapeDtypeStruct((BOUNDARY * size + EXTRA, width), BF),
            jax.ShapeDtypeStruct((EXTRA, width), BF),
        ],
        in_specs=[HBM] * 3,
        out_specs=[VMEM] * 2,
        scratch_shapes=[
            pltpu.VMEM(recv_sub.shape, jnp.int32),
            pltpu.VMEM(recv_cluster.shape, jnp.int32),
            pltpu.SemaphoreType.DMA((2 + CHUNKS,)),
        ],
        compiler_params=PARAMS,
        cost_estimate=cost(1024, 256 * 1024),
        name="edge",
    )(in_hbm(recv_sub), in_hbm(recv_cluster), in_hbm(features))

    def along(value, d):
        return swap(value, "cluster", cluster_count, d)

    def across(value, d):
        return swap(value, "sub", sub_count, d)

    even = list(range(2, sub_count, 2))
    direct = list(range(2, cluster_count, 2))
    relayed = list(range(3, cluster_count, 2))
    rows_at = BOUNDARY * size
    got = {0: (edge, 0, False, rows_at), sub_count: (edge, 0, False, rows_at)}
    for d in direct:
        got[sub_count + d] = (along(edge, d), 0, False, rows_at)
    for d in even:
        got[d] = (across(edge, d), 0, False, rows_at)
    got[sub_count + 1] = (along(edge, 1), 0, False, rows_at)
    dense, choice, features, w_self, w_neigh, grad_out, bias = pl.pallas_call(
        functools.partial(prepare_kernel, *counts),
        out_shape=[
            jax.ShapeDtypeStruct((rows, slots * size), BF),
            marks,
            narrow,
            square,
            square,
            narrow,
            jax.ShapeDtypeStruct(bias.shape, F32),
        ],
        in_specs=[HBM] * 10,
        out_specs=[VMEM] * 7,
        scratch_shapes=[
            pltpu.SMEM(tile_dst.shape, jnp.int32),
            pltpu.SMEM(tile_src.shape, jnp.int32),
            pltpu.SMEM(recv_sub.shape, jnp.int32),
            pltpu.SMEM(recv_cluster.shape, jnp.int32),
            pltpu.VMEM(tile_weight.shape, BF),
            pltpu.SemaphoreType.DMA((9 + CHUNKS,)),
        ],
        compiler_params=PARAMS,
        cost_estimate=cost(10**8, 6 * 1024 * 1024),
        name="prepare",
    )(
        *map(in_hbm, (tile_dst, tile_src, recv_sub, recv_cluster, tile_weight)),
        *map(in_hbm, (features, w_self, w_neigh, grad_out, bias)),
    )

    def call(kernel, out_shape, name, flops, *operands):
        return pl.pallas_call(
            kernel,
            out_shape=out_shape,
            in_specs=[VMEM] * len(operands),
            out_specs=jax.tree.map(lambda _: VMEM, out_shape),
            compiler_params=PARAMS,
            cost_estimate=cost(flops, 1024 * 1024),
            name=name,
        )(*operands)

    def unique(slots):
        arrays, at = [], {}
        for slot in slots:
            known = [i for i, array in enumerate(arrays) if array is got[slot][0]]
            at[slot] = known[0] if known else len(arrays)
            if not known:
                arrays.append(got[slot][0])
        return arrays, at

    def sum_call(kernel, out_shape, name, slots, *operands):
        arrays, at = unique(slots)
        halos = [(slot, at[slot], got[slot][1], got[slot][2]) for slot in slots]
        return pl.pallas_call(
            functools.partial(kernel, own, halos),
            out_shape=out_shape,
            in_specs=[VMEM] * (len(operands) + len(arrays)),
            out_specs=jax.tree.map(lambda _: VMEM, out_shape),
            scratch_shapes=[pltpu.VMEM((len(slots) * size, width), BF)],
            compiler_params=PARAMS,
            cost_estimate=cost(dict(first=10**9, near=10**9, late=10**10)[name], 3 * 1024 * 1024),
            name=name,
        )(*operands, *arrays)

    dense_t = call(
        functools.partial(flip_kernel, size), jax.ShapeDtypeStruct((slots * size, rows), BF), "flip", 10**7,
        after(dense, choice),
    )
    carried = []
    for d in relayed:
        far = got[sub_count + d - 1][0]
        far_rows = call(
            rows_kernel, jax.ShapeDtypeStruct((EXTRA, width), BF), "rows", 10**9, far
        )
        value = call(
            functools.partial(relay_kernel, sub_count, d - 1),
            block,
            "relay", 10**6, far, far_rows, after(got[sub_count + 1][0], dense_t),
        )
        carried.append(far_rows)
        relay_value = value
        got[sub_count + d] = (along(value, 1), 0, True, None)
    first_sum, own_pre, inverse = sum_call(
        first_kernel, [wide, wide, jax.ShapeDtypeStruct((rows, size), F32)], "first", [0, sub_count, *(sub_count + d for d in direct)],
        choice, dense, features, w_self, bias,
    )
    sibling_rows = across(after(rows_only, relay_value), 1)
    trade_value = relay_value
    for name, traded in (("trade", [0, *even[-1:]]), ("trade2", even[:-1])):
        trade_value = call(
            functools.partial(trade_kernel, traded),
            jax.ShapeDtypeStruct((len(traded) * (size + EXTRA), width), BF),
            name, 10**6 if name == 'trade' else 10**10, *[got[d][0] for d in traded], after(sibling_rows, (choice, trade_value)),
        )
        value = across(trade_value, 1)
        for i, d in enumerate(traded):
            got[d + 1] = (value, i * size, True, len(traded) * size + i * EXTRA)
    near_sum = sum_call(
        near_kernel, wide, "near", [sub_count + 1, *even], after(choice, trade_value), dense, first_sum
    )
    if relayed:
        slots_late = [*(sub_count + d for d in relayed), 1, even[-1] + 1]
        near_sum = sum_call(
            near_kernel, wide, "late", slots_late, choice, dense, near_sum
        )

    late = [d + 1 for d in even[:-1]]
    late_arrays, late_at = unique(late)
    late_halos = [(slot, late_at[slot], got[slot][1], got[slot][2]) for slot in late]
    outs = pl.pallas_call(
        functools.partial(middle_kernel, *counts, late_halos, len(late_arrays), len(carried)),
        out_shape=[jax.ShapeDtypeStruct((2 * size, width), BF)] * len(even)
        + [jax.ShapeDtypeStruct((size + len(carried) * EXTRA, width), BF)]
        + [block] * (cluster_count - 1)
        + [jax.ShapeDtypeStruct((2, size, width), BF), narrow, narrow],
        in_specs=[VMEM] * (8 + len(late_arrays) + len(carried)),
        out_specs=[VMEM] * (len(even) + cluster_count + 3),
        scratch_shapes=[pltpu.VMEM((len(late) * size, width), BF)],
        compiler_params=PARAMS,
        cost_estimate=cost(2 * rows * slots * size * width, 6 * 1024 * 1024),
        name="middle",
    )(
        choice, grad_out, w_neigh, dense, dense_t, near_sum, own_pre, inverse,
        *late_arrays, *carried,
    )
    *sent, sibling, kept, spread, grad_pre = outs

    far = [(sub_count + d, along(sent[len(even) + d - 1], d)) for d in range(1, cluster_count)]
    near = [(d, across(value, d)) for d, value in zip(even, sent)]
    soon, rest = near[-1:], near[:-1]
    early = call(
        turn_kernel, jax.ShapeDtypeStruct((2 * size, width), BF), "early", 10**8,
        sibling, *[value for _, value in soon],
    )
    order = [sub_count + 1, *(sub_count + d for d in direct), *even, *(d + 1 for d in even), 1]
    arrays, at = unique(order)
    total, owner = pl.pallas_call(
        functools.partial(
            own_kernel, own, sub_count, [(slot, at[slot], got[slot][3]) for slot in order],
            len(arrays),
        ),
        out_shape=[wide, marks],
        in_specs=[VMEM] * (6 + len(arrays)),
        out_specs=[VMEM] * 2,
        compiler_params=PARAMS,
        cost_estimate=cost(10**9, 2 * 1024 * 1024),
        name="own",
    )(*arrays, after(choice, (far[-1][1], early)), w_self, dense_t, kept, spread, grad_pre)

    early = across(early, 1)
    turned = call(
        turn_kernel, jax.ShapeDtypeStruct((len(rest) * size, width), BF), "turn", 10**6,
        *[after(value, total) for _, value in rest],
    )
    turned = across(turned, 1)
    more = [*far, *near[::-1]]
    places = {slot: (0, size + i * EXTRA) for i, slot in enumerate(sub_count + d for d in relayed)}
    total = call(
        functools.partial(
            add_kernel, own, sub_count, [(slot, i, 0) for i, (slot, _) in enumerate(more)], places
        ),
        wide, "add", 10**10, owner, total, *[value for _, value in more],
    )
    parts = [(1, 0, 0), *[(d + 1, 0, size) for d, _ in soon]]
    parts += [(d + 1, 1, i * size) for i, (d, _) in enumerate(rest)]
    values = [early]
    return pl.pallas_call(
        functools.partial(final_kernel, own, parts),
        out_shape=narrow,
        in_specs=[VMEM] * (3 + len(values)),
        out_specs=HBM,
        scratch_shapes=[pltpu.VMEM((rows, width), BF), pltpu.SemaphoreType.DMA((3,))],
        compiler_params=PARAMS,
        cost_estimate=cost(rows * width * 4, 1024 * 1024),
        name="final",
    )(owner, total, *values, turned)


def solution(mesh):
    placed = (
        P(("cluster", "sub"), None),
        P(("cluster", "sub"), None),
        P(),
        P(),
        P(),
        P(("cluster", "sub")),
        P(("cluster", "sub")),
        P(("cluster", "sub"), None, None),
        P(("cluster", "sub"), None),
        P(("cluster", "sub"), None),
    )
    return jax.shard_map(
        shards, mesh=mesh, in_specs=placed, out_specs=P(("cluster", "sub"), None), check_vma=False
    )
```

```python
import functools

import jax
import jax.numpy as jnp
from jax import lax
from jax.experimental import pallas as pl
from jax.experimental.pallas import tpu as pltpu
from jax.sharding import PartitionSpec as P

BF = jnp.bfloat16
F32 = jnp.float32
BOUNDARY = 2
EXTRA = 16
CHUNKS = 4
VMEM = pl.BlockSpec(memory_space=pltpu.VMEM)
HBM = pl.BlockSpec(memory_space=pltpu.HBM)
PARAMS = pltpu.CompilerParams(vmem_limit_bytes=24 * 1024 * 1024)


def dot(left, right):
    return jnp.dot(left, right, preferred_element_type=F32)


def dot_right_transposed(left, right):
    return lax.dot_general(left, right, (((1,), (1,)), ((), ())), preferred_element_type=F32)


def gelu_slope(v):
    scale = 0.7978845608028654
    t = jnp.tanh(scale * (v + 0.044715 * v * v * v))
    return 0.5 * (1.0 + t) + (0.5 * scale) * v * (1.0 - t * t) * (1.0 + 3.0 * 0.044715 * v * v)


def edge_kernel(recv_sub, recv_cluster, features, edge, rows, sub_row, cluster_row, sems):
    count = edge.shape[0] - EXTRA
    step = count // CHUNKS
    small = [
        pltpu.make_async_copy(recv_sub, sub_row, sems.at[0]),
        pltpu.make_async_copy(recv_cluster, cluster_row, sems.at[1]),
    ]
    large = []
    for i in range(CHUNKS):
        part = slice(i * step, (i + 1) * step)
        large.append(
            pltpu.make_async_copy(features.at[part, :], edge.at[part, :], sems.at[2 + i])
        )
    for copy in small + large:
        copy.start()
    for copy in small:
        copy.wait()
    sub_count, cluster_count = sub_row.shape[1], cluster_row.shape[1]
    pad = jnp.zeros((1, edge.shape[1] - sub_count - cluster_count), F32)
    row = jnp.concatenate([sub_row[...].astype(F32), cluster_row[...].astype(F32), pad], axis=1)
    value = jnp.broadcast_to(row, rows.shape).astype(BF)
    edge[count:, :] = value
    rows[...] = value
    for copy in large:
        copy.wait()


def prepare_kernel(
    own, sub_count, cluster_count,
    tile_dst_hbm, tile_src_hbm, recv_sub_hbm, recv_cluster_hbm, tile_weight_hbm,
    features_hbm, w_self_hbm, w_neigh_hbm, grad_out_hbm, bias_hbm,
    dense, choice, features, w_self, w_neigh, grad_out, bias,
    tile_dst, tile_src, recv_sub, recv_cluster, tile_weight, sems,
):
    size = tile_weight.shape[1]
    step = tile_weight.shape[0] // CHUNKS
    pairs = (
        (tile_dst_hbm, tile_dst), (tile_src_hbm, tile_src), (recv_sub_hbm, recv_sub),
        (recv_cluster_hbm, recv_cluster),
        *(
            (tile_weight_hbm.at[i * step : (i + 1) * step], tile_weight.at[i * step : (i + 1) * step])
            for i in range(CHUNKS)
        ),
        (features_hbm, features), (w_self_hbm, w_self), (w_neigh_hbm, w_neigh),
        (grad_out_hbm, grad_out), (bias_hbm, bias),
    )
    copies = [pltpu.make_async_copy(a, b, sems.at[i]) for i, (a, b) in enumerate(pairs)]
    for copy in copies:
        copy.start()
    sub_id = lax.axis_index("sub")
    cluster_id = lax.axis_index("cluster")
    dense[...] = jnp.zeros_like(dense)
    for copy in copies[: 4 + CHUNKS]:
        copy.wait()

    def place(t, carry):
        src = tile_src[t]
        from_sub = own + ((src - own) ^ sub_id)
        from_cluster = own + sub_count + ((src - own - sub_count) ^ cluster_id)
        slot = jnp.where(src < own, src, jnp.where(src < own + sub_count, from_sub, from_cluster))
        dst = pl.ds(pl.multiple_of(tile_dst[t] * size, size), size)
        col = pl.ds(pl.multiple_of(slot * size, size), size)
        dense[dst, col] = dense[dst, col] + tile_weight[t]
        return carry

    lax.fori_loop(0, tile_weight.shape[0], place, 0, unroll=4)
    for d in range(sub_count):
        index = recv_sub[0, sub_id ^ d].astype(F32)
        choice[d : d + 1, :] = jnp.full((1, choice.shape[1]), index, F32)
    for d in range(cluster_count):
        index = recv_cluster[0, cluster_id ^ d].astype(F32)
        choice[sub_count + d : sub_count + d + 1, :] = jnp.full((1, choice.shape[1]), index, F32)
    for copy in copies[4 + CHUNKS :]:
        copy.wait()


def index_row(message, size):
    return message[2 * size : 2 * size + EXTRA, :].astype(F32)[0:1, :]


def lane_of(row, lane):
    lanes = lax.broadcasted_iota(jnp.int32, row.shape, 1)
    return jnp.sum(jnp.where(lanes == lane, row, 0.0), axis=1, keepdims=True)


def pick(message, index, size):
    return jnp.where(
        index > 0.5, message[size : 2 * size, :].astype(F32), message[0:size, :].astype(F32)
    ).astype(BF)


def rows_kernel(message, out):
    out[...] = message[message.shape[0] - EXTRA :, :]


def relay_kernel(sub_count, d, far, rows, near, out):
    size = out.shape[0]
    index = lane_of(index_row(near, size), sub_count + (lax.axis_index("cluster") ^ d))
    out[...] = pick(far, index, size)


def trade_kernel(even, *rest):
    messages, (sibling, out) = rest[:-2], rest[-2:]
    size = out.shape[0] // len(even) - EXTRA
    row = sibling[...].astype(F32)[0:1, :]
    for i, (d, message) in enumerate(zip(even, messages)):
        index = lane_of(row, lax.axis_index("sub") ^ d)
        out[i * size : (i + 1) * size, :] = pick(message, index, size)
        at = len(even) * size + i * EXTRA
        out[at : at + EXTRA, :] = message[2 * size :, :]


def turn_kernel(*rest):
    messages, out = rest[:-1], rest[-1]
    size = out.shape[0] // len(messages)
    for i, message in enumerate(messages):
        last = message.shape[0]
        out[i * size : (i + 1) * size, :] = message[last - size : last, :]


def halo_sum(choice, dense, own, halos, refs, halo):
    size = dense.shape[0] // own
    columns = []
    for i, (slot, at, row, picked) in enumerate(halos):
        if picked:
            block = refs[at][row : row + size, :]
        else:
            block = pick(refs[at], choice[slot : slot + 1, :], size)
        halo[i * size : (i + 1) * size, :] = block
        columns.append(dense[:, (own + slot) * size : (own + slot + 1) * size])
    return dot(jnp.concatenate(columns, axis=1), halo[...])


def flip_kernel(size, dense, dense_t):
    for at in range(0, dense.shape[1], size):
        dense_t[at : at + size, :] = dense[:, at : at + size].T


def first_kernel(own, halos, choice, dense, features, w_self, bias, *rest):
    refs, (total, own_pre, inverse, halo) = rest[:-4], rest[-4:]
    size = dense.shape[0] // own
    count = dense[:, 0:size].astype(F32)
    for at in range(size, dense.shape[1], size):
        count = count + dense[:, at : at + size].astype(F32)
    degree = jnp.sum(count, axis=1, keepdims=True)
    inverse[...] = jnp.broadcast_to(1.0 / (degree + 1.0), inverse.shape)
    total[...] = dot(dense[:, 0 : own * size], features[...]) + halo_sum(
        choice, dense, own, halos, refs, halo
    )
    own_pre[...] = dot(features[...], w_self[...]) + bias[...].reshape(1, -1)


def near_kernel(own, halos, choice, dense, before, *rest):
    refs, (total, halo) = rest[:-2], rest[-2:]
    total[...] = before[...] + halo_sum(choice, dense, own, halos, refs, halo)


def middle_kernel(
    own, sub_count, cluster_count, halos, received, carried,
    choice, grad_out, w_neigh, dense, dense_t, before, own_pre, inverse,
    *rest,
):
    refs, rest = rest[:received], rest[received:]
    rows, rest = rest[:carried], rest[carried:]
    pairs, rest = rest[: sub_count // 2 - 1], rest[sub_count // 2 - 1 :]
    along, (sibling, kept, spread, grad_pre, halo) = rest[:-5], rest[-5:]
    size = dense.shape[0] // own
    aggregate = before[...] + halo_sum(choice, dense, own, halos, refs, halo)
    inv = jnp.concatenate([inverse[...]] * (grad_out.shape[1] // size), axis=1)
    mean = (aggregate * inv).astype(BF)
    pre = own_pre[...] + dot(mean, w_neigh[...])
    grad = (grad_out[...].astype(F32) * gelu_slope(pre)).astype(BF)
    grad_pre[...] = grad
    spread[...] = (dot_right_transposed(grad, w_neigh[...]) * inv).astype(BF)

    def partial(slot, count=1):
        rows = slice((own + slot) * size, (own + slot + count) * size)
        return dot(dense_t[rows, :], spread[...]).astype(BF)

    for i, target in enumerate(pairs):
        target[...] = partial(2 * (i + 1), 2)
    for i, target in enumerate(along):
        target[0:size, :] = partial(sub_count + 1 + i)
    for i, value in enumerate(rows):
        along[0][size + i * EXTRA : size + (i + 1) * EXTRA, :] = value[...]
    sibling[...] = partial(1)
    kept[0] = partial(0)
    kept[1] = partial(sub_count)


def split(total, value, second, size):
    zero = jnp.zeros_like(value)
    total[0:size, :] = total[0:size, :] + jnp.where(second, zero, value)
    total[size : 2 * size, :] = total[size : 2 * size, :] + jnp.where(second, value, zero)


def own_kernel(own, sub_count, rows, received, *rest):
    messages, rest = rest[:received], rest[received:]
    choice, w_self, dense_t, kept, spread, grad_pre, total, owner = rest
    size = kept.shape[1]
    width = total.shape[1]
    total[...] = dot_right_transposed(grad_pre[...], w_self[...]) + dot(
        dense_t[0 : own * size, :], spread[...]
    )
    for i, slot in enumerate((0, sub_count)):
        split(total, kept[i].astype(F32), choice[slot : slot + 1, :] > 0.5, size)
    for slot, at, row in rows:
        lane = lax.axis_index("sub")
        if slot > sub_count:
            lane = sub_count + lax.axis_index("cluster")
        index = lane_of(messages[at][row : row + EXTRA, :].astype(F32)[0:1, :], lane)
        owner[slot : slot + 1, :] = jnp.broadcast_to(index, (1, width))


def add_kernel(own, sub_count, parts, rows, owner, before, *rest):
    received, total = rest[:-1], rest[-1]
    size = total.shape[0] // own
    total[...] = before[...]
    for slot, at, row in parts:
        value = received[at][row : row + size, :].astype(F32)
        index = owner[slot : slot + 1, :]
        if slot in rows:
            where, first = rows[slot]
            indices = received[where][first : first + EXTRA, :].astype(F32)[0:1, :]
            index = lane_of(indices, sub_count + lax.axis_index("cluster"))
        split(total, value, index > 0.5, size)


def final_kernel(own, parts, owner, total, *rest):
    received, (out, done, sems) = rest[:-3], rest[-3:]
    size = total.shape[0] // own
    copies = []

    def leave(first, last, value):
        done[first:last, :] = value.astype(BF)
        copies.append(
            pltpu.make_async_copy(
                done.at[first:last, :], out.at[first:last, :], sems.at[len(copies)]
            )
        )
        copies[-1].start()

    leave(2 * size, own * size, total[2 * size :, :])
    for block in range(2):
        value = total[block * size : (block + 1) * size, :]
        for slot, at, row in parts:
            index = owner[slot : slot + 1, :]
            mine = index > 0.5 if block else index <= 0.5
            value = value + jnp.where(mine, received[at][row : row + size, :].astype(F32), 0.0)
        leave(block * size, (block + 1) * size, value)
    for copy in copies:
        copy.wait()


def swap(value, axis, count, d):
    return lax.ppermute(value, axis, [(i, i ^ d) for i in range(count)])


def after(value, other):
    return lax.optimization_barrier((value, other))[0]


def in_hbm(value):
    return pltpu.with_memory_space_constraint(value, pltpu.HBM)


def cost(flops, moved):
    return pl.CostEstimate(flops=flops, bytes_accessed=moved, transcendentals=0)


def shards(
    features, grad_out, w_self, w_neigh, bias, tile_dst, tile_src, tile_weight, recv_sub, recv_cluster
):
    sub_count = lax.axis_size("sub")
    cluster_count = lax.axis_size("cluster")
    peers = sub_count + cluster_count - 2
    size = tile_weight.shape[1]
    rows, width = features.shape
    own = rows // size
    slots = own + sub_count + cluster_count
    counts = (own, sub_count, cluster_count)

    wide = jax.ShapeDtypeStruct((rows, width), F32)
    narrow = jax.ShapeDtypeStruct((rows, width), BF)
    square = jax.ShapeDtypeStruct((width, width), BF)
    block = jax.ShapeDtypeStruct((size, width), BF)
    marks = jax.ShapeDtypeStruct((sub_count + cluster_count, width), F32)

    edge, rows_only = pl.pallas_call(
        edge_kernel,
        out_shape=[
            jax.ShapeDtypeStruct((BOUNDARY * size + EXTRA, width), BF),
            jax.ShapeDtypeStruct((EXTRA, width), BF),
        ],
        in_specs=[HBM] * 3,
        out_specs=[VMEM] * 2,
        scratch_shapes=[
            pltpu.VMEM(recv_sub.shape, jnp.int32),
            pltpu.VMEM(recv_cluster.shape, jnp.int32),
            pltpu.SemaphoreType.DMA((2 + CHUNKS,)),
        ],
        compiler_params=PARAMS,
        cost_estimate=cost(1024, 256 * 1024),
        name="edge",
    )(in_hbm(recv_sub), in_hbm(recv_cluster), in_hbm(features))

    def along(value, d):
        return swap(value, "cluster", cluster_count, d)

    def across(value, d):
        return swap(value, "sub", sub_count, d)

    even = list(range(2, sub_count, 2))
    direct = list(range(2, cluster_count, 2))
    relayed = list(range(3, cluster_count, 2))
    rows_at = BOUNDARY * size
    got = {0: (edge, 0, False, rows_at), sub_count: (edge, 0, False, rows_at)}
    for d in direct:
        got[sub_count + d] = (along(edge, d), 0, False, rows_at)
    for d in even:
        got[d] = (across(edge, d), 0, False, rows_at)
    got[sub_count + 1] = (along(edge, 1), 0, False, rows_at)
    dense, choice, features, w_self, w_neigh, grad_out, bias = pl.pallas_call(
        functools.partial(prepare_kernel, *counts),
        out_shape=[
            jax.ShapeDtypeStruct((rows, slots * size), BF),
            marks,
            narrow,
            square,
            square,
            narrow,
            jax.ShapeDtypeStruct(bias.shape, F32),
        ],
        in_specs=[HBM] * 10,
        out_specs=[VMEM] * 7,
        scratch_shapes=[
            pltpu.SMEM(tile_dst.shape, jnp.int32),
            pltpu.SMEM(tile_src.shape, jnp.int32),
            pltpu.SMEM(recv_sub.shape, jnp.int32),
            pltpu.SMEM(recv_cluster.shape, jnp.int32),
            pltpu.VMEM(tile_weight.shape, BF),
            pltpu.SemaphoreType.DMA((9 + CHUNKS,)),
        ],
        compiler_params=PARAMS,
        cost_estimate=cost(10**8, 6 * 1024 * 1024),
        name="prepare",
    )(
        *map(in_hbm, (tile_dst, tile_src, recv_sub, recv_cluster, tile_weight)),
        *map(in_hbm, (features, w_self, w_neigh, grad_out, bias)),
    )

    def call(kernel, out_shape, name, flops, *operands):
        return pl.pallas_call(
            kernel,
            out_shape=out_shape,
            in_specs=[VMEM] * len(operands),
            out_specs=jax.tree.map(lambda _: VMEM, out_shape),
            compiler_params=PARAMS,
            cost_estimate=cost(flops, 1024 * 1024),
            name=name,
        )(*operands)

    def unique(slots):
        arrays, at = [], {}
        for slot in slots:
            known = [i for i, array in enumerate(arrays) if array is got[slot][0]]
            at[slot] = known[0] if known else len(arrays)
            if not known:
                arrays.append(got[slot][0])
        return arrays, at

    def sum_call(kernel, out_shape, name, slots, *operands):
        arrays, at = unique(slots)
        halos = [(slot, at[slot], got[slot][1], got[slot][2]) for slot in slots]
        return pl.pallas_call(
            functools.partial(kernel, own, halos),
            out_shape=out_shape,
            in_specs=[VMEM] * (len(operands) + len(arrays)),
            out_specs=jax.tree.map(lambda _: VMEM, out_shape),
            scratch_shapes=[pltpu.VMEM((len(slots) * size, width), BF)],
            compiler_params=PARAMS,
            cost_estimate=cost(dict(first=10**9, near=10**9, late=10**10)[name], 3 * 1024 * 1024),
            name=name,
        )(*operands, *arrays)

    dense_t = call(
        functools.partial(flip_kernel, size), jax.ShapeDtypeStruct((slots * size, rows), BF), "flip", 10**7,
        after(dense, choice),
    )
    carried = []
    for d in relayed:
        far = got[sub_count + d - 1][0]
        far_rows = call(
            rows_kernel, jax.ShapeDtypeStruct((EXTRA, width), BF), "rows", 10**9, far
        )
        value = call(
            functools.partial(relay_kernel, sub_count, d - 1),
            block,
            "relay", 10**6, far, far_rows, after(got[sub_count + 1][0], dense_t),
        )
        carried.append(far_rows)
        got[sub_count + d] = (along(value, 1), 0, True, None)
    first_sum, own_pre, inverse = sum_call(
        first_kernel, [wide, wide, jax.ShapeDtypeStruct((rows, size), F32)], "first", [0, sub_count, *(sub_count + d for d in direct)],
        choice, dense, features, w_self, bias,
    )
    traded = [0, *even]
    sibling_rows = across(after(rows_only, value), 1)
    value = call(
        functools.partial(trade_kernel, traded),
        jax.ShapeDtypeStruct((len(traded) * (size + EXTRA), width), BF),
        "trade", 10**6, *[got[d][0] for d in traded], after(sibling_rows, (choice, value)),
    )
    trade_value = value
    value = across(value, 1)
    for i, d in enumerate(traded):
        got[d + 1] = (value, i * size, True, len(traded) * size + i * EXTRA)
    near_sum = sum_call(
        near_kernel, wide, "near", [sub_count + 1, *even], after(choice, trade_value), dense, first_sum
    )
    if relayed:
        slots_late = [sub_count + d for d in relayed]
        near_sum = sum_call(
            near_kernel, wide, "late", slots_late, choice, dense, near_sum
        )

    late = [1, *(d + 1 for d in even)]
    late_arrays, late_at = unique(late)
    late_halos = [(slot, late_at[slot], got[slot][1], got[slot][2]) for slot in late]
    outs = pl.pallas_call(
        functools.partial(middle_kernel, *counts, late_halos, len(late_arrays), len(carried)),
        out_shape=[jax.ShapeDtypeStruct((2 * size, width), BF)] * len(even)
        + [jax.ShapeDtypeStruct((size + len(carried) * EXTRA, width), BF)]
        + [block] * (cluster_count - 1)
        + [jax.ShapeDtypeStruct((2, size, width), BF), narrow, narrow],
        in_specs=[VMEM] * (8 + len(late_arrays) + len(carried)),
        out_specs=[VMEM] * (len(even) + cluster_count + 3),
        scratch_shapes=[pltpu.VMEM((len(late) * size, width), BF)],
        compiler_params=PARAMS,
        cost_estimate=cost(2 * rows * slots * size * width, 6 * 1024 * 1024),
        name="middle",
    )(
        choice, grad_out, w_neigh, dense, dense_t, near_sum, own_pre, inverse,
        *late_arrays, *carried,
    )
    *sent, sibling, kept, spread, grad_pre = outs

    far = [(sub_count + d, along(sent[len(even) + d - 1], d)) for d in range(1, cluster_count)]
    near = [(d, across(value, d)) for d, value in zip(even, sent)]
    soon, rest = near[-1:], near[:-1]
    early = call(
        turn_kernel, jax.ShapeDtypeStruct((2 * size, width), BF), "early", 10**8,
        after(sibling, far[0][1]), *[value for _, value in soon],
    )
    order = [sub_count + 1, *(sub_count + d for d in direct), *even, *(d + 1 for d in even), 1]
    arrays, at = unique(order)
    total, owner = pl.pallas_call(
        functools.partial(
            own_kernel, own, sub_count, [(slot, at[slot], got[slot][3]) for slot in order],
            len(arrays),
        ),
        out_shape=[wide, marks],
        in_specs=[VMEM] * (6 + len(arrays)),
        out_specs=[VMEM] * 2,
        compiler_params=PARAMS,
        cost_estimate=cost(10**9, 2 * 1024 * 1024),
        name="own",
    )(*arrays, after(choice, (far[-1][1], early)), w_self, dense_t, kept, spread, grad_pre)

    early = across(early, 1)
    turned = call(
        turn_kernel, jax.ShapeDtypeStruct((len(rest) * size, width), BF), "turn", 10**6,
        *[after(value, total) for _, value in rest],
    )
    turned = across(turned, 1)
    more = [*far, *near[::-1]]
    places = {slot: (0, size + i * EXTRA) for i, slot in enumerate(sub_count + d for d in relayed)}
    total = call(
        functools.partial(
            add_kernel, own, sub_count, [(slot, i, 0) for i, (slot, _) in enumerate(more)], places
        ),
        wide, "add", 10**10, owner, total, *[value for _, value in more],
    )
    parts = [(1, 0, 0), *[(d + 1, 0, size) for d, _ in soon]]
    parts += [(d + 1, 1, i * size) for i, (d, _) in enumerate(rest)]
    values = [early]
    return pl.pallas_call(
        functools.partial(final_kernel, own, parts),
        out_shape=narrow,
        in_specs=[VMEM] * (3 + len(values)),
        out_specs=HBM,
        scratch_shapes=[pltpu.VMEM((rows, width), BF), pltpu.SemaphoreType.DMA((3,))],
        compiler_params=PARAMS,
        cost_estimate=cost(rows * width * 4, 1024 * 1024),
        name="final",
    )(owner, total, *values, turned)


def solution(mesh):
    placed = (
        P(("cluster", "sub"), None),
        P(("cluster", "sub"), None),
        P(),
        P(),
        P(),
        P(("cluster", "sub")),
        P(("cluster", "sub")),
        P(("cluster", "sub"), None, None),
        P(("cluster", "sub"), None),
        P(("cluster", "sub"), None),
    )
    return jax.shard_map(
        shards, mesh=mesh, in_specs=placed, out_specs=P(("cluster", "sub"), None), check_vma=False
    )
```

```python
import functools

import jax
import jax.numpy as jnp
from jax import lax
from jax.experimental import pallas as pl
from jax.experimental.pallas import tpu as pltpu
from jax.sharding import PartitionSpec as P

BF = jnp.bfloat16
F32 = jnp.float32
BOUNDARY = 2
EXTRA = 16
CHUNKS = 4
VMEM = pl.BlockSpec(memory_space=pltpu.VMEM)
HBM = pl.BlockSpec(memory_space=pltpu.HBM)
PARAMS = pltpu.CompilerParams(vmem_limit_bytes=24 * 1024 * 1024)


def dot(left, right):
    return jnp.dot(left, right, preferred_element_type=F32)


def dot_right_transposed(left, right):
    return lax.dot_general(left, right, (((1,), (1,)), ((), ())), preferred_element_type=F32)


def gelu_slope(v):
    scale = 0.7978845608028654
    t = jnp.tanh(scale * (v + 0.044715 * v * v * v))
    return 0.5 * (1.0 + t) + (0.5 * scale) * v * (1.0 - t * t) * (1.0 + 3.0 * 0.044715 * v * v)


def edge_kernel(recv_sub, recv_cluster, features, edge, rows, sub_row, cluster_row, sems):
    count = edge.shape[0] - EXTRA
    step = count // CHUNKS
    small = [
        pltpu.make_async_copy(recv_sub, sub_row, sems.at[0]),
        pltpu.make_async_copy(recv_cluster, cluster_row, sems.at[1]),
    ]
    large = []
    for i in range(CHUNKS):
        part = slice(i * step, (i + 1) * step)
        large.append(
            pltpu.make_async_copy(features.at[part, :], edge.at[part, :], sems.at[2 + i])
        )
    for copy in small + large:
        copy.start()
    for copy in small:
        copy.wait()
    sub_count, cluster_count = sub_row.shape[1], cluster_row.shape[1]
    pad = jnp.zeros((1, edge.shape[1] - sub_count - cluster_count), F32)
    row = jnp.concatenate([sub_row[...].astype(F32), cluster_row[...].astype(F32), pad], axis=1)
    value = jnp.broadcast_to(row, rows.shape).astype(BF)
    edge[count:, :] = value
    rows[...] = value
    for copy in large:
        copy.wait()


def prepare_kernel(
    own, sub_count, cluster_count,
    tile_dst_hbm, tile_src_hbm, recv_sub_hbm, recv_cluster_hbm, tile_weight_hbm,
    features_hbm, w_self_hbm, w_neigh_hbm, grad_out_hbm, bias_hbm,
    dense, choice, features, w_self, w_neigh, grad_out, bias,
    tile_dst, tile_src, recv_sub, recv_cluster, tile_weight, sems,
):
    size = tile_weight.shape[1]
    step = tile_weight.shape[0] // CHUNKS
    pairs = (
        (tile_dst_hbm, tile_dst), (tile_src_hbm, tile_src), (recv_sub_hbm, recv_sub),
        (recv_cluster_hbm, recv_cluster),
        *(
            (tile_weight_hbm.at[i * step : (i + 1) * step], tile_weight.at[i * step : (i + 1) * step])
            for i in range(CHUNKS)
        ),
        (features_hbm, features), (w_self_hbm, w_self), (w_neigh_hbm, w_neigh),
        (grad_out_hbm, grad_out), (bias_hbm, bias),
    )
    copies = [pltpu.make_async_copy(a, b, sems.at[i]) for i, (a, b) in enumerate(pairs)]
    for copy in copies:
        copy.start()
    sub_id = lax.axis_index("sub")
    cluster_id = lax.axis_index("cluster")
    dense[...] = jnp.zeros_like(dense)
    for copy in copies[: 4 + CHUNKS]:
        copy.wait()

    def place(t, carry):
        src = tile_src[t]
        from_sub = own + ((src - own) ^ sub_id)
        from_cluster = own + sub_count + ((src - own - sub_count) ^ cluster_id)
        slot = jnp.where(src < own, src, jnp.where(src < own + sub_count, from_sub, from_cluster))
        dst = pl.ds(pl.multiple_of(tile_dst[t] * size, size), size)
        col = pl.ds(pl.multiple_of(slot * size, size), size)
        dense[dst, col] = dense[dst, col] + tile_weight[t]
        return carry

    lax.fori_loop(0, tile_weight.shape[0], place, 0, unroll=4)
    for d in range(sub_count):
        index = recv_sub[0, sub_id ^ d].astype(F32)
        choice[d : d + 1, :] = jnp.full((1, choice.shape[1]), index, F32)
    for d in range(cluster_count):
        index = recv_cluster[0, cluster_id ^ d].astype(F32)
        choice[sub_count + d : sub_count + d + 1, :] = jnp.full((1, choice.shape[1]), index, F32)
    for copy in copies[4 + CHUNKS :]:
        copy.wait()


def index_row(message, size):
    return message[2 * size : 2 * size + EXTRA, :].astype(F32)[0:1, :]


def lane_of(row, lane):
    lanes = lax.broadcasted_iota(jnp.int32, row.shape, 1)
    return jnp.sum(jnp.where(lanes == lane, row, 0.0), axis=1, keepdims=True)


def pick(message, index, size):
    return jnp.where(
        index > 0.5, message[size : 2 * size, :].astype(F32), message[0:size, :].astype(F32)
    ).astype(BF)


def rows_kernel(message, out):
    out[...] = message[message.shape[0] - EXTRA :, :]


def relay_kernel(sub_count, d, far, rows, near, out):
    size = out.shape[0]
    index = lane_of(index_row(near, size), sub_count + (lax.axis_index("cluster") ^ d))
    out[...] = pick(far, index, size)


def trade_kernel(even, *rest):
    messages, (sibling, out) = rest[:-2], rest[-2:]
    size = out.shape[0] // len(even) - EXTRA
    row = sibling[...].astype(F32)[0:1, :]
    for i, (d, message) in enumerate(zip(even, messages)):
        index = lane_of(row, lax.axis_index("sub") ^ d)
        out[i * size : (i + 1) * size, :] = pick(message, index, size)
        at = len(even) * size + i * EXTRA
        out[at : at + EXTRA, :] = message[2 * size :, :]


def turn_kernel(*rest):
    messages, out = rest[:-1], rest[-1]
    size = out.shape[0] // len(messages)
    for i, message in enumerate(messages):
        last = message.shape[0]
        out[i * size : (i + 1) * size, :] = message[last - size : last, :]


def halo_sum(choice, dense, own, halos, refs, halo):
    size = dense.shape[0] // own
    columns = []
    for i, (slot, at, row, picked) in enumerate(halos):
        if picked:
            block = refs[at][row : row + size, :]
        else:
            block = pick(refs[at], choice[slot : slot + 1, :], size)
        halo[i * size : (i + 1) * size, :] = block
        columns.append(dense[:, (own + slot) * size : (own + slot + 1) * size])
    return dot(jnp.concatenate(columns, axis=1), halo[...])


def flip_kernel(size, dense, dense_t):
    for at in range(0, dense.shape[1], size):
        dense_t[at : at + size, :] = dense[:, at : at + size].T


def first_kernel(own, halos, choice, dense, features, w_self, bias, *rest):
    refs, (total, own_pre, inverse, halo) = rest[:-4], rest[-4:]
    size = dense.shape[0] // own
    count = dense[:, 0:size].astype(F32)
    for at in range(size, dense.shape[1], size):
        count = count + dense[:, at : at + size].astype(F32)
    degree = jnp.sum(count, axis=1, keepdims=True)
    inverse[...] = jnp.broadcast_to(1.0 / (degree + 1.0), inverse.shape)
    total[...] = dot(dense[:, 0 : own * size], features[...]) + halo_sum(
        choice, dense, own, halos, refs, halo
    )
    own_pre[...] = dot(features[...], w_self[...]) + bias[...].reshape(1, -1)


def near_kernel(own, halos, choice, dense, before, *rest):
    refs, (total, halo) = rest[:-2], rest[-2:]
    total[...] = before[...] + halo_sum(choice, dense, own, halos, refs, halo)


def middle_kernel(
    own, sub_count, cluster_count, halos, received, carried,
    choice, grad_out, w_neigh, dense, dense_t, before, own_pre, inverse,
    *rest,
):
    refs, rest = rest[:received], rest[received:]
    rows, rest = rest[:carried], rest[carried:]
    pairs, rest = rest[: sub_count // 2 - 1], rest[sub_count // 2 - 1 :]
    along, (sibling, kept, spread, grad_pre, halo) = rest[:-5], rest[-5:]
    size = dense.shape[0] // own
    aggregate = before[...] + halo_sum(choice, dense, own, halos, refs, halo)
    inv = jnp.concatenate([inverse[...]] * (grad_out.shape[1] // size), axis=1)
    mean = (aggregate * inv).astype(BF)
    pre = own_pre[...] + dot(mean, w_neigh[...])
    grad = (grad_out[...].astype(F32) * gelu_slope(pre)).astype(BF)
    grad_pre[...] = grad
    spread[...] = (dot_right_transposed(grad, w_neigh[...]) * inv).astype(BF)

    def partial(slot, count=1):
        rows = slice((own + slot) * size, (own + slot + count) * size)
        return dot(dense_t[rows, :], spread[...]).astype(BF)

    for i, target in enumerate(pairs):
        target[...] = partial(2 * (i + 1), 2)
    for i, target in enumerate(along):
        target[0:size, :] = partial(sub_count + 1 + i)
    for i, value in enumerate(rows):
        along[0][size + i * EXTRA : size + (i + 1) * EXTRA, :] = value[...]
    sibling[...] = partial(1)
    kept[0] = partial(0)
    kept[1] = partial(sub_count)


def split(total, value, second, size):
    zero = jnp.zeros_like(value)
    total[0:size, :] = total[0:size, :] + jnp.where(second, zero, value)
    total[size : 2 * size, :] = total[size : 2 * size, :] + jnp.where(second, value, zero)


def own_kernel(own, sub_count, rows, received, *rest):
    messages, rest = rest[:received], rest[received:]
    choice, w_self, dense_t, kept, spread, grad_pre, total, owner = rest
    size = kept.shape[1]
    width = total.shape[1]
    total[...] = dot_right_transposed(grad_pre[...], w_self[...]) + dot(
        dense_t[0 : own * size, :], spread[...]
    )
    for i, slot in enumerate((0, sub_count)):
        split(total, kept[i].astype(F32), choice[slot : slot + 1, :] > 0.5, size)
    for slot, at, row in rows:
        lane = lax.axis_index("sub")
        if slot > sub_count:
            lane = sub_count + lax.axis_index("cluster")
        index = lane_of(messages[at][row : row + EXTRA, :].astype(F32)[0:1, :], lane)
        owner[slot : slot + 1, :] = jnp.broadcast_to(index, (1, width))


def add_kernel(own, sub_count, parts, rows, owner, before, *rest):
    received, total = rest[:-1], rest[-1]
    size = total.shape[0] // own
    total[...] = before[...]
    for slot, at, row in parts:
        value = received[at][row : row + size, :].astype(F32)
        index = owner[slot : slot + 1, :]
        if slot in rows:
            where, first = rows[slot]
            indices = received[where][first : first + EXTRA, :].astype(F32)[0:1, :]
            index = lane_of(indices, sub_count + lax.axis_index("cluster"))
        split(total, value, index > 0.5, size)


def final_kernel(own, parts, owner, total, *rest):
    received, (out, done, sems) = rest[:-3], rest[-3:]
    size = total.shape[0] // own
    copies = []

    def leave(first, last, value):
        done[first:last, :] = value.astype(BF)
        copies.append(
            pltpu.make_async_copy(
                done.at[first:last, :], out.at[first:last, :], sems.at[len(copies)]
            )
        )
        copies[-1].start()

    leave(2 * size, own * size, total[2 * size :, :])
    for block in range(2):
        value = total[block * size : (block + 1) * size, :]
        for slot, at, row in parts:
            index = owner[slot : slot + 1, :]
            mine = index > 0.5 if block else index <= 0.5
            value = value + jnp.where(mine, received[at][row : row + size, :].astype(F32), 0.0)
        leave(block * size, (block + 1) * size, value)
    for copy in copies:
        copy.wait()


def swap(value, axis, count, d):
    return lax.ppermute(value, axis, [(i, i ^ d) for i in range(count)])


def after(value, other):
    return lax.optimization_barrier((value, other))[0]


def in_hbm(value):
    return pltpu.with_memory_space_constraint(value, pltpu.HBM)


def cost(flops, moved):
    return pl.CostEstimate(flops=flops, bytes_accessed=moved, transcendentals=0)


def shards(
    features, grad_out, w_self, w_neigh, bias, tile_dst, tile_src, tile_weight, recv_sub, recv_cluster
):
    sub_count = lax.axis_size("sub")
    cluster_count = lax.axis_size("cluster")
    peers = sub_count + cluster_count - 2
    size = tile_weight.shape[1]
    rows, width = features.shape
    own = rows // size
    slots = own + sub_count + cluster_count
    counts = (own, sub_count, cluster_count)

    wide = jax.ShapeDtypeStruct((rows, width), F32)
    narrow = jax.ShapeDtypeStruct((rows, width), BF)
    square = jax.ShapeDtypeStruct((width, width), BF)
    block = jax.ShapeDtypeStruct((size, width), BF)
    marks = jax.ShapeDtypeStruct((sub_count + cluster_count, width), F32)

    edge, rows_only = pl.pallas_call(
        edge_kernel,
        out_shape=[
            jax.ShapeDtypeStruct((BOUNDARY * size + EXTRA, width), BF),
            jax.ShapeDtypeStruct((EXTRA, width), BF),
        ],
        in_specs=[HBM] * 3,
        out_specs=[VMEM] * 2,
        scratch_shapes=[
            pltpu.VMEM(recv_sub.shape, jnp.int32),
            pltpu.VMEM(recv_cluster.shape, jnp.int32),
            pltpu.SemaphoreType.DMA((2 + CHUNKS,)),
        ],
        compiler_params=PARAMS,
        cost_estimate=cost(1024, 256 * 1024),
        name="edge",
    )(in_hbm(recv_sub), in_hbm(recv_cluster), in_hbm(features))

    def along(value, d):
        return swap(value, "cluster", cluster_count, d)

    def across(value, d):
        return swap(value, "sub", sub_count, d)

    even = list(range(2, sub_count, 2))
    direct = list(range(2, cluster_count, 2))
    relayed = list(range(3, cluster_count, 2))
    rows_at = BOUNDARY * size
    got = {0: (edge, 0, False, rows_at), sub_count: (edge, 0, False, rows_at)}
    for d in direct:
        got[sub_count + d] = (along(edge, d), 0, False, rows_at)
    for d in even:
        got[d] = (across(edge, d), 0, False, rows_at)
    got[sub_count + 1] = (along(edge, 1), 0, False, rows_at)
    dense, choice, features, w_self, w_neigh, grad_out, bias = pl.pallas_call(
        functools.partial(prepare_kernel, *counts),
        out_shape=[
            jax.ShapeDtypeStruct((rows, slots * size), BF),
            marks,
            narrow,
            square,
            square,
            narrow,
            jax.ShapeDtypeStruct(bias.shape, F32),
        ],
        in_specs=[HBM] * 10,
        out_specs=[VMEM] * 7,
        scratch_shapes=[
            pltpu.SMEM(tile_dst.shape, jnp.int32),
            pltpu.SMEM(tile_src.shape, jnp.int32),
            pltpu.SMEM(recv_sub.shape, jnp.int32),
            pltpu.SMEM(recv_cluster.shape, jnp.int32),
            pltpu.VMEM(tile_weight.shape, BF),
            pltpu.SemaphoreType.DMA((9 + CHUNKS,)),
        ],
        compiler_params=PARAMS,
        cost_estimate=cost(10**8, 6 * 1024 * 1024),
        name="prepare",
    )(
        *map(in_hbm, (tile_dst, tile_src, recv_sub, recv_cluster, tile_weight)),
        *map(in_hbm, (features, w_self, w_neigh, grad_out, bias)),
    )

    def call(kernel, out_shape, name, flops, *operands):
        return pl.pallas_call(
            kernel,
            out_shape=out_shape,
            in_specs=[VMEM] * len(operands),
            out_specs=jax.tree.map(lambda _: VMEM, out_shape),
            compiler_params=PARAMS,
            cost_estimate=cost(flops, 1024 * 1024),
            name=name,
        )(*operands)

    def unique(slots):
        arrays, at = [], {}
        for slot in slots:
            known = [i for i, array in enumerate(arrays) if array is got[slot][0]]
            at[slot] = known[0] if known else len(arrays)
            if not known:
                arrays.append(got[slot][0])
        return arrays, at

    def sum_call(kernel, out_shape, name, slots, *operands):
        arrays, at = unique(slots)
        halos = [(slot, at[slot], got[slot][1], got[slot][2]) for slot in slots]
        return pl.pallas_call(
            functools.partial(kernel, own, halos),
            out_shape=out_shape,
            in_specs=[VMEM] * (len(operands) + len(arrays)),
            out_specs=jax.tree.map(lambda _: VMEM, out_shape),
            scratch_shapes=[pltpu.VMEM((len(slots) * size, width), BF)],
            compiler_params=PARAMS,
            cost_estimate=cost(dict(first=10**9, near=10**9, late=10**10)[name], 3 * 1024 * 1024),
            name=name,
        )(*operands, *arrays)

    carried = []
    for d in relayed:
        far = got[sub_count + d - 1][0]
        far_rows = call(
            rows_kernel, jax.ShapeDtypeStruct((EXTRA, width), BF), "rows", 10**9, far
        )
        value = call(
            functools.partial(relay_kernel, sub_count, d - 1),
            block,
            "relay", 10**6, far, far_rows, got[sub_count + 1][0],
        )
        carried.append(far_rows)
        got[sub_count + d] = (along(value, 1), 0, True, None)
    first_sum, own_pre, inverse = sum_call(
        first_kernel, [wide, wide, jax.ShapeDtypeStruct((rows, size), F32)], "first", [0, sub_count, *(sub_count + d for d in direct)],
        choice, dense, features, w_self, bias,
    )
    traded = [0, *even]
    sibling_rows = across(after(rows_only, value), 1)
    value = call(
        functools.partial(trade_kernel, traded),
        jax.ShapeDtypeStruct((len(traded) * (size + EXTRA), width), BF),
        "trade", 10**6, *[got[d][0] for d in traded], after(sibling_rows, (choice, value)),
    )
    trade_value = value
    value = across(value, 1)
    for i, d in enumerate(traded):
        got[d + 1] = (value, i * size, True, len(traded) * size + i * EXTRA)
    near_sum = sum_call(
        near_kernel, wide, "near", [sub_count + 1, *even], after(choice, trade_value), dense, first_sum
    )
    dense_t = call(
        functools.partial(flip_kernel, size), jax.ShapeDtypeStruct((slots * size, rows), BF), "flip", 10**7,
        after(dense, near_sum),
    )
    if relayed:
        slots_late = [sub_count + d for d in relayed]
        near_sum = sum_call(
            near_kernel, wide, "late", slots_late, after(choice, dense_t), dense, near_sum
        )

    late = [1, *(d + 1 for d in even)]
    late_arrays, late_at = unique(late)
    late_halos = [(slot, late_at[slot], got[slot][1], got[slot][2]) for slot in late]
    outs = pl.pallas_call(
        functools.partial(middle_kernel, *counts, late_halos, len(late_arrays), len(carried)),
        out_shape=[jax.ShapeDtypeStruct((2 * size, width), BF)] * len(even)
        + [jax.ShapeDtypeStruct((size + len(carried) * EXTRA, width), BF)]
        + [block] * (cluster_count - 1)
        + [jax.ShapeDtypeStruct((2, size, width), BF), narrow, narrow],
        in_specs=[VMEM] * (8 + len(late_arrays) + len(carried)),
        out_specs=[VMEM] * (len(even) + cluster_count + 3),
        scratch_shapes=[pltpu.VMEM((len(late) * size, width), BF)],
        compiler_params=PARAMS,
        cost_estimate=cost(2 * rows * slots * size * width, 6 * 1024 * 1024),
        name="middle",
    )(
        choice, grad_out, w_neigh, dense, dense_t, near_sum, own_pre, inverse,
        *late_arrays, *carried,
    )
    *sent, sibling, kept, spread, grad_pre = outs

    far = [(sub_count + d, along(sent[len(even) + d - 1], d)) for d in range(1, cluster_count)]
    near = [(d, across(value, d)) for d, value in zip(even, sent)]
    soon, rest = near[-1:], near[:-1]
    early = call(
        turn_kernel, jax.ShapeDtypeStruct((2 * size, width), BF), "early", 10**8,
        sibling, *[value for _, value in soon],
    )
    order = [sub_count + 1, *(sub_count + d for d in direct), *even, *(d + 1 for d in even), 1]
    arrays, at = unique(order)
    total, owner = pl.pallas_call(
        functools.partial(
            own_kernel, own, sub_count, [(slot, at[slot], got[slot][3]) for slot in order],
            len(arrays),
        ),
        out_shape=[wide, marks],
        in_specs=[VMEM] * (6 + len(arrays)),
        out_specs=[VMEM] * 2,
        compiler_params=PARAMS,
        cost_estimate=cost(10**9, 2 * 1024 * 1024),
        name="own",
    )(*arrays, after(choice, early), w_self, dense_t, kept, spread, grad_pre)

    early = across(early, 1)
    turned = call(
        turn_kernel, jax.ShapeDtypeStruct((len(rest) * size, width), BF), "turn", 10**6,
        *[after(value, (total, far[-1][1])) for _, value in rest],
    )
    turned = across(turned, 1)
    more = [*far, *near[::-1]]
    places = {slot: (0, size + i * EXTRA) for i, slot in enumerate(sub_count + d for d in relayed)}
    total = call(
        functools.partial(
            add_kernel, own, sub_count, [(slot, i, 0) for i, (slot, _) in enumerate(more)], places
        ),
        wide, "add", 10**10, owner, total, *[value for _, value in more],
    )
    parts = [(1, 0, 0), *[(d + 1, 0, size) for d, _ in soon]]
    parts += [(d + 1, 1, i * size) for i, (d, _) in enumerate(rest)]
    values = [early]
    return pl.pallas_call(
        functools.partial(final_kernel, own, parts),
        out_shape=narrow,
        in_specs=[VMEM] * (3 + len(values)),
        out_specs=HBM,
        scratch_shapes=[pltpu.VMEM((rows, width), BF), pltpu.SemaphoreType.DMA((3,))],
        compiler_params=PARAMS,
        cost_estimate=cost(rows * width * 4, 1024 * 1024),
        name="final",
    )(owner, total, *values, turned)


def solution(mesh):
    placed = (
        P(("cluster", "sub"), None),
        P(("cluster", "sub"), None),
        P(),
        P(),
        P(),
        P(("cluster", "sub")),
        P(("cluster", "sub")),
        P(("cluster", "sub"), None, None),
        P(("cluster", "sub"), None),
        P(("cluster", "sub"), None),
    )
    return jax.shard_map(
        shards, mesh=mesh, in_specs=placed, out_specs=P(("cluster", "sub"), None), check_vma=False
    )
```

```python
import functools

import jax
import jax.numpy as jnp
from jax import lax
from jax.experimental import pallas as pl
from jax.experimental.pallas import tpu as pltpu
from jax.sharding import PartitionSpec as P

BF = jnp.bfloat16
F32 = jnp.float32
BOUNDARY = 2
EXTRA = 16
CHUNKS = 4
VMEM = pl.BlockSpec(memory_space=pltpu.VMEM)
HBM = pl.BlockSpec(memory_space=pltpu.HBM)
PARAMS = pltpu.CompilerParams(vmem_limit_bytes=24 * 1024 * 1024)


def dot(left, right):
    return jnp.dot(left, right, preferred_element_type=F32)


def dot_right_transposed(left, right):
    return lax.dot_general(left, right, (((1,), (1,)), ((), ())), preferred_element_type=F32)


def gelu_slope(v):
    scale = 0.7978845608028654
    t = jnp.tanh(scale * (v + 0.044715 * v * v * v))
    return 0.5 * (1.0 + t) + (0.5 * scale) * v * (1.0 - t * t) * (1.0 + 3.0 * 0.044715 * v * v)


def edge_kernel(recv_sub, recv_cluster, features, edge, rows, sub_row, cluster_row, sems):
    count = edge.shape[0] - EXTRA
    step = count // CHUNKS
    small = [
        pltpu.make_async_copy(recv_sub, sub_row, sems.at[0]),
        pltpu.make_async_copy(recv_cluster, cluster_row, sems.at[1]),
    ]
    large = []
    for i in range(CHUNKS):
        part = slice(i * step, (i + 1) * step)
        large.append(
            pltpu.make_async_copy(features.at[part, :], edge.at[part, :], sems.at[2 + i])
        )
    for copy in small + large:
        copy.start()
    for copy in small:
        copy.wait()
    sub_count, cluster_count = sub_row.shape[1], cluster_row.shape[1]
    pad = jnp.zeros((1, edge.shape[1] - sub_count - cluster_count), F32)
    row = jnp.concatenate([sub_row[...].astype(F32), cluster_row[...].astype(F32), pad], axis=1)
    value = jnp.broadcast_to(row, rows.shape).astype(BF)
    edge[count:, :] = value
    rows[...] = value
    for copy in large:
        copy.wait()


def prepare_kernel(
    own, sub_count, cluster_count,
    tile_dst_hbm, tile_src_hbm, recv_sub_hbm, recv_cluster_hbm, tile_weight_hbm,
    features_hbm, w_self_hbm, w_neigh_hbm, grad_out_hbm, bias_hbm,
    dense, choice, features, w_self, w_neigh, grad_out, bias,
    tile_dst, tile_src, recv_sub, recv_cluster, tile_weight, sems,
):
    size = tile_weight.shape[1]
    step = tile_weight.shape[0] // CHUNKS
    pairs = (
        (tile_dst_hbm, tile_dst), (tile_src_hbm, tile_src), (recv_sub_hbm, recv_sub),
        (recv_cluster_hbm, recv_cluster),
        *(
            (tile_weight_hbm.at[i * step : (i + 1) * step], tile_weight.at[i * step : (i + 1) * step])
            for i in range(CHUNKS)
        ),
        (features_hbm, features), (w_self_hbm, w_self), (w_neigh_hbm, w_neigh),
        (grad_out_hbm, grad_out), (bias_hbm, bias),
    )
    copies = [pltpu.make_async_copy(a, b, sems.at[i]) for i, (a, b) in enumerate(pairs)]
    for copy in copies:
        copy.start()
    sub_id = lax.axis_index("sub")
    cluster_id = lax.axis_index("cluster")
    dense[...] = jnp.zeros_like(dense)
    for copy in copies[: 4 + CHUNKS]:
        copy.wait()

    def place(t, carry):
        src = tile_src[t]
        from_sub = own + ((src - own) ^ sub_id)
        from_cluster = own + sub_count + ((src - own - sub_count) ^ cluster_id)
        slot = jnp.where(src < own, src, jnp.where(src < own + sub_count, from_sub, from_cluster))
        dst = pl.ds(pl.multiple_of(tile_dst[t] * size, size), size)
        col = pl.ds(pl.multiple_of(slot * size, size), size)
        dense[dst, col] = dense[dst, col] + tile_weight[t]
        return carry

    lax.fori_loop(0, tile_weight.shape[0], place, 0, unroll=4)
    for d in range(sub_count):
        index = recv_sub[0, sub_id ^ d].astype(F32)
        choice[d : d + 1, :] = jnp.full((1, choice.shape[1]), index, F32)
    for d in range(cluster_count):
        index = recv_cluster[0, cluster_id ^ d].astype(F32)
        choice[sub_count + d : sub_count + d + 1, :] = jnp.full((1, choice.shape[1]), index, F32)
    for copy in copies[4 + CHUNKS :]:
        copy.wait()


def index_row(message, size):
    return message[2 * size : 2 * size + EXTRA, :].astype(F32)[0:1, :]


def lane_of(row, lane):
    lanes = lax.broadcasted_iota(jnp.int32, row.shape, 1)
    return jnp.sum(jnp.where(lanes == lane, row, 0.0), axis=1, keepdims=True)


def pick(message, index, size):
    return jnp.where(
        index > 0.5, message[size : 2 * size, :].astype(F32), message[0:size, :].astype(F32)
    ).astype(BF)


def rows_kernel(message, out):
    out[...] = message[message.shape[0] - EXTRA :, :]


def relay_kernel(sub_count, d, far, rows, near, out):
    size = out.shape[0]
    index = lane_of(index_row(near, size), sub_count + (lax.axis_index("cluster") ^ d))
    out[...] = pick(far, index, size)


def trade_kernel(even, *rest):
    messages, (sibling, out) = rest[:-2], rest[-2:]
    size = out.shape[0] // len(even) - EXTRA
    row = sibling[...].astype(F32)[0:1, :]
    for i, (d, message) in enumerate(zip(even, messages)):
        index = lane_of(row, lax.axis_index("sub") ^ d)
        out[i * size : (i + 1) * size, :] = pick(message, index, size)
        at = len(even) * size + i * EXTRA
        out[at : at + EXTRA, :] = message[2 * size :, :]


def turn_kernel(*rest):
    messages, out = rest[:-1], rest[-1]
    size = out.shape[0] // len(messages)
    for i, message in enumerate(messages):
        last = message.shape[0]
        out[i * size : (i + 1) * size, :] = message[last - size : last, :]


def halo_sum(choice, dense, own, halos, refs, halo):
    size = dense.shape[0] // own
    columns = []
    for i, (slot, at, row, picked) in enumerate(halos):
        if picked:
            block = refs[at][row : row + size, :]
        else:
            block = pick(refs[at], choice[slot : slot + 1, :], size)
        halo[i * size : (i + 1) * size, :] = block
        columns.append(dense[:, (own + slot) * size : (own + slot + 1) * size])
    return dot(jnp.concatenate(columns, axis=1), halo[...])


def flip_kernel(size, dense, dense_t):
    for at in range(0, dense.shape[1], size):
        dense_t[at : at + size, :] = dense[:, at : at + size].T


def first_kernel(own, halos, choice, dense, features, w_self, bias, *rest):
    refs, (total, own_pre, inverse, halo) = rest[:-4], rest[-4:]
    size = dense.shape[0] // own
    count = dense[:, 0:size].astype(F32)
    for at in range(size, dense.shape[1], size):
        count = count + dense[:, at : at + size].astype(F32)
    degree = jnp.sum(count, axis=1, keepdims=True)
    inverse[...] = jnp.broadcast_to(1.0 / (degree + 1.0), inverse.shape)
    total[...] = dot(dense[:, 0 : own * size], features[...]) + halo_sum(
        choice, dense, own, halos, refs, halo
    )
    own_pre[...] = dot(features[...], w_self[...]) + bias[...].reshape(1, -1)


def near_kernel(own, halos, choice, dense, before, *rest):
    refs, (total, halo) = rest[:-2], rest[-2:]
    total[...] = before[...] + halo_sum(choice, dense, own, halos, refs, halo)


def middle_kernel(
    own, sub_count, cluster_count, halos, received, carried,
    choice, grad_out, w_neigh, dense, dense_t, before, own_pre, inverse,
    *rest,
):
    refs, rest = rest[:received], rest[received:]
    rows, rest = rest[:carried], rest[carried:]
    pairs, rest = rest[: sub_count // 2 - 1], rest[sub_count // 2 - 1 :]
    along, (sibling, kept, spread, grad_pre, halo) = rest[:-5], rest[-5:]
    size = dense.shape[0] // own
    aggregate = before[...] + halo_sum(choice, dense, own, halos, refs, halo)
    inv = jnp.concatenate([inverse[...]] * (grad_out.shape[1] // size), axis=1)
    mean = (aggregate * inv).astype(BF)
    pre = own_pre[...] + dot(mean, w_neigh[...])
    grad = (grad_out[...].astype(F32) * gelu_slope(pre)).astype(BF)
    grad_pre[...] = grad
    spread[...] = (dot_right_transposed(grad, w_neigh[...]) * inv).astype(BF)

    def partial(slot, count=1):
        rows = slice((own + slot) * size, (own + slot + count) * size)
        return dot(dense_t[rows, :], spread[...]).astype(BF)

    for i, target in enumerate(pairs):
        target[...] = partial(2 * (i + 1), 2)
    for i, target in enumerate(along):
        target[0:size, :] = partial(sub_count + 1 + i)
    for i, value in enumerate(rows):
        along[0][size + i * EXTRA : size + (i + 1) * EXTRA, :] = value[...]
    sibling[...] = partial(1)
    kept[0] = partial(0)
    kept[1] = partial(sub_count)


def split(total, value, second, size):
    zero = jnp.zeros_like(value)
    total[0:size, :] = total[0:size, :] + jnp.where(second, zero, value)
    total[size : 2 * size, :] = total[size : 2 * size, :] + jnp.where(second, value, zero)


def own_kernel(own, sub_count, rows, received, *rest):
    messages, rest = rest[:received], rest[received:]
    choice, w_self, dense_t, kept, spread, grad_pre, total, owner = rest
    size = kept.shape[1]
    width = total.shape[1]
    total[...] = dot_right_transposed(grad_pre[...], w_self[...]) + dot(
        dense_t[0 : own * size, :], spread[...]
    )
    for i, slot in enumerate((0, sub_count)):
        split(total, kept[i].astype(F32), choice[slot : slot + 1, :] > 0.5, size)
    for slot, at, row in rows:
        lane = lax.axis_index("sub")
        if slot > sub_count:
            lane = sub_count + lax.axis_index("cluster")
        index = lane_of(messages[at][row : row + EXTRA, :].astype(F32)[0:1, :], lane)
        owner[slot : slot + 1, :] = jnp.broadcast_to(index, (1, width))


def add_kernel(own, sub_count, parts, rows, owner, before, *rest):
    received, total = rest[:-1], rest[-1]
    size = total.shape[0] // own
    total[...] = before[...]
    for slot, at, row in parts:
        value = received[at][row : row + size, :].astype(F32)
        index = owner[slot : slot + 1, :]
        if slot in rows:
            where, first = rows[slot]
            indices = received[where][first : first + EXTRA, :].astype(F32)[0:1, :]
            index = lane_of(indices, sub_count + lax.axis_index("cluster"))
        split(total, value, index > 0.5, size)


def final_kernel(own, parts, owner, total, *rest):
    received, (out, done, sems) = rest[:-3], rest[-3:]
    size = total.shape[0] // own
    copies = []

    def leave(first, last, value):
        done[first:last, :] = value.astype(BF)
        copies.append(
            pltpu.make_async_copy(
                done.at[first:last, :], out.at[first:last, :], sems.at[len(copies)]
            )
        )
        copies[-1].start()

    leave(2 * size, own * size, total[2 * size :, :])
    for block in range(2):
        value = total[block * size : (block + 1) * size, :]
        for slot, at, row in parts:
            index = owner[slot : slot + 1, :]
            mine = index > 0.5 if block else index <= 0.5
            value = value + jnp.where(mine, received[at][row : row + size, :].astype(F32), 0.0)
        leave(block * size, (block + 1) * size, value)
    for copy in copies:
        copy.wait()


def swap(value, axis, count, d):
    return lax.ppermute(value, axis, [(i, i ^ d) for i in range(count)])


def after(value, other):
    return lax.optimization_barrier((value, other))[0]


def in_hbm(value):
    return pltpu.with_memory_space_constraint(value, pltpu.HBM)


def cost(flops, moved):
    return pl.CostEstimate(flops=flops, bytes_accessed=moved, transcendentals=0)


def shards(
    features, grad_out, w_self, w_neigh, bias, tile_dst, tile_src, tile_weight, recv_sub, recv_cluster
):
    sub_count = lax.axis_size("sub")
    cluster_count = lax.axis_size("cluster")
    peers = sub_count + cluster_count - 2
    size = tile_weight.shape[1]
    rows, width = features.shape
    own = rows // size
    slots = own + sub_count + cluster_count
    counts = (own, sub_count, cluster_count)

    wide = jax.ShapeDtypeStruct((rows, width), F32)
    narrow = jax.ShapeDtypeStruct((rows, width), BF)
    square = jax.ShapeDtypeStruct((width, width), BF)
    block = jax.ShapeDtypeStruct((size, width), BF)
    marks = jax.ShapeDtypeStruct((sub_count + cluster_count, width), F32)

    edge, rows_only = pl.pallas_call(
        edge_kernel,
        out_shape=[
            jax.ShapeDtypeStruct((BOUNDARY * size + EXTRA, width), BF),
            jax.ShapeDtypeStruct((EXTRA, width), BF),
        ],
        in_specs=[HBM] * 3,
        out_specs=[VMEM] * 2,
        scratch_shapes=[
            pltpu.VMEM(recv_sub.shape, jnp.int32),
            pltpu.VMEM(recv_cluster.shape, jnp.int32),
            pltpu.SemaphoreType.DMA((2 + CHUNKS,)),
        ],
        compiler_params=PARAMS,
        cost_estimate=cost(1024, 256 * 1024),
        name="edge",
    )(in_hbm(recv_sub), in_hbm(recv_cluster), in_hbm(features))

    def along(value, d):
        return swap(value, "cluster", cluster_count, d)

    def across(value, d):
        return swap(value, "sub", sub_count, d)

    even = list(range(2, sub_count, 2))
    direct = list(range(2, cluster_count, 2))
    relayed = list(range(3, cluster_count, 2))
    rows_at = BOUNDARY * size
    got = {0: (edge, 0, False, rows_at), sub_count: (edge, 0, False, rows_at)}
    for d in direct:
        got[sub_count + d] = (along(edge, d), 0, False, rows_at)
    for d in even:
        got[d] = (across(edge, d), 0, False, rows_at)
    got[sub_count + 1] = (along(edge, 1), 0, False, rows_at)
    dense, choice, features, w_self, w_neigh, grad_out, bias = pl.pallas_call(
        functools.partial(prepare_kernel, *counts),
        out_shape=[
            jax.ShapeDtypeStruct((rows, slots * size), BF),
            marks,
            narrow,
            square,
            square,
            narrow,
            jax.ShapeDtypeStruct(bias.shape, F32),
        ],
        in_specs=[HBM] * 10,
        out_specs=[VMEM] * 7,
        scratch_shapes=[
            pltpu.SMEM(tile_dst.shape, jnp.int32),
            pltpu.SMEM(tile_src.shape, jnp.int32),
            pltpu.SMEM(recv_sub.shape, jnp.int32),
            pltpu.SMEM(recv_cluster.shape, jnp.int32),
            pltpu.VMEM(tile_weight.shape, BF),
            pltpu.SemaphoreType.DMA((9 + CHUNKS,)),
        ],
        compiler_params=PARAMS,
        cost_estimate=cost(10**8, 6 * 1024 * 1024),
        name="prepare",
    )(
        *map(in_hbm, (tile_dst, tile_src, recv_sub, recv_cluster, tile_weight)),
        *map(in_hbm, (features, w_self, w_neigh, grad_out, bias)),
    )

    def call(kernel, out_shape, name, flops, *operands):
        return pl.pallas_call(
            kernel,
            out_shape=out_shape,
            in_specs=[VMEM] * len(operands),
            out_specs=jax.tree.map(lambda _: VMEM, out_shape),
            compiler_params=PARAMS,
            cost_estimate=cost(flops, 1024 * 1024),
            name=name,
        )(*operands)

    def unique(slots):
        arrays, at = [], {}
        for slot in slots:
            known = [i for i, array in enumerate(arrays) if array is got[slot][0]]
            at[slot] = known[0] if known else len(arrays)
            if not known:
                arrays.append(got[slot][0])
        return arrays, at

    def sum_call(kernel, out_shape, name, slots, *operands):
        arrays, at = unique(slots)
        halos = [(slot, at[slot], got[slot][1], got[slot][2]) for slot in slots]
        return pl.pallas_call(
            functools.partial(kernel, own, halos),
            out_shape=out_shape,
            in_specs=[VMEM] * (len(operands) + len(arrays)),
            out_specs=jax.tree.map(lambda _: VMEM, out_shape),
            scratch_shapes=[pltpu.VMEM((len(slots) * size, width), BF)],
            compiler_params=PARAMS,
            cost_estimate=cost(dict(first=10**9, near=10**9, late=10**10)[name], 3 * 1024 * 1024),
            name=name,
        )(*operands, *arrays)

    dense_t = call(
        functools.partial(flip_kernel, size), jax.ShapeDtypeStruct((slots * size, rows), BF), "flip", 10**7,
        after(dense, choice),
    )
    carried = []
    for d in relayed:
        far = got[sub_count + d - 1][0]
        far_rows = call(
            rows_kernel, jax.ShapeDtypeStruct((EXTRA, width), BF), "rows", 10**9, far
        )
        value = call(
            functools.partial(relay_kernel, sub_count, d - 1),
            block,
            "relay", 10**6, far, far_rows, after(got[sub_count + 1][0], dense_t),
        )
        carried.append(far_rows)
        got[sub_count + d] = (along(value, 1), 0, True, None)
    first_sum, own_pre, inverse = sum_call(
        first_kernel, [wide, wide, jax.ShapeDtypeStruct((rows, size), F32)], "first", [0, sub_count, *(sub_count + d for d in direct)],
        choice, dense, features, w_self, bias,
    )
    traded = [0, *even]
    sibling_rows = across(after(rows_only, value), 1)
    value = call(
        functools.partial(trade_kernel, traded),
        jax.ShapeDtypeStruct((len(traded) * (size + EXTRA), width), BF),
        "trade", 10**6, *[got[d][0] for d in traded], after(sibling_rows, (choice, value)),
    )
    trade_value = value
    value = across(value, 1)
    for i, d in enumerate(traded):
        got[d + 1] = (value, i * size, True, len(traded) * size + i * EXTRA)
    near_sum = sum_call(
        near_kernel, wide, "near", [sub_count + 1, *even], after(choice, trade_value), dense, first_sum
    )
    if relayed:
        slots_late = [sub_count + d for d in relayed]
        near_sum = sum_call(
            near_kernel, wide, "late", slots_late, choice, dense, near_sum
        )

    late = [1, *(d + 1 for d in even)]
    late_arrays, late_at = unique(late)
    late_halos = [(slot, late_at[slot], got[slot][1], got[slot][2]) for slot in late]
    outs = pl.pallas_call(
        functools.partial(middle_kernel, *counts, late_halos, len(late_arrays), len(carried)),
        out_shape=[jax.ShapeDtypeStruct((2 * size, width), BF)] * len(even)
        + [jax.ShapeDtypeStruct((size + len(carried) * EXTRA, width), BF)]
        + [block] * (cluster_count - 1)
        + [jax.ShapeDtypeStruct((2, size, width), BF), narrow, narrow],
        in_specs=[VMEM] * (8 + len(late_arrays) + len(carried)),
        out_specs=[VMEM] * (len(even) + cluster_count + 3),
        scratch_shapes=[pltpu.VMEM((len(late) * size, width), BF)],
        compiler_params=PARAMS,
        cost_estimate=cost(2 * rows * slots * size * width, 6 * 1024 * 1024),
        name="middle",
    )(
        choice, grad_out, w_neigh, dense, dense_t, near_sum, own_pre, inverse,
        *late_arrays, *carried,
    )
    *sent, sibling, kept, spread, grad_pre = outs

    far = [(sub_count + d, along(sent[len(even) + d - 1], d)) for d in range(1, cluster_count)]
    near = [(d, across(value, d)) for d, value in zip(even, sent)]
    soon, rest = near[-1:], near[:-1]
    early = call(
        turn_kernel, jax.ShapeDtypeStruct((2 * size, width), BF), "early", 10**8,
        sibling, *[value for _, value in soon],
    )
    order = [sub_count + 1, *(sub_count + d for d in direct), *even, *(d + 1 for d in even), 1]
    arrays, at = unique(order)
    total, owner = pl.pallas_call(
        functools.partial(
            own_kernel, own, sub_count, [(slot, at[slot], got[slot][3]) for slot in order],
            len(arrays),
        ),
        out_shape=[wide, marks],
        in_specs=[VMEM] * (6 + len(arrays)),
        out_specs=[VMEM] * 2,
        compiler_params=PARAMS,
        cost_estimate=cost(10**9, 2 * 1024 * 1024),
        name="own",
    )(*arrays, after(choice, (far[-1][1], early)), w_self, dense_t, kept, spread, grad_pre)

    early = across(early, 1)
    turned = call(
        turn_kernel, jax.ShapeDtypeStruct((len(rest) * size, width), BF), "turn", 10**6,
        *[after(value, total) for _, value in rest],
    )
    turned = across(turned, 1)
    more = [*far, *near[::-1]]
    places = {slot: (0, size + i * EXTRA) for i, slot in enumerate(sub_count + d for d in relayed)}
    total = call(
        functools.partial(
            add_kernel, own, sub_count, [(slot, i, 0) for i, (slot, _) in enumerate(more)], places
        ),
        wide, "add", 10**10, owner, total, *[value for _, value in more],
    )
    parts = [(1, 0, 0), *[(d + 1, 0, size) for d, _ in soon]]
    parts += [(d + 1, 1, i * size) for i, (d, _) in enumerate(rest)]
    values = [early]
    return pl.pallas_call(
        functools.partial(final_kernel, own, parts),
        out_shape=narrow,
        in_specs=[VMEM] * (3 + len(values)),
        out_specs=HBM,
        scratch_shapes=[pltpu.VMEM((rows, width), BF), pltpu.SemaphoreType.DMA((3,))],
        compiler_params=PARAMS,
        cost_estimate=cost(rows * width * 4, 1024 * 1024),
        name="final",
    )(owner, total, *values, turned)


def solution(mesh):
    placed = (
        P(("cluster", "sub"), None),
        P(("cluster", "sub"), None),
        P(),
        P(),
        P(),
        P(("cluster", "sub")),
        P(("cluster", "sub")),
        P(("cluster", "sub"), None, None),
        P(("cluster", "sub"), None),
        P(("cluster", "sub"), None),
    )
    return jax.shard_map(
        shards, mesh=mesh, in_specs=placed, out_specs=P(("cluster", "sub"), None), check_vma=False
    )
```
